32 devices in a mesh: blk: 16 (over z, x, core), cd: 2 (over y).
Axes of the slice: x: 2, y: 2, z: 4, core: 2. Of those that a mesh axis runs over, the one named last changes fastest.
Arguments:
- t2_amps: bfloat16 [1024, 8192], P('blk', 'cd'), may hold values from -6 to 6
- integrals: bfloat16 [512, 64, 1024], P('blk', None, 'cd'), may hold values from -0.1875 to 0.1875
- ab_sym: int32 [512], P('blk'), may hold values from 0 to 7, as said below
- cd_sym: int32 [128], P('cd'), may hold values from 0 to 7, as said below
Outputs:
- ladder: bfloat16 [1024, 32768], P('cd', 'blk')
The draws below stay inside these ranges and needn't reach their ends.
Inputs may be any that keep to these rules, and one draw needn't show every extreme that they name: `ab_sym`: each aligned block of 32 ab tiles (the tiles of one index of blk) holds exactly 4 tiles of every irreducible representation. `cd_sym`: each group of 64 consecutive cd tiles holds exactly 8 tiles of every irreducible representation.
All inputs are finite; a program needn't handle non-finite values.
Results may differ from the reference program's by a relative error of at most 0.015.
Values may be sent and summed in bfloat16 or wider, within the bound.
No kernel may reach another device: no remote copies, remote signals or barrier semaphores. Data moves between devices by JAX's collectives and lax.ppermute only.
A program may use at most 128 MiB of HBM per device.

```python
import jax
import jax.numpy as jnp
from jax import lax

TILE = 64
NSYM = 8
NA_DEV = 32
CT_DEV = 64
KC = 512
NIJ = 1024
NA = 512
NC = 128
N_CD = 2


def balanced_labels(key, blocks, per_block):
    base = jnp.tile(jnp.arange(NSYM, dtype=jnp.int32), per_block // NSYM)
    keys = jax.random.split(key, blocks)
    rows = jax.vmap(lambda k: jax.random.permutation(k, base))(keys)
    return rows.reshape(blocks * per_block).astype(jnp.int32)


def draw_ab_sym(key, part):
    return balanced_labels(jax.random.fold_in(key, 11), NA // NA_DEV, NA_DEV)


def draw_cd_sym(key, part):
    return balanced_labels(jax.random.fold_in(key, 23), NC // CT_DEV, CT_DEV)


def steps_of(rng, dims, pieces, least, high):
    def one(dim, blocks):
        draws = jax.random.uniform(jax.random.fold_in(jax.random.fold_in(rng, 6), dim), (blocks,), jnp.float32, least / len(pieces), high / len(pieces))
        return jnp.repeat(jnp.exp(draws), dims[dim] // blocks).reshape((-1,) + (1,) * (len(dims) - dim - 1))

    loudness = one(*pieces[0])
    for cut in pieces[1:]:
        loudness = loudness * one(*cut)
    return loudness


def scatter_about(rng, extent, width, most, pieces=(), kind=jnp.bfloat16):
    loudness = steps_of(rng, extent, pieces, -0.22, 0.18) if pieces else 1.0
    entries = jax.random.normal(rng, extent, jnp.float32) * width * loudness
    return jnp.minimum(jnp.maximum(entries, -most), most).astype(kind)


def setup_inputs(seed: int = 0) -> dict:
    key_list = jax.random.split(jax.random.key(seed), 5)
    return {
        "t2_amps": scatter_about(key_list[0], (NIJ, NC * TILE), 1.0, 6.0, ((0, 16), (1, 2))),
        "integrals": scatter_about(key_list[1], (NA, TILE, N_CD * KC), (N_CD * KC) ** -0.5, 0.1875, ((0, 16), (2, 2))),
        "ab_sym": draw_ab_sym(jax.random.fold_in(key_list[4], 71), 0),
        "cd_sym": draw_cd_sym(jax.random.fold_in(key_list[4], 71), 0),
    }


def reference(t2_amps, integrals, ab_sym, cd_sym):
    packed = CT_DEV * TILE // NSYM
    per_sym = NA // NSYM
    order_ab = jnp.argsort(ab_sym, stable=True).astype(jnp.int32)
    inverse_ab = jnp.argsort(order_ab, stable=True).astype(jnp.int32)
    ints_sorted = jnp.take(integrals, order_ab, axis=0).reshape(NSYM, per_sym * TILE, N_CD * packed)

    def group_add(group, acc):
        group = jnp.asarray(group).astype(jnp.int32)
        cd_local = lax.dynamic_slice_in_dim(cd_sym, group * CT_DEV, CT_DEV, 0)
        order_cd = jnp.argsort(cd_local, stable=True).astype(jnp.int32)
        amp_part = lax.dynamic_slice_in_dim(t2_amps, group * (CT_DEV * TILE), CT_DEV * TILE, 1)
        amp_part = jnp.take(amp_part.reshape(NIJ, CT_DEV, TILE), order_cd, axis=1)
        amp_part = amp_part.reshape(NIJ, NSYM, packed).astype(jnp.float32)
        int_part = lax.dynamic_slice_in_dim(ints_sorted, group * packed, packed, 2).astype(jnp.float32)
        partial_value = jnp.einsum("isk,smk->ism", amp_part, int_part)
        rounded = lax.optimization_barrier(partial_value.astype(jnp.bfloat16))
        return acc + rounded.astype(jnp.float32)

    start = jnp.zeros((NIJ, NSYM, per_sym * TILE), jnp.float32)
    total = lax.fori_loop(0, N_CD, group_add, start)
    total = jnp.take(total.reshape(NIJ, NA, TILE), inverse_ab, axis=1)
    return total.reshape(NIJ, NA * TILE).astype(jnp.bfloat16)
```

```python
import functools

import jax
import jax.numpy as jnp
from jax import lax
from jax.experimental import pallas as pl
from jax.experimental.pallas import tpu as pltpu
from jax.sharding import PartitionSpec as P

NSYM = 8
CHUNKS = 4
LANES = 128


def half_turned(x):
    half = LANES // 2
    return jnp.concatenate([x[:, half:], x[:, :half]], axis=1)


def rank_tiles(sym_ref, count_ref, order_ref, place_ref, tiles):
    per_sym = tiles // NSYM
    for s in range(NSYM):
        count_ref[s] = s * per_sym

    def step(i, _):
        s = sym_ref[i]
        p = count_ref[s]
        count_ref[s] = p + 1
        order_ref[p] = i
        if place_ref is not None:
            place_ref[i] = p
        return 0

    lax.fori_loop(0, tiles, step, 0)


def sort_kernel(ab_ref, cd_ref, t2_ref, order_ab, place_ab, *rest):
    chunks, (both, count, order_cd) = rest[:-3], rest[-3:]
    cd_tiles = cd_ref.shape[0]
    rank_tiles(cd_ref, count, order_cd, None, cd_tiles)
    rows = t2_ref.shape[0]
    both[0] = t2_ref[...]
    both[1] = half_turned(t2_ref[...])
    left = lax.broadcasted_iota(jnp.int32, (rows, LANES), 1) < LANES // 2
    per_chunk = cd_tiles // 2 // len(chunks)
    for q in range(cd_tiles // 2):
        a, b = order_cd[2 * q], order_cd[2 * q + 1]
        b_col = lax.rem(lax.shift_right_logical(b + 1, 1) + cd_tiles // 2 - 1, cd_tiles // 2)
        a_col = lax.shift_right_logical(a, 1)
        xa = both[a & 1, :, pl.ds(pl.multiple_of(a_col * LANES, LANES), LANES)]
        xb = both[(b & 1) ^ 1, :, pl.ds(pl.multiple_of(b_col * LANES, LANES), LANES)]
        c, off = divmod(q, per_chunk)
        chunks[c][:, off * LANES : (off + 1) * LANES] = jnp.where(left, xa, xb)
    rank_tiles(ab_ref, count, order_ab, place_ab, ab_ref.shape[0])


def sort_amplitudes(t2, ab_sym, cd_sym):
    rows, cols = t2.shape
    ab_tiles = ab_sym.shape[0]
    smem, vmem = pl.BlockSpec(memory_space=pltpu.SMEM), pl.BlockSpec(memory_space=pltpu.VMEM)
    return pl.pallas_call(
        sort_kernel,
        out_shape=[jax.ShapeDtypeStruct((ab_tiles,), jnp.int32)] * 2
        + [jax.ShapeDtypeStruct((rows, cols // CHUNKS), t2.dtype)] * CHUNKS,
        in_specs=[smem, smem, vmem],
        out_specs=[smem, smem] + [vmem] * CHUNKS,
        scratch_shapes=[
            pltpu.VMEM((2, rows, cols), t2.dtype),
            pltpu.SMEM((NSYM,), jnp.int32),
            pltpu.SMEM((cd_sym.shape[0],), jnp.int32),
        ],
        compiler_params=pltpu.CompilerParams(vmem_limit_bytes=16 * 2**20),
        name="sort_amplitudes",
    )(ab_sym, cd_sym, t2)


def contract_kernel(order_ref, group_ref, t2_ref, *rest):
    tiles, out_ref = rest[:-1], rest[-1]
    per_sym = len(tiles) // (NSYM // CHUNKS)
    packed = tiles[0].shape[2]
    width = per_sym * tiles[0].shape[1]
    for s in range(NSYM // CHUNKS):
        ints = jnp.concatenate([t[0] for t in tiles[s * per_sym : (s + 1) * per_sym]], axis=0)
        part = lax.dot_general(
            t2_ref[:, s * packed : (s + 1) * packed],
            ints,
            (((1,), (1,)), ((), ())),
            preferred_element_type=jnp.float32,
        )
        out_ref[:, s * width : (s + 1) * width] = part.astype(out_ref.dtype)


def contract(order, group, t2_chunk, integrals, chunk, out_rows):
    ab_tiles, tile, packed = integrals.shape
    per_chunk = ab_tiles // CHUNKS
    cols = t2_chunk.shape[1]
    block = min(out_rows, 256)
    steps = out_rows // block

    def tile_spec(m):
        return pl.BlockSpec(
            (1, tile, packed), lambda i, order, group: (order[chunk * per_chunk + m], 0, 0)
        )

    return pl.pallas_call(
        contract_kernel,
        out_shape=jax.ShapeDtypeStruct((out_rows, per_chunk * tile), jnp.bfloat16),
        grid_spec=pltpu.PrefetchScalarGridSpec(
            num_scalar_prefetch=2,
            grid=(steps,),
            in_specs=[
                pl.BlockSpec((block, cols), lambda i, order, group: (group[0] * steps + i, 0))
            ]
            + [tile_spec(m) for m in range(per_chunk)],
            out_specs=pl.BlockSpec((block, per_chunk * tile), lambda i, order, group: (i, 0)),
        ),
        compiler_params=pltpu.CompilerParams(vmem_limit_bytes=24 * 2**20),
        cost_estimate=pl.CostEstimate(
            flops=2 * out_rows * per_chunk * tile * packed,
            bytes_accessed=2 * (out_rows * cols + per_chunk * tile * (packed + out_rows)),
            transcendentals=0,
        ),
        name="contract",
    )(order, group, t2_chunk, *([integrals] * per_chunk))


def add_kernel(n_parts, place_ref, *rest):
    parts, out_ref, both = rest[:-2], rest[-2], rest[-1]
    rows, cols = out_ref.shape
    for c in range(CHUNKS):
        group = parts[c * n_parts : (c + 1) * n_parts]
        total = group[0][...].astype(jnp.float32)
        for other in group[1:]:
            total += other[...].astype(jnp.float32)
        width = cols // CHUNKS
        both[0, :, c * width : (c + 1) * width] = total.astype(both.dtype)
    both[1] = half_turned(both[0])
    left = lax.broadcasted_iota(jnp.int32, (rows, LANES), 1) < LANES // 2
    columns = cols // LANES
    for q in range(columns):
        a, b = place_ref[2 * q], place_ref[2 * q + 1]
        b_col = lax.rem(lax.shift_right_logical(b + 1, 1) + columns - 1, columns)
        a_col = lax.shift_right_logical(a, 1)
        xa = both[a & 1, :, pl.ds(pl.multiple_of(a_col * LANES, LANES), LANES)]
        xb = both[(b & 1) ^ 1, :, pl.ds(pl.multiple_of(b_col * LANES, LANES), LANES)]
        out_ref[:, q * LANES : (q + 1) * LANES] = jnp.where(left, xa, xb)


def add_parts(place, parts):
    n_parts = len(parts[0])
    rows, width = parts[0][0].shape
    cols = width * CHUNKS
    block = min(rows, 128)
    spec = pl.BlockSpec((block, width), lambda i: (i, 0))
    return pl.pallas_call(
        functools.partial(add_kernel, n_parts),
        out_shape=jax.ShapeDtypeStruct((rows, cols), jnp.bfloat16),
        grid=(rows // block,),
        in_specs=[pl.BlockSpec(memory_space=pltpu.SMEM)] + [spec] * (CHUNKS * n_parts),
        out_specs=pl.BlockSpec((block, cols), lambda i: (i, 0)),
        scratch_shapes=[pltpu.VMEM((2, block, cols), jnp.bfloat16)],
        compiler_params=pltpu.CompilerParams(vmem_limit_bytes=24 * 2**20),
        name="add_parts",
    )(place, *[p for chunk in parts for p in chunk])


def per_device(t2_amps, integrals, ab_sym, cd_sym):
    n_blk, n_cd = lax.axis_size("blk"), lax.axis_size("cd")
    me = lax.axis_index("cd")
    out_rows = n_blk * t2_amps.shape[0] // n_cd
    order, place, *own = sort_amplitudes(t2_amps, ab_sym, cd_sym)
    gathered = [lax.all_gather(x, "blk", axis=0, tiled=True) for x in own]
    parts = []
    for c in range(CHUNKS):
        got = []
        for by in list(range(1, n_cd)) + [0]:
            group = lax.rem(me + by, n_cd).reshape(1)
            part = contract(order, group, gathered[c], integrals, c, out_rows)
            if by:
                part = lax.ppermute(part, "cd", [(i, (i + by) % n_cd) for i in range(n_cd)])
            got.append(part)
        parts.append(got)
    return add_parts(place, parts)


def solution(mesh):
    in_specs = (P("blk", "cd"), P("blk", None, "cd"), P("blk"), P("cd"))
    out_specs = P("cd", "blk")
    return jax.shard_map(
        per_device, mesh=mesh, in_specs=in_specs, out_specs=out_specs, check_vma=False
    )
```

```python
import functools

import jax
import jax.numpy as jnp
from jax import lax
from jax.experimental import pallas as pl
from jax.experimental.pallas import tpu as pltpu
from jax.sharding import PartitionSpec as P

NSYM = 8
SPLIT = (1, 2, 2, 2, 1)
LANES = 128
VMEM_LIMIT = 56 * 2**20

ANY = pl.BlockSpec(memory_space=pl.ANY)
SMEM = pl.BlockSpec(memory_space=pltpu.SMEM)
VMEM = pl.BlockSpec(memory_space=pltpu.VMEM)


def params():
    return pltpu.CompilerParams(vmem_limit_bytes=VMEM_LIMIT)


def half_turned(x):
    half = LANES // 2
    return jnp.concatenate([x[:, half:], x[:, :half]], axis=1)


def rank_tiles(sym_ref, count_ref, order_ref, place_ref, tiles):
    for s in range(NSYM):
        count_ref[s] = s * (tiles // NSYM)

    def step(i, _):
        s = sym_ref[i]
        p = count_ref[s]
        count_ref[s] = p + 1
        if order_ref is not None:
            order_ref[p] = i
        if place_ref is not None:
            place_ref[i] = p
        return 0

    lax.fori_loop(0, tiles, step, 0)


def pick_pair(both, a, b, left):
    columns = both.shape[2] // LANES
    a_col = lax.shift_right_logical(a, 1)
    b_col = lax.rem(lax.shift_right_logical(b + 1, 1) + columns - 1, columns)
    xa = both[a & 1, :, pl.ds(pl.multiple_of(a_col * LANES, LANES), LANES)]
    xb = both[(b & 1) ^ 1, :, pl.ds(pl.multiple_of(b_col * LANES, LANES), LANES)]
    return jnp.where(left, xa, xb)


def sort_amps_kernel(cd_ref, t2_ref, *rest):
    chunks, (both, count, order, sem) = rest[:-4], rest[-4:]
    rows, cols = t2_ref.shape
    load = pltpu.make_async_copy(t2_ref, both.at[0], sem)
    load.start()
    rank_tiles(cd_ref, count, order, None, cd_ref.shape[0])
    load.wait()
    both[1] = half_turned(both[0])
    left = lax.broadcasted_iota(jnp.int32, (rows, LANES), 1) < LANES // 2
    q = 0
    for chunk in chunks:
        for off in range(chunk.shape[1] // LANES):
            chunk[:, off * LANES : (off + 1) * LANES] = pick_pair(
                both, order[2 * q], order[2 * q + 1], left
            )
            q += 1


def sort_amps(t2, cd_sym):
    rows, cols = t2.shape
    return pl.pallas_call(
        sort_amps_kernel,
        out_shape=[jax.ShapeDtypeStruct((rows, cols // NSYM * m), t2.dtype) for m in SPLIT],
        in_specs=[SMEM, ANY],
        out_specs=[VMEM] * len(SPLIT),
        scratch_shapes=[
            pltpu.VMEM((2, rows, cols), t2.dtype),
            pltpu.SMEM((NSYM,), jnp.int32),
            pltpu.SMEM((cd_sym.shape[0],), jnp.int32),
            pltpu.SemaphoreType.DMA,
        ],
        compiler_params=params(),
        name="sort_amps",
    )(cd_sym, t2)


def sort_ints_kernel(ab_ref, ints_ref, *rest):
    chunks, (count, order, sems) = rest[:-3], rest[-3:]
    rank_tiles(ab_ref, count, order, None, ab_ref.shape[0])
    copies = []
    for chunk in chunks:
        for off in range(chunk.shape[0]):
            p = len(copies)
            copies.append(pltpu.make_async_copy(ints_ref.at[order[p]], chunk.at[off], sems.at[p]))
            copies[-1].start()
    for copy in copies:
        copy.wait()


def sort_ints(integrals, ab_sym):
    tiles, tile, packed = integrals.shape
    return pl.pallas_call(
        sort_ints_kernel,
        out_shape=[
            jax.ShapeDtypeStruct((tiles // NSYM * m, tile, packed), integrals.dtype) for m in SPLIT
        ],
        in_specs=[SMEM, ANY],
        out_specs=[ANY] * len(SPLIT),
        scratch_shapes=[
            pltpu.SMEM((NSYM,), jnp.int32),
            pltpu.SMEM((tiles,), jnp.int32),
            pltpu.SemaphoreType.DMA((tiles,)),
        ],
        compiler_params=params(),
        name="sort_ints",
    )(ab_sym, integrals)


def nothing(*refs):
    pass


def after(x, *earlier):
    return pl.pallas_call(
        nothing,
        out_shape=jax.ShapeDtypeStruct(x.shape, x.dtype),
        in_specs=[ANY] * (1 + len(earlier)),
        out_specs=ANY,
        input_output_aliases={0: 0},
        compiler_params=params(),
        name="after",
    )(x, *earlier)


def contract_kernel(n_cd, *rest):
    blocks, rest = rest[: -2 * n_cd - 4], rest[-2 * n_cd - 4 :]
    own_ref, sib_ref, outs, (lhs, sems) = rest[0], rest[1], rest[2:-2], rest[-2:]
    rows, packed = blocks[0].shape[0], own_ref.shape[2]
    chip = lax.axis_index("blk") // 2
    copies = []
    for i, block in enumerate(blocks):
        first = pl.multiple_of((chip ^ i) * rows, rows)
        copies.append(pltpu.make_async_copy(block, lhs.at[pl.ds(first, rows)], sems.at[i]))
        copies[-1].start()
    for copy in copies:
        copy.wait()
    per_group = lhs.shape[0] // n_cd
    syms = lhs.shape[1] // packed
    width = own_ref.shape[0] // syms * own_ref.shape[1]
    for by in list(range(1, n_cd)) + [0]:
        group = lax.rem(lax.axis_index("cd") + by, n_cd)
        these = pl.ds(pl.multiple_of(group * per_group, per_group), per_group)
        for side, ints_ref in enumerate((own_ref, sib_ref)):
            ints = ints_ref[...].reshape(syms, width, packed)
            for s in range(syms):
                part = lax.dot_general(
                    lhs[these, s * packed : (s + 1) * packed],
                    ints[s],
                    (((1,), (1,)), ((), ())),
                    preferred_element_type=jnp.float32,
                )
                out = outs[2 * by + side]
                out[:, s * width : (s + 1) * width] = part.astype(out.dtype)


def contract(n_cd, blocks, own_ints, sib_ints):
    rows, cols = blocks[0].shape
    all_rows = rows * len(blocks)
    tiles, tile, packed = own_ints.shape
    return pl.pallas_call(
        functools.partial(contract_kernel, n_cd),
        out_shape=[jax.ShapeDtypeStruct((all_rows // n_cd, tiles * tile), jnp.bfloat16)]
        * (2 * n_cd),
        in_specs=[ANY] * len(blocks) + [VMEM] * 2,
        out_specs=[VMEM] * (2 * n_cd),
        scratch_shapes=[
            pltpu.VMEM((all_rows, cols), jnp.bfloat16),
            pltpu.SemaphoreType.DMA((len(blocks),)),
        ],
        compiler_params=params(),
        cost_estimate=pl.CostEstimate(
            flops=4 * all_rows * tiles * tile * packed,
            bytes_accessed=2 * (all_rows * cols + 2 * tiles * tile * (packed + all_rows)),
            transcendentals=0,
        ),
        name="contract",
    )(*blocks, own_ints, sib_ints)


def add_kernel(n_cd, ab_ref, *rest):
    parts, (out_ref, both, count, place) = rest[:-4], rest[-4:]
    rows = both.shape[1]

    @pl.when(pl.program_id(0) == 0)
    def _():
        rank_tiles(ab_ref, count, None, place, ab_ref.shape[0])

    core = lax.rem(lax.axis_index("blk"), 2)
    left = lax.broadcasted_iota(jnp.int32, (rows, LANES), 1) < LANES // 2
    for side in range(2):
        first = 0
        for c in range(len(SPLIT)):
            mine = parts[c * 2 * n_cd + side : (c + 1) * 2 * n_cd : 2]
            total = mine[0][...].astype(jnp.float32)
            for other in mine[1:]:
                total += other[...].astype(jnp.float32)
            both[0, :, first : first + total.shape[1]] = total.astype(both.dtype)
            first += total.shape[1]
        both[1] = half_turned(both[0])
        these = pl.ds(pl.multiple_of((core ^ side) * rows, rows), rows)
        for q in range(out_ref.shape[1] // LANES):
            out_ref[these, q * LANES : (q + 1) * LANES] = pick_pair(
                both, place[2 * q], place[2 * q + 1], left
            )


def add_parts(n_cd, ab_sym, parts, rows):
    all_rows = 2 * parts[0].shape[0]
    cols = sum(p.shape[1] for p in parts[:: 2 * n_cd])
    return pl.pallas_call(
        functools.partial(add_kernel, n_cd),
        out_shape=jax.ShapeDtypeStruct((all_rows, cols), jnp.bfloat16),
        grid=(all_rows // (2 * rows),),
        in_specs=[SMEM] + [pl.BlockSpec((rows, p.shape[1]), lambda i: (i, 0)) for p in parts],
        out_specs=pl.BlockSpec((2 * rows, cols), lambda i: (i, 0)),
        scratch_shapes=[
            pltpu.VMEM((2, rows, cols), jnp.bfloat16),
            pltpu.SMEM((NSYM,), jnp.int32),
            pltpu.SMEM((ab_sym.shape[0],), jnp.int32),
        ],
        compiler_params=params(),
        name="add_parts",
    )(ab_sym, *parts)


def flipped(x, mask):
    return lax.ppermute(x, "blk", [(i, i ^ mask) for i in range(lax.axis_size("blk"))])


def sent(x, by, mask):
    n_blk, n_cd = lax.axis_size("blk"), lax.axis_size("cd")
    if not by:
        return flipped(x, mask)
    if not mask:
        return lax.ppermute(x, "cd", [(i, (i + by) % n_cd) for i in range(n_cd)])
    pairs = [
        (b * n_cd + i, (b ^ mask) * n_cd + (i + by) % n_cd)
        for b in range(n_blk)
        for i in range(n_cd)
    ]
    return lax.ppermute(x, ("blk", "cd"), pairs)


def per_device(t2_amps, integrals, ab_sym, cd_sym):
    n_blk, n_cd = lax.axis_size("blk"), lax.axis_size("cd")
    n_chunks = len(SPLIT)
    z_len = n_blk // 4
    own = list(sort_amps(t2_amps, cd_sym))
    ints = list(sort_ints(integrals, ab_sym))

    along_z = []
    for c in range(n_chunks):
        if c:
            earlier = along_z[max(0, c - 2)][1:]
            own[c] = after(own[c], *earlier)
            ints[c] = after(ints[c], *earlier)
        along_z.append([own[c]] + [flipped(own[c], 4 * d) for d in range(1, z_len)])

    parts = []
    for c in range(n_chunks):
        across = [flipped(x, 2) for x in along_z[c]]
        blocks = [x for pair in zip(along_z[c], across) for x in pair]
        sib_ints = flipped(ints[c], 1)
        made = contract(n_cd, blocks, ints[c], sib_ints)
        for by in range(n_cd):
            for side in range(2):
                part = made[2 * by + side]
                parts.append(sent(part, by, side) if by or side else part)
    return add_parts(n_cd, ab_sym, parts, t2_amps.shape[0])


def solution(mesh):
    in_specs = (P("blk", "cd"), P("blk", None, "cd"), P("blk"), P("cd"))
    out_specs = P("cd", "blk")
    return jax.shard_map(
        per_device, mesh=mesh, in_specs=in_specs, out_specs=out_specs, check_vma=False
    )
```

```python
import functools

import jax
import jax.numpy as jnp
from jax import lax
from jax.experimental import pallas as pl
from jax.experimental.pallas import tpu as pltpu
from jax.sharding import Mesh, PartitionSpec as P

NSYM = 8
SPLIT = (1, 2, 2, 2, 1)
LANES = 128
VMEM_LIMIT = 56 * 2**20

ANY = pl.BlockSpec(memory_space=pl.ANY)
SMEM = pl.BlockSpec(memory_space=pltpu.SMEM)
VMEM = pl.BlockSpec(memory_space=pltpu.VMEM)


def params():
    return pltpu.CompilerParams(vmem_limit_bytes=VMEM_LIMIT)


def half_turned(x):
    half = LANES // 2
    return jnp.concatenate([x[:, half:], x[:, :half]], axis=1)


def rank_tiles(sym_ref, count_ref, order_ref, place_ref, tiles):
    for s in range(NSYM):
        count_ref[s] = s * (tiles // NSYM)

    def step(i, _):
        s = sym_ref[i]
        p = count_ref[s]
        count_ref[s] = p + 1
        if order_ref is not None:
            order_ref[p] = i
        if place_ref is not None:
            place_ref[i] = p
        return 0

    lax.fori_loop(0, tiles, step, 0)


def pick_pair(both, a, b, left):
    columns = both.shape[2] // LANES
    a_col = lax.shift_right_logical(a, 1)
    b_col = lax.rem(lax.shift_right_logical(b + 1, 1) + columns - 1, columns)
    xa = both[a & 1, :, pl.ds(pl.multiple_of(a_col * LANES, LANES), LANES)]
    xb = both[(b & 1) ^ 1, :, pl.ds(pl.multiple_of(b_col * LANES, LANES), LANES)]
    return jnp.where(left, xa, xb)


def sort_amps_kernel(cd_ref, t2_ref, *rest):
    chunks, (both, count, order, sem) = rest[:-4], rest[-4:]
    rows = t2_ref.shape[0]
    load = pltpu.make_async_copy(t2_ref, both.at[0], sem)
    load.start()
    rank_tiles(cd_ref, count, order, None, cd_ref.shape[0])
    load.wait()
    both[1] = half_turned(both[0])
    left = lax.broadcasted_iota(jnp.int32, (rows, LANES), 1) < LANES // 2
    q = 0
    for chunk in chunks:
        for off in range(chunk.shape[2] // LANES):
            pair = pick_pair(both, order[2 * q], order[2 * q + 1], left)
            for copy in range(chunk.shape[0]):
                chunk[copy, :, off * LANES : (off + 1) * LANES] = pair
            q += 1


def sort_amps(t2, cd_sym, copies):
    rows, cols = t2.shape
    return pl.pallas_call(
        sort_amps_kernel,
        out_shape=[
            jax.ShapeDtypeStruct((copies, rows, cols // NSYM * m), t2.dtype) for m in SPLIT
        ],
        in_specs=[SMEM, ANY],
        out_specs=[VMEM] * len(SPLIT),
        scratch_shapes=[
            pltpu.VMEM((2, rows, cols), t2.dtype),
            pltpu.SMEM((NSYM,), jnp.int32),
            pltpu.SMEM((cd_sym.shape[0],), jnp.int32),
            pltpu.SemaphoreType.DMA,
        ],
        compiler_params=params(),
        name="sort_amps",
    )(cd_sym, t2)


def sort_ints_kernel(ab_ref, ints_ref, out_ref, count, order):
    tiles = ab_ref.shape[0]
    rank_tiles(ab_ref, count, order, None, tiles)
    for p in range(tiles):
        out_ref[p] = ints_ref[order[p]]


def sort_ints(integrals, ab_sym):
    tiles = integrals.shape[0]
    return pl.pallas_call(
        sort_ints_kernel,
        out_shape=jax.ShapeDtypeStruct(integrals.shape, integrals.dtype),
        in_specs=[SMEM, VMEM],
        out_specs=VMEM,
        scratch_shapes=[pltpu.SMEM((NSYM,), jnp.int32), pltpu.SMEM((tiles,), jnp.int32)],
        compiler_params=params(),
        name="sort_ints",
    )(ab_sym, integrals)


def nothing(*refs):
    pass


def after(x, *earlier):
    return pl.pallas_call(
        nothing,
        out_shape=jax.ShapeDtypeStruct(x.shape, x.dtype),
        in_specs=[ANY] * (1 + len(earlier)),
        out_specs=ANY,
        input_output_aliases={0: 0},
        compiler_params=params(),
        name="after",
    )(x, *earlier)


def contract_kernel(n_cd, t2_ref, t2_across, own_ref, sib_ref, out_ref, lhs, ints, sems):
    z_len, _, rows, cols = lhs.shape
    tiles, tile, packed = own_ref.shape
    x, core = lax.axis_index("x"), lax.axis_index("core")
    copies = [
        pltpu.make_async_copy(t2_ref, lhs.at[:, x], sems.at[0]),
        pltpu.make_async_copy(t2_across, lhs.at[:, 1 - x], sems.at[1]),
    ]
    for copy in copies:
        copy.start()
    ints[core] = own_ref[...]
    ints[1 - core] = sib_ref[...]
    for copy in copies:
        copy.wait()
    syms = cols // packed
    width = tiles // syms * tile
    per_group = z_len // n_cd
    for core_of in range(2):
        mine = ints[core_of].reshape(syms, width, packed)
        for group in range(n_cd):
            these = lhs[group * per_group : (group + 1) * per_group]
            these = these.reshape(per_group * 2 * rows, cols)
            for s in range(syms):
                part = lax.dot_general(
                    these[:, s * packed : (s + 1) * packed],
                    mine[s],
                    (((1,), (1,)), ((), ())),
                    preferred_element_type=jnp.float32,
                )
                out_ref[2 * group + core_of, :, s * width : (s + 1) * width] = part.astype(
                    out_ref.dtype
                )


def contract(n_cd, t2, t2_across, ints, sib_ints, first_sym, syms):
    z_len, rows, cols = t2.shape
    tile, packed = ints.shape[1:]
    tiles = ints.shape[0] // NSYM * syms
    out_rows = 2 * z_len * rows // n_cd
    spec = pl.BlockSpec(
        (pl.Element(tiles), pl.Element(tile), pl.Element(packed)),
        lambda i: (ints.shape[0] // NSYM * first_sym, 0, 0),
    )
    return pl.pallas_call(
        functools.partial(contract_kernel, n_cd),
        out_shape=jax.ShapeDtypeStruct((2 * n_cd, out_rows, tiles * tile), jnp.bfloat16),
        grid=(1,),
        in_specs=[ANY] * 2 + [spec] * 2,
        out_specs=pl.BlockSpec((2 * n_cd, out_rows, tiles * tile), lambda i: (0, 0, 0)),
        scratch_shapes=[
            pltpu.VMEM((z_len, 2, rows, cols), jnp.bfloat16),
            pltpu.VMEM((2, tiles, tile, packed), jnp.bfloat16),
            pltpu.SemaphoreType.DMA((2,)),
        ],
        compiler_params=params(),
        cost_estimate=pl.CostEstimate(
            flops=8 * z_len * rows * tiles * tile * packed,
            bytes_accessed=4 * (z_len * rows * (cols + 2 * tiles * tile) + tiles * tile * packed),
            transcendentals=0,
        ),
        name="contract",
    )(t2, t2_across, ints, sib_ints)


def add_kernel(n_cd, ab_ref, *rest):
    parts, (out_ref, both, count, place) = rest[:-4], rest[-4:]
    rows = both.shape[1]

    @pl.when(pl.program_id(0) == 0)
    def _():
        rank_tiles(ab_ref, count, None, place, ab_ref.shape[0])

    left = lax.broadcasted_iota(jnp.int32, (rows, LANES), 1) < LANES // 2
    for core in range(2):
        first = 0
        for part in parts:
            total = part[core].astype(jnp.float32)
            for group in range(1, n_cd):
                total += part[2 * group + core].astype(jnp.float32)
            both[0, :, first : first + part.shape[2]] = total.astype(both.dtype)
            first += part.shape[2]
        both[1] = half_turned(both[0])
        for q in range(out_ref.shape[1] // LANES):
            out_ref[core * rows : (core + 1) * rows, q * LANES : (q + 1) * LANES] = pick_pair(
                both, place[2 * q], place[2 * q + 1], left
            )


def add_parts(n_cd, ab_sym, parts, rows):
    all_rows = 2 * parts[0].shape[1]
    cols = sum(p.shape[2] for p in parts)
    return pl.pallas_call(
        functools.partial(add_kernel, n_cd),
        out_shape=jax.ShapeDtypeStruct((all_rows, cols), jnp.bfloat16),
        grid=(all_rows // (2 * rows),),
        in_specs=[SMEM]
        + [pl.BlockSpec((2 * n_cd, rows, p.shape[2]), lambda i: (0, i, 0)) for p in parts],
        out_specs=pl.BlockSpec((2 * rows, cols), lambda i: (i, 0)),
        scratch_shapes=[
            pltpu.VMEM((2, rows, cols), jnp.bfloat16),
            pltpu.SMEM((NSYM,), jnp.int32),
            pltpu.SMEM((ab_sym.shape[0],), jnp.int32),
        ],
        compiler_params=params(),
        name="add_parts",
    )(ab_sym, *parts)


SWAP = [(0, 1), (1, 0)]


def per_device(t2_amps, integrals, ab_sym, cd_sym):
    z_len, n_cd = lax.axis_size("z"), lax.axis_size("cd")
    own = list(sort_amps(t2_amps, cd_sym, z_len))
    ints = sort_ints(integrals, ab_sym)
    along_z = []
    for c in range(len(SPLIT)):
        if c:
            own[c] = after(own[c], along_z[max(0, c - 2)])
        along_z.append(lax.all_to_all(own[c], "z", 0, 0, tiled=True))
    sib_ints = lax.ppermute(ints, "core", SWAP)
    parts = []
    for c, syms in enumerate(SPLIT):
        across = lax.ppermute(along_z[c], "x", SWAP)
        made = contract(n_cd, along_z[c], across, ints, sib_ints, sum(SPLIT[:c]), syms)
        parts.append(lax.all_to_all(made, ("cd", "core"), 0, 0, tiled=True))
    return add_parts(n_cd, ab_sym, parts, t2_amps.shape[0])


def solution(mesh):
    n_blk, n_cd = mesh.devices.shape
    parted = Mesh(mesh.devices.reshape(n_blk // 4, 2, 2, n_cd), ("z", "x", "core", "cd"))
    blk = ("z", "x", "core")
    in_specs = (P(blk, "cd"), P(blk, None, "cd"), P(blk), P("cd"))
    return jax.shard_map(
        per_device, mesh=parted, in_specs=in_specs, out_specs=P("cd", blk), check_vma=False
    )
```

```python
import functools

import jax
import jax.numpy as jnp
from jax import lax
from jax.experimental import pallas as pl
from jax.experimental.pallas import tpu as pltpu
from jax.sharding import Mesh, PartitionSpec as P

NSYM = 8
SPLIT = (1, 2, 2, 2, 1)
INTS_SPLIT = (3, 5)
LANES = 128
VMEM_LIMIT = 56 * 2**20

ANY = pl.BlockSpec(memory_space=pl.ANY)
SMEM = pl.BlockSpec(memory_space=pltpu.SMEM)
VMEM = pl.BlockSpec(memory_space=pltpu.VMEM)

CHEAP = pl.CostEstimate(flops=1000, bytes_accessed=1000, transcendentals=0)


def params():
    return pltpu.CompilerParams(vmem_limit_bytes=VMEM_LIMIT)


def half_turned(x):
    half = LANES // 2
    return jnp.concatenate([x[:, half:], x[:, :half]], axis=1)


def rank_tiles(sym_ref, count_ref, order_ref, place_ref, tiles):
    for s in range(NSYM):
        count_ref[s] = s * (tiles // NSYM)

    def step(i, _):
        s = sym_ref[i]
        p = count_ref[s]
        count_ref[s] = p + 1
        if order_ref is not None:
            order_ref[p] = i
        if place_ref is not None:
            place_ref[i] = p
        return 0

    lax.fori_loop(0, tiles, step, 0)


def pick_pair(both, a, b, left):
    columns = both.shape[2] // LANES
    a_col = lax.shift_right_logical(a, 1)
    b_col = lax.rem(lax.shift_right_logical(b + 1, 1) + columns - 1, columns)
    xa = both[a & 1, :, pl.ds(pl.multiple_of(a_col * LANES, LANES), LANES)]
    xb = both[(b & 1) ^ 1, :, pl.ds(pl.multiple_of(b_col * LANES, LANES), LANES)]
    return jnp.where(left, xa, xb)


def sort_amps_kernel(cd_ref, t2_ref, *rest):
    chunks, (both, count, order, sem) = rest[:-4], rest[-4:]
    rows = t2_ref.shape[0]
    load = pltpu.make_async_copy(t2_ref, both.at[0], sem)
    load.start()
    rank_tiles(cd_ref, count, order, None, cd_ref.shape[0])
    load.wait()
    both[1] = half_turned(both[0])
    left = lax.broadcasted_iota(jnp.int32, (rows, LANES), 1) < LANES // 2
    q = 0
    for chunk in chunks:
        for off in range(chunk.shape[2] // LANES):
            pair = pick_pair(both, order[2 * q], order[2 * q + 1], left)
            for copy in range(chunk.shape[0]):
                chunk[copy, :, off * LANES : (off + 1) * LANES] = pair
            q += 1


def sort_amps(t2, cd_sym, copies):
    rows, cols = t2.shape
    return pl.pallas_call(
        sort_amps_kernel,
        out_shape=[
            jax.ShapeDtypeStruct((copies, rows, cols // NSYM * m), t2.dtype) for m in SPLIT
        ],
        in_specs=[SMEM, ANY],
        out_specs=[VMEM] * len(SPLIT),
        scratch_shapes=[
            pltpu.VMEM((2, rows, cols), t2.dtype),
            pltpu.SMEM((NSYM,), jnp.int32),
            pltpu.SMEM((cd_sym.shape[0],), jnp.int32),
            pltpu.SemaphoreType.DMA,
        ],
        compiler_params=params(),
        cost_estimate=CHEAP,
        name="sort_amps",
    )(cd_sym, t2)


def sort_ints_kernel(ab_ref, ints_ref, *rest):
    parts, (count, order) = rest[:-2], rest[-2:]
    tiles = ab_ref.shape[0]
    rank_tiles(ab_ref, count, order, None, tiles)
    per_sym = tiles // NSYM
    sym = 0
    for part in parts:
        for s in range(part.shape[0]):
            rows = [ints_ref[order[sym * per_sym + m]] for m in range(per_sym)]
            part[s] = jnp.concatenate(rows, axis=0).T
            sym += 1


def sort_ints(integrals, ab_sym):
    tiles, tile, packed = integrals.shape
    return pl.pallas_call(
        sort_ints_kernel,
        out_shape=[
            jax.ShapeDtypeStruct((m, packed, tiles // NSYM * tile), integrals.dtype)
            for m in INTS_SPLIT
        ],
        in_specs=[SMEM, VMEM],
        out_specs=[VMEM] * len(INTS_SPLIT),
        scratch_shapes=[pltpu.SMEM((NSYM,), jnp.int32), pltpu.SMEM((tiles,), jnp.int32)],
        compiler_params=params(),
        cost_estimate=CHEAP,
        name="sort_ints",
    )(ab_sym, integrals)


def nothing(*refs):
    pass


def after(x, *earlier):
    return pl.pallas_call(
        nothing,
        out_shape=jax.ShapeDtypeStruct(x.shape, x.dtype),
        in_specs=[ANY] * (1 + len(earlier)),
        out_specs=ANY,
        input_output_aliases={0: 0},
        compiler_params=params(),
        cost_estimate=CHEAP,
        name="after",
    )(x, *earlier)


def contract_kernel(n_cd, near, up, across, far, own_ref, sib_ref, *rest):
    out_ref, lhs = rest[-2:]
    zh, zl, xs, rows, cols = lhs.shape
    syms, packed, width = own_ref.shape
    z, x, core = lax.axis_index("zl"), lax.axis_index("x"), lax.axis_index("core")
    for i in range(zh):
        lhs[i, z, x] = near[i]
        lhs[i, 1 - z, x] = up[i]
        lhs[i, z, 1 - x] = across[i]
        lhs[i, 1 - z, 1 - x] = far[i]
    t2 = lhs[...].reshape(zh * zl * xs * rows, cols)
    group_rows = t2.shape[0] // n_cd
    for side, ints in enumerate((own_ref, sib_ref)):
        for s in range(syms):
            part = jnp.dot(
                t2[:, s * packed : (s + 1) * packed], ints[s], preferred_element_type=jnp.float32
            ).astype(out_ref.dtype)
            for group in range(n_cd):
                out_ref[2 * group + (core ^ side), :, s * width : (s + 1) * width] = part[
                    group * group_rows : (group + 1) * group_rows
                ]


def contract(n_cd, t2s, ints, sib_ints, first_sym, syms, earlier):
    zh, rows, cols = t2s[0].shape
    packed, width = ints.shape[1:]
    all_rows = 4 * zh * rows
    spec = pl.BlockSpec(
        (pl.Element(syms), pl.Element(packed), pl.Element(width)), lambda i: (first_sym, 0, 0)
    )
    out = (2 * n_cd, all_rows // n_cd, syms * width)
    return pl.pallas_call(
        functools.partial(contract_kernel, n_cd),
        out_shape=jax.ShapeDtypeStruct(out, jnp.bfloat16),
        grid=(1,),
        in_specs=[pl.BlockSpec(t2s[0].shape, lambda i: (0, 0, 0))] * 4
        + [spec] * 2
        + [ANY] * len(earlier),
        out_specs=pl.BlockSpec(out, lambda i: (0, 0, 0)),
        scratch_shapes=[pltpu.VMEM((zh, 2, 2, rows, cols), jnp.bfloat16)],
        compiler_params=params(),
        cost_estimate=CHEAP,
        name="contract",
    )(*t2s, ints, sib_ints, *earlier)


def add_kernel(n_cd, ab_ref, *rest):
    parts, (out_ref, both, count, place) = rest[:-4], rest[-4:]
    rows = both.shape[1]

    @pl.when(pl.program_id(0) == 0)
    def _():
        rank_tiles(ab_ref, count, None, place, ab_ref.shape[0])

    left = lax.broadcasted_iota(jnp.int32, (rows, LANES), 1) < LANES // 2
    for core in range(2):
        first = 0
        for part in parts:
            total = part[core].astype(jnp.float32)
            for group in range(1, n_cd):
                total += part[2 * group + core].astype(jnp.float32)
            both[0, :, first : first + part.shape[2]] = total.astype(both.dtype)
            first += part.shape[2]
        both[1] = half_turned(both[0])
        for q in range(out_ref.shape[3] // LANES):
            out_ref[0, core, :, q * LANES : (q + 1) * LANES] = pick_pair(
                both, place[2 * q], place[2 * q + 1], left
            )


def add_parts(n_cd, ab_sym, parts, rows):
    blocks = parts[0].shape[1] // rows
    cols = sum(p.shape[2] for p in parts)
    step = rows // 2
    out = pl.pallas_call(
        functools.partial(add_kernel, n_cd),
        out_shape=jax.ShapeDtypeStruct((blocks, 2, rows, cols), jnp.bfloat16),
        grid=(2 * blocks,),
        in_specs=[SMEM]
        + [pl.BlockSpec((2 * n_cd, step, p.shape[2]), lambda i: (0, i, 0)) for p in parts],
        out_specs=pl.BlockSpec((1, 2, step, cols), lambda i: (i // 2, 0, i % 2, 0)),
        scratch_shapes=[
            pltpu.VMEM((2, step, cols), jnp.bfloat16),
            pltpu.SMEM((NSYM,), jnp.int32),
            pltpu.SMEM((ab_sym.shape[0],), jnp.int32),
        ],
        compiler_params=params(),
        cost_estimate=CHEAP,
        name="add_parts",
    )(ab_sym, *parts)
    return out.reshape(2 * blocks * rows, cols)


SWAP = [(0, 1), (1, 0)]


def per_device(t2_amps, integrals, ab_sym, cd_sym):
    zh, n_cd = lax.axis_size("zh"), lax.axis_size("cd")
    own = list(sort_amps(t2_amps, cd_sym, zh))
    ints = list(sort_ints(integrals, ab_sym))
    sib_ints = [lax.ppermute(x, "core", SWAP) for x in ints]
    near = []
    for c in range(len(SPLIT)):
        if c > 1:
            own[c] = after(own[c], near[c - 2])
        near.append(lax.all_to_all(own[c], "zh", 0, 0, tiled=True))
    parts, made = [], []
    for c, syms in enumerate(SPLIT):
        up = lax.ppermute(near[c], "zl", SWAP)
        across, far = lax.ppermute(near[c], "x", SWAP), lax.ppermute(up, "x", SWAP)
        first = sum(SPLIT[:c])
        part = 0
        while first >= INTS_SPLIT[part]:
            first -= INTS_SPLIT[part]
            part += 1
        t2s = (near[c], up, across, far)
        made.append(contract(n_cd, t2s, ints[part], sib_ints[part], first, syms, made[-1:]))
        parts.append(lax.all_to_all(made[c], ("cd", "core"), 0, 0, tiled=True))
    return add_parts(n_cd, ab_sym, parts, t2_amps.shape[0])


def solution(mesh):
    n_blk, n_cd = mesh.devices.shape
    blk = ("zh", "zl", "x", "core")
    parted = Mesh(mesh.devices.reshape(n_blk // 8, 2, 2, 2, n_cd), blk + ("cd",))
    in_specs = (P(blk, "cd"), P(blk, None, "cd"), P(blk), P("cd"))
    return jax.shard_map(
        per_device, mesh=parted, in_specs=in_specs, out_specs=P("cd", blk), check_vma=False
    )
```

```python
import functools

import jax
import jax.numpy as jnp
from jax import lax
from jax.experimental import pallas as pl
from jax.experimental.pallas import tpu as pltpu
from jax.sharding import Mesh, PartitionSpec as P

NSYM = 8
SPLIT = (1, 2, 2, 2, 1)
LATE = 2
INTS_SPLIT = (3, 5)
LANES = 128
VMEM_LIMIT = 20 * 2**20

ANY = pl.BlockSpec(memory_space=pl.ANY)
SMEM = pl.BlockSpec(memory_space=pltpu.SMEM)
VMEM = pl.BlockSpec(memory_space=pltpu.VMEM)

CHEAP = pl.CostEstimate(flops=1000, bytes_accessed=1000, transcendentals=0)


def params(limit=VMEM_LIMIT):
    return pltpu.CompilerParams(vmem_limit_bytes=limit)


def half_turned(x):
    half = LANES // 2
    return jnp.concatenate([x[:, half:], x[:, :half]], axis=1)


def rank_tiles(sym_ref, count_ref, order_ref, place_ref, tiles):
    for s in range(NSYM):
        count_ref[s] = s * (tiles // NSYM)

    def step(i, _):
        s = sym_ref[i]
        p = count_ref[s]
        count_ref[s] = p + 1
        if order_ref is not None:
            order_ref[p] = i
        if place_ref is not None:
            place_ref[i] = p
        return 0

    lax.fori_loop(0, tiles, step, 0)


def pick_pair(both, a, b, left):
    columns = both.shape[2] // LANES
    a_col = lax.shift_right_logical(a, 1)
    b_col = lax.rem(lax.shift_right_logical(b + 1, 1) + columns - 1, columns)
    xa = both[a & 1, :, pl.ds(pl.multiple_of(a_col * LANES, LANES), LANES)]
    xb = both[(b & 1) ^ 1, :, pl.ds(pl.multiple_of(b_col * LANES, LANES), LANES)]
    return jnp.where(left, xa, xb)


def sort_amps_kernel(cd_ref, t2_ref, *rest):
    chunks, (both, count, order, sem) = rest[:-4], rest[-4:]
    rows = t2_ref.shape[0]
    load = pltpu.make_async_copy(t2_ref, both.at[0], sem)
    load.start()
    rank_tiles(cd_ref, count, order, None, cd_ref.shape[0])
    load.wait()
    both[1] = half_turned(both[0])
    left = lax.broadcasted_iota(jnp.int32, (rows, LANES), 1) < LANES // 2
    q = 0
    for chunk in chunks:
        for off in range(chunk.shape[1] // LANES):
            pair = pick_pair(both, order[2 * q], order[2 * q + 1], left)
            chunk[:, off * LANES : (off + 1) * LANES] = pair
            q += 1


def sort_amps(t2, cd_sym):
    rows, cols = t2.shape
    return pl.pallas_call(
        sort_amps_kernel,
        out_shape=[
            jax.ShapeDtypeStruct((rows, cols // NSYM * m), t2.dtype) for m in SPLIT
        ],
        in_specs=[SMEM, ANY],
        out_specs=[VMEM] * len(SPLIT),
        scratch_shapes=[
            pltpu.VMEM((2, rows, cols), t2.dtype),
            pltpu.SMEM((NSYM,), jnp.int32),
            pltpu.SMEM((cd_sym.shape[0],), jnp.int32),
            pltpu.SemaphoreType.DMA,
        ],
        compiler_params=params(),
        cost_estimate=CHEAP,
        name="sort_amps",
    )(cd_sym, t2)


def sort_ints_kernel(ab_ref, ints_ref, _, *rest):
    parts, (count, order) = rest[:-2], rest[-2:]
    tiles = ab_ref.shape[0]
    rank_tiles(ab_ref, count, order, None, tiles)
    per_sym = tiles // NSYM
    sym = 0
    for part in parts:
        for s in range(part.shape[0]):
            rows = [ints_ref[order[sym * per_sym + m]] for m in range(per_sym)]
            part[s] = jnp.concatenate(rows, axis=0).T
            sym += 1


def sort_ints(integrals, ab_sym, earlier):
    tiles, tile, packed = integrals.shape
    return pl.pallas_call(
        sort_ints_kernel,
        out_shape=[
            jax.ShapeDtypeStruct((m, packed, tiles // NSYM * tile), integrals.dtype)
            for m in INTS_SPLIT
        ],
        in_specs=[SMEM, VMEM, ANY],
        out_specs=[VMEM] * len(INTS_SPLIT),
        scratch_shapes=[pltpu.SMEM((NSYM,), jnp.int32), pltpu.SMEM((tiles,), jnp.int32)],
        compiler_params=params(),
        cost_estimate=CHEAP,
        name="sort_ints",
    )(ab_sym, integrals, earlier)


def merge_kernel(n, *refs):
    blocks, out_ref = refs[:n], refs[-1]
    me = lax.axis_index("zh")
    for d, block in enumerate(blocks):
        out_ref[me ^ d] = block[...]


def merge(blocks, earlier):
    return pl.pallas_call(
        functools.partial(merge_kernel, len(blocks)),
        out_shape=jax.ShapeDtypeStruct((len(blocks),) + blocks[0].shape, blocks[0].dtype),
        in_specs=[VMEM] * len(blocks) + [ANY] * len(earlier),
        out_specs=VMEM,
        compiler_params=params(),
        cost_estimate=CHEAP,
        name="merge",
    )(*blocks, *earlier)


def nothing(*refs):
    pass


def after(x, *earlier):
    return pl.pallas_call(
        nothing,
        out_shape=jax.ShapeDtypeStruct(x.shape, x.dtype),
        in_specs=[ANY] * (1 + len(earlier)),
        out_specs=ANY,
        input_output_aliases={0: 0},
        compiler_params=params(),
        cost_estimate=CHEAP,
        name="after",
    )(x, *earlier)


def contract_kernel(n_cd, apart, first_sym, syms, near, up, across, far, own_ref, sib_ref, *rest):
    outs, lhs = rest[-n_cd * (1 + apart) - 1 : -1], rest[-1]
    slots, rows, cols = lhs.shape
    packed, width = own_ref.shape[1:]
    z, x = lax.axis_index("zl"), lax.axis_index("x")
    first = lax.axis_index("cd") * (slots // n_cd)
    for i in range(slots // 4):
        for block, zl, xs in ((near, z, x), (up, 1 - z, x), (across, z, 1 - x), (far, 1 - z, 1 - x)):
            lhs[lax.rem(4 * i + 2 * zl + xs + slots - first, slots)] = block[i]
    t2 = lhs[...].reshape(slots * rows, cols)
    group_rows = t2.shape[0] // n_cd
    for side, ints in enumerate((own_ref, sib_ref)):
        for s in range(syms):
            part = jnp.dot(
                t2[:, s * packed : (s + 1) * packed],
                ints[first_sym + s],
                preferred_element_type=jnp.float32,
            ).astype(outs[0].dtype)
            for by in range(n_cd):
                these = part[by * group_rows : (by + 1) * group_rows]
                if apart:
                    outs[2 * by + side][:, s * width : (s + 1) * width] = these
                else:
                    outs[by][side, :, s * width : (s + 1) * width] = these


def contract(n_cd, apart, t2s, ints, sib_ints, first_sym, syms, earlier):
    zh, rows, cols = t2s[0].shape
    packed, width = ints.shape[1:]
    all_rows = 4 * zh * rows
    out = (all_rows // n_cd, syms * width)
    outs = [out] * (2 * n_cd) if apart else [(2,) + out] * n_cd
    return pl.pallas_call(
        functools.partial(contract_kernel, n_cd, apart, first_sym, syms),
        out_shape=[jax.ShapeDtypeStruct(x, jnp.bfloat16) for x in outs],
        in_specs=[VMEM] * 6 + [ANY] * len(earlier),
        out_specs=[VMEM] * len(outs),
        scratch_shapes=[pltpu.VMEM((4 * zh, rows, cols), jnp.bfloat16)],
        compiler_params=params(),
        cost_estimate=CHEAP,
        name="contract",
    )(*t2s, ints, sib_ints, *earlier)


def total(refs, these):
    value = refs[0][these].astype(jnp.float32)
    for ref in refs[1:]:
        value += ref[these].astype(jnp.float32)
    return value.astype(jnp.bfloat16)


def early_kernel(n_cd, chunks, *refs):
    parts, (own_ref, sib_ref) = refs[: chunks * n_cd], refs[-2:]
    step = own_ref.shape[0]
    for side, out_ref in enumerate((own_ref, sib_ref)):
        first = 0
        for c in range(chunks):
            mine = parts[c * n_cd : (c + 1) * n_cd]
            width = mine[0].shape[2]
            out_ref[:, first : first + width] = total(mine, side)
            first += width


def add_early(n_cd, parts, earlier):
    rows = parts[0].shape[1]
    cols = sum(p.shape[2] for p in parts[::n_cd])
    step = rows // 4
    spec = pl.BlockSpec((step, cols), lambda i: (i, 0))
    return pl.pallas_call(
        functools.partial(early_kernel, n_cd, len(parts) // n_cd),
        out_shape=[jax.ShapeDtypeStruct((rows, cols), jnp.bfloat16)] * 2,
        grid=(rows // step,),
        in_specs=[pl.BlockSpec((2, step, p.shape[2]), lambda i: (0, i, 0)) for p in parts]
        + [ANY] * len(earlier),
        out_specs=[spec, spec],
        compiler_params=params(),
        cost_estimate=CHEAP,
        name="add_early",
    )(*parts, *earlier)


def finish_kernel(n_cd, ab_ref, *rest):
    early, late, (out_ref, both, count, place) = rest[:2], rest[2:-4], rest[-4:]

    @pl.when(pl.program_id(0) == 0)
    def _():
        rank_tiles(ab_ref, count, None, place, ab_ref.shape[0])

    core = lax.axis_index("core")
    rows, cols = both.shape[1:]
    left = lax.broadcasted_iota(jnp.int32, (rows, LANES), 1) < LANES // 2
    for side in range(2):
        first = early[side].shape[1]
        both[0, :, :first] = early[side][...]
        for c in range(LATE):
            mine = late[c * 2 * n_cd + side : (c + 1) * 2 * n_cd : 2]
            both[0, :, first : first + mine[0].shape[1]] = total(mine, slice(None))
            first += mine[0].shape[1]
        both[1] = half_turned(both[0])
        for q in range(cols // LANES):
            out_ref[core ^ side, :, q * LANES : (q + 1) * LANES] = pick_pair(
                both, place[2 * q], place[2 * q + 1], left
            )


def finish(n_cd, ab_sym, early, late, rows):
    blocks = early[0].shape[0] // rows
    cols = early[0].shape[1] + sum(p.shape[1] for p in late[:: 2 * n_cd])
    out = pl.pallas_call(
        functools.partial(finish_kernel, n_cd),
        out_shape=jax.ShapeDtypeStruct((2 * blocks, rows, cols), jnp.bfloat16),
        grid=(blocks,),
        in_specs=[SMEM]
        + [pl.BlockSpec((rows, p.shape[1]), lambda i: (i, 0)) for p in [*early, *late]],
        out_specs=pl.BlockSpec((2, rows, cols), lambda i: (i, 0, 0)),
        scratch_shapes=[
            pltpu.VMEM((2, rows, cols), jnp.bfloat16),
            pltpu.SMEM((NSYM,), jnp.int32),
            pltpu.SMEM((ab_sym.shape[0],), jnp.int32),
        ],
        compiler_params=params(),
        cost_estimate=CHEAP,
        name="finish",
    )(ab_sym, *early, *late)
    return out.reshape(2 * blocks * rows, cols)


SWAP = [(0, 1), (1, 0)]


def sent(x, by, side):
    n_cd = lax.axis_size("cd")
    if not by:
        return lax.ppermute(x, "core", SWAP) if side else x
    if not side:
        return lax.ppermute(x, "cd", [(i, (i + by) % n_cd) for i in range(n_cd)])
    pairs = [(k * n_cd + i, (1 - k) * n_cd + (i + by) % n_cd) for k in range(2) for i in range(n_cd)]
    return lax.ppermute(x, ("core", "cd"), pairs)


def per_device(t2_amps, integrals, ab_sym, cd_sym):
    zh, n_cd = lax.axis_size("zh"), lax.axis_size("cd")
    n_chunks = len(SPLIT)
    own = list(sort_amps(t2_amps, cd_sym))
    ints = list(sort_ints(integrals, ab_sym, own[0]))
    sib_ints = [lax.ppermute(x, "core", SWAP) for x in ints]
    t2s, early, late, made, came = [], [], [], [], {}

    def gather(c, earlier):
        if c > 1:
            own[c] = after(own[c], t2s[c - 2][0])
        others = [lax.ppermute(own[c], "zh", [(i, i ^ d) for i in range(zh)]) for d in range(1, zh)]
        near = merge([own[c]] + others, earlier)
        up = lax.ppermute(near, "zl", SWAP)
        t2s.append((near, up, lax.ppermute(near, "x", SWAP), lax.ppermute(up, "x", SWAP)))

    gather(0, ints[:1])
    gather(1, list(t2s[0][:2]))
    for c, syms in enumerate(SPLIT):
        if c + 2 < n_chunks:
            gather(c + 2, [t2s[c + 1][1]] + made[:1])
        first = sum(SPLIT[:c])
        part = 0
        while first >= INTS_SPLIT[part]:
            first -= INTS_SPLIT[part]
            part += 1
        earlier = [t2s[c + 2][0]] if c + 2 < n_chunks else made[:1]
        if c + 2 == n_chunks:
            earlier.append(t2s[c + 1][1])
        if c in came:
            earlier += came[c]
        apart = c + LATE >= n_chunks
        made = list(contract(n_cd, apart, t2s[c], ints[part], sib_ints[part], first, syms, earlier))
        if apart:
            late += [sent(made[2 * by + k], by, k) for by in range(n_cd) for k in range(2)]
        else:
            early += [sent(made[by], by, 0) for by in range(n_cd)]
            came[c + (2 if c else 1)] = early[-n_cd + 1 :]
    sums = add_early(n_cd, early, made[:1])
    early = [sums[0], lax.ppermute(sums[1], "core", SWAP)]
    return finish(n_cd, ab_sym, early, late, t2_amps.shape[0])


def solution(mesh):
    n_blk, n_cd = mesh.devices.shape
    blk = ("zh", "zl", "x", "core")
    parted = Mesh(mesh.devices.reshape(n_blk // 8, 2, 2, 2, n_cd), blk + ("cd",))
    in_specs = (P(blk, "cd"), P(blk, None, "cd"), P(blk), P("cd"))
    return jax.shard_map(
        per_device, mesh=parted, in_specs=in_specs, out_specs=P("cd", blk), check_vma=False
    )
```

```python
import functools

import jax
import jax.numpy as jnp
from jax import lax
from jax.experimental import pallas as pl
from jax.experimental.pallas import tpu as pltpu
from jax.sharding import Mesh, PartitionSpec as P

NSYM = 8
SPLIT = (1, 2, 2, 2, 1)
SUMS = ((0, 1, 2, 3),)
ALONG_Z = (3,)
INTS_SPLIT = (3, 5)
LANES = 128
VMEM_LIMIT = 20 * 2**20

ANY = pl.BlockSpec(memory_space=pl.ANY)
SMEM = pl.BlockSpec(memory_space=pltpu.SMEM)
VMEM = pl.BlockSpec(memory_space=pltpu.VMEM)

CHEAP = pl.CostEstimate(flops=1000, bytes_accessed=1000, transcendentals=0)


def params(limit=VMEM_LIMIT):
    return pltpu.CompilerParams(vmem_limit_bytes=limit)


def half_turned(x):
    half = LANES // 2
    return jnp.concatenate([x[:, half:], x[:, :half]], axis=1)


def rank_tiles(sym_ref, count_ref, order_ref, place_ref, tiles):
    for s in range(NSYM):
        count_ref[s] = s * (tiles // NSYM)

    def step(i, _):
        s = sym_ref[i]
        p = count_ref[s]
        count_ref[s] = p + 1
        if order_ref is not None:
            order_ref[p] = i
        if place_ref is not None:
            place_ref[i] = p
        return 0

    lax.fori_loop(0, tiles, step, 0)


def pick_pair(both, a, b, left):
    columns = both.shape[2] // LANES
    a_col = lax.shift_right_logical(a, 1)
    b_col = lax.rem(lax.shift_right_logical(b + 1, 1) + columns - 1, columns)
    xa = both[a & 1, :, pl.ds(pl.multiple_of(a_col * LANES, LANES), LANES)]
    xb = both[(b & 1) ^ 1, :, pl.ds(pl.multiple_of(b_col * LANES, LANES), LANES)]
    return jnp.where(left, xa, xb)


def sort_amps_kernel(cd_ref, t2_ref, *rest):
    chunks, (both, count, order, sem) = rest[:-4], rest[-4:]
    rows = t2_ref.shape[0]
    load = pltpu.make_async_copy(t2_ref, both.at[0], sem)
    load.start()
    rank_tiles(cd_ref, count, order, None, cd_ref.shape[0])
    load.wait()
    both[1] = half_turned(both[0])
    left = lax.broadcasted_iota(jnp.int32, (rows, LANES), 1) < LANES // 2
    q = 0
    for chunk in chunks:
        for off in range(chunk.shape[1] // LANES):
            pair = pick_pair(both, order[2 * q], order[2 * q + 1], left)
            chunk[:, off * LANES : (off + 1) * LANES] = pair
            q += 1


def sort_amps(t2, cd_sym):
    rows, cols = t2.shape
    return pl.pallas_call(
        sort_amps_kernel,
        out_shape=[
            jax.ShapeDtypeStruct((rows, cols // NSYM * m), t2.dtype) for m in SPLIT
        ],
        in_specs=[SMEM, ANY],
        out_specs=[VMEM] * len(SPLIT),
        scratch_shapes=[
            pltpu.VMEM((2, rows, cols), t2.dtype),
            pltpu.SMEM((NSYM,), jnp.int32),
            pltpu.SMEM((cd_sym.shape[0],), jnp.int32),
            pltpu.SemaphoreType.DMA,
        ],
        compiler_params=params(),
        cost_estimate=CHEAP,
        name="sort_amps",
    )(cd_sym, t2)


def sort_ints_kernel(ab_ref, ints_ref, _, *rest):
    parts, (count, order) = rest[:-2], rest[-2:]
    tiles = ab_ref.shape[0]
    rank_tiles(ab_ref, count, order, None, tiles)
    per_sym = tiles // NSYM
    sym = 0
    for part in parts:
        for s in range(part.shape[0]):
            rows = [ints_ref[order[sym * per_sym + m]] for m in range(per_sym)]
            part[s] = jnp.concatenate(rows, axis=0).T
            sym += 1


def sort_ints(integrals, ab_sym, earlier):
    tiles, tile, packed = integrals.shape
    return pl.pallas_call(
        sort_ints_kernel,
        out_shape=[
            jax.ShapeDtypeStruct((m, packed, tiles // NSYM * tile), integrals.dtype)
            for m in INTS_SPLIT
        ],
        in_specs=[SMEM, VMEM, ANY],
        out_specs=[VMEM] * len(INTS_SPLIT),
        scratch_shapes=[pltpu.SMEM((NSYM,), jnp.int32), pltpu.SMEM((tiles,), jnp.int32)],
        compiler_params=params(),
        cost_estimate=CHEAP,
        name="sort_ints",
    )(ab_sym, integrals, earlier)


def merge_kernel(n, *refs):
    blocks, out_ref = refs[:n], refs[-1]
    me = lax.axis_index("zh")
    for d, block in enumerate(blocks):
        out_ref[me ^ d] = block[...]


def merge(blocks, earlier):
    return pl.pallas_call(
        functools.partial(merge_kernel, len(blocks)),
        out_shape=jax.ShapeDtypeStruct((len(blocks),) + blocks[0].shape, blocks[0].dtype),
        in_specs=[VMEM] * len(blocks) + [ANY] * len(earlier),
        out_specs=VMEM,
        compiler_params=params(),
        cost_estimate=CHEAP,
        name="merge",
    )(*blocks, *earlier)


def nothing(*refs):
    pass


def after(x, *earlier):
    return pl.pallas_call(
        nothing,
        out_shape=jax.ShapeDtypeStruct(x.shape, x.dtype),
        in_specs=[ANY] * (1 + len(earlier)),
        out_specs=ANY,
        input_output_aliases={0: 0},
        compiler_params=params(),
        cost_estimate=CHEAP,
        name="after",
    )(x, *earlier)


def contract_kernel(n_cd, apart, first_sym, syms, near, up, across, far, own_ref, sib_ref, *rest):
    outs, lhs = rest[-n_cd * (1 + apart) - 1 : -1], rest[-1]
    slots, rows, cols = lhs.shape
    packed, width = own_ref.shape[1:]
    z, x = lax.axis_index("zl"), lax.axis_index("x")
    first = lax.axis_index("cd") * (slots // n_cd)
    for i in range(slots // 4):
        for block, zl, xs in ((near, z, x), (up, 1 - z, x), (across, z, 1 - x), (far, 1 - z, 1 - x)):
            lhs[lax.rem(4 * i + 2 * zl + xs + slots - first, slots)] = block[i]
    t2 = lhs[...].reshape(slots * rows, cols)
    group_rows = t2.shape[0] // n_cd
    for side, ints in enumerate((own_ref, sib_ref)):
        for s in range(syms):
            part = jnp.dot(
                t2[:, s * packed : (s + 1) * packed],
                ints[first_sym + s],
                preferred_element_type=jnp.float32,
            ).astype(outs[0].dtype)
            for by in range(n_cd):
                these = part[by * group_rows : (by + 1) * group_rows]
                if apart:
                    outs[2 * by + side][:, s * width : (s + 1) * width] = these
                else:
                    outs[by][side, :, s * width : (s + 1) * width] = these


def contract(n_cd, apart, t2s, ints, sib_ints, first_sym, syms, earlier):
    zh, rows, cols = t2s[0].shape
    packed, width = ints.shape[1:]
    all_rows = 4 * zh * rows
    out = (all_rows // n_cd, syms * width)
    outs = [out] * (2 * n_cd) if apart else [(2,) + out] * n_cd
    return pl.pallas_call(
        functools.partial(contract_kernel, n_cd, apart, first_sym, syms),
        out_shape=[jax.ShapeDtypeStruct(x, jnp.bfloat16) for x in outs],
        in_specs=[VMEM] * 6 + [ANY] * len(earlier),
        out_specs=[VMEM] * len(outs),
        scratch_shapes=[pltpu.VMEM((4 * zh, rows, cols), jnp.bfloat16)],
        compiler_params=params(),
        cost_estimate=CHEAP,
        name="contract",
    )(*t2s, ints, sib_ints, *earlier)


def total(refs, these):
    value = refs[0][these].astype(jnp.float32)
    for ref in refs[1:]:
        value += ref[these].astype(jnp.float32)
    return value.astype(jnp.bfloat16)


def early_kernel(n_cd, chunks, *refs):
    parts, (own_ref, sib_ref) = refs[: chunks * n_cd], refs[-2:]
    step = own_ref.shape[0]
    for side, out_ref in enumerate((own_ref, sib_ref)):
        first = 0
        for c in range(chunks):
            mine = parts[c * n_cd : (c + 1) * n_cd]
            width = mine[0].shape[2]
            out_ref[:, first : first + width] = total(mine, side)
            first += width


def add_early(n_cd, parts, earlier):
    rows = parts[0].shape[1]
    cols = sum(p.shape[2] for p in parts[::n_cd])
    step = rows // 4
    spec = pl.BlockSpec((step, cols), lambda i: (i, 0))
    return pl.pallas_call(
        functools.partial(early_kernel, n_cd, len(parts) // n_cd),
        out_shape=[jax.ShapeDtypeStruct((rows, cols), jnp.bfloat16)] * 2,
        grid=(rows // step,),
        in_specs=[pl.BlockSpec((2, step, p.shape[2]), lambda i: (0, i, 0)) for p in parts]
        + [ANY] * len(earlier),
        out_specs=[spec, spec],
        compiler_params=params(),
        cost_estimate=CHEAP,
        name="add_early",
    )(*parts, *earlier)


def finish_kernel(n_cd, ab_ref, *rest):
    sums, late, (out_ref, made, both, count, place, sems) = rest[: 2 * len(SUMS)], rest[2 * len(SUMS) : -6], rest[-6:]
    blocks, rows, cols = made.shape
    rank_tiles(ab_ref, count, None, place, ab_ref.shape[0])
    core = lax.axis_index("core")
    left = lax.broadcasted_iota(jnp.int32, (rows, LANES), 1) < LANES // 2

    def copy_out(i):
        return pltpu.make_async_copy(made.at[i], out_ref.at[i], sems.at[i])

    def block(i, _):
        these = pl.ds(pl.multiple_of(i * rows, rows), rows)
        for side in range(2):
            first = 0
            for ref in sums[side::2]:
                both[0, :, first : first + ref.shape[1]] = ref[these]
                first += ref.shape[1]
            both[0, :, first:] = total(late[side::2], these)
            both[1] = half_turned(both[0])
            out = 2 * i + (core ^ side)
            for q in range(cols // LANES):
                made[out, :, q * LANES : (q + 1) * LANES] = pick_pair(
                    both, place[2 * q], place[2 * q + 1], left
                )
            copy_out(out).start()
        return 0

    lax.fori_loop(0, blocks // 2, block, 0)
    for i in range(blocks):
        copy_out(i).wait()


def finish(n_cd, ab_sym, sums, late, rows):
    blocks = 2 * late[0].shape[0] // rows
    cols = sum(p.shape[1] for p in sums[::2]) + late[0].shape[1]
    out = pl.pallas_call(
        functools.partial(finish_kernel, n_cd),
        out_shape=jax.ShapeDtypeStruct((blocks, rows, cols), jnp.bfloat16),
        in_specs=[SMEM] + [VMEM] * (len(sums) + len(late)),
        out_specs=ANY,
        scratch_shapes=[
            pltpu.VMEM((blocks, rows, cols), jnp.bfloat16),
            pltpu.VMEM((2, rows, cols), jnp.bfloat16),
            pltpu.SMEM((NSYM,), jnp.int32),
            pltpu.SMEM((ab_sym.shape[0],), jnp.int32),
            pltpu.SemaphoreType.DMA((blocks,)),
        ],
        compiler_params=params(),
        cost_estimate=CHEAP,
        name="finish",
    )(ab_sym, *sums, *late)
    return out.reshape(blocks * rows, cols)


SWAP = [(0, 1), (1, 0)]


def sent(x, by, side):
    n_cd = lax.axis_size("cd")
    if not by:
        return lax.ppermute(x, "core", SWAP) if side else x
    if not side:
        return lax.ppermute(x, "cd", [(i, (i + by) % n_cd) for i in range(n_cd)])
    pairs = [(k * n_cd + i, (1 - k) * n_cd + (i + by) % n_cd) for k in range(2) for i in range(n_cd)]
    return lax.ppermute(x, ("core", "cd"), pairs)


def per_device(t2_amps, integrals, ab_sym, cd_sym):
    zh, n_cd = lax.axis_size("zh"), lax.axis_size("cd")
    n_chunks = len(SPLIT)
    own = list(sort_amps(t2_amps, cd_sym))
    t2s, sent_on, late = [], [], []

    def gather(c, earlier):
        earlier = list(earlier)
        if c > 1:
            own[c] = after(own[c], t2s[c - 2][0])
        others = [lax.ppermute(own[c], "zh", [(i, i ^ d) for i in range(zh)]) for d in range(1, zh)]
        near = merge([own[c]] + others, earlier)
        up, across = lax.ppermute(near, "zl", SWAP), lax.ppermute(near, "x", SWAP)
        far = lax.ppermute(across, "zl", SWAP) if c in ALONG_Z else lax.ppermute(up, "x", SWAP)
        t2s.append((near, up, across, far))

    ints = list(sort_ints(integrals, ab_sym, own[0]))
    gather(0, ints[:1])
    ints = [after(x, t2s[0][0]) for x in ints]
    sib_ints = [lax.ppermute(x, "core", SWAP) for x in ints]
    gather(1, t2s[0][1:3])
    latest = t2s[1][0]
    for c, syms in enumerate(SPLIT):
        first = sum(SPLIT[:c])
        part = 0
        while first >= INTS_SPLIT[part]:
            first -= INTS_SPLIT[part]
            part += 1
        earlier = [latest]
        if c + 2 == n_chunks:
            earlier += t2s[c + 1][1:3]
        if c:
            earlier += sent_on[c - 1][1:]
        last = c + 1 == n_chunks
        made = list(contract(n_cd, last, t2s[c], ints[part], sib_ints[part], first, syms, earlier))
        latest = made[0]
        if last:
            late = [sent(made[2 * by + k], by, k) for by in range(n_cd) for k in range(2)]
        else:
            sent_on.append([sent(made[by], by, 0) for by in range(n_cd)])
        if c + 2 < n_chunks:
            gather(c + 2, [latest, t2s[c + 1][1], t2s[c + 1][2]])
            latest = t2s[c + 2][0]
    sums = []
    for chunks in SUMS:
        mine, other = add_early(n_cd, [p for c in chunks for p in sent_on[c]], [latest])
        latest = mine
        sums += [mine, lax.ppermute(other, "core", SWAP)]
    return finish(n_cd, ab_sym, sums, late, t2_amps.shape[0])


def solution(mesh):
    n_blk, n_cd = mesh.devices.shape
    blk = ("zh", "zl", "x", "core")
    parted = Mesh(mesh.devices.reshape(n_blk // 8, 2, 2, 2, n_cd), blk + ("cd",))
    in_specs = (P(blk, "cd"), P(blk, None, "cd"), P(blk), P("cd"))
    return jax.shard_map(
        per_device, mesh=parted, in_specs=in_specs, out_specs=P("cd", blk), check_vma=False
    )
```

```python
import functools

import jax
import jax.numpy as jnp
from jax import lax
from jax.experimental import pallas as pl
from jax.experimental.pallas import tpu as pltpu
from jax.sharding import Mesh, PartitionSpec as P

NSYM = 8
SPLIT = (2, 2, 2, 2)
ALONG_Z = (1, 3)
INTS_SPLIT = (2, 6)
LANES = 128
VMEM_LIMIT = 20 * 2**20

ANY = pl.BlockSpec(memory_space=pl.ANY)
SMEM = pl.BlockSpec(memory_space=pltpu.SMEM)
VMEM = pl.BlockSpec(memory_space=pltpu.VMEM)

CHEAP = pl.CostEstimate(flops=1000, bytes_accessed=1000, transcendentals=0)


def params(limit=VMEM_LIMIT):
    return pltpu.CompilerParams(vmem_limit_bytes=limit)


def half_turned(x):
    half = LANES // 2
    return jnp.concatenate([x[:, half:], x[:, :half]], axis=1)


def rank_tiles(sym_ref, count_ref, order_ref, place_ref, tiles):
    for s in range(NSYM):
        count_ref[s] = s * (tiles // NSYM)

    def step(i, _):
        s = sym_ref[i]
        p = count_ref[s]
        count_ref[s] = p + 1
        if order_ref is not None:
            order_ref[p] = i
        if place_ref is not None:
            place_ref[i] = p
        return 0

    lax.fori_loop(0, tiles, step, 0)


def pick_pair(both, a, b, left):
    columns = both.shape[2] // LANES
    a_col = lax.shift_right_logical(a, 1)
    b_col = lax.rem(lax.shift_right_logical(b + 1, 1) + columns - 1, columns)
    xa = both[a & 1, :, pl.ds(pl.multiple_of(a_col * LANES, LANES), LANES)]
    xb = both[(b & 1) ^ 1, :, pl.ds(pl.multiple_of(b_col * LANES, LANES), LANES)]
    return jnp.where(left, xa, xb)


def sort_amps_kernel(cd_ref, t2_ref, *rest):
    chunks, (both, count, order, sem) = rest[:-4], rest[-4:]
    rows = t2_ref.shape[0]
    load = pltpu.make_async_copy(t2_ref, both.at[0], sem)
    load.start()
    rank_tiles(cd_ref, count, order, None, cd_ref.shape[0])
    load.wait()
    both[1] = half_turned(both[0])
    left = lax.broadcasted_iota(jnp.int32, (rows, LANES), 1) < LANES // 2
    q = 0
    for chunk in chunks:
        for off in range(chunk.shape[1] // LANES):
            pair = pick_pair(both, order[2 * q], order[2 * q + 1], left)
            chunk[:, off * LANES : (off + 1) * LANES] = pair
            q += 1


def sort_amps(t2, cd_sym):
    rows, cols = t2.shape
    return pl.pallas_call(
        sort_amps_kernel,
        out_shape=[
            jax.ShapeDtypeStruct((rows, cols // NSYM * m), t2.dtype) for m in (SPLIT[0], NSYM - SPLIT[0])
        ],
        in_specs=[SMEM, ANY],
        out_specs=[VMEM] * 2,
        scratch_shapes=[
            pltpu.VMEM((2, rows, cols), t2.dtype),
            pltpu.SMEM((NSYM,), jnp.int32),
            pltpu.SMEM((cd_sym.shape[0],), jnp.int32),
            pltpu.SemaphoreType.DMA,
        ],
        compiler_params=params(),
        cost_estimate=CHEAP,
        name="sort_amps",
    )(cd_sym, t2)


def sort_ints_kernel(ab_ref, ints_ref, _, *rest):
    parts, (count, order) = rest[:-2], rest[-2:]
    tiles = ab_ref.shape[0]
    rank_tiles(ab_ref, count, order, None, tiles)
    per_sym = tiles // NSYM
    sym = 0
    for part in parts:
        for s in range(part.shape[0]):
            rows = [ints_ref[order[sym * per_sym + m]] for m in range(per_sym)]
            part[s] = jnp.concatenate(rows, axis=0).T
            sym += 1


def sort_ints(integrals, ab_sym, earlier):
    tiles, tile, packed = integrals.shape
    return pl.pallas_call(
        sort_ints_kernel,
        out_shape=[
            jax.ShapeDtypeStruct((m, packed, tiles // NSYM * tile), integrals.dtype)
            for m in INTS_SPLIT
        ],
        in_specs=[SMEM, VMEM, ANY],
        out_specs=[VMEM] * len(INTS_SPLIT),
        scratch_shapes=[pltpu.SMEM((NSYM,), jnp.int32), pltpu.SMEM((tiles,), jnp.int32)],
        compiler_params=params(),
        cost_estimate=CHEAP,
        name="sort_ints",
    )(ab_sym, integrals, earlier)


def merge_kernel(n, *refs):
    blocks, outs = refs[:n], refs[n:]
    me = lax.axis_index("zh")
    for d, block in enumerate(blocks):
        first = 0
        for out_ref in outs:
            width = out_ref.shape[2]
            out_ref[me ^ d] = block[:, first : first + width]
            first += width


def merge(blocks, widths, earlier):
    n = len(blocks)

    def kernel(*refs):
        merge_kernel(n, *refs[:n], *refs[n + len(earlier) :])

    return pl.pallas_call(
        kernel,
        out_shape=[
            jax.ShapeDtypeStruct((n, blocks[0].shape[0], w), blocks[0].dtype) for w in widths
        ],
        in_specs=[VMEM] * n + [ANY] * len(earlier),
        out_specs=[VMEM] * len(widths),
        compiler_params=params(),
        cost_estimate=CHEAP,
        name="merge",
    )(*blocks, *earlier)


def nothing(*refs):
    pass


def after(x, *earlier):
    return pl.pallas_call(
        nothing,
        out_shape=jax.ShapeDtypeStruct(x.shape, x.dtype),
        in_specs=[ANY] * (1 + len(earlier)),
        out_specs=ANY,
        input_output_aliases={0: 0},
        compiler_params=params(),
        cost_estimate=CHEAP,
        name="after",
    )(x, *earlier)


def contract_kernel(n_cd, apart, first_sym, syms, near, up, across, far, own_ref, sib_ref, *rest):
    outs, lhs = rest[-n_cd * (1 + apart) - 1 : -1], rest[-1]
    slots, rows, cols = lhs.shape
    packed, width = own_ref.shape[1:]
    z, x = lax.axis_index("zl"), lax.axis_index("x")
    first = lax.axis_index("cd") * (slots // n_cd)
    for i in range(slots // 4):
        for block, zl, xs in ((near, z, x), (up, 1 - z, x), (across, z, 1 - x), (far, 1 - z, 1 - x)):
            lhs[lax.rem(4 * i + 2 * zl + xs + slots - first, slots)] = block[i]
    t2 = lhs[...].reshape(slots * rows, cols)
    group_rows = t2.shape[0] // n_cd
    for side, ints in enumerate((own_ref, sib_ref)):
        for s in range(syms):
            part = jnp.dot(
                t2[:, s * packed : (s + 1) * packed],
                ints[first_sym + s],
                preferred_element_type=jnp.float32,
            ).astype(outs[0].dtype)
            for by in range(n_cd):
                these = part[by * group_rows : (by + 1) * group_rows]
                if apart:
                    outs[2 * by + side][:, s * width : (s + 1) * width] = these
                else:
                    outs[by][side, :, s * width : (s + 1) * width] = these


def contract(n_cd, apart, t2s, ints, sib_ints, first_sym, syms, earlier):
    zh, rows, cols = t2s[0].shape
    packed, width = ints.shape[1:]
    all_rows = 4 * zh * rows
    out = (all_rows // n_cd, syms * width)
    outs = [out] * (2 * n_cd) if apart else [(2,) + out] * n_cd
    return pl.pallas_call(
        functools.partial(contract_kernel, n_cd, apart, first_sym, syms),
        out_shape=[jax.ShapeDtypeStruct(x, jnp.bfloat16) for x in outs],
        in_specs=[VMEM] * 6 + [ANY] * len(earlier),
        out_specs=[VMEM] * len(outs),
        scratch_shapes=[pltpu.VMEM((4 * zh, rows, cols), jnp.bfloat16)],
        compiler_params=params(),
        cost_estimate=CHEAP,
        name="contract",
    )(*t2s, ints, sib_ints, *earlier)


def total(refs, these):
    value = refs[0][these].astype(jnp.float32)
    for ref in refs[1:]:
        value += ref[these].astype(jnp.float32)
    return value.astype(jnp.bfloat16)


def early_kernel(n_cd, chunks, *refs):
    parts, (own_ref, sib_ref) = refs[: chunks * n_cd], refs[-2:]
    step = own_ref.shape[0]
    for side, out_ref in enumerate((own_ref, sib_ref)):
        first = 0
        for c in range(chunks):
            mine = parts[c * n_cd : (c + 1) * n_cd]
            width = mine[0].shape[2]
            out_ref[:, first : first + width] = total(mine, side)
            first += width


def add_early(n_cd, parts, earlier):
    rows = parts[0].shape[1]
    cols = sum(p.shape[2] for p in parts[::n_cd])
    step = rows // 4
    spec = pl.BlockSpec((step, cols), lambda i: (i, 0))
    return pl.pallas_call(
        functools.partial(early_kernel, n_cd, len(parts) // n_cd),
        out_shape=[jax.ShapeDtypeStruct((rows, cols), jnp.bfloat16)] * 2,
        grid=(rows // step,),
        in_specs=[pl.BlockSpec((2, step, p.shape[2]), lambda i: (0, i, 0)) for p in parts]
        + [ANY] * len(earlier),
        out_specs=[spec, spec],
        compiler_params=params(),
        cost_estimate=CHEAP,
        name="add_early",
    )(*parts, *earlier)


def finish_kernel(n_cd, ab_ref, *rest):
    sums, late, (out_ref, made, both, count, place, sems) = rest[:2], rest[2:-6], rest[-6:]
    blocks, rows, cols = made.shape
    rank_tiles(ab_ref, count, None, place, ab_ref.shape[0])
    core = lax.axis_index("core")
    left = lax.broadcasted_iota(jnp.int32, (rows, LANES), 1) < LANES // 2

    def copy_out(i):
        return pltpu.make_async_copy(made.at[i], out_ref.at[i], sems.at[i])

    def block(i, _):
        these = pl.ds(pl.multiple_of(i * rows, rows), rows)
        for side in range(2):
            width = sums[side].shape[1]
            both[0, :, :width] = sums[side][these]
            both[0, :, width:] = total(late[side::2], these)
            both[1] = half_turned(both[0])
            out = 2 * i + (core ^ side)
            for q in range(cols // LANES):
                made[out, :, q * LANES : (q + 1) * LANES] = pick_pair(
                    both, place[2 * q], place[2 * q + 1], left
                )
            copy_out(out).start()
        return 0

    lax.fori_loop(0, blocks // 2, block, 0)
    for i in range(blocks):
        copy_out(i).wait()


def finish(n_cd, ab_sym, sums, late, rows):
    blocks = 2 * late[0].shape[0] // rows
    cols = sum(p.shape[1] for p in sums[::2]) + late[0].shape[1]
    out = pl.pallas_call(
        functools.partial(finish_kernel, n_cd),
        out_shape=jax.ShapeDtypeStruct((blocks, rows, cols), jnp.bfloat16),
        in_specs=[SMEM] + [VMEM] * (len(sums) + len(late)),
        out_specs=ANY,
        scratch_shapes=[
            pltpu.VMEM((blocks, rows, cols), jnp.bfloat16),
            pltpu.VMEM((2, rows, cols), jnp.bfloat16),
            pltpu.SMEM((NSYM,), jnp.int32),
            pltpu.SMEM((ab_sym.shape[0],), jnp.int32),
            pltpu.SemaphoreType.DMA((blocks,)),
        ],
        compiler_params=params(),
        cost_estimate=CHEAP,
        name="finish",
    )(ab_sym, *sums, *late)
    return out.reshape(blocks * rows, cols)


SWAP = [(0, 1), (1, 0)]


def sent(x, by, side):
    n_cd = lax.axis_size("cd")
    if not by:
        return lax.ppermute(x, "core", SWAP) if side else x
    if not side:
        return lax.ppermute(x, "cd", [(i, (i + by) % n_cd) for i in range(n_cd)])
    pairs = [(k * n_cd + i, (1 - k) * n_cd + (i + by) % n_cd) for k in range(2) for i in range(n_cd)]
    return lax.ppermute(x, ("core", "cd"), pairs)


def per_device(t2_amps, integrals, ab_sym, cd_sym):
    zh, n_cd = lax.axis_size("zh"), lax.axis_size("cd")
    n_chunks = len(SPLIT)
    own = list(sort_amps(t2_amps, cd_sym))
    widths = [t2_amps.shape[1] // NSYM * m for m in SPLIT]

    def along_zh(x, widths, earlier):
        others = [lax.ppermute(x, "zh", [(i, i ^ d) for i in range(zh)]) for d in range(1, zh)]
        return list(merge([x] + others, widths, earlier))

    def spread(near, c):
        up, across = lax.ppermute(near, "zl", SWAP), lax.ppermute(near, "x", SWAP)
        far = lax.ppermute(across, "zl", SWAP) if c in ALONG_Z else lax.ppermute(up, "x", SWAP)
        return near, up, across, far

    ints = list(sort_ints(integrals, ab_sym, own[0]))
    near = along_zh(own[0], widths[:1], ints[:1])
    t2s = [spread(near[0], 0)]
    ints = [after(x, near[0]) for x in ints]
    sib_ints = [lax.ppermute(x, "core", SWAP) for x in ints]
    latest, sent_on, late = near[0], [], []
    for c, syms in enumerate(SPLIT):
        first = sum(SPLIT[:c])
        part = 0
        while first >= INTS_SPLIT[part]:
            first -= INTS_SPLIT[part]
            part += 1
        earlier = [latest]
        if 0 < c < n_chunks - 1:
            earlier += t2s[c + 1][1:3]
        if c:
            earlier += sent_on[c - 1][1:]
        last = c + 1 == n_chunks
        if last:
            mine, other = add_early(n_cd, [p for x in sent_on for p in x], earlier + [t2s[c][3]])
            sums = [mine, lax.ppermute(other, "core", SWAP)]
            earlier.append(mine)
        made = list(contract(n_cd, last, t2s[c], ints[part], sib_ints[part], first, syms, earlier))
        latest = made[0]
        if last:
            late = [sent(made[2 * by + k], by, k) for by in range(n_cd) for k in range(2)]
        else:
            sent_on.append([sent(made[by], by, 0) for by in range(n_cd)])
        if not c:
            near = along_zh(own[1], widths[1:], [latest])
            t2s += [spread(x, i + 1) for i, x in enumerate(near)]
            latest = near[0]
    return finish(n_cd, ab_sym, sums, late, t2_amps.shape[0])


def solution(mesh):
    n_blk, n_cd = mesh.devices.shape
    blk = ("zh", "zl", "x", "core")
    parted = Mesh(mesh.devices.reshape(n_blk // 8, 2, 2, 2, n_cd), blk + ("cd",))
    in_specs = (P(blk, "cd"), P(blk, None, "cd"), P(blk), P("cd"))
    return jax.shard_map(
        per_device, mesh=parted, in_specs=in_specs, out_specs=P("cd", blk), check_vma=False
    )
```

```python
import functools

import jax
import jax.numpy as jnp
from jax import lax
from jax.experimental import pallas as pl
from jax.experimental.pallas import tpu as pltpu
from jax.sharding import Mesh, PartitionSpec as P

NSYM = 8
LATER = 4
LANES = 128
VMEM_LIMIT = 20 * 2**20

ANY = pl.BlockSpec(memory_space=pl.ANY)
SMEM = pl.BlockSpec(memory_space=pltpu.SMEM)
VMEM = pl.BlockSpec(memory_space=pltpu.VMEM)

CHEAP = pl.CostEstimate(flops=1000, bytes_accessed=1000, transcendentals=0)


def params(limit=VMEM_LIMIT):
    return pltpu.CompilerParams(vmem_limit_bytes=limit)


def half_turned(x):
    half = LANES // 2
    return jnp.concatenate([x[:, half:], x[:, :half]], axis=1)


def rank_tiles(sym_ref, count_ref, order_ref, place_ref, tiles):
    for s in range(NSYM):
        count_ref[s] = s * (tiles // NSYM)

    def step(i, _):
        s = sym_ref[i]
        p = count_ref[s]
        count_ref[s] = p + 1
        if order_ref is not None:
            order_ref[p] = i
        if place_ref is not None:
            place_ref[i] = p
        return 0

    lax.fori_loop(0, tiles, step, 0)


def pick_pair(both, a, b, left):
    columns = both.shape[2] // LANES
    a_col = lax.shift_right_logical(a, 1)
    b_col = lax.rem(lax.shift_right_logical(b + 1, 1) + columns - 1, columns)
    xa = both[a & 1, :, pl.ds(pl.multiple_of(a_col * LANES, LANES), LANES)]
    xb = both[(b & 1) ^ 1, :, pl.ds(pl.multiple_of(b_col * LANES, LANES), LANES)]
    return jnp.where(left, xa, xb)


def sort_amps_kernel(cd_ref, t2_ref, *rest):
    chunks, (both, count, order, sem) = rest[:-4], rest[-4:]
    rows = t2_ref.shape[0]
    load = pltpu.make_async_copy(t2_ref, both.at[0], sem)
    load.start()
    rank_tiles(cd_ref, count, order, None, cd_ref.shape[0])
    load.wait()
    both[1] = half_turned(both[0])
    left = lax.broadcasted_iota(jnp.int32, (rows, LANES), 1) < LANES // 2
    q = 0
    for chunk in chunks:
        for off in range(chunk.shape[1] // LANES):
            pair = pick_pair(both, order[2 * q], order[2 * q + 1], left)
            chunk[:, off * LANES : (off + 1) * LANES] = pair
            q += 1


def sort_amps(t2, cd_sym):
    rows, cols = t2.shape
    return pl.pallas_call(
        sort_amps_kernel,
        out_shape=[
            jax.ShapeDtypeStruct((rows, cols // NSYM * m), t2.dtype) for m in (NSYM - LATER, LATER)
        ],
        in_specs=[SMEM, ANY],
        out_specs=[VMEM] * 2,
        scratch_shapes=[
            pltpu.VMEM((2, rows, cols), t2.dtype),
            pltpu.SMEM((NSYM,), jnp.int32),
            pltpu.SMEM((cd_sym.shape[0],), jnp.int32),
            pltpu.SemaphoreType.DMA,
        ],
        compiler_params=params(),
        cost_estimate=CHEAP,
        name="sort_amps",
    )(cd_sym, t2)


def sort_ints_kernel(ab_ref, ints_ref, _, out_ref, later_ref, count, order):
    tiles = ab_ref.shape[0]
    rank_tiles(ab_ref, count, order, None, tiles)
    per_sym = tiles // NSYM
    for s in range(NSYM):
        rows = [ints_ref[order[s * per_sym + m]] for m in range(per_sym)]
        turned = jnp.concatenate(rows, axis=0).T
        out_ref[s] = turned
        if s >= NSYM - LATER:
            later_ref[s - NSYM + LATER] = turned


def sort_ints(integrals, ab_sym, earlier):
    tiles, tile, packed = integrals.shape
    return pl.pallas_call(
        sort_ints_kernel,
        out_shape=[
            jax.ShapeDtypeStruct((m, packed, tiles // NSYM * tile), integrals.dtype)
            for m in (NSYM, LATER)
        ],
        in_specs=[SMEM, VMEM, ANY],
        out_specs=[VMEM] * 2,
        scratch_shapes=[pltpu.SMEM((NSYM,), jnp.int32), pltpu.SMEM((tiles,), jnp.int32)],
        compiler_params=params(),
        cost_estimate=CHEAP,
        name="sort_ints",
    )(ab_sym, integrals, earlier)


def merge_kernel(n, *refs):
    blocks, out_ref = refs[:n], refs[-1]
    me = lax.axis_index("zh")
    for d, block in enumerate(blocks):
        out_ref[me ^ d] = block[...]


def merge(blocks, earlier):
    return pl.pallas_call(
        functools.partial(merge_kernel, len(blocks)),
        out_shape=jax.ShapeDtypeStruct((len(blocks),) + blocks[0].shape, blocks[0].dtype),
        in_specs=[VMEM] * len(blocks) + [ANY] * len(earlier),
        out_specs=VMEM,
        compiler_params=params(),
        cost_estimate=CHEAP,
        name="merge",
    )(*blocks, *earlier)


def nothing(*refs):
    pass


def after(x, *earlier):
    return pl.pallas_call(
        nothing,
        out_shape=jax.ShapeDtypeStruct(x.shape, x.dtype),
        in_specs=[ANY] * (1 + len(earlier)),
        out_specs=ANY,
        input_output_aliases={0: 0},
        compiler_params=params(),
        cost_estimate=CHEAP,
        name="after",
    )(x, *earlier)


def lay_out(lhs, blocks, place):
    z, x = lax.axis_index("zl"), lax.axis_index("x")
    near, up, across, far = blocks
    for i in range(lhs.shape[0] // 4):
        for block, zl, xs in ((near, z, x), (up, 1 - z, x), (across, z, 1 - x), (far, 1 - z, 1 - x)):
            lhs[place(4 * i + 2 * zl + xs)] = block[i]


def contract_kernel(n_cd, *refs):
    blocks, (own_ref, sib_ref), outs, lhs = refs[:4], refs[4:6], refs[-n_cd - 1 : -1], refs[-1]
    slots, rows, cols = lhs.shape
    packed, width = own_ref.shape[1:]
    first = lax.axis_index("cd") * (slots // n_cd)
    lay_out(lhs, blocks, lambda n: lax.rem(n + slots - first, slots))
    t2 = lhs[...].reshape(slots * rows, cols)
    group_rows = t2.shape[0] // n_cd
    for side, ints in enumerate((own_ref, sib_ref)):
        for s in range(cols // packed):
            part = jnp.dot(
                t2[:, s * packed : (s + 1) * packed], ints[s], preferred_element_type=jnp.float32
            ).astype(outs[0].dtype)
            for by in range(n_cd):
                outs[by][side, :, s * width : (s + 1) * width] = part[
                    by * group_rows : (by + 1) * group_rows
                ]


def contract(n_cd, t2s, ints, sib_ints, earlier):
    zh, rows, cols = t2s[0].shape
    packed, width = ints.shape[1:]
    all_rows = 4 * zh * rows
    out = (2, all_rows // n_cd, cols // packed * width)
    return pl.pallas_call(
        functools.partial(contract_kernel, n_cd),
        out_shape=[jax.ShapeDtypeStruct(out, jnp.bfloat16)] * n_cd,
        in_specs=[VMEM] * 6 + [ANY] * len(earlier),
        out_specs=[VMEM] * n_cd,
        scratch_shapes=[pltpu.VMEM((4 * zh, rows, cols), jnp.bfloat16)],
        compiler_params=params(),
        cost_estimate=CHEAP,
        name="contract",
    )(*t2s, ints, sib_ints, *earlier)


def total(parts):
    value = parts[0].astype(jnp.float32)
    for part in parts[1:]:
        value += part.astype(jnp.float32)
    return value.astype(jnp.bfloat16)


def later_kernel(n_cd, *refs):
    blocks, (own_ref, sib_ref), rest = refs[:4], refs[4:6], refs[6:]
    others, parts, (own_out, sib_out, lhs) = rest[: 2 * n_cd - 2], rest[2 * n_cd - 2 : -3], rest[-3:]
    slots, rows, cols = lhs.shape
    packed, width = own_ref.shape[1:]
    per_group, me = slots // n_cd, lax.axis_index("cd")

    def place(n):
        group = n // per_group
        return lax.rem(me + n_cd - group, n_cd) * per_group + (n - group * per_group)

    lay_out(lhs, blocks, place)
    t2 = lhs[...].reshape(n_cd, per_group * rows, cols)
    syms = cols // packed
    before = parts[0].shape[2]
    for side, out_ref in enumerate((own_out, sib_out)):
        out_ref[:, :before] = total([part[side] for part in parts])
        for s in range(syms):
            made = []
            for by in range(n_cd):
                if by:
                    ints = others[2 * (by - 1) + side][s]
                else:
                    ints = (own_ref, sib_ref)[side][own_ref.shape[0] - syms + s]
                made.append(
                    jnp.dot(
                        t2[by, :, s * packed : (s + 1) * packed],
                        ints,
                        preferred_element_type=jnp.float32,
                    ).astype(out_ref.dtype)
                )
            out_ref[:, before + s * width : before + (s + 1) * width] = total(made)


def contract_later(n_cd, t2s, ints, sib_ints, others, parts):
    zh, rows, cols = t2s[0].shape
    packed, width = ints.shape[1:]
    out = jax.ShapeDtypeStruct((parts[0].shape[1], ints.shape[0] * width), jnp.bfloat16)
    return pl.pallas_call(
        functools.partial(later_kernel, n_cd),
        out_shape=[out, out],
        in_specs=[VMEM] * (6 + len(others) + len(parts)),
        out_specs=[VMEM] * 2,
        scratch_shapes=[pltpu.VMEM((4 * zh, rows, cols), jnp.bfloat16)],
        compiler_params=params(),
        cost_estimate=CHEAP,
        name="contract_later",
    )(*t2s, ints, sib_ints, *others, *parts)


def finish_kernel(ab_ref, own_ref, sib_ref, out_ref, made, turned, count, place, sems):
    blocks, rows, cols = made.shape
    rank_tiles(ab_ref, count, None, place, ab_ref.shape[0])
    core = lax.axis_index("core")
    left = lax.broadcasted_iota(jnp.int32, (rows, LANES), 1) < LANES // 2

    def copy_out(i):
        return pltpu.make_async_copy(made.at[i], out_ref.at[i], sems.at[i])

    def block(i, _):
        these = pl.ds(pl.multiple_of(i * rows, rows), rows)
        for side, ref in enumerate((own_ref, sib_ref)):
            turned[0] = ref[these]
            turned[1] = half_turned(turned[0])
            out = 2 * i + (core ^ side)
            for q in range(cols // LANES):
                made[out, :, q * LANES : (q + 1) * LANES] = pick_pair(
                    turned, place[2 * q], place[2 * q + 1], left
                )
            copy_out(out).start()
        return 0

    lax.fori_loop(0, blocks // 2, block, 0)
    for i in range(blocks):
        copy_out(i).wait()


def finish(ab_sym, own, sib, rows):
    blocks, cols = 2 * own.shape[0] // rows, own.shape[1]
    out = pl.pallas_call(
        finish_kernel,
        out_shape=jax.ShapeDtypeStruct((blocks, rows, cols), jnp.bfloat16),
        in_specs=[SMEM] + [VMEM] * 2,
        out_specs=ANY,
        scratch_shapes=[
            pltpu.VMEM((blocks, rows, cols), jnp.bfloat16),
            pltpu.VMEM((2, rows, cols), jnp.bfloat16),
            pltpu.SMEM((NSYM,), jnp.int32),
            pltpu.SMEM((ab_sym.shape[0],), jnp.int32),
            pltpu.SemaphoreType.DMA((blocks,)),
        ],
        compiler_params=params(),
        cost_estimate=CHEAP,
        name="finish",
    )(ab_sym, own, sib)
    return out.reshape(blocks * rows, cols)


SWAP = [(0, 1), (1, 0)]


def further(x, by):
    n_cd = lax.axis_size("cd")
    return lax.ppermute(x, "cd", [(i, (i + by) % n_cd) for i in range(n_cd)])


def to_plane(x):
    n_cd = lax.axis_size("cd")
    z_len = 2 * lax.axis_size("zh")
    rest = z_len // n_cd
    pairs = []
    for z in range(z_len):
        group, i = divmod(z, rest)
        pairs += [(z * n_cd + y, (y * rest + i) * n_cd + group) for y in range(n_cd)]
    return lax.ppermute(x, ("zh", "zl", "cd"), pairs)


def per_device(t2_amps, integrals, ab_sym, cd_sym):
    zh, n_cd = lax.axis_size("zh"), lax.axis_size("cd")

    def along_zh(x, earlier):
        others = [lax.ppermute(x, "zh", [(i, i ^ d) for i in range(zh)]) for d in range(1, zh)]
        return merge([x] + others, earlier)

    def spread(near):
        across_both = [(0, 3), (1, 2), (2, 1), (3, 0)]
        return (
            near,
            lax.ppermute(near, "zl", SWAP),
            lax.ppermute(near, "x", SWAP),
            lax.ppermute(near, ("zl", "x"), across_both),
        )

    own, own_later = sort_amps(t2_amps, cd_sym)
    ints, ints_later = sort_ints(integrals, ab_sym, own)
    own_later = to_plane(own_later)
    near = along_zh(own, [ints])
    sib_ints = lax.ppermute(ints, "core", SWAP)
    ints_later = after(ints_later, near)
    others = [further(ints_later, by) for by in range(1, n_cd)]
    t2s = spread(near)
    near_later = along_zh(after(own_later, sib_ints), [*t2s[1:], *others])
    made = contract(n_cd, t2s, ints, sib_ints, [near_later])
    parts = [made[0]] + [further(made[by], by) for by in range(1, n_cd)]
    t2s_later = spread(near_later)
    others = [after(x, near_later) for x in others]
    others = [y for x in others for y in (x, lax.ppermute(x, "core", SWAP))]
    sums, sib_sums = contract_later(n_cd, t2s_later, ints, sib_ints, others, parts)
    return finish(ab_sym, sums, lax.ppermute(sib_sums, "core", SWAP), t2_amps.shape[0])


def solution(mesh):
    n_blk, n_cd = mesh.devices.shape
    blk = ("zh", "zl", "x", "core")
    parted = Mesh(mesh.devices.reshape(n_blk // 8, 2, 2, 2, n_cd), blk + ("cd",))
    in_specs = (P(blk, "cd"), P(blk, None, "cd"), P(blk), P("cd"))
    return jax.shard_map(
        per_device, mesh=parted, in_specs=in_specs, out_specs=P("cd", blk), check_vma=False
    )
```

```python
import functools

import jax
import jax.numpy as jnp
from jax import lax
from jax.experimental import pallas as pl
from jax.experimental.pallas import tpu as pltpu
from jax.sharding import Mesh, PartitionSpec as P

NSYM = 8
SPLIT = (1, 2, 2, 2, 1)
ALONG_Z = (3,)
INTS_SPLIT = (3, 5)
LANES = 128
VMEM_LIMIT = 20 * 2**20

ANY = pl.BlockSpec(memory_space=pl.ANY)
SMEM = pl.BlockSpec(memory_space=pltpu.SMEM)
VMEM = pl.BlockSpec(memory_space=pltpu.VMEM)

CHEAP = pl.CostEstimate(flops=1000, bytes_accessed=1000, transcendentals=0)


def params(limit=VMEM_LIMIT):
    return pltpu.CompilerParams(vmem_limit_bytes=limit)


def half_turned(x):
    half = LANES // 2
    return jnp.concatenate([x[:, half:], x[:, :half]], axis=1)


def rank_tiles(sym_ref, count_ref, order_ref, place_ref, tiles):
    for s in range(NSYM):
        count_ref[s] = s * (tiles // NSYM)

    def step(i, _):
        s = sym_ref[i]
        p = count_ref[s]
        count_ref[s] = p + 1
        if order_ref is not None:
            order_ref[p] = i
        if place_ref is not None:
            place_ref[i] = p
        return 0

    lax.fori_loop(0, tiles, step, 0)


def pick_pair(both, a, b, left):
    columns = both.shape[2] // LANES
    a_col = lax.shift_right_logical(a, 1)
    b_col = lax.rem(lax.shift_right_logical(b + 1, 1) + columns - 1, columns)
    xa = both[a & 1, :, pl.ds(pl.multiple_of(a_col * LANES, LANES), LANES)]
    xb = both[(b & 1) ^ 1, :, pl.ds(pl.multiple_of(b_col * LANES, LANES), LANES)]
    return jnp.where(left, xa, xb)


def sort_amps_kernel(cd_ref, t2_ref, *rest):
    chunks, (both, count, order, sem) = rest[:-4], rest[-4:]
    rows = t2_ref.shape[0]
    load = pltpu.make_async_copy(t2_ref, both.at[0], sem)
    load.start()
    rank_tiles(cd_ref, count, order, None, cd_ref.shape[0])
    load.wait()
    both[1] = half_turned(both[0])
    left = lax.broadcasted_iota(jnp.int32, (rows, LANES), 1) < LANES // 2
    q = 0
    for chunk in chunks:
        for off in range(chunk.shape[1] // LANES):
            pair = pick_pair(both, order[2 * q], order[2 * q + 1], left)
            chunk[:, off * LANES : (off + 1) * LANES] = pair
            q += 1


def sort_amps(t2, cd_sym):
    rows, cols = t2.shape
    return pl.pallas_call(
        sort_amps_kernel,
        out_shape=[
            jax.ShapeDtypeStruct((rows, cols // NSYM * m), t2.dtype) for m in SPLIT
        ],
        in_specs=[SMEM, ANY],
        out_specs=[VMEM] * len(SPLIT),
        scratch_shapes=[
            pltpu.VMEM((2, rows, cols), t2.dtype),
            pltpu.SMEM((NSYM,), jnp.int32),
            pltpu.SMEM((cd_sym.shape[0],), jnp.int32),
            pltpu.SemaphoreType.DMA,
        ],
        compiler_params=params(),
        cost_estimate=CHEAP,
        name="sort_amps",
    )(cd_sym, t2)


def sort_ints_kernel(ab_ref, ints_ref, _, *rest):
    parts, (count, order) = rest[:-2], rest[-2:]
    tiles = ab_ref.shape[0]
    rank_tiles(ab_ref, count, order, None, tiles)
    per_sym = tiles // NSYM
    sym = 0
    for part in parts:
        for s in range(part.shape[0]):
            rows = [ints_ref[order[sym * per_sym + m]] for m in range(per_sym)]
            part[s] = jnp.concatenate(rows, axis=0).T
            sym += 1


def sort_ints(integrals, ab_sym, earlier):
    tiles, tile, packed = integrals.shape
    return pl.pallas_call(
        sort_ints_kernel,
        out_shape=[
            jax.ShapeDtypeStruct((m, packed, tiles // NSYM * tile), integrals.dtype)
            for m in INTS_SPLIT
        ],
        in_specs=[SMEM, VMEM, ANY],
        out_specs=[VMEM] * len(INTS_SPLIT),
        scratch_shapes=[pltpu.SMEM((NSYM,), jnp.int32), pltpu.SMEM((tiles,), jnp.int32)],
        compiler_params=params(),
        cost_estimate=CHEAP,
        name="sort_ints",
    )(ab_sym, integrals, earlier)


def merge_kernel(n, *refs):
    blocks, out_ref = refs[:n], refs[-1]
    me = lax.axis_index("zh")
    for d, block in enumerate(blocks):
        out_ref[me ^ d] = block[...]


def merge(blocks, earlier):
    return pl.pallas_call(
        functools.partial(merge_kernel, len(blocks)),
        out_shape=jax.ShapeDtypeStruct((len(blocks),) + blocks[0].shape, blocks[0].dtype),
        in_specs=[VMEM] * len(blocks) + [ANY] * len(earlier),
        out_specs=VMEM,
        compiler_params=params(),
        cost_estimate=CHEAP,
        name="merge",
    )(*blocks, *earlier)


def nothing(*refs):
    pass


def after(x, *earlier):
    return pl.pallas_call(
        nothing,
        out_shape=jax.ShapeDtypeStruct(x.shape, x.dtype),
        in_specs=[ANY] * (1 + len(earlier)),
        out_specs=ANY,
        input_output_aliases={0: 0},
        compiler_params=params(),
        cost_estimate=CHEAP,
        name="after",
    )(x, *earlier)


def contract_kernel(n_cd, first_sym, near, up, across, far, own_ref, sib_ref, *rest):
    outs, lhs = rest[-n_cd - 1 : -1], rest[-1]
    slots, rows, cols = lhs.shape
    packed, width = own_ref.shape[1:]
    z, x = lax.axis_index("zl"), lax.axis_index("x")
    first = lax.axis_index("cd") * (slots // n_cd)
    for i in range(slots // 4):
        for block, zl, xs in ((near, z, x), (up, 1 - z, x), (across, z, 1 - x), (far, 1 - z, 1 - x)):
            lhs[lax.rem(4 * i + 2 * zl + xs + slots - first, slots)] = block[i]
    t2 = lhs[...].reshape(slots * rows, cols)
    group_rows = t2.shape[0] // n_cd
    for side, ints in enumerate((own_ref, sib_ref)):
        for s in range(cols // packed):
            part = jnp.dot(
                t2[:, s * packed : (s + 1) * packed],
                ints[first_sym + s],
                preferred_element_type=jnp.float32,
            ).astype(outs[0].dtype)
            for by in range(n_cd):
                outs[by][side, :, s * width : (s + 1) * width] = part[
                    by * group_rows : (by + 1) * group_rows
                ]


def contract(n_cd, t2s, ints, sib_ints, first_sym, earlier):
    zh, rows, cols = t2s[0].shape
    packed, width = ints.shape[1:]
    all_rows = 4 * zh * rows
    out = (2, all_rows // n_cd, cols // packed * width)
    return pl.pallas_call(
        functools.partial(contract_kernel, n_cd, first_sym),
        out_shape=[jax.ShapeDtypeStruct(out, jnp.bfloat16)] * n_cd,
        in_specs=[VMEM] * 6 + [ANY] * len(earlier),
        out_specs=[VMEM] * n_cd,
        scratch_shapes=[pltpu.VMEM((4 * zh, rows, cols), jnp.bfloat16)],
        compiler_params=params(),
        cost_estimate=CHEAP,
        name="contract",
    )(*t2s, ints, sib_ints, *earlier)


def add_kernel(n_cd, *refs):
    parts, outs = refs[:-2], refs[-2:]
    for side, out_ref in enumerate(outs):
        first = 0
        for c in range(0, len(parts), n_cd):
            value = parts[c][side].astype(jnp.float32)
            for other in parts[c + 1 : c + n_cd]:
                value += other[side].astype(jnp.float32)
            out_ref[:, first : first + value.shape[1]] = value.astype(out_ref.dtype)
            first += value.shape[1]


def add_parts(n_cd, parts):
    out = (parts[0].shape[1], sum(p.shape[2] for p in parts[::n_cd]))
    return pl.pallas_call(
        functools.partial(add_kernel, n_cd),
        out_shape=[jax.ShapeDtypeStruct(out, jnp.bfloat16)] * 2,
        in_specs=[VMEM] * len(parts),
        out_specs=[VMEM] * 2,
        compiler_params=params(),
        cost_estimate=CHEAP,
        name="add_parts",
    )(*parts)


def finish_kernel(ab_ref, own_ref, sib_ref, out_ref, made, turned, count, place, sems):
    blocks, rows, cols = made.shape
    rank_tiles(ab_ref, count, None, place, ab_ref.shape[0])
    core = lax.axis_index("core")
    left = lax.broadcasted_iota(jnp.int32, (rows, LANES), 1) < LANES // 2

    def copy_out(i):
        return pltpu.make_async_copy(made.at[i], out_ref.at[i], sems.at[i])

    def block(i, _):
        these = pl.ds(pl.multiple_of(i * rows, rows), rows)
        for side, ref in enumerate((own_ref, sib_ref)):
            turned[0] = ref[these]
            turned[1] = half_turned(turned[0])
            out = 2 * i + (core ^ side)
            for q in range(cols // LANES):
                made[out, :, q * LANES : (q + 1) * LANES] = pick_pair(
                    turned, place[2 * q], place[2 * q + 1], left
                )
            copy_out(out).start()
        return 0

    lax.fori_loop(0, blocks // 2, block, 0)
    for i in range(blocks):
        copy_out(i).wait()


def finish(ab_sym, own, sib, rows):
    blocks, cols = 2 * own.shape[0] // rows, own.shape[1]
    out = pl.pallas_call(
        finish_kernel,
        out_shape=jax.ShapeDtypeStruct((blocks, rows, cols), jnp.bfloat16),
        in_specs=[SMEM] + [VMEM] * 2,
        out_specs=ANY,
        scratch_shapes=[
            pltpu.VMEM((blocks, rows, cols), jnp.bfloat16),
            pltpu.VMEM((2, rows, cols), jnp.bfloat16),
            pltpu.SMEM((NSYM,), jnp.int32),
            pltpu.SMEM((ab_sym.shape[0],), jnp.int32),
            pltpu.SemaphoreType.DMA((blocks,)),
        ],
        compiler_params=params(),
        cost_estimate=CHEAP,
        name="finish",
    )(ab_sym, own, sib)
    return out.reshape(blocks * rows, cols)


SWAP = [(0, 1), (1, 0)]


def further(x, by):
    n_cd = lax.axis_size("cd")
    return lax.ppermute(x, "cd", [(i, (i + by) % n_cd) for i in range(n_cd)])


def per_device(t2_amps, integrals, ab_sym, cd_sym):
    zh, n_cd = lax.axis_size("zh"), lax.axis_size("cd")
    n_chunks = len(SPLIT)
    own = list(sort_amps(t2_amps, cd_sym))
    t2s, parts = [], []

    def along_zh(c, earlier):
        if earlier:
            own[c] = after(own[c], *earlier)
        others = [lax.ppermute(own[c], "zh", [(i, i ^ d) for i in range(zh)]) for d in range(1, zh)]
        return [own[c]] + others

    def gather(c, blocks, earlier):
        near = merge(blocks, list(earlier))
        up, across = lax.ppermute(near, "zl", SWAP), lax.ppermute(near, "x", SWAP)
        far = lax.ppermute(across, "zl", SWAP) if c in ALONG_Z else lax.ppermute(up, "x", SWAP)
        t2s.append((near, up, across, far))

    ints = list(sort_ints(integrals, ab_sym, own[0]))
    gather(0, along_zh(0, []), ints[:1])
    ints = [after(x, t2s[0][0]) for x in ints]
    sib_ints = [lax.ppermute(x, "core", SWAP) for x in ints]
    gather(1, along_zh(1, []), t2s[0][1:3])
    latest = t2s[1][0]
    for c in range(n_chunks):
        first = sum(SPLIT[:c])
        part = 0
        while first >= INTS_SPLIT[part]:
            first -= INTS_SPLIT[part]
            part += 1
        earlier = [latest]
        if c + 2 == n_chunks:
            earlier += t2s[c + 1][1:3]
        if 0 < c < n_chunks - 1:
            earlier += parts[1 - n_cd :]
        if c + 2 < n_chunks:
            blocks = along_zh(c + 2, [t2s[c][0]])
            earlier += blocks[1:]
        made = contract(n_cd, t2s[c], ints[part], sib_ints[part], first, earlier)
        latest = made[0]
        parts += [made[0]] + [further(made[by], by) for by in range(1, n_cd)]
        if c + 2 < n_chunks:
            gather(c + 2, blocks, [latest, t2s[c + 1][1], t2s[c + 1][2]])
            latest = t2s[c + 2][0]
    sums, sib_sums = add_parts(n_cd, parts)
    return finish(ab_sym, sums, lax.ppermute(sib_sums, "core", SWAP), t2_amps.shape[0])


def solution(mesh):
    n_blk, n_cd = mesh.devices.shape
    blk = ("zh", "zl", "x", "core")
    parted = Mesh(mesh.devices.reshape(n_blk // 8, 2, 2, 2, n_cd), blk + ("cd",))
    in_specs = (P(blk, "cd"), P(blk, None, "cd"), P(blk), P("cd"))
    return jax.shard_map(
        per_device, mesh=parted, in_specs=in_specs, out_specs=P("cd", blk), check_vma=False
    )
```

```python
import functools

import jax
import jax.numpy as jnp
from jax import lax
from jax.experimental import pallas as pl
from jax.experimental.pallas import tpu as pltpu
from jax.sharding import Mesh, PartitionSpec as P

NSYM = 8
SPLIT = (1, 2, 2, 2, 1)
ALONG_Z = (3,)
LANES = 128
VMEM_LIMIT = 20 * 2**20

ANY = pl.BlockSpec(memory_space=pl.ANY)
SMEM = pl.BlockSpec(memory_space=pltpu.SMEM)
VMEM = pl.BlockSpec(memory_space=pltpu.VMEM)

CHEAP = pl.CostEstimate(flops=1000, bytes_accessed=1000, transcendentals=0)


def params(limit=VMEM_LIMIT):
    return pltpu.CompilerParams(vmem_limit_bytes=limit)


def half_turned(x):
    half = LANES // 2
    return jnp.concatenate([x[:, half:], x[:, :half]], axis=1)


def rank_tiles(sym_ref, count_ref, order_ref, place_ref, tiles):
    for s in range(NSYM):
        count_ref[s] = s * (tiles // NSYM)

    def step(i, _):
        s = sym_ref[i]
        p = count_ref[s]
        count_ref[s] = p + 1
        if order_ref is not None:
            order_ref[p] = i
        if place_ref is not None:
            place_ref[i] = p
        return 0

    lax.fori_loop(0, tiles, step, 0)


def pick_pair(both, a, b, left):
    columns = both.shape[2] // LANES
    a_col = lax.shift_right_logical(a, 1)
    b_col = lax.rem(lax.shift_right_logical(b + 1, 1) + columns - 1, columns)
    xa = both[a & 1, :, pl.ds(pl.multiple_of(a_col * LANES, LANES), LANES)]
    xb = both[(b & 1) ^ 1, :, pl.ds(pl.multiple_of(b_col * LANES, LANES), LANES)]
    return jnp.where(left, xa, xb)


def sort_amps_kernel(cd_ref, t2_ref, *rest):
    chunks, (both, count, order, sem) = rest[:-4], rest[-4:]
    rows = t2_ref.shape[0]
    load = pltpu.make_async_copy(t2_ref, both.at[0], sem)
    load.start()
    rank_tiles(cd_ref, count, order, None, cd_ref.shape[0])
    load.wait()
    both[1] = half_turned(both[0])
    left = lax.broadcasted_iota(jnp.int32, (rows, LANES), 1) < LANES // 2
    q = 0
    for chunk in chunks:
        for off in range(chunk.shape[1] // LANES):
            pair = pick_pair(both, order[2 * q], order[2 * q + 1], left)
            chunk[:, off * LANES : (off + 1) * LANES] = pair
            q += 1


def sort_amps(t2, cd_sym):
    rows, cols = t2.shape
    return pl.pallas_call(
        sort_amps_kernel,
        out_shape=[
            jax.ShapeDtypeStruct((rows, cols // NSYM * m), t2.dtype) for m in SPLIT
        ],
        in_specs=[SMEM, ANY],
        out_specs=[VMEM] * len(SPLIT),
        scratch_shapes=[
            pltpu.VMEM((2, rows, cols), t2.dtype),
            pltpu.SMEM((NSYM,), jnp.int32),
            pltpu.SMEM((cd_sym.shape[0],), jnp.int32),
            pltpu.SemaphoreType.DMA,
        ],
        compiler_params=params(),
        cost_estimate=CHEAP,
        name="sort_amps",
    )(cd_sym, t2)


def sort_ints_kernel(ab_ref, ints_ref, _, out_ref, count, order):
    tiles = ab_ref.shape[0]
    rank_tiles(ab_ref, count, order, None, tiles)
    per_sym = tiles // NSYM
    for s in range(NSYM):
        rows = [ints_ref[order[s * per_sym + m]] for m in range(per_sym)]
        out_ref[s] = jnp.concatenate(rows, axis=0).T


def sort_ints(integrals, ab_sym, earlier):
    tiles, tile, packed = integrals.shape
    return pl.pallas_call(
        sort_ints_kernel,
        out_shape=jax.ShapeDtypeStruct((NSYM, packed, tiles // NSYM * tile), integrals.dtype),
        in_specs=[SMEM, VMEM, ANY],
        out_specs=VMEM,
        scratch_shapes=[pltpu.SMEM((NSYM,), jnp.int32), pltpu.SMEM((tiles,), jnp.int32)],
        compiler_params=params(),
        cost_estimate=CHEAP,
        name="sort_ints",
    )(ab_sym, integrals, earlier)


def merge_kernel(n, *refs):
    blocks, out_ref = refs[:n], refs[-1]
    me = lax.axis_index("zh")
    for d, block in enumerate(blocks):
        out_ref[me ^ d] = block[...]


def merge(blocks, earlier):
    return pl.pallas_call(
        functools.partial(merge_kernel, len(blocks)),
        out_shape=jax.ShapeDtypeStruct((len(blocks),) + blocks[0].shape, blocks[0].dtype),
        in_specs=[VMEM] * len(blocks) + [ANY] * len(earlier),
        out_specs=VMEM,
        compiler_params=params(),
        cost_estimate=CHEAP,
        name="merge",
    )(*blocks, *earlier)


def nothing(*refs):
    pass


def after(x, *earlier):
    return pl.pallas_call(
        nothing,
        out_shape=jax.ShapeDtypeStruct(x.shape, x.dtype),
        in_specs=[ANY] * (1 + len(earlier)),
        out_specs=ANY,
        input_output_aliases={0: 0},
        compiler_params=params(),
        cost_estimate=CHEAP,
        name="after",
    )(x, *earlier)


def contract_kernel(n_cd, first_sym, near, up, across, far, own_ref, sib_ref, *rest):
    outs, lhs = rest[-n_cd - 1 : -1], rest[-1]
    slots, rows, cols = lhs.shape
    packed, width = own_ref.shape[1:]
    z, x = lax.axis_index("zl"), lax.axis_index("x")
    first = lax.axis_index("cd") * (slots // n_cd)
    for i in range(slots // 4):
        for block, zl, xs in ((near, z, x), (up, 1 - z, x), (across, z, 1 - x), (far, 1 - z, 1 - x)):
            lhs[lax.rem(4 * i + 2 * zl + xs + slots - first, slots)] = block[i]
    t2 = lhs[...].reshape(slots * rows, cols)
    group_rows = t2.shape[0] // n_cd
    for side, ints in enumerate((own_ref, sib_ref)):
        for s in range(cols // packed):
            part = jnp.dot(
                t2[:, s * packed : (s + 1) * packed],
                ints[first_sym + s],
                preferred_element_type=jnp.float32,
            ).astype(outs[0].dtype)
            for by in range(n_cd):
                outs[by][side, :, s * width : (s + 1) * width] = part[
                    by * group_rows : (by + 1) * group_rows
                ]


def contract(n_cd, t2s, ints, sib_ints, first_sym, earlier):
    zh, rows, cols = t2s[0].shape
    packed, width = ints.shape[1:]
    all_rows = 4 * zh * rows
    out = (2, all_rows // n_cd, cols // packed * width)
    return pl.pallas_call(
        functools.partial(contract_kernel, n_cd, first_sym),
        out_shape=[jax.ShapeDtypeStruct(out, jnp.bfloat16)] * n_cd,
        in_specs=[VMEM] * 6 + [ANY] * len(earlier),
        out_specs=[VMEM] * n_cd,
        scratch_shapes=[pltpu.VMEM((4 * zh, rows, cols), jnp.bfloat16)],
        compiler_params=params(),
        cost_estimate=CHEAP,
        name="contract",
    )(*t2s, ints, sib_ints, *earlier)


def add_kernel(n_cd, *refs):
    parts, outs = refs[:-2], refs[-2:]
    for side, out_ref in enumerate(outs):
        first = 0
        for c in range(0, len(parts), n_cd):
            value = parts[c][side].astype(jnp.float32)
            for other in parts[c + 1 : c + n_cd]:
                value += other[side].astype(jnp.float32)
            out_ref[:, first : first + value.shape[1]] = value.astype(out_ref.dtype)
            first += value.shape[1]


def add_parts(n_cd, parts):
    out = (parts[0].shape[1], sum(p.shape[2] for p in parts[::n_cd]))
    return pl.pallas_call(
        functools.partial(add_kernel, n_cd),
        out_shape=[jax.ShapeDtypeStruct(out, jnp.bfloat16)] * 2,
        in_specs=[VMEM] * len(parts),
        out_specs=[VMEM] * 2,
        compiler_params=params(),
        cost_estimate=CHEAP,
        name="add_parts",
    )(*parts)


def finish_kernel(side, ab_ref, sums_ref, *rest):
    out_ref, made, moves, count, place, sems = rest[-6:]
    blocks, rows, cols = made.shape
    rank_tiles(ab_ref, count, None, place, ab_ref.shape[0])
    source = lax.broadcasted_iota(jnp.int32, (2 * LANES, LANES), 0)
    target = lax.broadcasted_iota(jnp.int32, (2 * LANES, LANES), 1)
    half = LANES // 2
    for i in range(2):
        for j in range(2):
            wanted = jnp.where(target < half, target + i * half, target + half + j * half)
            moves[2 * i + j] = jnp.where(source == wanted, 1.0, 0.0).astype(moves.dtype)

    def copy_out(i):
        block = 2 * i + (lax.axis_index("core") ^ side)
        return pltpu.make_async_copy(made.at[i], out_ref.at[block], sems.at[i])

    for q in range(cols // LANES):
        a, b = place[2 * q], place[2 * q + 1]
        a_col, b_col = lax.shift_right_logical(a, 1), lax.shift_right_logical(b, 1)
        pair = jnp.concatenate(
            [
                sums_ref[:, pl.ds(pl.multiple_of(a_col * LANES, LANES), LANES)],
                sums_ref[:, pl.ds(pl.multiple_of(b_col * LANES, LANES), LANES)],
            ],
            axis=1,
        )
        moved = jnp.dot(pair, moves[2 * (a & 1) + (b & 1)], preferred_element_type=jnp.float32)
        made[:, :, q * LANES : (q + 1) * LANES] = moved.astype(made.dtype).reshape(
            blocks, rows, LANES
        )
    for i in range(blocks):
        copy_out(i).start()
    for i in range(blocks):
        copy_out(i).wait()


def finish(side, ab_sym, sums, rows, out=None):
    blocks, cols = sums.shape[0] // rows, sums.shape[1]
    before = [] if out is None else [out]
    return pl.pallas_call(
        functools.partial(finish_kernel, side),
        out_shape=jax.ShapeDtypeStruct((2 * blocks, rows, cols), jnp.bfloat16),
        in_specs=[SMEM, VMEM] + [ANY] * len(before),
        out_specs=ANY,
        scratch_shapes=[
            pltpu.VMEM((blocks, rows, cols), jnp.bfloat16),
            pltpu.VMEM((4, 2 * LANES, LANES), jnp.bfloat16),
            pltpu.SMEM((NSYM,), jnp.int32),
            pltpu.SMEM((ab_sym.shape[0],), jnp.int32),
            pltpu.SemaphoreType.DMA((blocks,)),
        ],
        input_output_aliases={2: 0} if before else {},
        compiler_params=params(),
        cost_estimate=CHEAP,
        name="finish",
    )(ab_sym, sums, *before)


SWAP = [(0, 1), (1, 0)]


def further(x, by):
    n_cd = lax.axis_size("cd")
    return lax.ppermute(x, "cd", [(i, (i + by) % n_cd) for i in range(n_cd)])


def per_device(t2_amps, integrals, ab_sym, cd_sym):
    zh, n_cd = lax.axis_size("zh"), lax.axis_size("cd")
    n_chunks = len(SPLIT)
    own = list(sort_amps(t2_amps, cd_sym))
    t2s, parts = [], []

    def along_zh(c, earlier):
        if earlier:
            own[c] = after(own[c], *earlier)
        others = [lax.ppermute(own[c], "zh", [(i, i ^ d) for i in range(zh)]) for d in range(1, zh)]
        return [own[c]] + others

    def gather(c, blocks, earlier):
        near = merge(blocks, list(earlier))
        up, across = lax.ppermute(near, "zl", SWAP), lax.ppermute(near, "x", SWAP)
        far = lax.ppermute(across, "zl", SWAP) if c in ALONG_Z else lax.ppermute(up, "x", SWAP)
        t2s.append((near, up, across, far))

    ints = sort_ints(integrals, ab_sym, own[0])
    gather(0, along_zh(0, []), [ints])
    gather(1, along_zh(1, []), t2s[0][1:3])
    ints = after(ints, t2s[1][0])
    sib_ints = lax.ppermute(ints, "core", SWAP)
    latest = t2s[1][0]
    for c in range(n_chunks):
        earlier = [latest]
        if c + 1 < n_chunks:
            earlier += t2s[c + 1][2:3]
        if c + 2 == n_chunks:
            earlier += t2s[c + 1][1:2]
        if 0 < c < n_chunks - 1:
            earlier += parts[1 - n_cd :]
        if c + 2 < n_chunks:
            blocks = along_zh(c + 2, [t2s[c][0]])
            earlier += blocks[1:]
        made = contract(n_cd, t2s[c], ints, sib_ints, sum(SPLIT[:c]), earlier)
        latest = made[0]
        parts += [made[0]] + [further(made[by], by) for by in range(1, n_cd)]
        if c + 2 < n_chunks:
            gather(c + 2, blocks, [latest, t2s[c + 1][1], t2s[c + 1][2]])
            latest = t2s[c + 2][0]
    sums, sib_sums = add_parts(n_cd, parts)
    sib_sums = lax.ppermute(sib_sums, "core", SWAP)
    rows = t2_amps.shape[0]
    out = finish(0, ab_sym, sums, rows)
    out = finish(1, ab_sym, sib_sums, rows, out)
    return out.reshape(-1, out.shape[2])


def solution(mesh):
    n_blk, n_cd = mesh.devices.shape
    blk = ("zh", "zl", "x", "core")
    parted = Mesh(mesh.devices.reshape(n_blk // 8, 2, 2, 2, n_cd), blk + ("cd",))
    in_specs = (P(blk, "cd"), P(blk, None, "cd"), P(blk), P("cd"))
    return jax.shard_map(
        per_device, mesh=parted, in_specs=in_specs, out_specs=P("cd", blk), check_vma=False
    )
```

```python
import functools

import jax
import jax.numpy as jnp
from jax import lax
from jax.experimental import pallas as pl
from jax.experimental.pallas import tpu as pltpu
from jax.sharding import Mesh, PartitionSpec as P

NSYM = 8
SPLIT = (2, 3)
LATER_SPLIT = (2, 1)
LATER = sum(LATER_SPLIT)
LANES = 128
VMEM_LIMIT = 20 * 2**20

ANY = pl.BlockSpec(memory_space=pl.ANY)
SMEM = pl.BlockSpec(memory_space=pltpu.SMEM)
VMEM = pl.BlockSpec(memory_space=pltpu.VMEM)

CHEAP = pl.CostEstimate(flops=1000, bytes_accessed=1000, transcendentals=0)


def params(limit=VMEM_LIMIT):
    return pltpu.CompilerParams(vmem_limit_bytes=limit)


def half_turned(x):
    half = LANES // 2
    return jnp.concatenate([x[:, half:], x[:, :half]], axis=1)


def rank_tiles(sym_ref, count_ref, order_ref, place_ref, tiles):
    for s in range(NSYM):
        count_ref[s] = s * (tiles // NSYM)

    def step(i, _):
        s = sym_ref[i]
        p = count_ref[s]
        count_ref[s] = p + 1
        order_ref[p] = i
        if place_ref is not None:
            place_ref[i] = p
        return 0

    lax.fori_loop(0, tiles, step, 0)


def pick_pair(both, a, b, left):
    columns = both.shape[2] // LANES
    a_col = lax.shift_right_logical(a, 1)
    b_col = lax.rem(lax.shift_right_logical(b + 1, 1) + columns - 1, columns)
    xa = both[a & 1, :, pl.ds(pl.multiple_of(a_col * LANES, LANES), LANES)]
    xb = both[(b & 1) ^ 1, :, pl.ds(pl.multiple_of(b_col * LANES, LANES), LANES)]
    return jnp.where(left, xa, xb)


def sort_amps_kernel(cd_ref, t2_ref, *rest):
    chunks, (both, count, order, sem) = rest[:-4], rest[-4:]
    rows = t2_ref.shape[0]
    load = pltpu.make_async_copy(t2_ref, both.at[0], sem)
    load.start()
    rank_tiles(cd_ref, count, order, None, cd_ref.shape[0])
    load.wait()
    both[1] = half_turned(both[0])
    left = lax.broadcasted_iota(jnp.int32, (rows, LANES), 1) < LANES // 2
    q = 0
    for chunk in chunks:
        for off in range(chunk.shape[1] // LANES):
            pair = pick_pair(both, order[2 * q], order[2 * q + 1], left)
            chunk[:, off * LANES : (off + 1) * LANES] = pair
            q += 1


def sort_amps(t2, cd_sym):
    rows, cols = t2.shape
    return pl.pallas_call(
        sort_amps_kernel,
        out_shape=[
            jax.ShapeDtypeStruct((rows, cols // NSYM * m), t2.dtype) for m in (*SPLIT, LATER)
        ],
        in_specs=[SMEM, ANY],
        out_specs=[VMEM] * (len(SPLIT) + 1),
        scratch_shapes=[
            pltpu.VMEM((2, rows, cols), t2.dtype),
            pltpu.SMEM((NSYM,), jnp.int32),
            pltpu.SMEM((cd_sym.shape[0],), jnp.int32),
            pltpu.SemaphoreType.DMA,
        ],
        compiler_params=params(),
        cost_estimate=CHEAP,
        name="sort_amps",
    )(cd_sym, t2)


def sort_ints_kernel(ab_ref, ints_ref, _, place, *rest):
    outs, (count, order) = rest[:-2], rest[-2:]
    tiles = ab_ref.shape[0]
    rank_tiles(ab_ref, count, order, place, tiles)
    per_sym = tiles // NSYM
    sym = 0
    for out_ref in outs:
        for s in range(out_ref.shape[0]):
            rows = [ints_ref[order[sym * per_sym + m]] for m in range(per_sym)]
            out_ref[s] = jnp.concatenate(rows, axis=0).T
            sym += 1


def sort_ints(integrals, ab_sym, earlier):
    tiles, tile, packed = integrals.shape
    return pl.pallas_call(
        sort_ints_kernel,
        out_shape=[jax.ShapeDtypeStruct((tiles,), jnp.int32)]
        + [
            jax.ShapeDtypeStruct((m, packed, tiles // NSYM * tile), integrals.dtype)
            for m in (NSYM - LATER, *LATER_SPLIT)
        ],
        in_specs=[SMEM, VMEM, ANY],
        out_specs=[SMEM, VMEM] + [VMEM] * len(LATER_SPLIT),
        scratch_shapes=[pltpu.SMEM((NSYM,), jnp.int32), pltpu.SMEM((tiles,), jnp.int32)],
        compiler_params=params(),
        cost_estimate=CHEAP,
        name="sort_ints",
    )(ab_sym, integrals, earlier)


def merge_kernel(n, *refs):
    blocks, out_ref = refs[:n], refs[-1]
    me = lax.axis_index("zh")
    for d, block in enumerate(blocks):
        out_ref[me ^ d] = block[...]


def merge(blocks, earlier):
    return pl.pallas_call(
        functools.partial(merge_kernel, len(blocks)),
        out_shape=jax.ShapeDtypeStruct((len(blocks),) + blocks[0].shape, blocks[0].dtype),
        in_specs=[VMEM] * len(blocks) + [ANY] * len(earlier),
        out_specs=VMEM,
        compiler_params=params(),
        cost_estimate=CHEAP,
        name="merge",
    )(*blocks, *earlier)


def nothing(*refs):
    pass


def after(x, *earlier):
    return pl.pallas_call(
        nothing,
        out_shape=jax.ShapeDtypeStruct(x.shape, x.dtype),
        in_specs=[ANY] * (1 + len(earlier)),
        out_specs=ANY,
        input_output_aliases={0: 0},
        compiler_params=params(),
        cost_estimate=CHEAP,
        name="after",
    )(x, *earlier)


def lay_out(lhs, blocks, place):
    z, x = lax.axis_index("zl"), lax.axis_index("x")
    near, up, across, far = blocks
    for i in range(lhs.shape[0] // 4):
        for block, zl, xs in ((near, z, x), (up, 1 - z, x), (across, z, 1 - x), (far, 1 - z, 1 - x)):
            lhs[place(4 * i + 2 * zl + xs)] = block[i]


def contract_kernel(n_cd, first_sym, *refs):
    blocks, (own_ref, sib_ref), outs, lhs = refs[:4], refs[4:6], refs[-n_cd - 1 : -1], refs[-1]
    slots, rows, cols = lhs.shape
    packed, width = own_ref.shape[1:]
    first = lax.axis_index("cd") * (slots // n_cd)
    lay_out(lhs, blocks, lambda n: lax.rem(n + slots - first, slots))
    t2 = lhs[...].reshape(slots * rows, cols)
    group_rows = t2.shape[0] // n_cd
    for side, ints in enumerate((own_ref, sib_ref)):
        for s in range(cols // packed):
            part = jnp.dot(
                t2[:, s * packed : (s + 1) * packed],
                ints[first_sym + s],
                preferred_element_type=jnp.float32,
            ).astype(outs[0].dtype)
            for by in range(n_cd):
                outs[by][side, :, s * width : (s + 1) * width] = part[
                    by * group_rows : (by + 1) * group_rows
                ]


def contract(n_cd, t2s, ints, sib_ints, first_sym, earlier):
    zh, rows, cols = t2s[0].shape
    packed, width = ints.shape[1:]
    all_rows = 4 * zh * rows
    out = (2, all_rows // n_cd, cols // packed * width)
    return pl.pallas_call(
        functools.partial(contract_kernel, n_cd, first_sym),
        out_shape=[jax.ShapeDtypeStruct(out, jnp.bfloat16)] * n_cd,
        in_specs=[VMEM] * 6 + [ANY] * len(earlier),
        out_specs=[VMEM] * n_cd,
        scratch_shapes=[pltpu.VMEM((4 * zh, rows, cols), jnp.bfloat16)],
        compiler_params=params(),
        cost_estimate=CHEAP,
        name="contract",
    )(*t2s, ints, sib_ints, *earlier)


def total(parts):
    value = parts[0].astype(jnp.float32)
    for part in parts[1:]:
        value += part.astype(jnp.float32)
    return value.astype(jnp.bfloat16)


def join_kernel(n, *refs):
    out_ref, first = refs[-1], 0
    for ref in refs[:n]:
        out_ref[first : first + ref.shape[0]] = ref[...]
        first += ref.shape[0]


def join(arrays, earlier):
    n = len(arrays)
    out = (sum(x.shape[0] for x in arrays), *arrays[0].shape[1:])
    return pl.pallas_call(
        functools.partial(join_kernel, n),
        out_shape=jax.ShapeDtypeStruct(out, arrays[0].dtype),
        in_specs=[VMEM] * n + [ANY] * len(earlier),
        out_specs=VMEM,
        compiler_params=params(),
        cost_estimate=CHEAP,
        name="join",
    )(*arrays, *earlier)


def later_kernel(n_cd, *refs):
    blocks, ints, parts, (own_out, sib_out, lhs) = refs[:4], refs[4:6], refs[6:-3], refs[-3:]
    slots, rows, cols = lhs.shape
    packed, width = ints[0].shape[1:]
    per_group, me = slots // n_cd, lax.axis_index("cd")

    def place(n):
        group = n // per_group
        return lax.rem(me + n_cd - group, n_cd) * per_group + (n - group * per_group)

    lay_out(lhs, blocks, place)
    t2 = lhs[...].reshape(n_cd, per_group * rows, cols)
    for side, out_ref in enumerate((own_out, sib_out)):
        first = 0
        for c in range(0, len(parts), n_cd):
            value = total([part[side] for part in parts[c : c + n_cd]])
            out_ref[:, first : first + value.shape[1]] = value
            first += value.shape[1]
        for s in range(LATER):
            out_ref[:, first : first + width] = total(
                [
                    jnp.dot(
                        t2[by, :, s * packed : (s + 1) * packed],
                        ints[side][by * LATER + s],
                        preferred_element_type=jnp.float32,
                    ).astype(out_ref.dtype)
                    for by in range(n_cd)
                ]
            )
            first += width


def contract_later(n_cd, t2s, ints, parts):
    zh, rows, cols = t2s[0].shape
    width = ints[0].shape[2] * LATER + sum(p.shape[2] for p in parts[::n_cd])
    out = jax.ShapeDtypeStruct((parts[0].shape[1], width), jnp.bfloat16)
    return pl.pallas_call(
        functools.partial(later_kernel, n_cd),
        out_shape=[out, out],
        in_specs=[VMEM] * (6 + len(parts)),
        out_specs=[VMEM] * 2,
        scratch_shapes=[pltpu.VMEM((4 * zh, rows, cols), jnp.bfloat16)],
        compiler_params=params(),
        cost_estimate=CHEAP,
        name="contract_later",
    )(*t2s, *ints, *parts)


def finish_kernel(side, place, sums_ref, *rest):
    out_ref, made, moves, sems = rest[-4:]
    blocks, rows, cols = made.shape
    source = lax.broadcasted_iota(jnp.int32, (2 * LANES, LANES), 0)
    target = lax.broadcasted_iota(jnp.int32, (2 * LANES, LANES), 1)
    half = LANES // 2
    for i in range(2):
        for j in range(2):
            wanted = jnp.where(target < half, target + i * half, target + half + j * half)
            moves[2 * i + j] = jnp.where(source == wanted, 1.0, 0.0).astype(moves.dtype)

    def copy_out(i):
        block = 2 * i + (lax.axis_index("core") ^ side)
        return pltpu.make_async_copy(made.at[i], out_ref.at[block], sems.at[i])

    for q in range(cols // LANES):
        a, b = place[2 * q], place[2 * q + 1]
        a_col, b_col = lax.shift_right_logical(a, 1), lax.shift_right_logical(b, 1)
        pair = jnp.concatenate(
            [
                sums_ref[:, pl.ds(pl.multiple_of(a_col * LANES, LANES), LANES)],
                sums_ref[:, pl.ds(pl.multiple_of(b_col * LANES, LANES), LANES)],
            ],
            axis=1,
        )
        moved = jnp.dot(pair, moves[2 * (a & 1) + (b & 1)], preferred_element_type=jnp.float32)
        made[:, :, q * LANES : (q + 1) * LANES] = moved.astype(made.dtype).reshape(
            blocks, rows, LANES
        )
    for i in range(blocks):
        copy_out(i).start()
    for i in range(blocks):
        copy_out(i).wait()


def finish(side, place, sums, rows, out=None):
    blocks, cols = sums.shape[0] // rows, sums.shape[1]
    before = [] if out is None else [out]
    return pl.pallas_call(
        functools.partial(finish_kernel, side),
        out_shape=jax.ShapeDtypeStruct((2 * blocks, rows, cols), jnp.bfloat16),
        in_specs=[SMEM, VMEM] + [ANY] * len(before),
        out_specs=ANY,
        scratch_shapes=[
            pltpu.VMEM((blocks, rows, cols), jnp.bfloat16),
            pltpu.VMEM((4, 2 * LANES, LANES), jnp.bfloat16),
            pltpu.SemaphoreType.DMA((blocks,)),
        ],
        input_output_aliases={2: 0} if before else {},
        compiler_params=params(),
        cost_estimate=CHEAP,
        name="finish",
    )(place, sums, *before)


SWAP = [(0, 1), (1, 0)]


def further(x, by):
    n_cd = lax.axis_size("cd")
    return lax.ppermute(x, "cd", [(i, (i + by) % n_cd) for i in range(n_cd)])


def to_plane(x):
    n_cd = lax.axis_size("cd")
    z_len = 2 * lax.axis_size("zh")
    rest = z_len // n_cd
    pairs = []
    for z in range(z_len):
        group, i = divmod(z, rest)
        pairs += [(z * n_cd + y, (y * rest + i) * n_cd + group) for y in range(n_cd)]
    return lax.ppermute(x, ("zh", "zl", "cd"), pairs)


def per_device(t2_amps, integrals, ab_sym, cd_sym):
    zh, n_cd = lax.axis_size("zh"), lax.axis_size("cd")
    n_chunks = len(SPLIT)
    *own, own_later = sort_amps(t2_amps, cd_sym)
    t2s, parts = [], []

    def along_zh(x):
        return [x] + [lax.ppermute(x, "zh", [(i, i ^ d) for i in range(zh)]) for d in range(1, zh)]

    def gather(blocks, earlier):
        near = merge(blocks, list(earlier))
        up, across = lax.ppermute(near, "zl", SWAP), lax.ppermute(near, "x", SWAP)
        t2s.append((near, up, across, lax.ppermute(up, "x", SWAP)))
        return near

    place, ints, *ints_later = sort_ints(integrals, ab_sym, own[0])
    latest = gather(along_zh(own[0]), [ints])
    ints = after(ints, latest)
    sib_ints = lax.ppermute(ints, "core", SWAP)
    later = []

    def send_later(s, latest):
        x = after(ints_later[s], latest)
        later.append([x] + [further(x, by) for by in range(1, n_cd)])
        return later[-1][1:]

    latest = gather(along_zh(own[1]), [*t2s[0][1:3], sib_ints, *send_later(0, latest)])
    own_later = to_plane(after(own_later, latest))
    for c in range(n_chunks):
        if c:
            earlier = [latest]
        else:
            earlier = [latest, own_later, t2s[1][2], *send_later(1, latest)]
        made = contract(n_cd, t2s[c], ints, sib_ints, sum(SPLIT[:c]), earlier)
        latest = made[0]
        parts += [made[0]] + [further(made[by], by) for by in range(1, n_cd)]
        if c + 1 < n_chunks:
            blocks = along_zh(after(own_later, latest))
            latest = gather(blocks, [latest, t2s[1][3], *parts[1:]])
            ints_later = join([x[by] for by in range(n_cd) for x in later], [latest])
            ints_later = (ints_later, lax.ppermute(ints_later, "core", SWAP))
    sums, sib_sums = contract_later(n_cd, t2s[-1], ints_later, parts)
    sib_sums = lax.ppermute(sib_sums, "core", SWAP)
    rows = t2_amps.shape[0]
    out = finish(0, place, sums, rows)
    out = finish(1, place, sib_sums, rows, out)
    return out.reshape(-1, out.shape[2])


def solution(mesh):
    n_blk, n_cd = mesh.devices.shape
    blk = ("zh", "zl", "x", "core")
    parted = Mesh(mesh.devices.reshape(n_blk // 8, 2, 2, 2, n_cd), blk + ("cd",))
    in_specs = (P(blk, "cd"), P(blk, None, "cd"), P(blk), P("cd"))
    return jax.shard_map(
        per_device, mesh=parted, in_specs=in_specs, out_specs=P("cd", blk), check_vma=False
    )
```

```python
import functools

import jax
import jax.numpy as jnp
from jax import lax
from jax.experimental import pallas as pl
from jax.experimental.pallas import tpu as pltpu
from jax.sharding import Mesh, PartitionSpec as P

NSYM = 8
SPLIT = (2, 3)
LATER_SPLIT = (2, 1)
LATER = sum(LATER_SPLIT)
LANES = 128
VMEM_LIMIT = 20 * 2**20

ANY = pl.BlockSpec(memory_space=pl.ANY)
SMEM = pl.BlockSpec(memory_space=pltpu.SMEM)
VMEM = pl.BlockSpec(memory_space=pltpu.VMEM)

CHEAP = pl.CostEstimate(flops=1000, bytes_accessed=1000, transcendentals=0)


def params(limit=VMEM_LIMIT):
    return pltpu.CompilerParams(vmem_limit_bytes=limit)


def half_turned(x):
    half = LANES // 2
    return jnp.concatenate([x[:, half:], x[:, :half]], axis=1)


def rank_tiles(sym_ref, count_ref, order_ref, place_ref, tiles):
    for s in range(NSYM):
        count_ref[s] = s * (tiles // NSYM)

    def step(i, _):
        s = sym_ref[i]
        p = count_ref[s]
        count_ref[s] = p + 1
        order_ref[p] = i
        if place_ref is not None:
            place_ref[i] = p
        return 0

    lax.fori_loop(0, tiles, step, 0)


def pick_pair(both, a, b, left):
    columns = both.shape[2] // LANES
    a_col = lax.shift_right_logical(a, 1)
    b_col = lax.rem(lax.shift_right_logical(b + 1, 1) + columns - 1, columns)
    xa = both[a & 1, :, pl.ds(pl.multiple_of(a_col * LANES, LANES), LANES)]
    xb = both[(b & 1) ^ 1, :, pl.ds(pl.multiple_of(b_col * LANES, LANES), LANES)]
    return jnp.where(left, xa, xb)


def sort_amps_kernel(cd_ref, t2_ref, *rest):
    chunks, (both, count, order, sem) = rest[:-4], rest[-4:]
    rows = t2_ref.shape[0]
    load = pltpu.make_async_copy(t2_ref, both.at[0], sem)
    load.start()
    rank_tiles(cd_ref, count, order, None, cd_ref.shape[0])
    load.wait()
    both[1] = half_turned(both[0])
    left = lax.broadcasted_iota(jnp.int32, (rows, LANES), 1) < LANES // 2
    q = 0
    for chunk in chunks:
        for off in range(chunk.shape[1] // LANES):
            pair = pick_pair(both, order[2 * q], order[2 * q + 1], left)
            chunk[:, off * LANES : (off + 1) * LANES] = pair
            q += 1


def sort_amps(t2, cd_sym):
    rows, cols = t2.shape
    return pl.pallas_call(
        sort_amps_kernel,
        out_shape=[
            jax.ShapeDtypeStruct((rows, cols // NSYM * m), t2.dtype) for m in (*SPLIT, LATER)
        ],
        in_specs=[SMEM, ANY],
        out_specs=[VMEM] * (len(SPLIT) + 1),
        scratch_shapes=[
            pltpu.VMEM((2, rows, cols), t2.dtype),
            pltpu.SMEM((NSYM,), jnp.int32),
            pltpu.SMEM((cd_sym.shape[0],), jnp.int32),
            pltpu.SemaphoreType.DMA,
        ],
        compiler_params=params(),
        cost_estimate=CHEAP,
        name="sort_amps",
    )(cd_sym, t2)


def sort_ints_kernel(ab_ref, ints_ref, _, place, *rest):
    outs, (count, order) = rest[:-2], rest[-2:]
    tiles = ab_ref.shape[0]
    rank_tiles(ab_ref, count, order, place, tiles)
    per_sym = tiles // NSYM
    sym = 0
    for out_ref in outs:
        for s in range(out_ref.shape[0]):
            rows = [ints_ref[order[sym * per_sym + m]] for m in range(per_sym)]
            out_ref[s] = jnp.concatenate(rows, axis=0).T
            sym += 1


def sort_ints(integrals, ab_sym, earlier):
    tiles, tile, packed = integrals.shape
    return pl.pallas_call(
        sort_ints_kernel,
        out_shape=[jax.ShapeDtypeStruct((tiles,), jnp.int32)]
        + [
            jax.ShapeDtypeStruct((m, packed, tiles // NSYM * tile), integrals.dtype)
            for m in (NSYM - LATER, *LATER_SPLIT)
        ],
        in_specs=[SMEM, VMEM, ANY],
        out_specs=[SMEM, VMEM] + [VMEM] * len(LATER_SPLIT),
        scratch_shapes=[pltpu.SMEM((NSYM,), jnp.int32), pltpu.SMEM((tiles,), jnp.int32)],
        compiler_params=params(),
        cost_estimate=CHEAP,
        name="sort_ints",
    )(ab_sym, integrals, earlier)


def merge_kernel(n, *refs):
    blocks, out_ref = refs[:n], refs[-1]
    me = lax.axis_index("zh")
    for d, block in enumerate(blocks):
        out_ref[me ^ d] = block[...]


def merge(blocks, earlier):
    return pl.pallas_call(
        functools.partial(merge_kernel, len(blocks)),
        out_shape=jax.ShapeDtypeStruct((len(blocks),) + blocks[0].shape, blocks[0].dtype),
        in_specs=[VMEM] * len(blocks) + [ANY] * len(earlier),
        out_specs=VMEM,
        compiler_params=params(),
        cost_estimate=CHEAP,
        name="merge",
    )(*blocks, *earlier)


def nothing(*refs):
    pass


def after(x, *earlier):
    return pl.pallas_call(
        nothing,
        out_shape=jax.ShapeDtypeStruct(x.shape, x.dtype),
        in_specs=[ANY] * (1 + len(earlier)),
        out_specs=ANY,
        input_output_aliases={0: 0},
        compiler_params=params(),
        cost_estimate=CHEAP,
        name="after",
    )(x, *earlier)


def lay_out(lhs, refs, where, place):
    h, z, x = lax.axis_index("zh"), lax.axis_index("zl"), lax.axis_index("x")
    for k, quarter in enumerate(where):
        for d, (array, entry) in enumerate(quarter):
            ref = refs[array]
            slot = 4 * (h ^ d) + 2 * (z ^ (k // 2)) + (x ^ (k % 2))
            lhs[place(slot)] = ref[...] if entry is None else ref[h ^ d if entry < 0 else entry]


def contract_kernel(n_cd, first_sym, n_blocks, where, *refs):
    blocks, (own_ref, sib_ref) = refs[:n_blocks], refs[n_blocks : n_blocks + 2]
    outs, lhs = refs[-n_cd - 1 : -1], refs[-1]
    slots, rows, cols = lhs.shape
    packed, width = own_ref.shape[1:]
    first = lax.axis_index("cd") * (slots // n_cd)
    lay_out(lhs, blocks, where, lambda n: lax.rem(n + slots - first, slots))
    t2 = lhs[...].reshape(slots * rows, cols)
    group_rows = t2.shape[0] // n_cd
    for side, ints in enumerate((own_ref, sib_ref)):
        for s in range(cols // packed):
            part = jnp.dot(
                t2[:, s * packed : (s + 1) * packed],
                ints[first_sym + s],
                preferred_element_type=jnp.float32,
            ).astype(outs[0].dtype)
            for by in range(n_cd):
                outs[by][side, :, s * width : (s + 1) * width] = part[
                    by * group_rows : (by + 1) * group_rows
                ]


def contract(n_cd, t2s, ints, sib_ints, first_sym, earlier):
    blocks, where = t2s
    rows, cols = blocks[0].shape[-2:]
    slots = 4 * len(where[0])
    packed, width = ints.shape[1:]
    out = (2, slots * rows // n_cd, cols // packed * width)
    return pl.pallas_call(
        functools.partial(contract_kernel, n_cd, first_sym, len(blocks), where),
        out_shape=[jax.ShapeDtypeStruct(out, jnp.bfloat16)] * n_cd,
        in_specs=[VMEM] * (len(blocks) + 2) + [ANY] * len(earlier),
        out_specs=[VMEM] * n_cd,
        scratch_shapes=[pltpu.VMEM((slots, rows, cols), jnp.bfloat16)],
        compiler_params=params(),
        cost_estimate=CHEAP,
        name="contract",
    )(*blocks, ints, sib_ints, *earlier)


def total(parts):
    value = parts[0].astype(jnp.float32)
    for part in parts[1:]:
        value += part.astype(jnp.float32)
    return value.astype(jnp.bfloat16)


def join_kernel(n, *refs):
    out_ref, first = refs[-1], 0
    for ref in refs[:n]:
        out_ref[first : first + ref.shape[0]] = ref[...]
        first += ref.shape[0]


def join(arrays, earlier):
    n = len(arrays)
    out = (sum(x.shape[0] for x in arrays), *arrays[0].shape[1:])
    return pl.pallas_call(
        functools.partial(join_kernel, n),
        out_shape=jax.ShapeDtypeStruct(out, arrays[0].dtype),
        in_specs=[VMEM] * n + [ANY] * len(earlier),
        out_specs=VMEM,
        compiler_params=params(),
        cost_estimate=CHEAP,
        name="join",
    )(*arrays, *earlier)


def later_kernel(n_cd, n_blocks, where, *refs):
    blocks, ints, parts = refs[:n_blocks], refs[n_blocks : n_blocks + 2], refs[n_blocks + 2 : -3]
    own_out, sib_out, lhs = refs[-3:]
    slots, rows, cols = lhs.shape
    packed, width = ints[0].shape[1:]
    per_group, me = slots // n_cd, lax.axis_index("cd")

    def place(n):
        group = lax.div(n, per_group)
        return lax.rem(me + n_cd - group, n_cd) * per_group + (n - group * per_group)

    lay_out(lhs, blocks, where, place)
    t2 = lhs[...].reshape(n_cd, per_group * rows, cols)
    for side, out_ref in enumerate((own_out, sib_out)):
        first = 0
        for c in range(0, len(parts), n_cd):
            value = total([part[side] for part in parts[c : c + n_cd]])
            out_ref[:, first : first + value.shape[1]] = value
            first += value.shape[1]
        for s in range(LATER):
            out_ref[:, first : first + width] = total(
                [
                    jnp.dot(
                        t2[by, :, s * packed : (s + 1) * packed],
                        ints[side][by * LATER + s],
                        preferred_element_type=jnp.float32,
                    ).astype(out_ref.dtype)
                    for by in range(n_cd)
                ]
            )
            first += width


def contract_later(n_cd, t2s, ints, parts):
    blocks, where = t2s
    rows, cols = blocks[0].shape[-2:]
    width = ints[0].shape[2] * LATER + sum(p.shape[2] for p in parts[::n_cd])
    out = jax.ShapeDtypeStruct((parts[0].shape[1], width), jnp.bfloat16)
    return pl.pallas_call(
        functools.partial(later_kernel, n_cd, len(blocks), where),
        out_shape=[out, out],
        in_specs=[VMEM] * (len(blocks) + 2 + len(parts)),
        out_specs=[VMEM] * 2,
        scratch_shapes=[pltpu.VMEM((4 * len(where[0]), rows, cols), jnp.bfloat16)],
        compiler_params=params(),
        cost_estimate=CHEAP,
        name="contract_later",
    )(*blocks, *ints, *parts)


def finish_kernel(side, place, sums_ref, *rest):
    out_ref, made, moves, sems = rest[-4:]
    blocks, rows, cols = made.shape
    source = lax.broadcasted_iota(jnp.int32, (2 * LANES, LANES), 0)
    target = lax.broadcasted_iota(jnp.int32, (2 * LANES, LANES), 1)
    half = LANES // 2
    for i in range(2):
        for j in range(2):
            wanted = jnp.where(target < half, target + i * half, target + half + j * half)
            moves[2 * i + j] = jnp.where(source == wanted, 1.0, 0.0).astype(moves.dtype)

    def copy_out(i):
        block = 2 * i + (lax.axis_index("core") ^ side)
        return pltpu.make_async_copy(made.at[i], out_ref.at[block], sems.at[i])

    for q in range(cols // LANES):
        a, b = place[2 * q], place[2 * q + 1]
        a_col, b_col = lax.shift_right_logical(a, 1), lax.shift_right_logical(b, 1)
        pair = jnp.concatenate(
            [
                sums_ref[:, pl.ds(pl.multiple_of(a_col * LANES, LANES), LANES)],
                sums_ref[:, pl.ds(pl.multiple_of(b_col * LANES, LANES), LANES)],
            ],
            axis=1,
        )
        moved = jnp.dot(pair, moves[2 * (a & 1) + (b & 1)], preferred_element_type=jnp.float32)
        made[:, :, q * LANES : (q + 1) * LANES] = moved.astype(made.dtype).reshape(
            blocks, rows, LANES
        )
    for i in range(blocks):
        copy_out(i).start()
    for i in range(blocks):
        copy_out(i).wait()


def finish(side, place, sums, rows, out=None):
    blocks, cols = sums.shape[0] // rows, sums.shape[1]
    before = [] if out is None else [out]
    return pl.pallas_call(
        functools.partial(finish_kernel, side),
        out_shape=jax.ShapeDtypeStruct((2 * blocks, rows, cols), jnp.bfloat16),
        in_specs=[SMEM, VMEM] + [ANY] * len(before),
        out_specs=ANY,
        scratch_shapes=[
            pltpu.VMEM((blocks, rows, cols), jnp.bfloat16),
            pltpu.VMEM((4, 2 * LANES, LANES), jnp.bfloat16),
            pltpu.SemaphoreType.DMA((blocks,)),
        ],
        input_output_aliases={2: 0} if before else {},
        compiler_params=params(),
        cost_estimate=CHEAP,
        name="finish",
    )(place, sums, *before)


SWAP = [(0, 1), (1, 0)]


def further(x, by):
    n_cd = lax.axis_size("cd")
    return lax.ppermute(x, "cd", [(i, (i + by) % n_cd) for i in range(n_cd)])


def to_plane(x):
    n_cd = lax.axis_size("cd")
    z_len = 2 * lax.axis_size("zh")
    rest = z_len // n_cd
    pairs = []
    for z in range(z_len):
        group, i = divmod(z, rest)
        pairs += [(z * n_cd + y, (y * rest + i) * n_cd + group) for y in range(n_cd)]
    return lax.ppermute(x, ("zh", "zl", "cd"), pairs)


def per_device(t2_amps, integrals, ab_sym, cd_sym):
    zh, n_cd = lax.axis_size("zh"), lax.axis_size("cd")
    own0, own1, own2 = sort_amps(t2_amps, cd_sym)

    def over(x, axis):
        return lax.ppermute(x, axis, SWAP)

    def along_zh(x):
        return [lax.ppermute(x, "zh", [(i, i ^ d) for i in range(zh)]) for d in range(1, zh)]

    later = []

    def send_later(s, latest):
        x = after(ints_later[s], latest)
        later.append([x] + [further(x, by) for by in range(1, n_cd)])
        return later[-1][1:]

    place, ints, *ints_later = sort_ints(integrals, ab_sym, own0)
    across1 = [over(own1, "x")]
    near0 = merge([own0] + along_zh(own0), [ints, *across1])
    ints = after(ints, near0)
    sib_ints = over(ints, "core")
    up0, across0 = over(near0, "zl"), over(near0, "x")
    others1 = along_zh(own1)
    near1 = merge([own1] + others1, [sib_ints, up0, across0, *send_later(0, near0)])
    far0 = over(up0, "x")
    up1 = over(near1, "zl")
    across1 += [over(after(x, near1), "x") for x in others1]
    own2 = to_plane(after(own2, near1))
    stacked = [tuple((k, -1) for d in range(zh)) for k in range(4)]
    made0 = contract(
        n_cd,
        ((near0, across0, up0, far0), tuple(stacked)),
        ints,
        sib_ints,
        0,
        [own2, *across1, *send_later(1, near1)],
    )
    parts = [made0[0]] + [further(made0[by], by) for by in range(1, n_cd)]
    far1 = over(up1, "x")
    own2 = after(own2, made0[0])
    others2 = along_zh(own2)
    blocks = [near1, up1, far1, *across1]
    stacked[1] = tuple((3 + d, None) for d in range(zh))
    stacked[2:] = [tuple((k, -1) for d in range(zh)) for k in (1, 2)]
    made1 = contract(n_cd, (blocks, tuple(stacked)), ints, sib_ints, SPLIT[0], parts[1:])
    parts += [made1[0]] + [further(made1[by], by) for by in range(1, n_cd)]
    up2, across2 = over(own2, "zl"), over(own2, "x")
    turned = join([x[None] for x in [*others2, up2]], [across2, made1[0]])
    across_turned = over(turned, "x")
    ups2 = [up2] + [over(after(x, turned), "zl") for x in others2]
    fars2 = [over(x, "x") for x in ups2[1:]]
    ints_later = join([x[by] for by in range(n_cd) for x in later], [turned])
    ints_later = (ints_later, over(ints_later, "core"))
    blocks = [own2, *others2, *ups2, across2, across_turned, *fars2]
    where = (
        tuple((d, None) for d in range(zh)),
        ((2 * zh, None),) + tuple((2 * zh + 1, d - 1) for d in range(1, zh)),
        tuple((zh + d, None) for d in range(zh)),
        ((2 * zh + 1, zh - 1),) + tuple((2 * zh + 1 + d, None) for d in range(1, zh)),
    )
    t2s = blocks, where
    sums, sib_sums = contract_later(n_cd, t2s, ints_later, parts)
    sib_sums = lax.ppermute(sib_sums, "core", SWAP)
    rows = t2_amps.shape[0]
    out = finish(0, place, sums, rows)
    out = finish(1, place, sib_sums, rows, out)
    return out.reshape(-1, out.shape[2])


def solution(mesh):
    n_blk, n_cd = mesh.devices.shape
    blk = ("zh", "zl", "x", "core")
    parted = Mesh(mesh.devices.reshape(n_blk // 8, 2, 2, 2, n_cd), blk + ("cd",))
    in_specs = (P(blk, "cd"), P(blk, None, "cd"), P(blk), P("cd"))
    return jax.shard_map(
        per_device, mesh=parted, in_specs=in_specs, out_specs=P("cd", blk), check_vma=False
    )
```

```python
import functools

import jax
import jax.numpy as jnp
from jax import lax
from jax.experimental import pallas as pl
from jax.experimental.pallas import tpu as pltpu
from jax.sharding import Mesh, PartitionSpec as P

NSYM = 8
SPLIT = (3, 2)
LATER_SPLIT = (2, 1)
LATER = sum(LATER_SPLIT)
LANES = 128
VMEM_LIMIT = 20 * 2**20

ANY = pl.BlockSpec(memory_space=pl.ANY)
SMEM = pl.BlockSpec(memory_space=pltpu.SMEM)
VMEM = pl.BlockSpec(memory_space=pltpu.VMEM)

CHEAP = pl.CostEstimate(flops=1000, bytes_accessed=1000, transcendentals=0)


def params(limit=VMEM_LIMIT):
    return pltpu.CompilerParams(vmem_limit_bytes=limit)


def half_turned(x):
    half = LANES // 2
    return jnp.concatenate([x[:, half:], x[:, :half]], axis=1)


def rank_tiles(sym_ref, count_ref, order_ref, place_ref, tiles):
    for s in range(NSYM):
        count_ref[s] = s * (tiles // NSYM)

    def step(i, _):
        s = sym_ref[i]
        p = count_ref[s]
        count_ref[s] = p + 1
        order_ref[p] = i
        if place_ref is not None:
            place_ref[i] = p
        return 0

    lax.fori_loop(0, tiles, step, 0)


def pick_pair(both, a, b, left):
    columns = both.shape[2] // LANES
    a_col = lax.shift_right_logical(a, 1)
    b_col = lax.rem(lax.shift_right_logical(b + 1, 1) + columns - 1, columns)
    xa = both[a & 1, :, pl.ds(pl.multiple_of(a_col * LANES, LANES), LANES)]
    xb = both[(b & 1) ^ 1, :, pl.ds(pl.multiple_of(b_col * LANES, LANES), LANES)]
    return jnp.where(left, xa, xb)


def sort_amps_kernel(cd_ref, t2_ref, *rest):
    chunks, (both, count, order, sem) = rest[:-4], rest[-4:]
    rows = t2_ref.shape[0]
    load = pltpu.make_async_copy(t2_ref, both.at[0], sem)
    load.start()
    rank_tiles(cd_ref, count, order, None, cd_ref.shape[0])
    load.wait()
    both[1] = half_turned(both[0])
    left = lax.broadcasted_iota(jnp.int32, (rows, LANES), 1) < LANES // 2
    q = 0
    for chunk in chunks:
        for off in range(chunk.shape[1] // LANES):
            pair = pick_pair(both, order[2 * q], order[2 * q + 1], left)
            chunk[:, off * LANES : (off + 1) * LANES] = pair
            q += 1


def sort_amps(t2, cd_sym):
    rows, cols = t2.shape
    return pl.pallas_call(
        sort_amps_kernel,
        out_shape=[
            jax.ShapeDtypeStruct((rows, cols // NSYM * m), t2.dtype) for m in (*SPLIT, LATER)
        ],
        in_specs=[SMEM, ANY],
        out_specs=[VMEM] * (len(SPLIT) + 1),
        scratch_shapes=[
            pltpu.VMEM((2, rows, cols), t2.dtype),
            pltpu.SMEM((NSYM,), jnp.int32),
            pltpu.SMEM((cd_sym.shape[0],), jnp.int32),
            pltpu.SemaphoreType.DMA,
        ],
        compiler_params=params(),
        cost_estimate=CHEAP,
        name="sort_amps",
    )(cd_sym, t2)


def sort_ints_kernel(ab_ref, ints_ref, _, place, *rest):
    outs, (count, order) = rest[:-2], rest[-2:]
    tiles = ab_ref.shape[0]
    rank_tiles(ab_ref, count, order, place, tiles)
    per_sym = tiles // NSYM
    sym = 0
    for out_ref in outs:
        for s in range(out_ref.shape[0]):
            rows = [ints_ref[order[sym * per_sym + m]] for m in range(per_sym)]
            out_ref[s] = jnp.concatenate(rows, axis=0).T
            sym += 1


def sort_ints(integrals, ab_sym, earlier):
    tiles, tile, packed = integrals.shape
    return pl.pallas_call(
        sort_ints_kernel,
        out_shape=[jax.ShapeDtypeStruct((tiles,), jnp.int32)]
        + [
            jax.ShapeDtypeStruct((m, packed, tiles // NSYM * tile), integrals.dtype)
            for m in (NSYM - LATER, *LATER_SPLIT)
        ],
        in_specs=[SMEM, VMEM, ANY],
        out_specs=[SMEM, VMEM] + [VMEM] * len(LATER_SPLIT),
        scratch_shapes=[pltpu.SMEM((NSYM,), jnp.int32), pltpu.SMEM((tiles,), jnp.int32)],
        compiler_params=params(),
        cost_estimate=CHEAP,
        name="sort_ints",
    )(ab_sym, integrals, earlier)


def merge_kernel(n, *refs):
    blocks, out_ref = refs[:n], refs[-1]
    me = lax.axis_index("zh")
    for d, block in enumerate(blocks):
        out_ref[me ^ d] = block[...]


def merge(blocks, earlier):
    return pl.pallas_call(
        functools.partial(merge_kernel, len(blocks)),
        out_shape=jax.ShapeDtypeStruct((len(blocks),) + blocks[0].shape, blocks[0].dtype),
        in_specs=[VMEM] * len(blocks) + [ANY] * len(earlier),
        out_specs=VMEM,
        compiler_params=params(),
        cost_estimate=CHEAP,
        name="merge",
    )(*blocks, *earlier)


def nothing(*refs):
    pass


def after(x, *earlier):
    return pl.pallas_call(
        nothing,
        out_shape=jax.ShapeDtypeStruct(x.shape, x.dtype),
        in_specs=[ANY] * (1 + len(earlier)),
        out_specs=ANY,
        input_output_aliases={0: 0},
        compiler_params=params(),
        cost_estimate=CHEAP,
        name="after",
    )(x, *earlier)


def lay_out(lhs, refs, where, place):
    h, z, x = lax.axis_index("zh"), lax.axis_index("zl"), lax.axis_index("x")
    for k, quarter in enumerate(where):
        for d, (array, entry) in enumerate(quarter):
            ref = refs[array]
            slot = 4 * (h ^ d) + 2 * (z ^ (k // 2)) + (x ^ (k % 2))
            lhs[place(slot)] = ref[...] if entry is None else ref[h ^ d if entry < 0 else entry]


def contract_kernel(n_cd, first_sym, n_blocks, where, *refs):
    blocks, (own_ref, sib_ref) = refs[:n_blocks], refs[n_blocks : n_blocks + 2]
    outs, lhs = refs[-n_cd - 1 : -1], refs[-1]
    slots, rows, cols = lhs.shape
    packed, width = own_ref.shape[1:]
    first = lax.axis_index("cd") * (slots // n_cd)
    lay_out(lhs, blocks, where, lambda n: lax.rem(n + slots - first, slots))
    t2 = lhs[...].reshape(slots * rows, cols)
    group_rows = t2.shape[0] // n_cd
    for side, ints in enumerate((own_ref, sib_ref)):
        for s in range(cols // packed):
            part = jnp.dot(
                t2[:, s * packed : (s + 1) * packed],
                ints[first_sym + s],
                preferred_element_type=jnp.float32,
            ).astype(outs[0].dtype)
            for by in range(n_cd):
                outs[by][side, :, s * width : (s + 1) * width] = part[
                    by * group_rows : (by + 1) * group_rows
                ]


def contract(n_cd, t2s, ints, sib_ints, first_sym, earlier):
    blocks, where = t2s
    rows, cols = blocks[0].shape[-2:]
    slots = 4 * len(where[0])
    packed, width = ints.shape[1:]
    out = (2, slots * rows // n_cd, cols // packed * width)
    return pl.pallas_call(
        functools.partial(contract_kernel, n_cd, first_sym, len(blocks), where),
        out_shape=[jax.ShapeDtypeStruct(out, jnp.bfloat16)] * n_cd,
        in_specs=[VMEM] * (len(blocks) + 2) + [ANY] * len(earlier),
        out_specs=[VMEM] * n_cd,
        scratch_shapes=[pltpu.VMEM((slots, rows, cols), jnp.bfloat16)],
        compiler_params=params(),
        cost_estimate=CHEAP,
        name="contract",
    )(*blocks, ints, sib_ints, *earlier)


def total(parts):
    value = parts[0].astype(jnp.float32)
    for part in parts[1:]:
        value += part.astype(jnp.float32)
    return value.astype(jnp.bfloat16)


def join_kernel(n, *refs):
    out_ref, first = refs[-1], 0
    for ref in refs[:n]:
        out_ref[first : first + ref.shape[0]] = ref[...]
        first += ref.shape[0]


def join(arrays, earlier):
    n = len(arrays)
    out = (sum(x.shape[0] for x in arrays), *arrays[0].shape[1:])
    return pl.pallas_call(
        functools.partial(join_kernel, n),
        out_shape=jax.ShapeDtypeStruct(out, arrays[0].dtype),
        in_specs=[VMEM] * n + [ANY] * len(earlier),
        out_specs=VMEM,
        compiler_params=params(),
        cost_estimate=CHEAP,
        name="join",
    )(*arrays, *earlier)


def later_kernel(n_cd, n_blocks, where, *refs):
    blocks, ints, parts = refs[:n_blocks], refs[n_blocks : n_blocks + 2], refs[n_blocks + 2 : -3]
    own_out, sib_out, lhs = refs[-3:]
    slots, rows, cols = lhs.shape
    packed, width = ints[0].shape[1:]
    per_group, me = slots // n_cd, lax.axis_index("cd")

    def place(n):
        group = lax.div(n, per_group)
        return lax.rem(me + n_cd - group, n_cd) * per_group + (n - group * per_group)

    lay_out(lhs, blocks, where, place)
    t2 = lhs[...].reshape(n_cd, per_group * rows, cols)
    for side, out_ref in enumerate((own_out, sib_out)):
        first = 0
        for c in range(0, len(parts), n_cd):
            value = total([part[side] for part in parts[c : c + n_cd]])
            out_ref[:, first : first + value.shape[1]] = value
            first += value.shape[1]
        for s in range(LATER):
            out_ref[:, first : first + width] = total(
                [
                    jnp.dot(
                        t2[by, :, s * packed : (s + 1) * packed],
                        ints[side][by * LATER + s],
                        preferred_element_type=jnp.float32,
                    ).astype(out_ref.dtype)
                    for by in range(n_cd)
                ]
            )
            first += width


def contract_later(n_cd, t2s, ints, parts):
    blocks, where = t2s
    rows, cols = blocks[0].shape[-2:]
    width = ints[0].shape[2] * LATER + sum(p.shape[2] for p in parts[::n_cd])
    out = jax.ShapeDtypeStruct((parts[0].shape[1], width), jnp.bfloat16)
    return pl.pallas_call(
        functools.partial(later_kernel, n_cd, len(blocks), where),
        out_shape=[out, out],
        in_specs=[VMEM] * (len(blocks) + 2 + len(parts)),
        out_specs=[VMEM] * 2,
        scratch_shapes=[pltpu.VMEM((4 * len(where[0]), rows, cols), jnp.bfloat16)],
        compiler_params=params(),
        cost_estimate=CHEAP,
        name="contract_later",
    )(*blocks, *ints, *parts)


def finish_kernel(side, place, sums_ref, *rest):
    out_ref, both, made, sems = rest[-4:]
    blocks, rows, cols = made.shape
    left = lax.broadcasted_iota(jnp.int32, (rows, LANES), 1) < LANES // 2

    def copy_out(i):
        block = 2 * i + (lax.axis_index("core") ^ side)
        return pltpu.make_async_copy(made.at[i], out_ref.at[block], sems.at[i])

    for i in range(blocks):
        both[0] = sums_ref[i * rows : (i + 1) * rows]
        both[1] = half_turned(both[0])
        for q in range(cols // LANES):
            made[i, :, q * LANES : (q + 1) * LANES] = pick_pair(
                both, place[2 * q], place[2 * q + 1], left
            )
        copy_out(i).start()
    for i in range(blocks):
        copy_out(i).wait()


def finish(side, place, sums, rows, out=None):
    blocks, cols = sums.shape[0] // rows, sums.shape[1]
    before = [] if out is None else [out]
    return pl.pallas_call(
        functools.partial(finish_kernel, side),
        out_shape=jax.ShapeDtypeStruct((2 * blocks, rows, cols), jnp.bfloat16),
        in_specs=[SMEM, VMEM] + [ANY] * len(before),
        out_specs=ANY,
        scratch_shapes=[
            pltpu.VMEM((2, rows, cols), jnp.bfloat16),
            pltpu.VMEM((blocks, rows, cols), jnp.bfloat16),
            pltpu.SemaphoreType.DMA((blocks,)),
        ],
        input_output_aliases={2: 0} if before else {},
        compiler_params=params(),
        cost_estimate=CHEAP,
        name="finish",
    )(place, sums, *before)


SWAP = [(0, 1), (1, 0)]


def further(x, by):
    n_cd = lax.axis_size("cd")
    return lax.ppermute(x, "cd", [(i, (i + by) % n_cd) for i in range(n_cd)])


def to_plane(x):
    n_cd = lax.axis_size("cd")
    z_len = 2 * lax.axis_size("zh")
    rest = z_len // n_cd
    pairs = []
    for z in range(z_len):
        group, i = divmod(z, rest)
        pairs += [(z * n_cd + y, (y * rest + i) * n_cd + group) for y in range(n_cd)]
    return lax.ppermute(x, ("zh", "zl", "cd"), pairs)


def per_device(t2_amps, integrals, ab_sym, cd_sym):
    zh, n_cd = lax.axis_size("zh"), lax.axis_size("cd")
    own0, own1, own2 = sort_amps(t2_amps, cd_sym)

    def over(x, axis):
        return lax.ppermute(x, axis, SWAP)

    def along_zh(x):
        return [lax.ppermute(x, "zh", [(i, i ^ d) for i in range(zh)]) for d in range(1, zh)]

    later = []

    def send_later(s, latest):
        x = after(ints_later[s], latest)
        later.append([x] + [further(x, by) for by in range(1, n_cd)])
        return later[-1][1:]

    place, ints, *ints_later = sort_ints(integrals, ab_sym, own0)
    across1 = [over(own1, "x")]
    near0 = merge([own0] + along_zh(own0), [ints, *across1])
    ints = after(ints, near0)
    sib_ints = over(ints, "core")
    up0, across0 = over(near0, "zl"), over(near0, "x")
    others1 = along_zh(own1)
    near1 = merge([own1] + others1, [sib_ints, up0, across0, *send_later(0, near0)])
    far0 = over(up0, "x")
    up1 = over(near1, "zl")
    across1 += [over(after(x, near1), "x") for x in others1]
    own2 = to_plane(after(own2, near1))
    stacked = [tuple((k, -1) for d in range(zh)) for k in range(4)]
    made0 = contract(
        n_cd,
        ((near0, across0, up0, far0), tuple(stacked)),
        ints,
        sib_ints,
        0,
        [own2, *across1, *send_later(1, near1)],
    )
    parts = [made0[0]] + [further(made0[by], by) for by in range(1, n_cd)]
    far1 = over(up1, "x")
    own2 = after(own2, made0[0])
    others2 = along_zh(own2)
    blocks = [near1, up1, far1, *across1]
    stacked[1] = tuple((3 + d, None) for d in range(zh))
    stacked[2:] = [tuple((k, -1) for d in range(zh)) for k in (1, 2)]
    made1 = contract(n_cd, (blocks, tuple(stacked)), ints, sib_ints, SPLIT[0], parts[:1])
    parts += [made1[0]] + [further(made1[by], by) for by in range(1, n_cd)]
    up2, across2 = over(own2, "zl"), over(own2, "x")
    turned = join([x[None] for x in [*others2, up2]], [across2, made1[0]])
    across_turned = over(turned, "x")
    ups2 = [up2] + [over(after(x, turned), "zl") for x in others2]
    fars2 = [over(x, "x") for x in ups2[1:]]
    ints_later = join([x[by] for by in range(n_cd) for x in later], [turned])
    ints_later = (ints_later, over(ints_later, "core"))
    blocks = [own2, *others2, *ups2, across2, across_turned, *fars2]
    where = (
        tuple((d, None) for d in range(zh)),
        ((2 * zh, None),) + tuple((2 * zh + 1, d - 1) for d in range(1, zh)),
        tuple((zh + d, None) for d in range(zh)),
        ((2 * zh + 1, zh - 1),) + tuple((2 * zh + 1 + d, None) for d in range(1, zh)),
    )
    t2s = blocks, where
    sums, sib_sums = contract_later(n_cd, t2s, ints_later, parts)
    sib_sums = lax.ppermute(sib_sums, "core", SWAP)
    rows = t2_amps.shape[0]
    out = finish(0, place, sums, rows)
    out = finish(1, place, sib_sums, rows, out)
    return out.reshape(-1, out.shape[2])


def solution(mesh):
    n_blk, n_cd = mesh.devices.shape
    blk = ("zh", "zl", "x", "core")
    parted = Mesh(mesh.devices.reshape(n_blk // 8, 2, 2, 2, n_cd), blk + ("cd",))
    in_specs = (P(blk, "cd"), P(blk, None, "cd"), P(blk), P("cd"))
    return jax.shard_map(
        per_device, mesh=parted, in_specs=in_specs, out_specs=P("cd", blk), check_vma=False
    )
```

```python
import functools

import jax
import jax.numpy as jnp
from jax import lax
from jax.experimental import pallas as pl
from jax.experimental.pallas import tpu as pltpu
from jax.sharding import Mesh, PartitionSpec as P

NSYM = 8
SPLIT = (4,)
LATER_SPLIT = (4,)
LATER = sum(LATER_SPLIT)
LANES = 128
VMEM_LIMIT = 20 * 2**20

ANY = pl.BlockSpec(memory_space=pl.ANY)
SMEM = pl.BlockSpec(memory_space=pltpu.SMEM)
VMEM = pl.BlockSpec(memory_space=pltpu.VMEM)

CHEAP = pl.CostEstimate(flops=1000, bytes_accessed=1000, transcendentals=0)


def params(limit=VMEM_LIMIT):
    return pltpu.CompilerParams(vmem_limit_bytes=limit)


def half_turned(x):
    half = LANES // 2
    return jnp.concatenate([x[:, half:], x[:, :half]], axis=1)


def rank_tiles(sym_ref, count_ref, order_ref, place_ref, tiles):
    for s in range(NSYM):
        count_ref[s] = s * (tiles // NSYM)

    def step(i, _):
        s = sym_ref[i]
        p = count_ref[s]
        count_ref[s] = p + 1
        order_ref[p] = i
        if place_ref is not None:
            place_ref[i] = p
        return 0

    lax.fori_loop(0, tiles, step, 0)


def pick_pair(both, a, b, left):
    columns = both.shape[2] // LANES
    a_col = lax.shift_right_logical(a, 1)
    b_col = lax.rem(lax.shift_right_logical(b + 1, 1) + columns - 1, columns)
    xa = both[a & 1, :, pl.ds(pl.multiple_of(a_col * LANES, LANES), LANES)]
    xb = both[(b & 1) ^ 1, :, pl.ds(pl.multiple_of(b_col * LANES, LANES), LANES)]
    return jnp.where(left, xa, xb)


def sort_amps_kernel(cd_ref, t2_ref, *rest):
    chunks, (both, count, order, sem) = rest[:-4], rest[-4:]
    rows = t2_ref.shape[0]
    load = pltpu.make_async_copy(t2_ref, both.at[0], sem)
    load.start()
    rank_tiles(cd_ref, count, order, None, cd_ref.shape[0])
    load.wait()
    both[1] = half_turned(both[0])
    left = lax.broadcasted_iota(jnp.int32, (rows, LANES), 1) < LANES // 2
    q = 0
    for chunk in chunks:
        for off in range(chunk.shape[1] // LANES):
            pair = pick_pair(both, order[2 * q], order[2 * q + 1], left)
            chunk[:, off * LANES : (off + 1) * LANES] = pair
            q += 1


def sort_amps(t2, cd_sym):
    rows, cols = t2.shape
    return pl.pallas_call(
        sort_amps_kernel,
        out_shape=[
            jax.ShapeDtypeStruct((rows, cols // NSYM * m), t2.dtype) for m in (*SPLIT, LATER)
        ],
        in_specs=[SMEM, ANY],
        out_specs=[VMEM] * (len(SPLIT) + 1),
        scratch_shapes=[
            pltpu.VMEM((2, rows, cols), t2.dtype),
            pltpu.SMEM((NSYM,), jnp.int32),
            pltpu.SMEM((cd_sym.shape[0],), jnp.int32),
            pltpu.SemaphoreType.DMA,
        ],
        compiler_params=params(),
        cost_estimate=CHEAP,
        name="sort_amps",
    )(cd_sym, t2)


def sort_ints_kernel(ab_ref, ints_ref, _, place, *rest):
    outs, (count, order) = rest[:-2], rest[-2:]
    tiles = ab_ref.shape[0]
    rank_tiles(ab_ref, count, order, place, tiles)
    per_sym = tiles // NSYM
    sym = 0
    for out_ref in outs:
        for s in range(out_ref.shape[0]):
            rows = [ints_ref[order[sym * per_sym + m]] for m in range(per_sym)]
            out_ref[s] = jnp.concatenate(rows, axis=0).T
            sym += 1


def sort_ints(integrals, ab_sym, earlier):
    tiles, tile, packed = integrals.shape
    return pl.pallas_call(
        sort_ints_kernel,
        out_shape=[jax.ShapeDtypeStruct((tiles,), jnp.int32)]
        + [
            jax.ShapeDtypeStruct((m, packed, tiles // NSYM * tile), integrals.dtype)
            for m in (NSYM - LATER, *LATER_SPLIT)
        ],
        in_specs=[SMEM, VMEM, ANY],
        out_specs=[SMEM, VMEM] + [VMEM] * len(LATER_SPLIT),
        scratch_shapes=[pltpu.SMEM((NSYM,), jnp.int32), pltpu.SMEM((tiles,), jnp.int32)],
        compiler_params=params(),
        cost_estimate=CHEAP,
        name="sort_ints",
    )(ab_sym, integrals, earlier)


def merge_kernel(n, *refs):
    blocks, out_ref = refs[:n], refs[-1]
    me = lax.axis_index("zh")
    for d, block in enumerate(blocks):
        out_ref[me ^ d] = block[...]


def merge(blocks, earlier):
    return pl.pallas_call(
        functools.partial(merge_kernel, len(blocks)),
        out_shape=jax.ShapeDtypeStruct((len(blocks),) + blocks[0].shape, blocks[0].dtype),
        in_specs=[VMEM] * len(blocks) + [ANY] * len(earlier),
        out_specs=VMEM,
        compiler_params=params(),
        cost_estimate=CHEAP,
        name="merge",
    )(*blocks, *earlier)


def nothing(*refs):
    pass


def after(x, *earlier):
    return pl.pallas_call(
        nothing,
        out_shape=jax.ShapeDtypeStruct(x.shape, x.dtype),
        in_specs=[ANY] * (1 + len(earlier)),
        out_specs=ANY,
        input_output_aliases={0: 0},
        compiler_params=params(),
        cost_estimate=CHEAP,
        name="after",
    )(x, *earlier)


def lay_out(lhs, refs, where, place):
    h, z, x = lax.axis_index("zh"), lax.axis_index("zl"), lax.axis_index("x")
    for k, quarter in enumerate(where):
        for d, (array, entry) in enumerate(quarter):
            ref = refs[array]
            slot = 4 * (h ^ d) + 2 * (z ^ (k // 2)) + (x ^ (k % 2))
            lhs[place(slot)] = ref[...] if entry is None else ref[h ^ d if entry < 0 else entry]


def contract_kernel(n_cd, first_sym, n_blocks, where, *refs):
    blocks, (own_ref, sib_ref) = refs[:n_blocks], refs[n_blocks : n_blocks + 2]
    outs, lhs = refs[-n_cd - 1 : -1], refs[-1]
    slots, rows, cols = lhs.shape
    packed, width = own_ref.shape[1:]
    first = lax.axis_index("cd") * (slots // n_cd)
    lay_out(lhs, blocks, where, lambda n: lax.rem(n + slots - first, slots))
    t2 = lhs[...].reshape(slots * rows, cols)
    group_rows = t2.shape[0] // n_cd
    for side, ints in enumerate((own_ref, sib_ref)):
        for s in range(cols // packed):
            part = jnp.dot(
                t2[:, s * packed : (s + 1) * packed],
                ints[first_sym + s],
                preferred_element_type=jnp.float32,
            ).astype(outs[0].dtype)
            for by in range(n_cd):
                outs[by][side, :, s * width : (s + 1) * width] = part[
                    by * group_rows : (by + 1) * group_rows
                ]


def contract(n_cd, t2s, ints, sib_ints, first_sym, earlier):
    blocks, where = t2s
    rows, cols = blocks[0].shape[-2:]
    slots = 4 * len(where[0])
    packed, width = ints.shape[1:]
    out = (2, slots * rows // n_cd, cols // packed * width)
    return pl.pallas_call(
        functools.partial(contract_kernel, n_cd, first_sym, len(blocks), where),
        out_shape=[jax.ShapeDtypeStruct(out, jnp.bfloat16)] * n_cd,
        in_specs=[VMEM] * (len(blocks) + 2) + [ANY] * len(earlier),
        out_specs=[VMEM] * n_cd,
        scratch_shapes=[pltpu.VMEM((slots, rows, cols), jnp.bfloat16)],
        compiler_params=params(),
        cost_estimate=CHEAP,
        name="contract",
    )(*blocks, ints, sib_ints, *earlier)


def total(parts):
    value = parts[0].astype(jnp.float32)
    for part in parts[1:]:
        value += part.astype(jnp.float32)
    return value.astype(jnp.bfloat16)


def join_kernel(n, *refs):
    out_ref, first = refs[-1], 0
    for ref in refs[:n]:
        out_ref[first : first + ref.shape[0]] = ref[...]
        first += ref.shape[0]


def join(arrays, earlier):
    n = len(arrays)
    out = (sum(x.shape[0] for x in arrays), *arrays[0].shape[1:])
    return pl.pallas_call(
        functools.partial(join_kernel, n),
        out_shape=jax.ShapeDtypeStruct(out, arrays[0].dtype),
        in_specs=[VMEM] * n + [ANY] * len(earlier),
        out_specs=VMEM,
        compiler_params=params(),
        cost_estimate=CHEAP,
        name="join",
    )(*arrays, *earlier)


def later_kernel(n_cd, n_blocks, where, *refs):
    blocks, ints, parts = refs[:n_blocks], refs[n_blocks : n_blocks + 2], refs[n_blocks + 2 : -3]
    own_out, sib_out, lhs = refs[-3:]
    slots, rows, cols = lhs.shape
    packed, width = ints[0].shape[1:]
    per_group, me = slots // n_cd, lax.axis_index("cd")

    def place(n):
        group = lax.div(n, per_group)
        return lax.rem(me + n_cd - group, n_cd) * per_group + (n - group * per_group)

    lay_out(lhs, blocks, where, place)
    t2 = lhs[...].reshape(n_cd, per_group * rows, cols)
    for side, out_ref in enumerate((own_out, sib_out)):
        first = 0
        for c in range(0, len(parts), n_cd):
            value = total([part[side] for part in parts[c : c + n_cd]])
            out_ref[:, first : first + value.shape[1]] = value
            first += value.shape[1]
        for s in range(LATER):
            out_ref[:, first : first + width] = total(
                [
                    jnp.dot(
                        t2[by, :, s * packed : (s + 1) * packed],
                        ints[side][by * LATER + s],
                        preferred_element_type=jnp.float32,
                    ).astype(out_ref.dtype)
                    for by in range(n_cd)
                ]
            )
            first += width


def contract_later(n_cd, t2s, ints, parts):
    blocks, where = t2s
    rows, cols = blocks[0].shape[-2:]
    width = ints[0].shape[2] * LATER + sum(p.shape[2] for p in parts[::n_cd])
    out = jax.ShapeDtypeStruct((parts[0].shape[1], width), jnp.bfloat16)
    return pl.pallas_call(
        functools.partial(later_kernel, n_cd, len(blocks), where),
        out_shape=[out, out],
        in_specs=[VMEM] * (len(blocks) + 2 + len(parts)),
        out_specs=[VMEM] * 2,
        scratch_shapes=[pltpu.VMEM((4 * len(where[0]), rows, cols), jnp.bfloat16)],
        compiler_params=params(),
        cost_estimate=CHEAP,
        name="contract_later",
    )(*blocks, *ints, *parts)


def finish_kernel(side, place, sums_ref, *rest):
    out_ref, both, made, sems = rest[-4:]
    blocks, rows, cols = made.shape
    left = lax.broadcasted_iota(jnp.int32, (rows, LANES), 1) < LANES // 2

    def copy_out(i):
        block = 2 * i + (lax.axis_index("core") ^ side)
        return pltpu.make_async_copy(made.at[i], out_ref.at[block], sems.at[i])

    for i in range(blocks):
        both[0] = sums_ref[i * rows : (i + 1) * rows]
        both[1] = half_turned(both[0])
        for q in range(cols // LANES):
            made[i, :, q * LANES : (q + 1) * LANES] = pick_pair(
                both, place[2 * q], place[2 * q + 1], left
            )
        copy_out(i).start()
    for i in range(blocks):
        copy_out(i).wait()


def finish(side, place, sums, rows, out=None):
    blocks, cols = sums.shape[0] // rows, sums.shape[1]
    before = [] if out is None else [out]
    return pl.pallas_call(
        functools.partial(finish_kernel, side),
        out_shape=jax.ShapeDtypeStruct((2 * blocks, rows, cols), jnp.bfloat16),
        in_specs=[SMEM, VMEM] + [ANY] * len(before),
        out_specs=ANY,
        scratch_shapes=[
            pltpu.VMEM((2, rows, cols), jnp.bfloat16),
            pltpu.VMEM((blocks, rows, cols), jnp.bfloat16),
            pltpu.SemaphoreType.DMA((blocks,)),
        ],
        input_output_aliases={2: 0} if before else {},
        compiler_params=params(),
        cost_estimate=CHEAP,
        name="finish",
    )(place, sums, *before)


SWAP = [(0, 1), (1, 0)]


def further(x, by):
    n_cd = lax.axis_size("cd")
    return lax.ppermute(x, "cd", [(i, (i + by) % n_cd) for i in range(n_cd)])


def to_plane(x):
    n_cd = lax.axis_size("cd")
    z_len = 2 * lax.axis_size("zh")
    rest = z_len // n_cd
    pairs = []
    for z in range(z_len):
        group, i = divmod(z, rest)
        pairs += [(z * n_cd + y, (y * rest + i) * n_cd + group) for y in range(n_cd)]
    return lax.ppermute(x, ("zh", "zl", "cd"), pairs)


def per_device(t2_amps, integrals, ab_sym, cd_sym):
    zh, n_cd = lax.axis_size("zh"), lax.axis_size("cd")
    own, own_later = sort_amps(t2_amps, cd_sym)

    def over(x, axis):
        return lax.ppermute(x, axis, SWAP)

    def along_zh(x):
        return [lax.ppermute(x, "zh", [(i, i ^ d) for i in range(zh)]) for d in range(1, zh)]

    quarters = (
        tuple((d, None) for d in range(zh)),
        ((2 * zh, None),) + tuple((2 * zh + 1, d - 1) for d in range(1, zh)),
        tuple((zh + d, None) for d in range(zh)),
        ((2 * zh + 1, zh - 1),) + tuple((2 * zh + 1 + d, None) for d in range(1, zh)),
    )

    def first_step(x):
        return x, along_zh(x), over(x, "zl"), over(x, "x")

    def next_steps(step, earlier):
        x, others, up, across = step
        turned = join([y[None] for y in [*others, up]], [across, *earlier])
        across_turned = over(turned, "x")
        ups = [up] + [over(after(y, turned), "zl") for y in others]
        fars = [over(y, "x") for y in ups[1:]]
        return turned, ([x, *others, *ups, across, across_turned, *fars], quarters)

    place, ints, ints_later = sort_ints(integrals, ab_sym, own)
    turned, t2s = next_steps(first_step(own), [ints])
    ints, ints_later = after(ints, turned), after(ints_later, turned)
    sib_ints = over(ints, "core")
    later = [ints_later] + [further(ints_later, by) for by in range(1, n_cd)]
    own_later = to_plane(after(own_later, turned))
    step = first_step(after(own_later, t2s[0][2 * zh + 1], sib_ints))
    made = contract(n_cd, t2s, ints, sib_ints, 0, [*step[1], *step[2:], *later[1:]])
    parts = [made[0]] + [further(made[by], by) for by in range(1, n_cd)]
    _, t2s = next_steps(step, made[:1])
    ints_later = join(later, made[:1])
    ints_later = (ints_later, over(ints_later, "core"))
    sums, sib_sums = contract_later(n_cd, t2s, ints_later, parts)
    sib_sums = lax.ppermute(sib_sums, "core", SWAP)
    rows = t2_amps.shape[0]
    out = finish(0, place, sums, rows)
    out = finish(1, place, sib_sums, rows, out)
    return out.reshape(-1, out.shape[2])


def solution(mesh):
    n_blk, n_cd = mesh.devices.shape
    blk = ("zh", "zl", "x", "core")
    parted = Mesh(mesh.devices.reshape(n_blk // 8, 2, 2, 2, n_cd), blk + ("cd",))
    in_specs = (P(blk, "cd"), P(blk, None, "cd"), P(blk), P("cd"))
    return jax.shard_map(
        per_device, mesh=parted, in_specs=in_specs, out_specs=P("cd", blk), check_vma=False
    )
```

```python
import functools

import jax
import jax.numpy as jnp
from jax import lax
from jax.experimental import pallas as pl
from jax.experimental.pallas import tpu as pltpu
from jax.sharding import Mesh, PartitionSpec as P

NSYM = 8
SPLIT = (4,)
LATER_SPLIT = (2, 2)
LATER = sum(LATER_SPLIT)
LANES = 128
VMEM_LIMIT = 20 * 2**20

ANY = pl.BlockSpec(memory_space=pl.ANY)
SMEM = pl.BlockSpec(memory_space=pltpu.SMEM)
VMEM = pl.BlockSpec(memory_space=pltpu.VMEM)

CHEAP = pl.CostEstimate(flops=1000, bytes_accessed=1000, transcendentals=0)


def params(limit=VMEM_LIMIT):
    return pltpu.CompilerParams(vmem_limit_bytes=limit)


def half_turned(x):
    half = LANES // 2
    return jnp.concatenate([x[:, half:], x[:, :half]], axis=1)


def rank_tiles(sym_ref, count_ref, order_ref, place_ref, tiles):
    for s in range(NSYM):
        count_ref[s] = s * (tiles // NSYM)

    def step(i, _):
        s = sym_ref[i]
        p = count_ref[s]
        count_ref[s] = p + 1
        order_ref[p] = i
        if place_ref is not None:
            place_ref[i] = p
        return 0

    lax.fori_loop(0, tiles, step, 0)


def pick_pair(both, a, b, left):
    columns = both.shape[2] // LANES
    a_col = lax.shift_right_logical(a, 1)
    b_col = lax.rem(lax.shift_right_logical(b + 1, 1) + columns - 1, columns)
    xa = both[a & 1, :, pl.ds(pl.multiple_of(a_col * LANES, LANES), LANES)]
    xb = both[(b & 1) ^ 1, :, pl.ds(pl.multiple_of(b_col * LANES, LANES), LANES)]
    return jnp.where(left, xa, xb)


def sort_amps_kernel(cd_ref, t2_ref, *rest):
    chunks, (both, count, order, sem) = rest[:-4], rest[-4:]
    rows = t2_ref.shape[0]
    load = pltpu.make_async_copy(t2_ref, both.at[0], sem)
    load.start()
    rank_tiles(cd_ref, count, order, None, cd_ref.shape[0])
    load.wait()
    both[1] = half_turned(both[0])
    left = lax.broadcasted_iota(jnp.int32, (rows, LANES), 1) < LANES // 2
    q = 0
    for chunk in chunks:
        for off in range(chunk.shape[1] // LANES):
            pair = pick_pair(both, order[2 * q], order[2 * q + 1], left)
            chunk[:, off * LANES : (off + 1) * LANES] = pair
            q += 1


def sort_amps(t2, cd_sym):
    rows, cols = t2.shape
    return pl.pallas_call(
        sort_amps_kernel,
        out_shape=[
            jax.ShapeDtypeStruct((rows, cols // NSYM * m), t2.dtype) for m in (*SPLIT, LATER)
        ],
        in_specs=[SMEM, ANY],
        out_specs=[VMEM] * (len(SPLIT) + 1),
        scratch_shapes=[
            pltpu.VMEM((2, rows, cols), t2.dtype),
            pltpu.SMEM((NSYM,), jnp.int32),
            pltpu.SMEM((cd_sym.shape[0],), jnp.int32),
            pltpu.SemaphoreType.DMA,
        ],
        compiler_params=params(),
        cost_estimate=CHEAP,
        name="sort_amps",
    )(cd_sym, t2)


def sort_ints_kernel(first, ab_ref, ints_ref, _, place, *rest):
    outs, (rows, count, order, sems) = rest[:-4], rest[-4:]
    tiles, tile = ab_ref.shape[0], rows.shape[1]
    rank_tiles(ab_ref, count, order, place, tiles)
    per_sym = tiles // NSYM
    copies = [
        pltpu.make_async_copy(ints_ref.at[order[first * per_sym + p]], rows.at[p], sems.at[p])
        for p in range(rows.shape[0])
    ]
    for copy in copies:
        copy.start()
    for copy in copies:
        copy.wait()
    p = 0
    for out_ref in outs:
        for s in range(out_ref.shape[0]):
            out_ref[s] = rows[p : p + per_sym].reshape(per_sym * tile, rows.shape[2]).T
            p += per_sym


def sort_ints(integrals, ab_sym, first, sizes, limit, earlier):
    tiles, tile, packed = integrals.shape
    per_sym = tiles // NSYM
    used = sum(sizes) * per_sym
    return pl.pallas_call(
        functools.partial(sort_ints_kernel, first),
        out_shape=[jax.ShapeDtypeStruct((tiles,), jnp.int32)]
        + [jax.ShapeDtypeStruct((m, packed, per_sym * tile), integrals.dtype) for m in sizes],
        in_specs=[SMEM, ANY, ANY],
        out_specs=[SMEM] + [VMEM] * len(sizes),
        scratch_shapes=[
            pltpu.VMEM((used, tile, packed), integrals.dtype),
            pltpu.SMEM((NSYM,), jnp.int32),
            pltpu.SMEM((tiles,), jnp.int32),
            pltpu.SemaphoreType.DMA((used,)),
        ],
        compiler_params=params(limit),
        cost_estimate=CHEAP,
        name="sort_ints",
    )(ab_sym, integrals, earlier)


def merge_kernel(n, *refs):
    blocks, out_ref = refs[:n], refs[-1]
    me = lax.axis_index("zh")
    for d, block in enumerate(blocks):
        out_ref[me ^ d] = block[...]


def merge(blocks, earlier):
    return pl.pallas_call(
        functools.partial(merge_kernel, len(blocks)),
        out_shape=jax.ShapeDtypeStruct((len(blocks),) + blocks[0].shape, blocks[0].dtype),
        in_specs=[VMEM] * len(blocks) + [ANY] * len(earlier),
        out_specs=VMEM,
        compiler_params=params(),
        cost_estimate=CHEAP,
        name="merge",
    )(*blocks, *earlier)


def nothing(*refs):
    pass


def after(x, *earlier):
    return pl.pallas_call(
        nothing,
        out_shape=jax.ShapeDtypeStruct(x.shape, x.dtype),
        in_specs=[ANY] * (1 + len(earlier)),
        out_specs=ANY,
        input_output_aliases={0: 0},
        compiler_params=params(),
        cost_estimate=CHEAP,
        name="after",
    )(x, *earlier)


def lay_out(lhs, refs, where, place):
    h, z, x = lax.axis_index("zh"), lax.axis_index("zl"), lax.axis_index("x")
    for k, quarter in enumerate(where):
        for d, (array, entry) in enumerate(quarter):
            ref = refs[array]
            slot = 4 * (h ^ d) + 2 * (z ^ (k // 2)) + (x ^ (k % 2))
            lhs[place(slot)] = ref[...] if entry is None else ref[h ^ d if entry < 0 else entry]


def contract_kernel(n_cd, first_sym, n_blocks, where, *refs):
    blocks, (own_ref, sib_ref) = refs[:n_blocks], refs[n_blocks : n_blocks + 2]
    outs, lhs = refs[-n_cd - 1 : -1], refs[-1]
    slots, rows, cols = lhs.shape
    packed, width = own_ref.shape[1:]
    first = lax.axis_index("cd") * (slots // n_cd)
    lay_out(lhs, blocks, where, lambda n: lax.rem(n + slots - first, slots))
    t2 = lhs[...].reshape(slots * rows, cols)
    group_rows = t2.shape[0] // n_cd
    for side, ints in enumerate((own_ref, sib_ref)):
        for s in range(cols // packed):
            part = jnp.dot(
                t2[:, s * packed : (s + 1) * packed],
                ints[first_sym + s],
                preferred_element_type=jnp.float32,
            ).astype(outs[0].dtype)
            for by in range(n_cd):
                outs[by][side, :, s * width : (s + 1) * width] = part[
                    by * group_rows : (by + 1) * group_rows
                ]


def contract(n_cd, t2s, ints, sib_ints, first_sym, earlier):
    blocks, where = t2s
    rows, cols = blocks[0].shape[-2:]
    slots = 4 * len(where[0])
    packed, width = ints.shape[1:]
    out = (2, slots * rows // n_cd, cols // packed * width)
    return pl.pallas_call(
        functools.partial(contract_kernel, n_cd, first_sym, len(blocks), where),
        out_shape=[jax.ShapeDtypeStruct(out, jnp.bfloat16)] * n_cd,
        in_specs=[VMEM] * (len(blocks) + 2) + [ANY] * len(earlier),
        out_specs=[VMEM] * n_cd,
        scratch_shapes=[pltpu.VMEM((slots, rows, cols), jnp.bfloat16)],
        compiler_params=params(),
        cost_estimate=CHEAP,
        name="contract",
    )(*blocks, ints, sib_ints, *earlier)


def total(parts):
    value = parts[0].astype(jnp.float32)
    for part in parts[1:]:
        value += part.astype(jnp.float32)
    return value.astype(jnp.bfloat16)


def join_kernel(n, *refs):
    out_ref, first = refs[-1], 0
    for ref in refs[:n]:
        out_ref[first : first + ref.shape[0]] = ref[...]
        first += ref.shape[0]


def join(arrays, earlier):
    n = len(arrays)
    out = (sum(x.shape[0] for x in arrays), *arrays[0].shape[1:])
    return pl.pallas_call(
        functools.partial(join_kernel, n),
        out_shape=jax.ShapeDtypeStruct(out, arrays[0].dtype),
        in_specs=[VMEM] * n + [ANY] * len(earlier),
        out_specs=VMEM,
        compiler_params=params(),
        cost_estimate=CHEAP,
        name="join",
    )(*arrays, *earlier)


def later_kernel(n_cd, n_blocks, where, *refs):
    blocks, ints, parts = refs[:n_blocks], refs[n_blocks : n_blocks + 2], refs[n_blocks + 2 : -3]
    own_out, sib_out, lhs = refs[-3:]
    slots, rows, cols = lhs.shape
    packed, width = ints[0].shape[1:]
    per_group, me = slots // n_cd, lax.axis_index("cd")

    def place(n):
        group = lax.div(n, per_group)
        return lax.rem(me + n_cd - group, n_cd) * per_group + (n - group * per_group)

    lay_out(lhs, blocks, where, place)
    t2 = lhs[...].reshape(n_cd, per_group * rows, cols)
    for side, out_ref in enumerate((own_out, sib_out)):
        first = 0
        for c in range(0, len(parts), n_cd):
            value = total([part[side] for part in parts[c : c + n_cd]])
            out_ref[:, first : first + value.shape[1]] = value
            first += value.shape[1]
        for s in range(LATER):
            out_ref[:, first : first + width] = total(
                [
                    jnp.dot(
                        t2[by, :, s * packed : (s + 1) * packed],
                        ints[side][by * LATER + s],
                        preferred_element_type=jnp.float32,
                    ).astype(out_ref.dtype)
                    for by in range(n_cd)
                ]
            )
            first += width


def contract_later(n_cd, t2s, ints, parts):
    blocks, where = t2s
    rows, cols = blocks[0].shape[-2:]
    width = ints[0].shape[2] * LATER + sum(p.shape[2] for p in parts[::n_cd])
    out = jax.ShapeDtypeStruct((parts[0].shape[1], width), jnp.bfloat16)
    return pl.pallas_call(
        functools.partial(later_kernel, n_cd, len(blocks), where),
        out_shape=[out, out],
        in_specs=[VMEM] * (len(blocks) + 2 + len(parts)),
        out_specs=[VMEM] * 2,
        scratch_shapes=[pltpu.VMEM((4 * len(where[0]), rows, cols), jnp.bfloat16)],
        compiler_params=params(),
        cost_estimate=CHEAP,
        name="contract_later",
    )(*blocks, *ints, *parts)


def finish_kernel(side, place, sums_ref, *rest):
    out_ref, both, made, sems = rest[-4:]
    blocks, rows, cols = made.shape
    left = lax.broadcasted_iota(jnp.int32, (rows, LANES), 1) < LANES // 2

    def copy_out(i):
        block = 2 * i + (lax.axis_index("core") ^ side)
        return pltpu.make_async_copy(made.at[i], out_ref.at[block], sems.at[i])

    for i in range(blocks):
        both[0] = sums_ref[i * rows : (i + 1) * rows]
        both[1] = half_turned(both[0])
        for q in range(cols // LANES):
            made[i, :, q * LANES : (q + 1) * LANES] = pick_pair(
                both, place[2 * q], place[2 * q + 1], left
            )
        copy_out(i).start()
    for i in range(blocks):
        copy_out(i).wait()


def finish(side, place, sums, rows, out=None):
    blocks, cols = sums.shape[0] // rows, sums.shape[1]
    before = [] if out is None else [out]
    return pl.pallas_call(
        functools.partial(finish_kernel, side),
        out_shape=jax.ShapeDtypeStruct((2 * blocks, rows, cols), jnp.bfloat16),
        in_specs=[SMEM, VMEM] + [ANY] * len(before),
        out_specs=ANY,
        scratch_shapes=[
            pltpu.VMEM((2, rows, cols), jnp.bfloat16),
            pltpu.VMEM((blocks, rows, cols), jnp.bfloat16),
            pltpu.SemaphoreType.DMA((blocks,)),
        ],
        input_output_aliases={2: 0} if before else {},
        compiler_params=params(),
        cost_estimate=CHEAP,
        name="finish",
    )(place, sums, *before)


SWAP = [(0, 1), (1, 0)]


def further(x, by):
    n_cd = lax.axis_size("cd")
    return lax.ppermute(x, "cd", [(i, (i + by) % n_cd) for i in range(n_cd)])


def to_plane(x, d):
    n_cd = lax.axis_size("cd")
    z_len = 2 * lax.axis_size("zh")
    rest = z_len // n_cd
    pairs = []
    for z in range(z_len):
        group, i = divmod(z, rest)
        for y in range(n_cd):
            pairs.append((z * n_cd + y, ((y * rest + i) ^ (2 * d)) * n_cd + group))
    return lax.ppermute(x, ("zh", "zl", "cd"), pairs)


def per_device(t2_amps, integrals, ab_sym, cd_sym):
    zh, n_cd = lax.axis_size("zh"), lax.axis_size("cd")
    own, own_later = sort_amps(t2_amps, cd_sym)

    def over(x, axis):
        return lax.ppermute(x, axis, SWAP)

    def along_zh(x):
        return [lax.ppermute(x, "zh", [(i, i ^ d) for i in range(zh)]) for d in range(1, zh)]

    quarters = (
        tuple((d, None) for d in range(zh)),
        ((2 * zh, None),) + tuple((2 * zh + 1, d - 1) for d in range(1, zh)),
        tuple((zh + d, None) for d in range(zh)),
        ((2 * zh + 1, zh - 1),) + tuple((2 * zh + 1 + d, None) for d in range(1, zh)),
    )

    def first_step(x):
        return x, along_zh(x), over(x, "zl"), over(x, "x")

    def next_steps(step, earlier):
        x, others, up, across = step
        turned = join([y[None] for y in [*others, up]], [across, *earlier])
        across_turned = over(turned, "x")
        ups = [up] + [over(after(y, turned), "zl") for y in others]
        fars = [over(y, "x") for y in ups[1:]]
        return turned, ([x, *others, *ups, across, across_turned, *fars], quarters)

    _, *ints_later = sort_ints(integrals, ab_sym, NSYM - LATER, LATER_SPLIT, 60 * 2**20, cd_sym)
    later = [[x] for x in ints_later]
    later[0] += [further(later[0][0], by) for by in range(1, n_cd)]
    place, ints = sort_ints(integrals, ab_sym, 0, SPLIT, VMEM_LIMIT, own)
    turned, t2s = next_steps(first_step(own), [ints, *later[0][1:]])
    ints = after(ints, turned)
    sib_ints = over(ints, "core")
    later[1][0] = after(later[1][0], turned)
    later[1] += [further(later[1][0], by) for by in range(1, n_cd)]
    blocks = [to_plane(after(own_later, turned), 0)]
    blocks += [to_plane(after(own_later, sib_ints), d) for d in range(1, zh)]
    near = merge(blocks, [t2s[0][2 * zh + 1]])
    made = contract(n_cd, t2s, ints, sib_ints, 0, [near, *later[1][1:]])
    parts = [made[0]] + [further(made[by], by) for by in range(1, n_cd)]
    up = over(near, "zl")
    t2s = (near, over(near, "x"), up, over(up, "x"))
    t2s = t2s, tuple(tuple((k, -1) for d in range(zh)) for k in range(4))
    ints_later = join([x[by] for by in range(n_cd) for x in later], made[:1])
    ints_later = (ints_later, over(ints_later, "core"))
    sums, sib_sums = contract_later(n_cd, t2s, ints_later, parts)
    sib_sums = lax.ppermute(sib_sums, "core", SWAP)
    rows = t2_amps.shape[0]
    out = finish(0, place, sums, rows)
    out = finish(1, place, sib_sums, rows, out)
    return out.reshape(-1, out.shape[2])


def solution(mesh):
    n_blk, n_cd = mesh.devices.shape
    blk = ("zh", "zl", "x", "core")
    parted = Mesh(mesh.devices.reshape(n_blk // 8, 2, 2, 2, n_cd), blk + ("cd",))
    in_specs = (P(blk, "cd"), P(blk, None, "cd"), P(blk), P("cd"))
    return jax.shard_map(
        per_device, mesh=parted, in_specs=in_specs, out_specs=P("cd", blk), check_vma=False
    )
```

```python
import functools

import jax
import jax.numpy as jnp
from jax import lax
from jax.experimental import pallas as pl
from jax.experimental.pallas import tpu as pltpu
from jax.sharding import Mesh, PartitionSpec as P

NSYM = 8
LATER = 4
FIRST_SENT = 2
LANES = 128
VMEM_LIMIT = 20 * 2**20

ANY = pl.BlockSpec(memory_space=pl.ANY)
SMEM = pl.BlockSpec(memory_space=pltpu.SMEM)
VMEM = pl.BlockSpec(memory_space=pltpu.VMEM)

CHEAP = pl.CostEstimate(flops=1000, bytes_accessed=1000, transcendentals=0)


def params(limit=VMEM_LIMIT):
    return pltpu.CompilerParams(vmem_limit_bytes=limit)


def half_turned(x):
    half = LANES // 2
    return jnp.concatenate([x[:, half:], x[:, :half]], axis=1)


def rank_tiles(sym_ref, count_ref, order_ref, place_ref, tiles):
    for s in range(NSYM):
        count_ref[s] = s * (tiles // NSYM)

    def step(i, _):
        s = sym_ref[i]
        p = count_ref[s]
        count_ref[s] = p + 1
        order_ref[p] = i
        if place_ref is not None:
            place_ref[i] = p
        return 0

    lax.fori_loop(0, tiles, step, 0)


def pick_pair(both, a, b, left):
    columns = both.shape[2] // LANES
    a_col = lax.shift_right_logical(a, 1)
    b_col = lax.rem(lax.shift_right_logical(b + 1, 1) + columns - 1, columns)
    xa = both[a & 1, :, pl.ds(pl.multiple_of(a_col * LANES, LANES), LANES)]
    xb = both[(b & 1) ^ 1, :, pl.ds(pl.multiple_of(b_col * LANES, LANES), LANES)]
    return jnp.where(left, xa, xb)


def sort_amps_kernel(cd_ref, t2_ref, *rest):
    chunks, (both, count, order, sem) = rest[:-4], rest[-4:]
    rows = t2_ref.shape[0]
    load = pltpu.make_async_copy(t2_ref, both.at[0], sem)
    load.start()
    rank_tiles(cd_ref, count, order, None, cd_ref.shape[0])
    load.wait()
    both[1] = half_turned(both[0])
    left = lax.broadcasted_iota(jnp.int32, (rows, LANES), 1) < LANES // 2
    q = 0
    for chunk in chunks:
        for off in range(chunk.shape[1] // LANES):
            pair = pick_pair(both, order[2 * q], order[2 * q + 1], left)
            chunk[:, off * LANES : (off + 1) * LANES] = pair
            q += 1


def sort_amps(t2, cd_sym):
    rows, cols = t2.shape
    return pl.pallas_call(
        sort_amps_kernel,
        out_shape=[
            jax.ShapeDtypeStruct((rows, cols // NSYM * m), t2.dtype) for m in (NSYM - LATER, LATER)
        ],
        in_specs=[SMEM, ANY],
        out_specs=[VMEM] * 2,
        scratch_shapes=[
            pltpu.VMEM((2, rows, cols), t2.dtype),
            pltpu.SMEM((NSYM,), jnp.int32),
            pltpu.SMEM((cd_sym.shape[0],), jnp.int32),
            pltpu.SemaphoreType.DMA,
        ],
        compiler_params=params(),
        cost_estimate=CHEAP,
        name="sort_amps",
    )(cd_sym, t2)


def sort_ints_kernel(syms, ab_ref, ints_ref, _, place, *rest):
    outs, (rows, count, order, sems) = rest[:-4], rest[-4:]
    tiles, tile = ab_ref.shape[0], rows.shape[1]
    rank_tiles(ab_ref, count, order, place, tiles)
    per_sym = tiles // NSYM
    copies = []
    for sym in [sym for part in syms for sym in part]:
        for m in range(per_sym):
            p = len(copies)
            tile_ref = ints_ref.at[order[sym * per_sym + m]]
            copies.append(pltpu.make_async_copy(tile_ref, rows.at[p], sems.at[p]))
            copies[-1].start()
    for copy in copies:
        copy.wait()
    p = 0
    for out_ref in outs:
        for s in range(out_ref.shape[0]):
            out_ref[s] = rows[p : p + per_sym].reshape(per_sym * tile, rows.shape[2]).T
            p += per_sym


def sort_ints(integrals, ab_sym, syms, limit, earlier):
    tiles, tile, packed = integrals.shape
    per_sym = tiles // NSYM
    used = sum(len(part) for part in syms) * per_sym
    return pl.pallas_call(
        functools.partial(sort_ints_kernel, syms),
        out_shape=[jax.ShapeDtypeStruct((tiles,), jnp.int32)]
        + [
            jax.ShapeDtypeStruct((len(part), packed, per_sym * tile), integrals.dtype)
            for part in syms
        ],
        in_specs=[SMEM, ANY, ANY],
        out_specs=[SMEM] + [VMEM] * len(syms),
        scratch_shapes=[
            pltpu.VMEM((used, tile, packed), integrals.dtype),
            pltpu.SMEM((NSYM,), jnp.int32),
            pltpu.SMEM((tiles,), jnp.int32),
            pltpu.SemaphoreType.DMA((used,)),
        ],
        compiler_params=params(limit),
        cost_estimate=CHEAP,
        name="sort_ints",
    )(ab_sym, integrals, earlier)


def merge_kernel(n, *refs):
    blocks, out_ref = refs[:n], refs[-1]
    me = lax.axis_index("zh")
    for d, block in enumerate(blocks):
        out_ref[me ^ d] = block[...]


def merge(blocks, earlier):
    return pl.pallas_call(
        functools.partial(merge_kernel, len(blocks)),
        out_shape=jax.ShapeDtypeStruct((len(blocks),) + blocks[0].shape, blocks[0].dtype),
        in_specs=[VMEM] * len(blocks) + [ANY] * len(earlier),
        out_specs=VMEM,
        compiler_params=params(),
        cost_estimate=CHEAP,
        name="merge",
    )(*blocks, *earlier)


def nothing(*refs):
    pass


def after(x, *earlier):
    n = len(earlier)
    return pl.pallas_call(
        nothing,
        out_shape=jax.ShapeDtypeStruct(x.shape, x.dtype),
        in_specs=[ANY] * (n + 1),
        out_specs=ANY,
        input_output_aliases={n: 0},
        compiler_params=params(),
        cost_estimate=CHEAP,
        name="after",
    )(*earlier, x)


def lay_out(lhs, refs, where, place):
    h, z, x = lax.axis_index("zh"), lax.axis_index("zl"), lax.axis_index("x")
    for k, (by_difference, quarter) in enumerate(where):
        for i, (array, entry) in enumerate(quarter):
            slot = 4 * (h ^ i if by_difference else i) + 2 * (z ^ (k // 2)) + (x ^ (k % 2))
            ref = refs[array]
            lhs[place(slot)] = ref[...] if entry is None else ref[entry]


def contract_kernel(n_cd, first_sym, n_blocks, where, *refs):
    blocks, (own_ref, sib_ref) = refs[:n_blocks], refs[n_blocks : n_blocks + 2]
    outs, lhs = refs[-n_cd - 1 : -1], refs[-1]
    slots, rows, cols = lhs.shape
    packed, width = own_ref.shape[1:]
    first = lax.axis_index("cd") * (slots // n_cd)
    lay_out(lhs, blocks, where, lambda n: lax.rem(n + slots - first, slots))
    t2 = lhs[...].reshape(slots * rows, cols)
    group_rows = t2.shape[0] // n_cd
    for side, ints in enumerate((own_ref, sib_ref)):
        for s in range(cols // packed):
            part = jnp.dot(
                t2[:, s * packed : (s + 1) * packed],
                ints[first_sym + s],
                preferred_element_type=jnp.float32,
            ).astype(outs[0].dtype)
            for by in range(n_cd):
                outs[by][side, :, s * width : (s + 1) * width] = part[
                    by * group_rows : (by + 1) * group_rows
                ]


def contract(n_cd, t2s, ints, sib_ints, first_sym, earlier):
    blocks, where = t2s
    rows, cols = blocks[0].shape[-2:]
    slots = 4 * len(where[0][1])
    packed, width = ints.shape[1:]
    out = (2, slots * rows // n_cd, cols // packed * width)
    return pl.pallas_call(
        functools.partial(contract_kernel, n_cd, first_sym, len(blocks), where),
        out_shape=[jax.ShapeDtypeStruct(out, jnp.bfloat16)] * n_cd,
        in_specs=[VMEM] * (len(blocks) + 2) + [ANY] * len(earlier),
        out_specs=[VMEM] * n_cd,
        scratch_shapes=[pltpu.VMEM((slots, rows, cols), jnp.bfloat16)],
        compiler_params=params(),
        cost_estimate=CHEAP,
        name="contract",
    )(*blocks, ints, sib_ints, *earlier)


def total(parts):
    value = parts[0].astype(jnp.float32)
    for part in parts[1:]:
        value += part.astype(jnp.float32)
    return value.astype(jnp.bfloat16)


def join_kernel(n, *refs):
    out_ref, first = refs[-1], 0
    for ref in refs[:n]:
        out_ref[first : first + ref.shape[0]] = ref[...]
        first += ref.shape[0]


def join(arrays, earlier):
    n = len(arrays)
    out = (sum(x.shape[0] for x in arrays), *arrays[0].shape[1:])
    return pl.pallas_call(
        functools.partial(join_kernel, n),
        out_shape=jax.ShapeDtypeStruct(out, arrays[0].dtype),
        in_specs=[VMEM] * n + [ANY] * len(earlier),
        out_specs=VMEM,
        compiler_params=params(),
        cost_estimate=CHEAP,
        name="join",
    )(*arrays, *earlier)


def later_kernel(n_cd, n_blocks, where, *refs):
    blocks, ints, parts = refs[:n_blocks], refs[n_blocks : n_blocks + 2], refs[n_blocks + 2 : -3]
    own_out, sib_out, lhs = refs[-3:]
    slots, rows, cols = lhs.shape
    packed, width = ints[0].shape[1:]
    per_group, me = slots // n_cd, lax.axis_index("cd")

    def place(n):
        group = lax.div(n, per_group)
        return lax.rem(me + n_cd - group, n_cd) * per_group + (n - group * per_group)

    lay_out(lhs, blocks, where, place)
    t2 = lhs[...].reshape(n_cd, per_group * rows, cols)
    for side, out_ref in enumerate((own_out, sib_out)):
        first = 0
        for c in range(0, len(parts), n_cd):
            value = total([part[side] for part in parts[c : c + n_cd]])
            out_ref[:, first : first + value.shape[1]] = value
            first += value.shape[1]
        for s in range(LATER):
            out_ref[:, first : first + width] = total(
                [
                    jnp.dot(
                        t2[by, :, s * packed : (s + 1) * packed],
                        ints[side][by * LATER + s],
                        preferred_element_type=jnp.float32,
                    ).astype(out_ref.dtype)
                    for by in range(n_cd)
                ]
            )
            first += width


def contract_later(n_cd, t2s, ints, parts):
    blocks, where = t2s
    rows, cols = blocks[0].shape[-2:]
    width = ints[0].shape[2] * LATER + sum(p.shape[2] for p in parts[::n_cd])
    out = jax.ShapeDtypeStruct((parts[0].shape[1], width), jnp.bfloat16)
    return pl.pallas_call(
        functools.partial(later_kernel, n_cd, len(blocks), where),
        out_shape=[out, out],
        in_specs=[VMEM] * (len(blocks) + 2 + len(parts)),
        out_specs=[VMEM] * 2,
        scratch_shapes=[pltpu.VMEM((4 * len(where[0][1]), rows, cols), jnp.bfloat16)],
        compiler_params=params(),
        cost_estimate=CHEAP,
        name="contract_later",
    )(*blocks, *ints, *parts)


def finish_kernel(side, place, sums_ref, *rest):
    out_ref, both, made, sems = rest[-4:]
    blocks, rows, cols = made.shape
    left = lax.broadcasted_iota(jnp.int32, (rows, LANES), 1) < LANES // 2

    def copy_out(i):
        block = 2 * i + (lax.axis_index("core") ^ side)
        return pltpu.make_async_copy(made.at[i], out_ref.at[block], sems.at[i])

    for i in range(blocks):
        both[0] = sums_ref[i * rows : (i + 1) * rows]
        both[1] = half_turned(both[0])
        for q in range(cols // LANES):
            made[i, :, q * LANES : (q + 1) * LANES] = pick_pair(
                both, place[2 * q], place[2 * q + 1], left
            )
        copy_out(i).start()
    for i in range(blocks):
        copy_out(i).wait()


def finish(side, place, sums, rows, out=None):
    blocks, cols = sums.shape[0] // rows, sums.shape[1]
    before = [] if out is None else [out]
    return pl.pallas_call(
        functools.partial(finish_kernel, side),
        out_shape=jax.ShapeDtypeStruct((2 * blocks, rows, cols), jnp.bfloat16),
        in_specs=[SMEM, VMEM] + [ANY] * len(before),
        out_specs=ANY,
        scratch_shapes=[
            pltpu.VMEM((2, rows, cols), jnp.bfloat16),
            pltpu.VMEM((blocks, rows, cols), jnp.bfloat16),
            pltpu.SemaphoreType.DMA((blocks,)),
        ],
        input_output_aliases={2: 0} if before else {},
        compiler_params=params(),
        cost_estimate=CHEAP,
        name="finish",
    )(place, sums, *before)


SWAP = [(0, 1), (1, 0)]


def further(x, by):
    n_cd = lax.axis_size("cd")
    return lax.ppermute(x, "cd", [(i, (i + by) % n_cd) for i in range(n_cd)])


def to_plane(x, d):
    n_cd = lax.axis_size("cd")
    z_len = 2 * lax.axis_size("zh")
    rest = z_len // n_cd
    pairs = []
    for z in range(z_len):
        group, i = divmod(z, rest)
        for y in range(n_cd):
            pairs.append((z * n_cd + y, ((y * rest + i) ^ (2 * d)) * n_cd + group))
    return lax.ppermute(x, ("zh", "zl", "cd"), pairs)


def per_device(t2_amps, integrals, ab_sym, cd_sym):
    zh, n_cd = lax.axis_size("zh"), lax.axis_size("cd")
    own, own_later = sort_amps(t2_amps, cd_sym)

    def over(x, axis):
        return lax.ppermute(x, axis, SWAP)

    def along_zh(x):
        return [lax.ppermute(x, "zh", [(i, i ^ d) for i in range(zh)]) for d in range(1, zh)]

    first_later = tuple(range(NSYM - LATER, NSYM - LATER + FIRST_SENT))
    _, ints_later = sort_ints(integrals, ab_sym, (first_later,), 60 * 2**20, cd_sym)
    later = [[ints_later] + [further(ints_later, by) for by in range(1, n_cd)]]
    syms = (tuple(range(NSYM - LATER)), tuple(range(NSYM - LATER + FIRST_SENT, NSYM)))
    place, ints, ints_later = sort_ints(integrals, ab_sym, syms, VMEM_LIMIT, own)
    x_o, block_l = over(own, "x"), over(own, "zl")
    blocks_h = along_zh(own)
    x_l = over(block_l, "x")
    blocks_h[0] = after(blocks_h[0], *later[0][1:], ints, x_o, x_l, *blocks_h[1:])
    fence = blocks_h[0]
    x_h = [over(after(y, fence) if i else y, "x") for i, y in enumerate(blocks_h)]
    blocks_hl = [over(y, "zl") for y in blocks_h]
    ints = after(ints, fence)
    sib_ints = over(ints, "core")
    ints_later = after(ints_later, fence)
    later.append([ints_later] + [further(ints_later, by) for by in range(1, n_cd)])
    near = [to_plane(after(own_later, fence), 0)]
    near += [to_plane(after(own_later, sib_ints), d) for d in range(1, zh)]
    near = merge(near, x_h)
    x_hl = [over(y, "x") for y in blocks_hl]
    where = tuple(
        (True, tuple((zh * k + d, None) for d in range(zh)))
        for k in range(4)
    )
    blocks = [own, *blocks_h, x_o, *x_h, block_l, *blocks_hl, x_l, *x_hl]
    made = contract(n_cd, (blocks, where), ints, sib_ints, 0, [near, *later[1][1:]])
    parts = [made[0]] + [further(made[by], by) for by in range(1, n_cd)]
    up, across = over(near, "zl"), over(near, "x")
    half = zh // 2
    blocks = [near, across, up, over(up[:half], "x"), over(across[half:], "zl")]
    where = tuple((False, tuple((k, i) for i in range(zh))) for k in range(3))
    where += ((False, tuple((3 + i // half, i % half) for i in range(zh))),)
    t2s = blocks, where
    ints_later = join([x[by] for by in range(n_cd) for x in later], made[:1])
    ints_later = (ints_later, over(ints_later, "core"))
    sums, sib_sums = contract_later(n_cd, t2s, ints_later, parts)
    sib_sums = lax.ppermute(sib_sums, "core", SWAP)
    rows = t2_amps.shape[0]
    out = finish(0, place, sums, rows)
    out = finish(1, place, sib_sums, rows, out)
    return out.reshape(-1, out.shape[2])


def solution(mesh):
    n_blk, n_cd = mesh.devices.shape
    blk = ("zh", "zl", "x", "core")
    parted = Mesh(mesh.devices.reshape(n_blk // 8, 2, 2, 2, n_cd), blk + ("cd",))
    in_specs = (P(blk, "cd"), P(blk, None, "cd"), P(blk), P("cd"))
    return jax.shard_map(
        per_device, mesh=parted, in_specs=in_specs, out_specs=P("cd", blk), check_vma=False
    )
```

```python
import functools

import jax
import jax.numpy as jnp
from jax import lax
from jax.experimental import pallas as pl
from jax.experimental.pallas import tpu as pltpu
from jax.sharding import Mesh, PartitionSpec as P

NSYM = 8
LATER = 4
FIRST_SENT = 2
LANES = 128
VMEM_LIMIT = 20 * 2**20

ANY = pl.BlockSpec(memory_space=pl.ANY)
SMEM = pl.BlockSpec(memory_space=pltpu.SMEM)
VMEM = pl.BlockSpec(memory_space=pltpu.VMEM)

CHEAP = pl.CostEstimate(flops=1000, bytes_accessed=1000, transcendentals=0)


def params(limit=VMEM_LIMIT):
    return pltpu.CompilerParams(vmem_limit_bytes=limit)


def half_turned(x):
    half = LANES // 2
    return jnp.concatenate([x[:, half:], x[:, :half]], axis=1)


def rank_tiles(sym_ref, count_ref, order_ref, place_ref, tiles):
    for s in range(NSYM):
        count_ref[s] = s * (tiles // NSYM)

    def step(i, _):
        s = sym_ref[i]
        p = count_ref[s]
        count_ref[s] = p + 1
        order_ref[p] = i
        if place_ref is not None:
            place_ref[i] = p
        return 0

    lax.fori_loop(0, tiles, step, 0)


def pick_pair(both, a, b, left):
    columns = both.shape[2] // LANES
    a_col = lax.shift_right_logical(a, 1)
    b_col = lax.rem(lax.shift_right_logical(b + 1, 1) + columns - 1, columns)
    xa = both[a & 1, :, pl.ds(pl.multiple_of(a_col * LANES, LANES), LANES)]
    xb = both[(b & 1) ^ 1, :, pl.ds(pl.multiple_of(b_col * LANES, LANES), LANES)]
    return jnp.where(left, xa, xb)


def sort_amps_kernel(cd_ref, t2_ref, *rest):
    chunks, (both, count, order, sem) = rest[:-4], rest[-4:]
    rows = t2_ref.shape[0]
    load = pltpu.make_async_copy(t2_ref, both.at[0], sem)
    load.start()
    rank_tiles(cd_ref, count, order, None, cd_ref.shape[0])
    load.wait()
    both[1] = half_turned(both[0])
    left = lax.broadcasted_iota(jnp.int32, (rows, LANES), 1) < LANES // 2
    q = 0
    for chunk in chunks:
        for off in range(chunk.shape[1] // LANES):
            pair = pick_pair(both, order[2 * q], order[2 * q + 1], left)
            chunk[:, off * LANES : (off + 1) * LANES] = pair
            q += 1


def sort_amps(t2, cd_sym):
    rows, cols = t2.shape
    return pl.pallas_call(
        sort_amps_kernel,
        out_shape=[
            jax.ShapeDtypeStruct((rows, cols // NSYM * m), t2.dtype) for m in (NSYM - LATER, LATER)
        ],
        in_specs=[SMEM, ANY],
        out_specs=[VMEM] * 2,
        scratch_shapes=[
            pltpu.VMEM((2, rows, cols), t2.dtype),
            pltpu.SMEM((NSYM,), jnp.int32),
            pltpu.SMEM((cd_sym.shape[0],), jnp.int32),
            pltpu.SemaphoreType.DMA,
        ],
        compiler_params=params(60 * 2**20),
        cost_estimate=CHEAP,
        name="sort_amps",
    )(cd_sym, t2)


def sort_ints_kernel(syms, ab_ref, ints_ref, _, place, *rest):
    outs, (rows, count, order, sems) = rest[:-4], rest[-4:]
    tiles, tile = ab_ref.shape[0], rows.shape[1]
    rank_tiles(ab_ref, count, order, place, tiles)
    per_sym = tiles // NSYM
    copies = []
    for sym in [sym for part in syms for sym in part]:
        for m in range(per_sym):
            p = len(copies)
            tile_ref = ints_ref.at[order[sym * per_sym + m]]
            copies.append(pltpu.make_async_copy(tile_ref, rows.at[p], sems.at[p]))
            copies[-1].start()
    for copy in copies:
        copy.wait()
    p = 0
    for out_ref in outs:
        for s in range(out_ref.shape[0]):
            out_ref[s] = rows[p : p + per_sym].reshape(per_sym * tile, rows.shape[2]).T
            p += per_sym


def sort_ints(integrals, ab_sym, syms, limit, earlier):
    tiles, tile, packed = integrals.shape
    per_sym = tiles // NSYM
    used = sum(len(part) for part in syms) * per_sym
    return pl.pallas_call(
        functools.partial(sort_ints_kernel, syms),
        out_shape=[jax.ShapeDtypeStruct((tiles,), jnp.int32)]
        + [
            jax.ShapeDtypeStruct((len(part), packed, per_sym * tile), integrals.dtype)
            for part in syms
        ],
        in_specs=[SMEM, ANY, ANY],
        out_specs=[SMEM] + [VMEM] * len(syms),
        scratch_shapes=[
            pltpu.VMEM((used, tile, packed), integrals.dtype),
            pltpu.SMEM((NSYM,), jnp.int32),
            pltpu.SMEM((tiles,), jnp.int32),
            pltpu.SemaphoreType.DMA((used,)),
        ],
        compiler_params=params(limit),
        cost_estimate=CHEAP,
        name="sort_ints",
    )(ab_sym, integrals, earlier)


def merge_kernel(n, *refs):
    blocks, out_ref = refs[:n], refs[-1]
    me = lax.axis_index("zh")
    for d, block in enumerate(blocks):
        out_ref[me ^ d] = block[...]


def merge(blocks, earlier):
    return pl.pallas_call(
        functools.partial(merge_kernel, len(blocks)),
        out_shape=jax.ShapeDtypeStruct((len(blocks),) + blocks[0].shape, blocks[0].dtype),
        in_specs=[VMEM] * len(blocks) + [ANY] * len(earlier),
        out_specs=VMEM,
        compiler_params=params(),
        cost_estimate=CHEAP,
        name="merge",
    )(*blocks, *earlier)


def nothing(*refs):
    pass


def after(x, *earlier):
    n = len(earlier)
    return pl.pallas_call(
        nothing,
        out_shape=jax.ShapeDtypeStruct(x.shape, x.dtype),
        in_specs=[ANY] * (n + 1),
        out_specs=ANY,
        input_output_aliases={n: 0},
        compiler_params=params(),
        cost_estimate=CHEAP,
        name="after",
    )(*earlier, x)


def lay_out(lhs, refs, where, place):
    h, z, x = lax.axis_index("zh"), lax.axis_index("zl"), lax.axis_index("x")
    for k, (by_difference, quarter) in enumerate(where):
        for i, (array, entry) in enumerate(quarter):
            slot = 4 * (h ^ i if by_difference else i) + 2 * (z ^ (k // 2)) + (x ^ (k % 2))
            ref = refs[array]
            lhs[place(slot)] = ref[...] if entry is None else ref[entry]


def contract_kernel(n_cd, first_sym, n_blocks, where, *refs):
    blocks, (own_ref, sib_ref) = refs[:n_blocks], refs[n_blocks : n_blocks + 2]
    outs, lhs = refs[-n_cd - 1 : -1], refs[-1]
    slots, rows, cols = lhs.shape
    packed, width = own_ref.shape[1:]
    first = lax.axis_index("cd") * (slots // n_cd)
    lay_out(lhs, blocks, where, lambda n: lax.rem(n + slots - first, slots))
    t2 = lhs[...].reshape(slots * rows, cols)
    group_rows = t2.shape[0] // n_cd
    for side, ints in enumerate((own_ref, sib_ref)):
        for s in range(cols // packed):
            part = jnp.dot(
                t2[:, s * packed : (s + 1) * packed],
                ints[first_sym + s],
                preferred_element_type=jnp.float32,
            ).astype(outs[0].dtype)
            for by in range(n_cd):
                outs[by][side, :, s * width : (s + 1) * width] = part[
                    by * group_rows : (by + 1) * group_rows
                ]


def contract(n_cd, t2s, ints, sib_ints, first_sym, earlier):
    blocks, where = t2s
    rows, cols = blocks[0].shape[-2:]
    slots = 4 * len(where[0][1])
    packed, width = ints.shape[1:]
    out = (2, slots * rows // n_cd, cols // packed * width)
    return pl.pallas_call(
        functools.partial(contract_kernel, n_cd, first_sym, len(blocks), where),
        out_shape=[jax.ShapeDtypeStruct(out, jnp.bfloat16)] * n_cd,
        in_specs=[VMEM] * (len(blocks) + 2) + [ANY] * len(earlier),
        out_specs=[VMEM] * n_cd,
        scratch_shapes=[pltpu.VMEM((slots, rows, cols), jnp.bfloat16)],
        compiler_params=params(),
        cost_estimate=CHEAP,
        name="contract",
    )(*blocks, ints, sib_ints, *earlier)


def total(parts):
    value = parts[0].astype(jnp.float32)
    for part in parts[1:]:
        value += part.astype(jnp.float32)
    return value.astype(jnp.bfloat16)


def join_kernel(n, *refs):
    out_ref, first = refs[-1], 0
    for ref in refs[:n]:
        out_ref[first : first + ref.shape[0]] = ref[...]
        first += ref.shape[0]


def join(arrays, earlier):
    n = len(arrays)
    out = (sum(x.shape[0] for x in arrays), *arrays[0].shape[1:])
    return pl.pallas_call(
        functools.partial(join_kernel, n),
        out_shape=jax.ShapeDtypeStruct(out, arrays[0].dtype),
        in_specs=[VMEM] * n + [ANY] * len(earlier),
        out_specs=VMEM,
        compiler_params=params(),
        cost_estimate=CHEAP,
        name="join",
    )(*arrays, *earlier)


def later_kernel(n_cd, n_blocks, where, *refs):
    blocks, ints, parts = refs[:n_blocks], refs[n_blocks : n_blocks + 2], refs[n_blocks + 2 : -3]
    own_out, sib_out, lhs = refs[-3:]
    slots, rows, cols = lhs.shape
    packed, width = ints[0].shape[1:]
    per_group, me = slots // n_cd, lax.axis_index("cd")

    def place(n):
        group = lax.div(n, per_group)
        return lax.rem(me + n_cd - group, n_cd) * per_group + (n - group * per_group)

    lay_out(lhs, blocks, where, place)
    t2 = lhs[...].reshape(n_cd, per_group * rows, cols)
    for side, out_ref in enumerate((own_out, sib_out)):
        first = 0
        for c in range(0, len(parts), n_cd):
            value = total([part[side] for part in parts[c : c + n_cd]])
            out_ref[:, first : first + value.shape[1]] = value
            first += value.shape[1]
        for s in range(LATER):
            out_ref[:, first : first + width] = total(
                [
                    jnp.dot(
                        t2[by, :, s * packed : (s + 1) * packed],
                        ints[side][by * LATER + s],
                        preferred_element_type=jnp.float32,
                    ).astype(out_ref.dtype)
                    for by in range(n_cd)
                ]
            )
            first += width


def contract_later(n_cd, t2s, ints, parts):
    blocks, where = t2s
    rows, cols = blocks[0].shape[-2:]
    width = ints[0].shape[2] * LATER + sum(p.shape[2] for p in parts[::n_cd])
    out = jax.ShapeDtypeStruct((parts[0].shape[1], width), jnp.bfloat16)
    return pl.pallas_call(
        functools.partial(later_kernel, n_cd, len(blocks), where),
        out_shape=[out, out],
        in_specs=[VMEM] * (len(blocks) + 2 + len(parts)),
        out_specs=[VMEM] * 2,
        scratch_shapes=[pltpu.VMEM((4 * len(where[0][1]), rows, cols), jnp.bfloat16)],
        compiler_params=params(),
        cost_estimate=CHEAP,
        name="contract_later",
    )(*blocks, *ints, *parts)


def finish_kernel(side, place, sums_ref, *rest):
    out_ref, both, made, sems = rest[-4:]
    blocks, rows, cols = made.shape
    left = lax.broadcasted_iota(jnp.int32, (rows, LANES), 1) < LANES // 2

    def copy_out(i):
        block = 2 * i + (lax.axis_index("core") ^ side)
        return pltpu.make_async_copy(made.at[i], out_ref.at[block], sems.at[i])

    for i in range(blocks):
        both[0] = sums_ref[i * rows : (i + 1) * rows]
        both[1] = half_turned(both[0])
        for q in range(cols // LANES):
            made[i, :, q * LANES : (q + 1) * LANES] = pick_pair(
                both, place[2 * q], place[2 * q + 1], left
            )
        copy_out(i).start()
    for i in range(blocks):
        copy_out(i).wait()


def finish(side, place, sums, rows, out=None):
    blocks, cols = sums.shape[0] // rows, sums.shape[1]
    before = [] if out is None else [out]
    return pl.pallas_call(
        functools.partial(finish_kernel, side),
        out_shape=jax.ShapeDtypeStruct((2 * blocks, rows, cols), jnp.bfloat16),
        in_specs=[SMEM, VMEM] + [ANY] * len(before),
        out_specs=ANY,
        scratch_shapes=[
            pltpu.VMEM((2, rows, cols), jnp.bfloat16),
            pltpu.VMEM((blocks, rows, cols), jnp.bfloat16),
            pltpu.SemaphoreType.DMA((blocks,)),
        ],
        input_output_aliases={2: 0} if before else {},
        compiler_params=params(),
        cost_estimate=CHEAP,
        name="finish",
    )(place, sums, *before)


SWAP = [(0, 1), (1, 0)]


def further(x, by):
    n_cd = lax.axis_size("cd")
    return lax.ppermute(x, "cd", [(i, (i + by) % n_cd) for i in range(n_cd)])


def to_plane(x, d):
    n_cd = lax.axis_size("cd")
    z_len = 2 * lax.axis_size("zh")
    rest = z_len // n_cd
    pairs = []
    for z in range(z_len):
        group, i = divmod(z, rest)
        for y in range(n_cd):
            pairs.append((z * n_cd + y, ((y * rest + i) ^ (2 * d)) * n_cd + group))
    return lax.ppermute(x, ("zh", "zl", "cd"), pairs)


def per_device(t2_amps, integrals, ab_sym, cd_sym):
    zh, n_cd = lax.axis_size("zh"), lax.axis_size("cd")
    own, own_later = sort_amps(t2_amps, cd_sym)

    def over(x, axis):
        return lax.ppermute(x, axis, SWAP)

    def along_zh(x):
        return [lax.ppermute(x, "zh", [(i, i ^ d) for i in range(zh)]) for d in range(1, zh)]

    first_later = tuple(range(NSYM - LATER, NSYM - LATER + FIRST_SENT))
    _, ints_later = sort_ints(integrals, ab_sym, (first_later,), 60 * 2**20, cd_sym)
    later = [[ints_later] + [further(ints_later, by) for by in range(1, n_cd)]]
    syms = (tuple(range(NSYM - LATER)), tuple(range(NSYM - LATER + FIRST_SENT, NSYM)))
    place, ints, ints_later = sort_ints(integrals, ab_sym, syms, VMEM_LIMIT, own)
    x_o, block_l = over(own, "x"), over(own, "zl")
    blocks_h = along_zh(own)
    x_l = over(block_l, "x")
    blocks_h[0] = after(blocks_h[0], *later[0][1:], ints, x_o, x_l, *blocks_h[1:])
    fence = blocks_h[0]
    x_h = [over(after(y, fence) if i else y, "x") for i, y in enumerate(blocks_h)]
    blocks_hl = [over(y, "zl") for y in blocks_h]
    ints = after(ints, fence)
    sib_ints = over(ints, "core")
    ints_later = after(ints_later, fence)
    later.append([ints_later] + [further(ints_later, by) for by in range(1, n_cd)])
    near = [to_plane(after(own_later, fence), d) for d in range(1, zh)]
    near = merge([to_plane(after(own_later, sib_ints), 0)] + near, [])
    x_hl = [over(y, "x") for y in blocks_hl]
    where = tuple(
        (True, tuple((zh * k + d, None) for d in range(zh)))
        for k in range(4)
    )
    blocks = [own, *blocks_h, x_o, *x_h, block_l, *blocks_hl, x_l, *x_hl]
    made = contract(n_cd, (blocks, where), ints, sib_ints, 0, [near, *later[1][1:]])
    parts = [made[0]] + [further(made[by], by) for by in range(1, n_cd)]
    up, across = over(near, "zl"), over(near, "x")
    half = zh // 2
    blocks = [near, across, up, over(up[:half], "x"), over(across[half:], "zl")]
    where = tuple((False, tuple((k, i) for i in range(zh))) for k in range(3))
    where += ((False, tuple((3 + i // half, i % half) for i in range(zh))),)
    t2s = blocks, where
    ints_later = join([x[by] for by in range(n_cd) for x in later], made[:1])
    ints_later = (ints_later, over(ints_later, "core"))
    sums, sib_sums = contract_later(n_cd, t2s, ints_later, parts)
    sib_sums = lax.ppermute(sib_sums, "core", SWAP)
    rows = t2_amps.shape[0]
    out = finish(0, place, sums, rows)
    out = finish(1, place, sib_sums, rows, out)
    return out.reshape(-1, out.shape[2])


def solution(mesh):
    n_blk, n_cd = mesh.devices.shape
    blk = ("zh", "zl", "x", "core")
    parted = Mesh(mesh.devices.reshape(n_blk // 8, 2, 2, 2, n_cd), blk + ("cd",))
    in_specs = (P(blk, "cd"), P(blk, None, "cd"), P(blk), P("cd"))
    return jax.shard_map(
        per_device, mesh=parted, in_specs=in_specs, out_specs=P("cd", blk), check_vma=False
    )
```

```python
import functools

import jax
import jax.numpy as jnp
from jax import lax
from jax.experimental import pallas as pl
from jax.experimental.pallas import tpu as pltpu
from jax.sharding import Mesh, PartitionSpec as P

NSYM = 8
LATER = 4
FIRST_SENT = 2
LANES = 128
VMEM_LIMIT = 20 * 2**20

ANY = pl.BlockSpec(memory_space=pl.ANY)
SMEM = pl.BlockSpec(memory_space=pltpu.SMEM)
VMEM = pl.BlockSpec(memory_space=pltpu.VMEM)

CHEAP = pl.CostEstimate(flops=1000, bytes_accessed=1000, transcendentals=0)


def params(limit=VMEM_LIMIT):
    return pltpu.CompilerParams(vmem_limit_bytes=limit)


def half_turned(x):
    half = LANES // 2
    return jnp.concatenate([x[:, half:], x[:, :half]], axis=1)


def rank_tiles(sym_ref, count_ref, order_ref, place_ref, tiles):
    for s in range(NSYM):
        count_ref[s] = s * (tiles // NSYM)

    def step(i, _):
        s = sym_ref[i]
        p = count_ref[s]
        count_ref[s] = p + 1
        order_ref[p] = i
        if place_ref is not None:
            place_ref[i] = p
        return 0

    lax.fori_loop(0, tiles, step, 0)


def pick_pair(both, a, b, left):
    columns = both.shape[2] // LANES
    a_col = lax.shift_right_logical(a, 1)
    b_col = lax.rem(lax.shift_right_logical(b + 1, 1) + columns - 1, columns)
    xa = both[a & 1, :, pl.ds(pl.multiple_of(a_col * LANES, LANES), LANES)]
    xb = both[(b & 1) ^ 1, :, pl.ds(pl.multiple_of(b_col * LANES, LANES), LANES)]
    return jnp.where(left, xa, xb)


def fetch_tiles(ints_ref, rows, order, syms, per_sym, sems):
    copies = []
    for sym in syms:
        for m in range(per_sym):
            p = len(copies)
            tile_ref = ints_ref.at[order[sym * per_sym + m]]
            copies.append(pltpu.make_async_copy(tile_ref, rows.at[p], sems.at[p]))
            copies[-1].start()
    return copies


def turn_tiles(rows, outs, per_sym):
    p = 0
    for out_ref in outs:
        for s in range(out_ref.shape[0]):
            tiles = rows[p : p + per_sym]
            out_ref[s] = tiles.reshape(per_sym * rows.shape[1], rows.shape[2]).T
            p += per_sym


def sort_first_kernel(syms, cd_ref, ab_ref, t2_ref, ints_ref, own_ref, later_ref, ints_out, *scratch):
    both, rows, count, order, order_ab, place, sem, sems = scratch
    load = pltpu.make_async_copy(t2_ref, both.at[0], sem)
    load.start()
    tiles = ab_ref.shape[0]
    rank_tiles(ab_ref, count, order_ab, place, tiles)
    copies = fetch_tiles(ints_ref, rows, order_ab, syms, tiles // NSYM, sems)
    rank_tiles(cd_ref, count, order, None, cd_ref.shape[0])
    load.wait()
    both[1] = half_turned(both[0])
    left = lax.broadcasted_iota(jnp.int32, (t2_ref.shape[0], LANES), 1) < LANES // 2
    q = 0
    for chunk in (own_ref, later_ref):
        for off in range(chunk.shape[1] // LANES):
            chunk[:, off * LANES : (off + 1) * LANES] = pick_pair(
                both, order[2 * q], order[2 * q + 1], left
            )
            q += 1
    for copy in copies:
        copy.wait()
    turn_tiles(rows, (ints_out,), tiles // NSYM)


def sort_first(t2, integrals, cd_sym, ab_sym, syms):
    rows, cols = t2.shape
    tiles, tile, packed = integrals.shape
    per_sym = tiles // NSYM
    return pl.pallas_call(
        functools.partial(sort_first_kernel, syms),
        out_shape=[
            jax.ShapeDtypeStruct((rows, cols // NSYM * m), t2.dtype) for m in (NSYM - LATER, LATER)
        ]
        + [jax.ShapeDtypeStruct((len(syms), packed, per_sym * tile), integrals.dtype)],
        in_specs=[SMEM, SMEM, ANY, ANY],
        out_specs=[VMEM] * 3,
        scratch_shapes=[
            pltpu.VMEM((2, rows, cols), t2.dtype),
            pltpu.VMEM((len(syms) * per_sym, tile, packed), integrals.dtype),
            pltpu.SMEM((NSYM,), jnp.int32),
            pltpu.SMEM((cd_sym.shape[0],), jnp.int32),
            pltpu.SMEM((tiles,), jnp.int32),
            pltpu.SMEM((tiles,), jnp.int32),
            pltpu.SemaphoreType.DMA,
            pltpu.SemaphoreType.DMA((len(syms) * per_sym,)),
        ],
        compiler_params=params(60 * 2**20),
        cost_estimate=CHEAP,
        name="sort_first",
    )(cd_sym, ab_sym, t2, integrals)


def sort_ints_kernel(syms, ab_ref, ints_ref, _, place, *rest):
    outs, (rows, count, order, sems) = rest[:-4], rest[-4:]
    tiles = ab_ref.shape[0]
    rank_tiles(ab_ref, count, order, place, tiles)
    every = [sym for part in syms for sym in part]
    for copy in fetch_tiles(ints_ref, rows, order, every, tiles // NSYM, sems):
        copy.wait()
    turn_tiles(rows, outs, tiles // NSYM)


def sort_ints(integrals, ab_sym, syms, earlier):
    tiles, tile, packed = integrals.shape
    per_sym = tiles // NSYM
    used = sum(len(part) for part in syms) * per_sym
    return pl.pallas_call(
        functools.partial(sort_ints_kernel, syms),
        out_shape=[jax.ShapeDtypeStruct((tiles,), jnp.int32)]
        + [
            jax.ShapeDtypeStruct((len(part), packed, per_sym * tile), integrals.dtype)
            for part in syms
        ],
        in_specs=[SMEM, ANY, ANY],
        out_specs=[SMEM] + [VMEM] * len(syms),
        scratch_shapes=[
            pltpu.VMEM((used, tile, packed), integrals.dtype),
            pltpu.SMEM((NSYM,), jnp.int32),
            pltpu.SMEM((tiles,), jnp.int32),
            pltpu.SemaphoreType.DMA((used,)),
        ],
        compiler_params=params(),
        cost_estimate=CHEAP,
        name="sort_ints",
    )(ab_sym, integrals, earlier)


def merge_kernel(n, *refs):
    blocks, out_ref = refs[:n], refs[-1]
    me = lax.axis_index("zh")
    for d, block in enumerate(blocks):
        out_ref[me ^ d] = block[...]


def merge(blocks, earlier):
    return pl.pallas_call(
        functools.partial(merge_kernel, len(blocks)),
        out_shape=jax.ShapeDtypeStruct((len(blocks),) + blocks[0].shape, blocks[0].dtype),
        in_specs=[VMEM] * len(blocks) + [ANY] * len(earlier),
        out_specs=VMEM,
        compiler_params=params(),
        cost_estimate=CHEAP,
        name="merge",
    )(*blocks, *earlier)


def nothing(*refs):
    pass


def after(x, *earlier):
    n = len(earlier)
    return pl.pallas_call(
        nothing,
        out_shape=jax.ShapeDtypeStruct(x.shape, x.dtype),
        in_specs=[ANY] * (n + 1),
        out_specs=ANY,
        input_output_aliases={n: 0},
        compiler_params=params(),
        cost_estimate=CHEAP,
        name="after",
    )(*earlier, x)


def lay_out(lhs, refs, where, place):
    h, z, x = lax.axis_index("zh"), lax.axis_index("zl"), lax.axis_index("x")
    for k, (by_difference, quarter) in enumerate(where):
        for i, (array, entry) in enumerate(quarter):
            slot = 4 * (h ^ i if by_difference else i) + 2 * (z ^ (k // 2)) + (x ^ (k % 2))
            ref = refs[array]
            lhs[place(slot)] = ref[...] if entry is None else ref[entry]


def contract_kernel(n_cd, first_sym, n_blocks, where, *refs):
    blocks, (own_ref, sib_ref) = refs[:n_blocks], refs[n_blocks : n_blocks + 2]
    outs, lhs = refs[-n_cd - 1 : -1], refs[-1]
    slots, rows, cols = lhs.shape
    packed, width = own_ref.shape[1:]
    first = lax.axis_index("cd") * (slots // n_cd)
    lay_out(lhs, blocks, where, lambda n: lax.rem(n + slots - first, slots))
    t2 = lhs[...].reshape(slots * rows, cols)
    group_rows = t2.shape[0] // n_cd
    for side, ints in enumerate((own_ref, sib_ref)):
        for s in range(cols // packed):
            part = jnp.dot(
                t2[:, s * packed : (s + 1) * packed],
                ints[first_sym + s],
                preferred_element_type=jnp.float32,
            ).astype(outs[0].dtype)
            for by in range(n_cd):
                outs[by][side, :, s * width : (s + 1) * width] = part[
                    by * group_rows : (by + 1) * group_rows
                ]


def contract(n_cd, t2s, ints, sib_ints, first_sym, earlier):
    blocks, where = t2s
    rows, cols = blocks[0].shape[-2:]
    slots = 4 * len(where[0][1])
    packed, width = ints.shape[1:]
    out = (2, slots * rows // n_cd, cols // packed * width)
    return pl.pallas_call(
        functools.partial(contract_kernel, n_cd, first_sym, len(blocks), where),
        out_shape=[jax.ShapeDtypeStruct(out, jnp.bfloat16)] * n_cd,
        in_specs=[VMEM] * (len(blocks) + 2) + [ANY] * len(earlier),
        out_specs=[VMEM] * n_cd,
        scratch_shapes=[pltpu.VMEM((slots, rows, cols), jnp.bfloat16)],
        compiler_params=params(),
        cost_estimate=CHEAP,
        name="contract",
    )(*blocks, ints, sib_ints, *earlier)


def total(parts):
    value = parts[0].astype(jnp.float32)
    for part in parts[1:]:
        value += part.astype(jnp.float32)
    return value.astype(jnp.bfloat16)


def join_kernel(n, *refs):
    out_ref, first = refs[-1], 0
    for ref in refs[:n]:
        out_ref[first : first + ref.shape[0]] = ref[...]
        first += ref.shape[0]


def join(arrays, earlier):
    n = len(arrays)
    out = (sum(x.shape[0] for x in arrays), *arrays[0].shape[1:])
    return pl.pallas_call(
        functools.partial(join_kernel, n),
        out_shape=jax.ShapeDtypeStruct(out, arrays[0].dtype),
        in_specs=[VMEM] * n + [ANY] * len(earlier),
        out_specs=VMEM,
        compiler_params=params(),
        cost_estimate=CHEAP,
        name="join",
    )(*arrays, *earlier)


def later_kernel(n_cd, n_blocks, where, *refs):
    blocks, ints, parts = refs[:n_blocks], refs[n_blocks : n_blocks + 2], refs[n_blocks + 2 : -3]
    own_out, sib_out, lhs = refs[-3:]
    slots, rows, cols = lhs.shape
    packed, width = ints[0].shape[1:]
    per_group, me = slots // n_cd, lax.axis_index("cd")

    def place(n):
        group = lax.div(n, per_group)
        return lax.rem(me + n_cd - group, n_cd) * per_group + (n - group * per_group)

    lay_out(lhs, blocks, where, place)
    t2 = lhs[...].reshape(n_cd, per_group * rows, cols)
    for side, out_ref in enumerate((own_out, sib_out)):
        first = 0
        for c in range(0, len(parts), n_cd):
            value = total([part[side] for part in parts[c : c + n_cd]])
            out_ref[:, first : first + value.shape[1]] = value
            first += value.shape[1]
        for s in range(LATER):
            out_ref[:, first : first + width] = total(
                [
                    jnp.dot(
                        t2[by, :, s * packed : (s + 1) * packed],
                        ints[side][by * LATER + s],
                        preferred_element_type=jnp.float32,
                    ).astype(out_ref.dtype)
                    for by in range(n_cd)
                ]
            )
            first += width


def contract_later(n_cd, t2s, ints, parts):
    blocks, where = t2s
    rows, cols = blocks[0].shape[-2:]
    width = ints[0].shape[2] * LATER + sum(p.shape[2] for p in parts[::n_cd])
    out = jax.ShapeDtypeStruct((parts[0].shape[1], width), jnp.bfloat16)
    return pl.pallas_call(
        functools.partial(later_kernel, n_cd, len(blocks), where),
        out_shape=[out, out],
        in_specs=[VMEM] * (len(blocks) + 2 + len(parts)),
        out_specs=[VMEM] * 2,
        scratch_shapes=[pltpu.VMEM((4 * len(where[0][1]), rows, cols), jnp.bfloat16)],
        compiler_params=params(),
        cost_estimate=CHEAP,
        name="contract_later",
    )(*blocks, *ints, *parts)


def finish_kernel(side, place, sums_ref, *rest):
    out_ref, both, made, sems = rest[-4:]
    blocks, rows, cols = made.shape
    left = lax.broadcasted_iota(jnp.int32, (rows, LANES), 1) < LANES // 2

    def copy_out(i):
        block = 2 * i + (lax.axis_index("core") ^ side)
        return pltpu.make_async_copy(made.at[i], out_ref.at[block], sems.at[i])

    for i in range(blocks):
        both[0] = sums_ref[i * rows : (i + 1) * rows]
        both[1] = half_turned(both[0])
        for q in range(cols // LANES):
            made[i, :, q * LANES : (q + 1) * LANES] = pick_pair(
                both, place[2 * q], place[2 * q + 1], left
            )
        copy_out(i).start()
    for i in range(blocks):
        copy_out(i).wait()


def finish(side, place, sums, rows, out=None):
    blocks, cols = sums.shape[0] // rows, sums.shape[1]
    before = [] if out is None else [out]
    return pl.pallas_call(
        functools.partial(finish_kernel, side),
        out_shape=jax.ShapeDtypeStruct((2 * blocks, rows, cols), jnp.bfloat16),
        in_specs=[SMEM, VMEM] + [ANY] * len(before),
        out_specs=ANY,
        scratch_shapes=[
            pltpu.VMEM((2, rows, cols), jnp.bfloat16),
            pltpu.VMEM((blocks, rows, cols), jnp.bfloat16),
            pltpu.SemaphoreType.DMA((blocks,)),
        ],
        input_output_aliases={2: 0} if before else {},
        compiler_params=params(),
        cost_estimate=CHEAP,
        name="finish",
    )(place, sums, *before)


SWAP = [(0, 1), (1, 0)]


def further(x, by):
    n_cd = lax.axis_size("cd")
    return lax.ppermute(x, "cd", [(i, (i + by) % n_cd) for i in range(n_cd)])


def to_plane(x, d):
    n_cd = lax.axis_size("cd")
    z_len = 2 * lax.axis_size("zh")
    rest = z_len // n_cd
    pairs = []
    for z in range(z_len):
        group, i = divmod(z, rest)
        for y in range(n_cd):
            pairs.append((z * n_cd + y, ((y * rest + i) ^ (2 * d)) * n_cd + group))
    return lax.ppermute(x, ("zh", "zl", "cd"), pairs)


def per_device(t2_amps, integrals, ab_sym, cd_sym):
    zh, n_cd = lax.axis_size("zh"), lax.axis_size("cd")
    def over(x, axis):
        return lax.ppermute(x, axis, SWAP)

    def along_zh(x):
        return [lax.ppermute(x, "zh", [(i, i ^ d) for i in range(zh)]) for d in range(1, zh)]

    first_later = tuple(range(NSYM - LATER, NSYM - LATER + FIRST_SENT))
    own, own_later, ints_later = sort_first(t2_amps, integrals, cd_sym, ab_sym, first_later)
    later = [[ints_later] + [further(ints_later, by) for by in range(1, n_cd)]]
    syms = (tuple(range(NSYM - LATER)), tuple(range(NSYM - LATER + FIRST_SENT, NSYM)))
    place, ints, ints_later = sort_ints(integrals, ab_sym, syms, own)
    x_o, block_l = over(own, "x"), over(own, "zl")
    blocks_h = along_zh(own)
    x_l = over(block_l, "x")
    blocks_h[0] = after(blocks_h[0], *later[0][1:], ints, x_o, x_l, *blocks_h[1:])
    fence = blocks_h[0]
    x_h = [over(after(y, fence) if i else y, "x") for i, y in enumerate(blocks_h)]
    blocks_hl = [over(y, "zl") for y in blocks_h]
    ints = after(ints, fence)
    sib_ints = over(ints, "core")
    ints_later = after(ints_later, fence)
    later.append([ints_later] + [further(ints_later, by) for by in range(1, n_cd)])
    near = [to_plane(after(own_later, fence), d) for d in range(1, zh)]
    near = merge([to_plane(after(own_later, sib_ints), 0)] + near, [])
    x_hl = [over(y, "x") for y in blocks_hl]
    where = tuple(
        (True, tuple((zh * k + d, None) for d in range(zh)))
        for k in range(4)
    )
    blocks = [own, *blocks_h, x_o, *x_h, block_l, *blocks_hl, x_l, *x_hl]
    made = contract(n_cd, (blocks, where), ints, sib_ints, 0, [near, *later[1][1:]])
    parts = [made[0]] + [further(made[by], by) for by in range(1, n_cd)]
    up, across = over(near, "zl"), over(near, "x")
    half = zh // 2
    blocks = [near, across, up, over(up[:half], "x"), over(across[half:], "zl")]
    where = tuple((False, tuple((k, i) for i in range(zh))) for k in range(3))
    where += ((False, tuple((3 + i // half, i % half) for i in range(zh))),)
    t2s = blocks, where
    ints_later = join([x[by] for by in range(n_cd) for x in later], made[:1])
    ints_later = (ints_later, over(ints_later, "core"))
    sums, sib_sums = contract_later(n_cd, t2s, ints_later, parts)
    sib_sums = lax.ppermute(sib_sums, "core", SWAP)
    rows = t2_amps.shape[0]
    out = finish(0, place, sums, rows)
    out = finish(1, place, sib_sums, rows, out)
    return out.reshape(-1, out.shape[2])


def solution(mesh):
    n_blk, n_cd = mesh.devices.shape
    blk = ("zh", "zl", "x", "core")
    parted = Mesh(mesh.devices.reshape(n_blk // 8, 2, 2, 2, n_cd), blk + ("cd",))
    in_specs = (P(blk, "cd"), P(blk, None, "cd"), P(blk), P("cd"))
    return jax.shard_map(
        per_device, mesh=parted, in_specs=in_specs, out_specs=P("cd", blk), check_vma=False
    )
```

```python
import functools

import jax
import jax.numpy as jnp
from jax import lax
from jax.experimental import pallas as pl
from jax.experimental.pallas import tpu as pltpu
from jax.sharding import Mesh, PartitionSpec as P

NSYM = 8
LATER = 4
FIRST_SENT = 2
LANES = 128
VMEM_LIMIT = 20 * 2**20

ANY = pl.BlockSpec(memory_space=pl.ANY)
SMEM = pl.BlockSpec(memory_space=pltpu.SMEM)
VMEM = pl.BlockSpec(memory_space=pltpu.VMEM)

CHEAP = pl.CostEstimate(flops=1000, bytes_accessed=1000, transcendentals=0)


def params(limit=VMEM_LIMIT):
    return pltpu.CompilerParams(vmem_limit_bytes=limit)


def half_turned(x):
    half = LANES // 2
    return jnp.concatenate([x[:, half:], x[:, :half]], axis=1)


def rank_tiles(sym_ref, count_ref, order_ref, place_ref, tiles):
    for s in range(NSYM):
        count_ref[s] = s * (tiles // NSYM)

    def step(i, _):
        s = sym_ref[i]
        p = count_ref[s]
        count_ref[s] = p + 1
        order_ref[p] = i
        if place_ref is not None:
            place_ref[i] = p
        return 0

    lax.fori_loop(0, tiles, step, 0)


def pick_pair(both, a, b, left):
    columns = both.shape[2] // LANES
    a_col = lax.shift_right_logical(a, 1)
    b_col = lax.rem(lax.shift_right_logical(b + 1, 1) + columns - 1, columns)
    xa = both[a & 1, :, pl.ds(pl.multiple_of(a_col * LANES, LANES), LANES)]
    xb = both[(b & 1) ^ 1, :, pl.ds(pl.multiple_of(b_col * LANES, LANES), LANES)]
    return jnp.where(left, xa, xb)


def fetch_tiles(ints_ref, rows, order, syms, per_sym, sems):
    copies = []
    for sym in syms:
        for m in range(per_sym):
            p = len(copies)
            tile_ref = ints_ref.at[order[sym * per_sym + m]]
            copies.append(pltpu.make_async_copy(tile_ref, rows.at[p], sems.at[p]))
            copies[-1].start()
    return copies


def turn_tiles(rows, outs, per_sym):
    p = 0
    for out_ref in outs:
        for s in range(out_ref.shape[0]):
            tiles = rows[p : p + per_sym]
            out_ref[s] = tiles.reshape(per_sym * rows.shape[1], rows.shape[2]).T
            p += per_sym


def sort_first_kernel(syms, cd_ref, ab_ref, t2_ref, ints_ref, own_ref, later_ref, ints_out, *scratch):
    both, rows, count, order, order_ab, place, sem, sems = scratch
    load = pltpu.make_async_copy(t2_ref, both.at[0], sem)
    load.start()
    tiles = ab_ref.shape[0]
    rank_tiles(ab_ref, count, order_ab, place, tiles)
    copies = fetch_tiles(ints_ref, rows, order_ab, syms, tiles // NSYM, sems)
    rank_tiles(cd_ref, count, order, None, cd_ref.shape[0])
    load.wait()
    both[1] = half_turned(both[0])
    left = lax.broadcasted_iota(jnp.int32, (t2_ref.shape[0], LANES), 1) < LANES // 2
    q = 0
    for chunk in (own_ref, later_ref):
        for off in range(chunk.shape[1] // LANES):
            chunk[:, off * LANES : (off + 1) * LANES] = pick_pair(
                both, order[2 * q], order[2 * q + 1], left
            )
            q += 1
    for copy in copies:
        copy.wait()
    turn_tiles(rows, (ints_out,), tiles // NSYM)


def sort_first(t2, integrals, cd_sym, ab_sym, syms):
    rows, cols = t2.shape
    tiles, tile, packed = integrals.shape
    per_sym = tiles // NSYM
    return pl.pallas_call(
        functools.partial(sort_first_kernel, syms),
        out_shape=[
            jax.ShapeDtypeStruct((rows, cols // NSYM * m), t2.dtype) for m in (NSYM - LATER, LATER)
        ]
        + [jax.ShapeDtypeStruct((len(syms), packed, per_sym * tile), integrals.dtype)],
        in_specs=[SMEM, SMEM, ANY, ANY],
        out_specs=[VMEM] * 3,
        scratch_shapes=[
            pltpu.VMEM((2, rows, cols), t2.dtype),
            pltpu.VMEM((len(syms) * per_sym, tile, packed), integrals.dtype),
            pltpu.SMEM((NSYM,), jnp.int32),
            pltpu.SMEM((cd_sym.shape[0],), jnp.int32),
            pltpu.SMEM((tiles,), jnp.int32),
            pltpu.SMEM((tiles,), jnp.int32),
            pltpu.SemaphoreType.DMA,
            pltpu.SemaphoreType.DMA((len(syms) * per_sym,)),
        ],
        compiler_params=params(60 * 2**20),
        cost_estimate=CHEAP,
        name="sort_first",
    )(cd_sym, ab_sym, t2, integrals)


def sort_ints_kernel(syms, ab_ref, ints_ref, _, place, *rest):
    outs, (rows, count, order, sems) = rest[:-4], rest[-4:]
    tiles = ab_ref.shape[0]
    rank_tiles(ab_ref, count, order, place, tiles)
    every = [sym for part in syms for sym in part]
    for copy in fetch_tiles(ints_ref, rows, order, every, tiles // NSYM, sems):
        copy.wait()
    turn_tiles(rows, outs, tiles // NSYM)


def sort_ints(integrals, ab_sym, syms, earlier):
    tiles, tile, packed = integrals.shape
    per_sym = tiles // NSYM
    used = sum(len(part) for part in syms) * per_sym
    return pl.pallas_call(
        functools.partial(sort_ints_kernel, syms),
        out_shape=[jax.ShapeDtypeStruct((tiles,), jnp.int32)]
        + [
            jax.ShapeDtypeStruct((len(part), packed, per_sym * tile), integrals.dtype)
            for part in syms
        ],
        in_specs=[SMEM, ANY, ANY],
        out_specs=[SMEM] + [VMEM] * len(syms),
        scratch_shapes=[
            pltpu.VMEM((used, tile, packed), integrals.dtype),
            pltpu.SMEM((NSYM,), jnp.int32),
            pltpu.SMEM((tiles,), jnp.int32),
            pltpu.SemaphoreType.DMA((used,)),
        ],
        compiler_params=params(),
        cost_estimate=CHEAP,
        name="sort_ints",
    )(ab_sym, integrals, earlier)


def merge_kernel(n, *refs):
    blocks, out_ref = refs[:n], refs[-1]
    me = lax.axis_index("zh")
    for d, block in enumerate(blocks):
        out_ref[me ^ d] = block[...]


def merge(blocks, earlier):
    return pl.pallas_call(
        functools.partial(merge_kernel, len(blocks)),
        out_shape=jax.ShapeDtypeStruct((len(blocks),) + blocks[0].shape, blocks[0].dtype),
        in_specs=[VMEM] * len(blocks) + [ANY] * len(earlier),
        out_specs=VMEM,
        compiler_params=params(),
        cost_estimate=CHEAP,
        name="merge",
    )(*blocks, *earlier)


def nothing(*refs):
    pass


def after(x, *earlier):
    n = len(earlier)
    return pl.pallas_call(
        nothing,
        out_shape=jax.ShapeDtypeStruct(x.shape, x.dtype),
        in_specs=[ANY] * (n + 1),
        out_specs=ANY,
        input_output_aliases={n: 0},
        compiler_params=params(),
        cost_estimate=CHEAP,
        name="after",
    )(*earlier, x)


def lay_out(lhs, refs, where, place):
    h, z, x = lax.axis_index("zh"), lax.axis_index("zl"), lax.axis_index("x")
    for k, (by_difference, quarter) in enumerate(where):
        for i, (array, entry) in enumerate(quarter):
            slot = 4 * (h ^ i if by_difference else i) + 2 * (z ^ (k // 2)) + (x ^ (k % 2))
            ref = refs[array]
            lhs[place(slot)] = ref[...] if entry is None else ref[entry]


def contract_kernel(n_cd, first_sym, n_blocks, where, *refs):
    blocks, (own_ref, sib_ref) = refs[:n_blocks], refs[n_blocks : n_blocks + 2]
    outs, lhs = refs[-n_cd - 1 : -1], refs[-1]
    slots, rows, cols = lhs.shape
    packed, width = own_ref.shape[1:]
    first = lax.axis_index("cd") * (slots // n_cd)
    lay_out(lhs, blocks, where, lambda n: lax.rem(n + slots - first, slots))
    t2 = lhs[...].reshape(slots * rows, cols)
    group_rows = t2.shape[0] // n_cd
    for side, ints in enumerate((own_ref, sib_ref)):
        for s in range(cols // packed):
            part = jnp.dot(
                t2[:, s * packed : (s + 1) * packed],
                ints[first_sym + s],
                preferred_element_type=jnp.float32,
            ).astype(outs[0].dtype)
            for by in range(n_cd):
                outs[by][side, :, s * width : (s + 1) * width] = part[
                    by * group_rows : (by + 1) * group_rows
                ]


def contract(n_cd, t2s, ints, sib_ints, first_sym, earlier):
    blocks, where = t2s
    rows, cols = blocks[0].shape[-2:]
    slots = 4 * len(where[0][1])
    packed, width = ints.shape[1:]
    out = (2, slots * rows // n_cd, cols // packed * width)
    return pl.pallas_call(
        functools.partial(contract_kernel, n_cd, first_sym, len(blocks), where),
        out_shape=[jax.ShapeDtypeStruct(out, jnp.bfloat16)] * n_cd,
        in_specs=[VMEM] * (len(blocks) + 2) + [ANY] * len(earlier),
        out_specs=[VMEM] * n_cd,
        scratch_shapes=[pltpu.VMEM((slots, rows, cols), jnp.bfloat16)],
        compiler_params=params(),
        cost_estimate=CHEAP,
        name="contract",
    )(*blocks, ints, sib_ints, *earlier)


def total(parts):
    value = parts[0].astype(jnp.float32)
    for part in parts[1:]:
        value += part.astype(jnp.float32)
    return value.astype(jnp.bfloat16)


def join_kernel(n, *refs):
    out_ref, first = refs[-1], 0
    for ref in refs[-n - 1 : -1]:
        out_ref[first : first + ref.shape[0]] = ref[...]
        first += ref.shape[0]


def join(arrays, earlier):
    n = len(arrays)
    out = (sum(x.shape[0] for x in arrays), *arrays[0].shape[1:])
    return pl.pallas_call(
        functools.partial(join_kernel, n),
        out_shape=jax.ShapeDtypeStruct(out, arrays[0].dtype),
        in_specs=[ANY] * len(earlier) + [VMEM] * n,
        out_specs=VMEM,
        compiler_params=params(),
        cost_estimate=CHEAP,
        name="join",
    )(*earlier, *arrays)


def later_kernel(n_cd, n_blocks, where, *refs):
    blocks, ints, parts = refs[:n_blocks], refs[n_blocks : n_blocks + 2], refs[n_blocks + 2 : -3]
    own_out, sib_out, lhs = refs[-3:]
    slots, rows, cols = lhs.shape
    packed, width = ints[0].shape[1:]
    per_group, me = slots // n_cd, lax.axis_index("cd")

    def place(n):
        group = lax.div(n, per_group)
        return lax.rem(me + n_cd - group, n_cd) * per_group + (n - group * per_group)

    lay_out(lhs, blocks, where, place)
    t2 = lhs[...].reshape(n_cd, per_group * rows, cols)
    for side, out_ref in enumerate((own_out, sib_out)):
        first = 0
        for c in range(0, len(parts), n_cd):
            value = total([part[side] for part in parts[c : c + n_cd]])
            out_ref[:, first : first + value.shape[1]] = value
            first += value.shape[1]
        for s in range(LATER):
            out_ref[:, first : first + width] = total(
                [
                    jnp.dot(
                        t2[by, :, s * packed : (s + 1) * packed],
                        ints[side][by * LATER + s],
                        preferred_element_type=jnp.float32,
                    ).astype(out_ref.dtype)
                    for by in range(n_cd)
                ]
            )
            first += width


def contract_later(n_cd, t2s, ints, parts):
    blocks, where = t2s
    rows, cols = blocks[0].shape[-2:]
    width = ints[0].shape[2] * LATER + sum(p.shape[2] for p in parts[::n_cd])
    out = jax.ShapeDtypeStruct((parts[0].shape[1], width), jnp.bfloat16)
    return pl.pallas_call(
        functools.partial(later_kernel, n_cd, len(blocks), where),
        out_shape=[out, out],
        in_specs=[VMEM] * (len(blocks) + 2 + len(parts)),
        out_specs=[VMEM] * 2,
        scratch_shapes=[pltpu.VMEM((4 * len(where[0][1]), rows, cols), jnp.bfloat16)],
        compiler_params=params(),
        cost_estimate=CHEAP,
        name="contract_later",
    )(*blocks, *ints, *parts)


def finish_kernel(side, place, sums_ref, *rest):
    out_ref, both, made, sems = rest[-4:]
    blocks, rows, cols = made.shape
    left = lax.broadcasted_iota(jnp.int32, (rows, LANES), 1) < LANES // 2

    def copy_out(i):
        block = 2 * i + (lax.axis_index("core") ^ side)
        return pltpu.make_async_copy(made.at[i], out_ref.at[block], sems.at[i])

    for i in range(blocks):
        both[0] = sums_ref[i * rows : (i + 1) * rows]
        both[1] = half_turned(both[0])
        for q in range(cols // LANES):
            made[i, :, q * LANES : (q + 1) * LANES] = pick_pair(
                both, place[2 * q], place[2 * q + 1], left
            )
        copy_out(i).start()
    for i in range(blocks):
        copy_out(i).wait()


def finish(side, place, sums, rows, out=None):
    blocks, cols = sums.shape[0] // rows, sums.shape[1]
    before = [] if out is None else [out]
    return pl.pallas_call(
        functools.partial(finish_kernel, side),
        out_shape=jax.ShapeDtypeStruct((2 * blocks, rows, cols), jnp.bfloat16),
        in_specs=[SMEM, VMEM] + [ANY] * len(before),
        out_specs=ANY,
        scratch_shapes=[
            pltpu.VMEM((2, rows, cols), jnp.bfloat16),
            pltpu.VMEM((blocks, rows, cols), jnp.bfloat16),
            pltpu.SemaphoreType.DMA((blocks,)),
        ],
        input_output_aliases={2: 0} if before else {},
        compiler_params=params(),
        cost_estimate=CHEAP,
        name="finish",
    )(place, sums, *before)


SWAP = [(0, 1), (1, 0)]


def further(x, by):
    n_cd = lax.axis_size("cd")
    return lax.ppermute(x, "cd", [(i, (i + by) % n_cd) for i in range(n_cd)])


def to_plane(x, d):
    n_cd = lax.axis_size("cd")
    z_len = 2 * lax.axis_size("zh")
    rest = z_len // n_cd
    pairs = []
    for z in range(z_len):
        group, i = divmod(z, rest)
        for y in range(n_cd):
            pairs.append((z * n_cd + y, ((y * rest + i) ^ (2 * d)) * n_cd + group))
    return lax.ppermute(x, ("zh", "zl", "cd"), pairs)


def per_device(t2_amps, integrals, ab_sym, cd_sym):
    zh, n_cd = lax.axis_size("zh"), lax.axis_size("cd")
    def over(x, axis):
        return lax.ppermute(x, axis, SWAP)

    def along_zh(x):
        return [lax.ppermute(x, "zh", [(i, i ^ d) for i in range(zh)]) for d in range(1, zh)]

    first_later = tuple(range(NSYM - LATER, NSYM - LATER + FIRST_SENT))
    own, own_later, ints_later = sort_first(t2_amps, integrals, cd_sym, ab_sym, first_later)
    later = [[ints_later] + [further(ints_later, by) for by in range(1, n_cd)]]
    syms = (tuple(range(NSYM - LATER)), tuple(range(NSYM - LATER + FIRST_SENT, NSYM)))
    place, ints, ints_later = sort_ints(integrals, ab_sym, syms, own)
    x_o, block_l = over(own, "x"), over(own, "zl")
    blocks_h = along_zh(own)
    fence = join([y[None] for y in [block_l, *blocks_h]], [*later[0][1:], ints, x_o])
    x_lh = over(fence, "x")
    blocks_hl = [over(y, "zl") for y in blocks_h]
    ints = after(ints, fence)
    sib_ints = over(ints, "core")
    ints_later = after(ints_later, fence)
    later.append([ints_later] + [further(ints_later, by) for by in range(1, n_cd)])
    near = [to_plane(after(own_later, fence), d) for d in range(1, zh)]
    near = merge([to_plane(after(own_later, sib_ints), 0)] + near, [])
    x_hl = [over(y, "x") for y in blocks_hl]
    blocks = [own, *blocks_h, x_o, x_lh, block_l, *blocks_hl, *x_hl]
    where = (
        tuple((d, None) for d in range(zh)),
        ((zh, None),) + tuple((zh + 1, d) for d in range(1, zh)),
        tuple((zh + 2 + d, None) for d in range(zh)),
        ((zh + 1, 0),) + tuple((2 * zh + 1 + d, None) for d in range(1, zh)),
    )
    where = tuple((True, quarter) for quarter in where)
    made = contract(n_cd, (blocks, where), ints, sib_ints, 0, [near, *later[1][1:]])
    parts = [made[0]] + [further(made[by], by) for by in range(1, n_cd)]
    up, across = over(near, "zl"), over(near, "x")
    half = zh // 2
    blocks = [near, across, up, over(up[:half], "x"), over(across[half:], "zl")]
    where = tuple((False, tuple((k, i) for i in range(zh))) for k in range(3))
    where += ((False, tuple((3 + i // half, i % half) for i in range(zh))),)
    t2s = blocks, where
    ints_later = join([x[by] for by in range(n_cd) for x in later], made[:1])
    ints_later = (ints_later, over(ints_later, "core"))
    sums, sib_sums = contract_later(n_cd, t2s, ints_later, parts)
    sib_sums = lax.ppermute(sib_sums, "core", SWAP)
    rows = t2_amps.shape[0]
    out = finish(0, place, sums, rows)
    out = finish(1, place, sib_sums, rows, out)
    return out.reshape(-1, out.shape[2])


def solution(mesh):
    n_blk, n_cd = mesh.devices.shape
    blk = ("zh", "zl", "x", "core")
    parted = Mesh(mesh.devices.reshape(n_blk // 8, 2, 2, 2, n_cd), blk + ("cd",))
    in_specs = (P(blk, "cd"), P(blk, None, "cd"), P(blk), P("cd"))
    return jax.shard_map(
        per_device, mesh=parted, in_specs=in_specs, out_specs=P("cd", blk), check_vma=False
    )
```

```python
import functools

import jax
import jax.numpy as jnp
from jax import lax
from jax.experimental import pallas as pl
from jax.experimental.pallas import tpu as pltpu
from jax.sharding import Mesh, PartitionSpec as P

NSYM = 8
LATER = 4
FIRST_SENT = 2
FIRST_MADE = 2
LANES = 128
VMEM_LIMIT = 20 * 2**20

ANY = pl.BlockSpec(memory_space=pl.ANY)
SMEM = pl.BlockSpec(memory_space=pltpu.SMEM)
VMEM = pl.BlockSpec(memory_space=pltpu.VMEM)

CHEAP = pl.CostEstimate(flops=1000, bytes_accessed=1000, transcendentals=0)


def params(limit=VMEM_LIMIT):
    return pltpu.CompilerParams(vmem_limit_bytes=limit)


def half_turned(x):
    half = LANES // 2
    return jnp.concatenate([x[:, half:], x[:, :half]], axis=1)


def rank_tiles(sym_ref, count_ref, order_ref, place_ref, tiles):
    for s in range(NSYM):
        count_ref[s] = s * (tiles // NSYM)

    def step(i, _):
        s = sym_ref[i]
        p = count_ref[s]
        count_ref[s] = p + 1
        order_ref[p] = i
        if place_ref is not None:
            place_ref[i] = p
        return 0

    lax.fori_loop(0, tiles, step, 0, unroll=8)


def pick_pair(both, a, b, left):
    columns = both.shape[2] // LANES
    a_col = lax.shift_right_logical(a, 1)
    b_col = lax.rem(lax.shift_right_logical(b + 1, 1) + columns - 1, columns)
    xa = both[a & 1, :, pl.ds(pl.multiple_of(a_col * LANES, LANES), LANES)]
    xb = both[(b & 1) ^ 1, :, pl.ds(pl.multiple_of(b_col * LANES, LANES), LANES)]
    return jnp.where(left, xa, xb)


def fetch_tiles(ints_ref, rows, order, syms, per_sym, sems):
    copies = []
    for sym in syms:
        for m in range(per_sym):
            p = len(copies)
            tile_ref = ints_ref.at[order[sym * per_sym + m]]
            copies.append(pltpu.make_async_copy(tile_ref, rows.at[p], sems.at[p]))
            copies[-1].start()
    return copies


def turn_tiles(rows, outs, per_sym):
    p = 0
    for out_ref in outs:
        for s in range(out_ref.shape[0]):
            tiles = rows[p : p + per_sym]
            out_ref[s] = tiles.reshape(per_sym * rows.shape[1], rows.shape[2]).T
            p += per_sym


def sort_first_kernel(syms, cd_ref, ab_ref, t2_ref, ints_ref, own_ref, later_ref, ints_out, *scratch):
    both, rows, count, order, order_ab, place, sem, sems = scratch
    load = pltpu.make_async_copy(t2_ref, both.at[0], sem)
    load.start()
    tiles = ab_ref.shape[0]
    rank_tiles(ab_ref, count, order_ab, place, tiles)
    copies = fetch_tiles(ints_ref, rows, order_ab, syms, tiles // NSYM, sems)
    rank_tiles(cd_ref, count, order, None, cd_ref.shape[0])
    load.wait()
    both[1] = half_turned(both[0])
    left = lax.broadcasted_iota(jnp.int32, (t2_ref.shape[0], LANES), 1) < LANES // 2
    q = 0
    for chunk in (own_ref, later_ref):
        for off in range(chunk.shape[1] // LANES):
            chunk[:, off * LANES : (off + 1) * LANES] = pick_pair(
                both, order[2 * q], order[2 * q + 1], left
            )
            q += 1
    for copy in copies:
        copy.wait()
    turn_tiles(rows, (ints_out,), tiles // NSYM)


def sort_first(t2, integrals, cd_sym, ab_sym, syms):
    rows, cols = t2.shape
    tiles, tile, packed = integrals.shape
    per_sym = tiles // NSYM
    return pl.pallas_call(
        functools.partial(sort_first_kernel, syms),
        out_shape=[
            jax.ShapeDtypeStruct((rows, cols // NSYM * m), t2.dtype) for m in (NSYM - LATER, LATER)
        ]
        + [jax.ShapeDtypeStruct((len(syms), packed, per_sym * tile), integrals.dtype)],
        in_specs=[SMEM, SMEM, ANY, ANY],
        out_specs=[VMEM] * 3,
        scratch_shapes=[
            pltpu.VMEM((2, rows, cols), t2.dtype),
            pltpu.VMEM((len(syms) * per_sym, tile, packed), integrals.dtype),
            pltpu.SMEM((NSYM,), jnp.int32),
            pltpu.SMEM((cd_sym.shape[0],), jnp.int32),
            pltpu.SMEM((tiles,), jnp.int32),
            pltpu.SMEM((tiles,), jnp.int32),
            pltpu.SemaphoreType.DMA,
            pltpu.SemaphoreType.DMA((len(syms) * per_sym,)),
        ],
        compiler_params=params(60 * 2**20),
        cost_estimate=CHEAP,
        name="sort_first",
    )(cd_sym, ab_sym, t2, integrals)


def sort_ints_kernel(syms, ab_ref, ints_ref, _, place, *rest):
    outs, (rows, count, order, sems) = rest[:-4], rest[-4:]
    tiles = ab_ref.shape[0]
    rank_tiles(ab_ref, count, order, place, tiles)
    every = [sym for part in syms for sym in part]
    for copy in fetch_tiles(ints_ref, rows, order, every, tiles // NSYM, sems):
        copy.wait()
    turn_tiles(rows, outs, tiles // NSYM)


def sort_ints(integrals, ab_sym, syms, earlier):
    tiles, tile, packed = integrals.shape
    per_sym = tiles // NSYM
    used = sum(len(part) for part in syms) * per_sym
    return pl.pallas_call(
        functools.partial(sort_ints_kernel, syms),
        out_shape=[jax.ShapeDtypeStruct((tiles,), jnp.int32)]
        + [
            jax.ShapeDtypeStruct((len(part), packed, per_sym * tile), integrals.dtype)
            for part in syms
        ],
        in_specs=[SMEM, ANY, ANY],
        out_specs=[SMEM] + [VMEM] * len(syms),
        scratch_shapes=[
            pltpu.VMEM((used, tile, packed), integrals.dtype),
            pltpu.SMEM((NSYM,), jnp.int32),
            pltpu.SMEM((tiles,), jnp.int32),
            pltpu.SemaphoreType.DMA((used,)),
        ],
        compiler_params=params(),
        cost_estimate=CHEAP,
        name="sort_ints",
    )(ab_sym, integrals, earlier)


def merge_kernel(n, *refs):
    blocks, out_ref = refs[:n], refs[-1]
    me = lax.axis_index("zh")
    for d, block in enumerate(blocks):
        out_ref[me ^ d] = block[...]


def merge(blocks, earlier):
    return pl.pallas_call(
        functools.partial(merge_kernel, len(blocks)),
        out_shape=jax.ShapeDtypeStruct((len(blocks),) + blocks[0].shape, blocks[0].dtype),
        in_specs=[VMEM] * len(blocks) + [ANY] * len(earlier),
        out_specs=VMEM,
        compiler_params=params(),
        cost_estimate=CHEAP,
        name="merge",
    )(*blocks, *earlier)


def nothing(*refs):
    pass


def after(x, *earlier):
    n = len(earlier)
    return pl.pallas_call(
        nothing,
        out_shape=jax.ShapeDtypeStruct(x.shape, x.dtype),
        in_specs=[ANY] * (n + 1),
        out_specs=ANY,
        input_output_aliases={n: 0},
        compiler_params=params(),
        cost_estimate=CHEAP,
        name="after",
    )(*earlier, x)


def lay_out(lhs, refs, where, place):
    h, z, x = lax.axis_index("zh"), lax.axis_index("zl"), lax.axis_index("x")
    for k, by_difference, quarter in where:
        for i, (array, entry) in enumerate(quarter):
            row = place(2 * (h ^ i if by_difference else i) + (z ^ (k // 2)), x ^ (k % 2))
            lhs[row] = refs[array][...] if entry is None else refs[array][entry]


def contract_kernel(n_cd, n_blocks, jobs, *refs):
    blocks, ints_refs = refs[:n_blocks], refs[n_blocks : n_blocks + 2]
    outs, lhs = refs[-n_cd - 1 : -1], refs[-1]
    z_len, rows, cols = lhs.shape
    packed, width = ints_refs[0].shape[1:]
    first = lax.axis_index("cd") * (z_len // n_cd)
    column = 0
    for where, syms in jobs:
        lay_out(lhs, blocks, where, lambda z, x: lax.rem(z + z_len - first, z_len))
        t2 = lhs[...].reshape(z_len * rows, cols)
        group_rows = t2.shape[0] // n_cd
        for s in syms:
            for side, ints in enumerate(ints_refs):
                part = jnp.dot(
                    t2[:, s * packed : (s + 1) * packed],
                    ints[s],
                    preferred_element_type=jnp.float32,
                ).astype(outs[0].dtype)
                for by in range(n_cd):
                    outs[by][side, :, column : column + width] = part[
                        by * group_rows : (by + 1) * group_rows
                    ]
            column += width


def contract(n_cd, blocks, jobs, ints, sib_ints, earlier):
    rows, cols = blocks[0].shape[-2:]
    z_len = 2 * len(jobs[0][0][0][2])
    width = ints.shape[2] * sum(len(syms) for _, syms in jobs)
    out = (2, z_len * rows // n_cd, width)
    return pl.pallas_call(
        functools.partial(contract_kernel, n_cd, len(blocks), jobs),
        out_shape=[jax.ShapeDtypeStruct(out, jnp.bfloat16)] * n_cd,
        in_specs=[VMEM] * (len(blocks) + 2) + [ANY] * len(earlier),
        out_specs=[VMEM] * n_cd,
        scratch_shapes=[pltpu.VMEM((z_len, rows, cols), jnp.bfloat16)],
        compiler_params=params(),
        cost_estimate=CHEAP,
        name="contract",
    )(*blocks, ints, sib_ints, *earlier)


def total(parts):
    value = parts[0].astype(jnp.float32)
    for part in parts[1:]:
        value += part.astype(jnp.float32)
    return value.astype(jnp.bfloat16)


def join_kernel(n, *refs):
    out_ref, first = refs[-1], 0
    for ref in refs[-n - 1 : -1]:
        out_ref[first : first + ref.shape[0]] = ref[...]
        first += ref.shape[0]


def join(arrays, earlier):
    n = len(arrays)
    out = (sum(x.shape[0] for x in arrays), *arrays[0].shape[1:])
    return pl.pallas_call(
        functools.partial(join_kernel, n),
        out_shape=jax.ShapeDtypeStruct(out, arrays[0].dtype),
        in_specs=[ANY] * len(earlier) + [VMEM] * n,
        out_specs=VMEM,
        compiler_params=params(),
        cost_estimate=CHEAP,
        name="join",
    )(*earlier, *arrays)


def later_kernel(n_cd, n_blocks, where, *refs):
    blocks, ints, parts = refs[:n_blocks], refs[n_blocks : n_blocks + 2], refs[n_blocks + 2 : -3]
    own_out, sib_out, lhs = refs[-3:]
    slots, rows, cols = lhs.shape
    packed, width = ints[0].shape[1:]
    per_group, me, x = slots // n_cd, lax.axis_index("cd"), lax.axis_index("x")

    def place(z, x):
        n = 2 * z + x
        group = lax.div(n, per_group)
        return lax.rem(me + n_cd - group, n_cd) * per_group + (n - group * per_group)

    lay_out(lhs, blocks, where, place)
    t2 = lhs[...].reshape(n_cd, per_group * rows, cols)
    for side, out_ref in enumerate((own_out, sib_out)):
        early, first = FIRST_MADE * width, (NSYM - LATER) * width
        pieces = (
            (0, 0, early, parts[:n_cd], 0),
            (0, early, first, parts[n_cd:], first),
            (1, 0, first, parts[n_cd:], 0),
        )
        for half, start, stop, mine, at in pieces:
            for z in range(per_group // 2):
                these = pl.ds(pl.multiple_of((2 * z + (x ^ half)) * rows, rows), rows)
                out_ref[these, start:stop] = total(
                    [
                        part[side, z * rows : (z + 1) * rows, at : at + stop - start]
                        for part in mine
                    ]
                )
        for s in range(LATER):
            out_ref[:, first : first + width] = total(
                [
                    jnp.dot(
                        t2[by, :, s * packed : (s + 1) * packed],
                        ints[side][by * LATER + s],
                        preferred_element_type=jnp.float32,
                    ).astype(out_ref.dtype)
                    for by in range(n_cd)
                ]
            )
            first += width


def contract_later(n_cd, blocks, where, ints, parts):
    rows, cols = blocks[0].shape[-2:]
    slots = 4 * len(where[0][2])
    out = (slots * rows // n_cd, ints[0].shape[2] * NSYM)
    return pl.pallas_call(
        functools.partial(later_kernel, n_cd, len(blocks), where),
        out_shape=[jax.ShapeDtypeStruct(out, jnp.bfloat16)] * 2,
        in_specs=[VMEM] * (len(blocks) + 2 + len(parts)),
        out_specs=[VMEM] * 2,
        scratch_shapes=[pltpu.VMEM((slots, rows, cols), jnp.bfloat16)],
        compiler_params=params(),
        cost_estimate=CHEAP,
        name="contract_later",
    )(*blocks, *ints, *parts)


def finish_kernel(side, place, sums_ref, *rest):
    out_ref, both, made, sems = rest[-4:]
    blocks, rows, cols = made.shape
    left = lax.broadcasted_iota(jnp.int32, (rows, LANES), 1) < LANES // 2

    def copy_out(i):
        block = 2 * i + (lax.axis_index("core") ^ side)
        return pltpu.make_async_copy(made.at[i], out_ref.at[block], sems.at[i])

    for i in range(blocks):
        both[0] = sums_ref[i * rows : (i + 1) * rows]
        both[1] = half_turned(both[0])
        for q in range(cols // LANES):
            made[i, :, q * LANES : (q + 1) * LANES] = pick_pair(
                both, place[2 * q], place[2 * q + 1], left
            )
        copy_out(i).start()
    for i in range(blocks):
        copy_out(i).wait()


def finish(side, place, sums, rows, out=None):
    blocks, cols = sums.shape[0] // rows, sums.shape[1]
    before = [] if out is None else [out]
    return pl.pallas_call(
        functools.partial(finish_kernel, side),
        out_shape=jax.ShapeDtypeStruct((2 * blocks, rows, cols), jnp.bfloat16),
        in_specs=[SMEM, VMEM] + [ANY] * len(before),
        out_specs=ANY,
        scratch_shapes=[
            pltpu.VMEM((2, rows, cols), jnp.bfloat16),
            pltpu.VMEM((blocks, rows, cols), jnp.bfloat16),
            pltpu.SemaphoreType.DMA((blocks,)),
        ],
        input_output_aliases={2: 0} if before else {},
        compiler_params=params(),
        cost_estimate=CHEAP,
        name="finish",
    )(place, sums, *before)


SWAP = [(0, 1), (1, 0)]


def further(x, by):
    n_cd = lax.axis_size("cd")
    return lax.ppermute(x, "cd", [(i, (i + by) % n_cd) for i in range(n_cd)])


def to_plane(x, d):
    n_cd = lax.axis_size("cd")
    z_len = 2 * lax.axis_size("zh")
    rest = z_len // n_cd
    pairs = []
    for z in range(z_len):
        group, i = divmod(z, rest)
        for y in range(n_cd):
            pairs.append((z * n_cd + y, ((y * rest + i) ^ (2 * d)) * n_cd + group))
    return lax.ppermute(x, ("zh", "zl", "cd"), pairs)


def per_device(t2_amps, integrals, ab_sym, cd_sym):
    zh, n_cd = lax.axis_size("zh"), lax.axis_size("cd")
    def over(x, axis):
        return lax.ppermute(x, axis, SWAP)

    def along_zh(x):
        return [lax.ppermute(x, "zh", [(i, i ^ d) for i in range(zh)]) for d in range(1, zh)]

    first_later = tuple(range(NSYM - LATER, NSYM - LATER + FIRST_SENT))
    own, own_later, ints_later = sort_first(t2_amps, integrals, cd_sym, ab_sym, first_later)
    later = [[ints_later] + [further(ints_later, by) for by in range(1, n_cd)]]
    syms = (tuple(range(NSYM - LATER)), tuple(range(NSYM - LATER + FIRST_SENT, NSYM)))
    place, ints, ints_later = sort_ints(integrals, ab_sym, syms, own)
    x_o, block_l = over(own, "x"), over(own, "zl")
    blocks_h = along_zh(own)
    fence = join([y[None] for y in [block_l, *blocks_h]], [*later[0][1:], ints, x_o])
    x_lh = over(fence, "x")
    blocks_hl = [over(y, "zl") for y in blocks_h]
    ints = after(ints, fence)
    sib_ints = over(ints, "core")
    ints_later = after(ints_later, sib_ints)
    later.append([ints_later] + [further(ints_later, by) for by in range(1, n_cd)])
    own_later = after(own_later, fence)
    near = merge([to_plane(own_later, d) for d in range(zh)], [])
    x_hl = [over(y, "x") for y in blocks_hl]
    parts = []

    def send_parts(made):
        parts.extend([made[0]] + [further(made[by], by) for by in range(1, n_cd)])

    blocks = [own, *blocks_h, block_l, *blocks_hl]
    near_x = tuple(
        (k, True, tuple((zh * (k // 2) + d, None) for d in range(zh))) for k in (0, 2)
    )
    jobs = ((near_x, tuple(range(FIRST_MADE))),)
    send_parts(contract(n_cd, blocks, jobs, ints, sib_ints, later[1][1:]))
    n = len(blocks)
    blocks += [x_o, x_lh, *x_hl]
    far_x = (
        (1, True, ((n, None),) + tuple((n + 1, d) for d in range(1, zh))),
        (3, True, ((n + 1, 0),) + tuple((n + 1 + d, None) for d in range(1, zh))),
    )
    jobs = ((far_x, syms[0]), (near_x, syms[0][FIRST_MADE:]))
    made = contract(n_cd, blocks, jobs, ints, sib_ints, [near, *parts[1:]])
    send_parts(made)
    up, across = over(near, "zl"), over(near, "x")
    half = zh // 2
    blocks = [near, across, up, over(up[:half], "x"), over(across[half:], "zl")]
    where = [(k, False, tuple((k, i) for i in range(zh))) for k in range(3)]
    where.append((3, False, tuple((3 + i // half, i % half) for i in range(zh))))
    ints_later = join([x[by] for by in range(n_cd) for x in later], made[:1])
    ints_later = (ints_later, over(ints_later, "core"))
    sums, sib_sums = contract_later(n_cd, blocks, tuple(where), ints_later, parts)
    sib_sums = lax.ppermute(sib_sums, "core", SWAP)
    rows = t2_amps.shape[0]
    out = finish(0, place, sums, rows)
    out = finish(1, place, sib_sums, rows, out)
    return out.reshape(-1, out.shape[2])


def solution(mesh):
    n_blk, n_cd = mesh.devices.shape
    blk = ("zh", "zl", "x", "core")
    parted = Mesh(mesh.devices.reshape(n_blk // 8, 2, 2, 2, n_cd), blk + ("cd",))
    in_specs = (P(blk, "cd"), P(blk, None, "cd"), P(blk), P("cd"))
    return jax.shard_map(
        per_device, mesh=parted, in_specs=in_specs, out_specs=P("cd", blk), check_vma=False
    )
```

```python
import functools

import jax
import jax.numpy as jnp
from jax import lax
from jax.experimental import pallas as pl
from jax.experimental.pallas import tpu as pltpu
from jax.sharding import Mesh, PartitionSpec as P

NSYM = 8
LATER = 4
FIRST_SENT = 2
LANES = 128
VMEM_LIMIT = 20 * 2**20

ANY = pl.BlockSpec(memory_space=pl.ANY)
SMEM = pl.BlockSpec(memory_space=pltpu.SMEM)
VMEM = pl.BlockSpec(memory_space=pltpu.VMEM)

CHEAP = pl.CostEstimate(flops=1000, bytes_accessed=1000, transcendentals=0)


def params(limit=VMEM_LIMIT):
    return pltpu.CompilerParams(vmem_limit_bytes=limit)


def half_turned(x):
    half = LANES // 2
    return jnp.concatenate([x[:, half:], x[:, :half]], axis=1)


def rank_tiles(sym_ref, count_ref, order_ref, place_ref, tiles):
    for s in range(NSYM):
        count_ref[s] = s * (tiles // NSYM)

    def step(i, _):
        s = sym_ref[i]
        p = count_ref[s]
        count_ref[s] = p + 1
        order_ref[p] = i
        if place_ref is not None:
            place_ref[i] = p
        return 0

    lax.fori_loop(0, tiles, step, 0, unroll=8)


def pick_pair(both, a, b, left):
    columns = both.shape[2] // LANES
    a_col = lax.shift_right_logical(a, 1)
    b_col = lax.rem(lax.shift_right_logical(b + 1, 1) + columns - 1, columns)
    xa = both[a & 1, :, pl.ds(pl.multiple_of(a_col * LANES, LANES), LANES)]
    xb = both[(b & 1) ^ 1, :, pl.ds(pl.multiple_of(b_col * LANES, LANES), LANES)]
    return jnp.where(left, xa, xb)


def fetch_tiles(ints_ref, rows, order, syms, per_sym, sems):
    copies = []
    for sym in syms:
        for m in range(per_sym):
            p = len(copies)
            tile_ref = ints_ref.at[order[sym * per_sym + m]]
            copies.append(pltpu.make_async_copy(tile_ref, rows.at[p], sems.at[p]))
            copies[-1].start()
    return copies


def turn_tiles(rows, outs, per_sym):
    p = 0
    for out_ref in outs:
        for s in range(out_ref.shape[0]):
            tiles = rows[p : p + per_sym]
            out_ref[s] = tiles.reshape(per_sym * rows.shape[1], rows.shape[2]).T
            p += per_sym


def sort_first_kernel(syms, cd_ref, ab_ref, t2_ref, ints_ref, own_ref, later_ref, ints_out, *scratch):
    both, rows, count, order, order_ab, place, sem, sems = scratch
    load = pltpu.make_async_copy(t2_ref, both.at[0], sem)
    load.start()
    tiles = ab_ref.shape[0]
    rank_tiles(ab_ref, count, order_ab, place, tiles)
    copies = fetch_tiles(ints_ref, rows, order_ab, syms, tiles // NSYM, sems)
    rank_tiles(cd_ref, count, order, None, cd_ref.shape[0])
    load.wait()
    both[1] = half_turned(both[0])
    left = lax.broadcasted_iota(jnp.int32, (t2_ref.shape[0], LANES), 1) < LANES // 2
    q = 0
    for chunk in (own_ref, later_ref):
        for off in range(chunk.shape[1] // LANES):
            chunk[:, off * LANES : (off + 1) * LANES] = pick_pair(
                both, order[2 * q], order[2 * q + 1], left
            )
            q += 1
    for copy in copies:
        copy.wait()
    turn_tiles(rows, (ints_out,), tiles // NSYM)


def sort_first(t2, integrals, cd_sym, ab_sym, syms):
    rows, cols = t2.shape
    tiles, tile, packed = integrals.shape
    per_sym = tiles // NSYM
    return pl.pallas_call(
        functools.partial(sort_first_kernel, syms),
        out_shape=[
            jax.ShapeDtypeStruct((rows, cols // NSYM * m), t2.dtype) for m in (NSYM - LATER, LATER)
        ]
        + [jax.ShapeDtypeStruct((len(syms), packed, per_sym * tile), integrals.dtype)],
        in_specs=[SMEM, SMEM, ANY, ANY],
        out_specs=[VMEM] * 3,
        scratch_shapes=[
            pltpu.VMEM((2, rows, cols), t2.dtype),
            pltpu.VMEM((len(syms) * per_sym, tile, packed), integrals.dtype),
            pltpu.SMEM((NSYM,), jnp.int32),
            pltpu.SMEM((cd_sym.shape[0],), jnp.int32),
            pltpu.SMEM((tiles,), jnp.int32),
            pltpu.SMEM((tiles,), jnp.int32),
            pltpu.SemaphoreType.DMA,
            pltpu.SemaphoreType.DMA((len(syms) * per_sym,)),
        ],
        compiler_params=params(60 * 2**20),
        cost_estimate=CHEAP,
        name="sort_first",
    )(cd_sym, ab_sym, t2, integrals)


def sort_ints_kernel(syms, ab_ref, ints_ref, _, place, *rest):
    outs, (rows, count, order, sems) = rest[:-4], rest[-4:]
    tiles = ab_ref.shape[0]
    rank_tiles(ab_ref, count, order, place, tiles)
    every = [sym for part in syms for sym in part]
    for copy in fetch_tiles(ints_ref, rows, order, every, tiles // NSYM, sems):
        copy.wait()
    turn_tiles(rows, outs, tiles // NSYM)


def sort_ints(integrals, ab_sym, syms, earlier):
    tiles, tile, packed = integrals.shape
    per_sym = tiles // NSYM
    used = sum(len(part) for part in syms) * per_sym
    return pl.pallas_call(
        functools.partial(sort_ints_kernel, syms),
        out_shape=[jax.ShapeDtypeStruct((tiles,), jnp.int32)]
        + [
            jax.ShapeDtypeStruct((len(part), packed, per_sym * tile), integrals.dtype)
            for part in syms
        ],
        in_specs=[SMEM, ANY, ANY],
        out_specs=[SMEM] + [VMEM] * len(syms),
        scratch_shapes=[
            pltpu.VMEM((used, tile, packed), integrals.dtype),
            pltpu.SMEM((NSYM,), jnp.int32),
            pltpu.SMEM((tiles,), jnp.int32),
            pltpu.SemaphoreType.DMA((used,)),
        ],
        compiler_params=params(),
        cost_estimate=CHEAP,
        name="sort_ints",
    )(ab_sym, integrals, earlier)


def merge_kernel(n, *refs):
    blocks, out_ref = refs[:n], refs[-1]
    me = lax.axis_index("zh")
    for d, block in enumerate(blocks):
        out_ref[me ^ d] = block[...]


def merge(blocks, earlier):
    return pl.pallas_call(
        functools.partial(merge_kernel, len(blocks)),
        out_shape=jax.ShapeDtypeStruct((len(blocks),) + blocks[0].shape, blocks[0].dtype),
        in_specs=[VMEM] * len(blocks) + [ANY] * len(earlier),
        out_specs=VMEM,
        compiler_params=params(),
        cost_estimate=CHEAP,
        name="merge",
    )(*blocks, *earlier)


def nothing(*refs):
    pass


def after(x, *earlier):
    n = len(earlier)
    return pl.pallas_call(
        nothing,
        out_shape=jax.ShapeDtypeStruct(x.shape, x.dtype),
        in_specs=[ANY] * (n + 1),
        out_specs=ANY,
        input_output_aliases={n: 0},
        compiler_params=params(),
        cost_estimate=CHEAP,
        name="after",
    )(*earlier, x)


def lay_out(lhs, refs, where, place):
    h, z, x = lax.axis_index("zh"), lax.axis_index("zl"), lax.axis_index("x")
    for k, (by_difference, quarter) in enumerate(where):
        for i, (array, entry) in enumerate(quarter):
            slot = 4 * (h ^ i if by_difference else i) + 2 * (z ^ (k // 2)) + (x ^ (k % 2))
            ref = refs[array]
            lhs[place(slot)] = ref[...] if entry is None else ref[entry]


def contract_kernel(n_cd, first_sym, n_blocks, where, *refs):
    blocks, (own_ref, sib_ref) = refs[:n_blocks], refs[n_blocks : n_blocks + 2]
    outs, lhs = refs[-n_cd - 1 : -1], refs[-1]
    slots, rows, cols = lhs.shape
    packed, width = own_ref.shape[1:]
    first = lax.axis_index("cd") * (slots // n_cd)
    lay_out(lhs, blocks, where, lambda n: lax.rem(n + slots - first, slots))
    t2 = lhs[...].reshape(slots * rows, cols)
    group_rows = t2.shape[0] // n_cd
    for side, ints in enumerate((own_ref, sib_ref)):
        for s in range(cols // packed):
            part = jnp.dot(
                t2[:, s * packed : (s + 1) * packed],
                ints[first_sym + s],
                preferred_element_type=jnp.float32,
            ).astype(outs[0].dtype)
            for by in range(n_cd):
                outs[by][side, :, s * width : (s + 1) * width] = part[
                    by * group_rows : (by + 1) * group_rows
                ]


def contract(n_cd, t2s, ints, sib_ints, first_sym, earlier):
    blocks, where = t2s
    rows, cols = blocks[0].shape[-2:]
    slots = 4 * len(where[0][1])
    packed, width = ints.shape[1:]
    out = (2, slots * rows // n_cd, cols // packed * width)
    return pl.pallas_call(
        functools.partial(contract_kernel, n_cd, first_sym, len(blocks), where),
        out_shape=[jax.ShapeDtypeStruct(out, jnp.bfloat16)] * n_cd,
        in_specs=[VMEM] * (len(blocks) + 2) + [ANY] * len(earlier),
        out_specs=[VMEM] * n_cd,
        scratch_shapes=[pltpu.VMEM((slots, rows, cols), jnp.bfloat16)],
        compiler_params=params(),
        cost_estimate=CHEAP,
        name="contract",
    )(*blocks, ints, sib_ints, *earlier)


def total(parts):
    value = parts[0].astype(jnp.float32)
    for part in parts[1:]:
        value += part.astype(jnp.float32)
    return value.astype(jnp.bfloat16)


def join_kernel(n, *refs):
    out_ref, first = refs[-1], 0
    for ref in refs[-n - 1 : -1]:
        out_ref[first : first + ref.shape[0]] = ref[...]
        first += ref.shape[0]


def join(arrays, earlier):
    n = len(arrays)
    out = (sum(x.shape[0] for x in arrays), *arrays[0].shape[1:])
    return pl.pallas_call(
        functools.partial(join_kernel, n),
        out_shape=jax.ShapeDtypeStruct(out, arrays[0].dtype),
        in_specs=[ANY] * len(earlier) + [VMEM] * n,
        out_specs=VMEM,
        compiler_params=params(),
        cost_estimate=CHEAP,
        name="join",
    )(*earlier, *arrays)


def later_kernel(n_cd, n_blocks, where, *refs):
    blocks, ints, parts = refs[:n_blocks], refs[n_blocks : n_blocks + 2], refs[n_blocks + 2 : -3]
    own_out, sib_out, lhs = refs[-3:]
    slots, rows, cols = lhs.shape
    packed, width = ints[0].shape[1:]
    per_group, me = slots // n_cd, lax.axis_index("cd")

    def place(n):
        group = lax.div(n, per_group)
        return lax.rem(me + n_cd - group, n_cd) * per_group + (n - group * per_group)

    lay_out(lhs, blocks, where, place)
    t2 = lhs[...].reshape(n_cd, per_group * rows, cols)
    for side, out_ref in enumerate((own_out, sib_out)):
        first = 0
        for c in range(0, len(parts), n_cd):
            value = total([part[side] for part in parts[c : c + n_cd]])
            out_ref[:, first : first + value.shape[1]] = value
            first += value.shape[1]
        for s in range(LATER):
            out_ref[:, first : first + width] = total(
                [
                    jnp.dot(
                        t2[by, :, s * packed : (s + 1) * packed],
                        ints[side][by * LATER + s],
                        preferred_element_type=jnp.float32,
                    ).astype(out_ref.dtype)
                    for by in range(n_cd)
                ]
            )
            first += width


def contract_later(n_cd, t2s, ints, parts):
    blocks, where = t2s
    rows, cols = blocks[0].shape[-2:]
    width = ints[0].shape[2] * LATER + sum(p.shape[2] for p in parts[::n_cd])
    out = jax.ShapeDtypeStruct((parts[0].shape[1], width), jnp.bfloat16)
    return pl.pallas_call(
        functools.partial(later_kernel, n_cd, len(blocks), where),
        out_shape=[out, out],
        in_specs=[VMEM] * (len(blocks) + 2 + len(parts)),
        out_specs=[VMEM] * 2,
        scratch_shapes=[pltpu.VMEM((4 * len(where[0][1]), rows, cols), jnp.bfloat16)],
        compiler_params=params(),
        cost_estimate=CHEAP,
        name="contract_later",
    )(*blocks, *ints, *parts)


def finish_kernel(side, place, sums_ref, *rest):
    out_ref, both, made, sems = rest[-4:]
    blocks, rows, cols = made.shape
    left = lax.broadcasted_iota(jnp.int32, (rows, LANES), 1) < LANES // 2

    def copy_out(i):
        block = 2 * i + (lax.axis_index("core") ^ side)
        return pltpu.make_async_copy(made.at[i], out_ref.at[block], sems.at[i])

    for i in range(blocks):
        both[0] = sums_ref[i * rows : (i + 1) * rows]
        both[1] = half_turned(both[0])
        for q in range(cols // LANES):
            made[i, :, q * LANES : (q + 1) * LANES] = pick_pair(
                both, place[2 * q], place[2 * q + 1], left
            )
        copy_out(i).start()
    for i in range(blocks):
        copy_out(i).wait()


def finish(side, place, sums, rows, out=None):
    blocks, cols = sums.shape[0] // rows, sums.shape[1]
    before = [] if out is None else [out]
    return pl.pallas_call(
        functools.partial(finish_kernel, side),
        out_shape=jax.ShapeDtypeStruct((2 * blocks, rows, cols), jnp.bfloat16),
        in_specs=[SMEM, VMEM] + [ANY] * len(before),
        out_specs=ANY,
        scratch_shapes=[
            pltpu.VMEM((2, rows, cols), jnp.bfloat16),
            pltpu.VMEM((blocks, rows, cols), jnp.bfloat16),
            pltpu.SemaphoreType.DMA((blocks,)),
        ],
        input_output_aliases={2: 0} if before else {},
        compiler_params=params(),
        cost_estimate=CHEAP,
        name="finish",
    )(place, sums, *before)


SWAP = [(0, 1), (1, 0)]


def further(x, by):
    n_cd = lax.axis_size("cd")
    return lax.ppermute(x, "cd", [(i, (i + by) % n_cd) for i in range(n_cd)])


def to_plane(x, d):
    n_cd = lax.axis_size("cd")
    z_len = 2 * lax.axis_size("zh")
    rest = z_len // n_cd
    pairs = []
    for z in range(z_len):
        group, i = divmod(z, rest)
        for y in range(n_cd):
            pairs.append((z * n_cd + y, ((y * rest + i) ^ (2 * d)) * n_cd + group))
    return lax.ppermute(x, ("zh", "zl", "cd"), pairs)


def per_device(t2_amps, integrals, ab_sym, cd_sym):
    zh, n_cd = lax.axis_size("zh"), lax.axis_size("cd")
    def over(x, axis):
        return lax.ppermute(x, axis, SWAP)

    def along_zh(x):
        return [lax.ppermute(x, "zh", [(i, i ^ d) for i in range(zh)]) for d in range(1, zh)]

    first_later = tuple(range(NSYM - LATER, NSYM - LATER + FIRST_SENT))
    own, own_later, ints_later = sort_first(t2_amps, integrals, cd_sym, ab_sym, first_later)
    later = [[ints_later] + [further(ints_later, by) for by in range(1, n_cd)]]
    syms = (tuple(range(NSYM - LATER)), tuple(range(NSYM - LATER + FIRST_SENT, NSYM)))
    place, ints, ints_later = sort_ints(integrals, ab_sym, syms, own)
    x_o, block_l = over(own, "x"), over(own, "zl")
    blocks_h = along_zh(own)
    fence = join([y[None] for y in [block_l, *blocks_h]], [*later[0][1:], ints, x_o])
    x_lh = over(fence, "x")
    blocks_hl = [over(y, "zl") for y in blocks_h]
    ints = after(ints, fence)
    sib_ints = over(ints, "core")
    ints_later = after(ints_later, sib_ints)
    later.append([ints_later] + [further(ints_later, by) for by in range(1, n_cd)])
    near = [to_plane(after(own_later, fence), d) for d in range(1, zh)]
    near = merge([to_plane(after(own_later, fence), 0)] + near, [])
    x_hl = [over(y, "x") for y in blocks_hl]
    blocks = [own, *blocks_h, x_o, x_lh, block_l, *blocks_hl, *x_hl]
    where = (
        tuple((d, None) for d in range(zh)),
        ((zh, None),) + tuple((zh + 1, d) for d in range(1, zh)),
        tuple((zh + 2 + d, None) for d in range(zh)),
        ((zh + 1, 0),) + tuple((2 * zh + 1 + d, None) for d in range(1, zh)),
    )
    where = tuple((True, quarter) for quarter in where)
    made = contract(n_cd, (blocks, where), ints, sib_ints, 0, [near, *later[1][1:]])
    parts = [made[0]] + [further(made[by], by) for by in range(1, n_cd)]
    up, across = over(near, "zl"), over(near, "x")
    half = zh // 2
    blocks = [near, across, up, over(up[:half], "x"), over(across[half:], "zl")]
    where = tuple((False, tuple((k, i) for i in range(zh))) for k in range(3))
    where += ((False, tuple((3 + i // half, i % half) for i in range(zh))),)
    t2s = blocks, where
    ints_later = join([x[by] for by in range(n_cd) for x in later], made[:1])
    ints_later = (ints_later, over(ints_later, "core"))
    sums, sib_sums = contract_later(n_cd, t2s, ints_later, parts)
    sib_sums = lax.ppermute(sib_sums, "core", SWAP)
    rows = t2_amps.shape[0]
    out = finish(0, place, sums, rows)
    out = finish(1, place, sib_sums, rows, out)
    return out.reshape(-1, out.shape[2])


def solution(mesh):
    n_blk, n_cd = mesh.devices.shape
    blk = ("zh", "zl", "x", "core")
    parted = Mesh(mesh.devices.reshape(n_blk // 8, 2, 2, 2, n_cd), blk + ("cd",))
    in_specs = (P(blk, "cd"), P(blk, None, "cd"), P(blk), P("cd"))
    return jax.shard_map(
        per_device, mesh=parted, in_specs=in_specs, out_specs=P("cd", blk), check_vma=False
    )
```

```python
import functools

import jax
import jax.numpy as jnp
from jax import lax
from jax.experimental import pallas as pl
from jax.experimental.pallas import tpu as pltpu
from jax.sharding import Mesh, PartitionSpec as P

NSYM = 8
LATER = 4
FIRST_SENT = 2
LANES = 128
VMEM_LIMIT = 20 * 2**20

ANY = pl.BlockSpec(memory_space=pl.ANY)
SMEM = pl.BlockSpec(memory_space=pltpu.SMEM)
VMEM = pl.BlockSpec(memory_space=pltpu.VMEM)

CHEAP = pl.CostEstimate(flops=1000, bytes_accessed=1000, transcendentals=0)


def params(limit=VMEM_LIMIT):
    return pltpu.CompilerParams(vmem_limit_bytes=limit)


def half_turned(x):
    half = LANES // 2
    return jnp.concatenate([x[:, half:], x[:, :half]], axis=1)


def rank_tiles(sym_ref, count_ref, order_ref, place_ref, tiles):
    for s in range(NSYM):
        count_ref[s] = s * (tiles // NSYM)

    def step(i, _):
        s = sym_ref[i]
        p = count_ref[s]
        count_ref[s] = p + 1
        order_ref[p] = i
        if place_ref is not None:
            place_ref[i] = p
        return 0

    lax.fori_loop(0, tiles, step, 0, unroll=8)


def pick_pair(both, a, b, left):
    columns = both.shape[2] // LANES
    a_col = lax.shift_right_logical(a, 1)
    b_col = lax.rem(lax.shift_right_logical(b + 1, 1) + columns - 1, columns)
    xa = both[a & 1, :, pl.ds(pl.multiple_of(a_col * LANES, LANES), LANES)]
    xb = both[(b & 1) ^ 1, :, pl.ds(pl.multiple_of(b_col * LANES, LANES), LANES)]
    return jnp.where(left, xa, xb)


def fetch_tiles(ints_ref, rows, order, syms, per_sym, sems):
    copies = []
    for sym in syms:
        for m in range(per_sym):
            p = len(copies)
            tile_ref = ints_ref.at[order[sym * per_sym + m]]
            copies.append(pltpu.make_async_copy(tile_ref, rows.at[p], sems.at[p]))
            copies[-1].start()
    return copies


def turn_tiles(rows, outs, per_sym):
    p = 0
    for out_ref in outs:
        for s in range(out_ref.shape[0]):
            tiles = rows[p : p + per_sym]
            out_ref[s] = tiles.reshape(per_sym * rows.shape[1], rows.shape[2]).T
            p += per_sym


def sort_first_kernel(syms, cd_ref, ab_ref, t2_ref, ints_ref, own_ref, later_ref, ints_out, *scratch):
    both, rows, count, order, order_ab, place, sem, sems = scratch
    load = pltpu.make_async_copy(t2_ref, both.at[0], sem)
    load.start()
    tiles = ab_ref.shape[0]
    rank_tiles(ab_ref, count, order_ab, place, tiles)
    copies = fetch_tiles(ints_ref, rows, order_ab, syms, tiles // NSYM, sems)
    rank_tiles(cd_ref, count, order, None, cd_ref.shape[0])
    load.wait()
    both[1] = half_turned(both[0])
    left = lax.broadcasted_iota(jnp.int32, (t2_ref.shape[0], LANES), 1) < LANES // 2
    q = 0
    for chunk in (own_ref, later_ref):
        for off in range(chunk.shape[1] // LANES):
            chunk[:, off * LANES : (off + 1) * LANES] = pick_pair(
                both, order[2 * q], order[2 * q + 1], left
            )
            q += 1
    for copy in copies:
        copy.wait()
    turn_tiles(rows, (ints_out,), tiles // NSYM)


def sort_first(t2, integrals, cd_sym, ab_sym, syms):
    rows, cols = t2.shape
    tiles, tile, packed = integrals.shape
    per_sym = tiles // NSYM
    return pl.pallas_call(
        functools.partial(sort_first_kernel, syms),
        out_shape=[
            jax.ShapeDtypeStruct((rows, cols // NSYM * m), t2.dtype) for m in (NSYM - LATER, LATER)
        ]
        + [jax.ShapeDtypeStruct((len(syms), packed, per_sym * tile), integrals.dtype)],
        in_specs=[SMEM, SMEM, ANY, ANY],
        out_specs=[VMEM] * 3,
        scratch_shapes=[
            pltpu.VMEM((2, rows, cols), t2.dtype),
            pltpu.VMEM((len(syms) * per_sym, tile, packed), integrals.dtype),
            pltpu.SMEM((NSYM,), jnp.int32),
            pltpu.SMEM((cd_sym.shape[0],), jnp.int32),
            pltpu.SMEM((tiles,), jnp.int32),
            pltpu.SMEM((tiles,), jnp.int32),
            pltpu.SemaphoreType.DMA,
            pltpu.SemaphoreType.DMA((len(syms) * per_sym,)),
        ],
        compiler_params=params(60 * 2**20),
        cost_estimate=CHEAP,
        name="sort_first",
    )(cd_sym, ab_sym, t2, integrals)


def sort_ints_kernel(syms, ab_ref, ints_ref, _, place, *rest):
    outs, (rows, count, order, sems) = rest[:-4], rest[-4:]
    tiles = ab_ref.shape[0]
    rank_tiles(ab_ref, count, order, place, tiles)
    every = [sym for part in syms for sym in part]
    for copy in fetch_tiles(ints_ref, rows, order, every, tiles // NSYM, sems):
        copy.wait()
    turn_tiles(rows, outs, tiles // NSYM)


def sort_ints(integrals, ab_sym, syms, earlier):
    tiles, tile, packed = integrals.shape
    per_sym = tiles // NSYM
    used = sum(len(part) for part in syms) * per_sym
    return pl.pallas_call(
        functools.partial(sort_ints_kernel, syms),
        out_shape=[jax.ShapeDtypeStruct((tiles,), jnp.int32)]
        + [
            jax.ShapeDtypeStruct((len(part), packed, per_sym * tile), integrals.dtype)
            for part in syms
        ],
        in_specs=[SMEM, ANY, ANY],
        out_specs=[SMEM] + [VMEM] * len(syms),
        scratch_shapes=[
            pltpu.VMEM((used, tile, packed), integrals.dtype),
            pltpu.SMEM((NSYM,), jnp.int32),
            pltpu.SMEM((tiles,), jnp.int32),
            pltpu.SemaphoreType.DMA((used,)),
        ],
        compiler_params=params(),
        cost_estimate=CHEAP,
        name="sort_ints",
    )(ab_sym, integrals, earlier)


def merge_kernel(n, *refs):
    blocks, out_ref = refs[:n], refs[-1]
    me = lax.axis_index("zh")
    for d, block in enumerate(blocks):
        out_ref[me ^ d] = block[...]


def merge(blocks, earlier):
    return pl.pallas_call(
        functools.partial(merge_kernel, len(blocks)),
        out_shape=jax.ShapeDtypeStruct((len(blocks),) + blocks[0].shape, blocks[0].dtype),
        in_specs=[VMEM] * len(blocks) + [ANY] * len(earlier),
        out_specs=VMEM,
        compiler_params=params(),
        cost_estimate=CHEAP,
        name="merge",
    )(*blocks, *earlier)


def nothing(*refs):
    pass


def after(x, *earlier):
    n = len(earlier)
    return pl.pallas_call(
        nothing,
        out_shape=jax.ShapeDtypeStruct(x.shape, x.dtype),
        in_specs=[ANY] * (n + 1),
        out_specs=ANY,
        input_output_aliases={n: 0},
        compiler_params=params(),
        cost_estimate=CHEAP,
        name="after",
    )(*earlier, x)


def lay_out(lhs, refs, where, place):
    h, z, x = lax.axis_index("zh"), lax.axis_index("zl"), lax.axis_index("x")
    for k, by_difference, quarter in where:
        for i, (array, entry) in enumerate(quarter):
            row = place(2 * (h ^ i if by_difference else i) + (z ^ (k // 2)), x ^ (k % 2))
            lhs[row] = refs[array][...] if entry is None else refs[array][entry]


def contract_kernel(n_cd, n_blocks, n_before, where, *refs):
    blocks, ints_refs = refs[:n_blocks], refs[n_blocks : n_blocks + 2]
    before = refs[n_blocks + 2 : n_blocks + 2 + n_before]
    outs, lhs = refs[-n_cd - 1 : -1], refs[-1]
    start = before[0].shape[1] if before else 0
    for out, ref in zip(outs, before):
        out[:, :start] = ref[...]
    z_len, rows, cols = lhs.shape
    packed, width = ints_refs[0].shape[1:]
    first = lax.axis_index("cd") * (z_len // n_cd)
    lay_out(lhs, blocks, where, lambda z, x: lax.rem(z + z_len - first, z_len))
    t2 = lhs[...].reshape(z_len * rows, cols)
    group_rows = t2.shape[0] // n_cd
    for side, ints in enumerate(ints_refs):
        for s in range(cols // packed):
            part = jnp.dot(
                t2[:, s * packed : (s + 1) * packed], ints[s], preferred_element_type=jnp.float32
            ).astype(outs[0].dtype)
            for by in range(n_cd):
                outs[by][side, start:, s * width : (s + 1) * width] = part[
                    by * group_rows : (by + 1) * group_rows
                ]


def contract(n_cd, blocks, where, ints, sib_ints, before, earlier):
    rows, cols = blocks[0].shape[-2:]
    z_len = 2 * len(where[0][2])
    packed, width = ints.shape[1:]
    start = before[0].shape[1] if before else 0
    out = (2, start + z_len * rows // n_cd, cols // packed * width)
    return pl.pallas_call(
        functools.partial(contract_kernel, n_cd, len(blocks), len(before), where),
        out_shape=[jax.ShapeDtypeStruct(out, jnp.bfloat16)] * n_cd,
        in_specs=[VMEM] * (len(blocks) + 2 + len(before)) + [ANY] * len(earlier),
        out_specs=[VMEM] * n_cd,
        scratch_shapes=[pltpu.VMEM((z_len, rows, cols), jnp.bfloat16)],
        compiler_params=params(),
        cost_estimate=CHEAP,
        name="contract",
    )(*blocks, ints, sib_ints, *before, *earlier)


def total(parts):
    value = parts[0].astype(jnp.float32)
    for part in parts[1:]:
        value += part.astype(jnp.float32)
    return value.astype(jnp.bfloat16)


def join_kernel(n, *refs):
    out_ref, first = refs[-1], 0
    for ref in refs[-n - 1 : -1]:
        out_ref[first : first + ref.shape[0]] = ref[...]
        first += ref.shape[0]


def join(arrays, earlier):
    n = len(arrays)
    out = (sum(x.shape[0] for x in arrays), *arrays[0].shape[1:])
    return pl.pallas_call(
        functools.partial(join_kernel, n),
        out_shape=jax.ShapeDtypeStruct(out, arrays[0].dtype),
        in_specs=[ANY] * len(earlier) + [VMEM] * n,
        out_specs=VMEM,
        compiler_params=params(),
        cost_estimate=CHEAP,
        name="join",
    )(*earlier, *arrays)


def later_kernel(n_cd, n_blocks, where, *refs):
    blocks, ints, parts = refs[:n_blocks], refs[n_blocks : n_blocks + 2], refs[n_blocks + 2 : -3]
    own_out, sib_out, lhs = refs[-3:]
    slots, rows, cols = lhs.shape
    packed, width = ints[0].shape[1:]
    per_group, me, x = slots // n_cd, lax.axis_index("cd"), lax.axis_index("x")

    def place(z, x):
        n = 2 * z + x
        group = lax.div(n, per_group)
        return lax.rem(me + n_cd - group, n_cd) * per_group + (n - group * per_group)

    lay_out(lhs, blocks, where, place)
    t2 = lhs[...].reshape(n_cd, per_group * rows, cols)
    for side, out_ref in enumerate((own_out, sib_out)):
        first = parts[0].shape[2]
        for half in range(2):
            for z in range(per_group // 2):
                these = pl.ds(pl.multiple_of((2 * z + (x ^ half)) * rows, rows), rows)
                at = (half * per_group // 2 + z) * rows
                out_ref[these, :first] = total([part[side, at : at + rows] for part in parts])
        for s in range(LATER):
            out_ref[:, first : first + width] = total(
                [
                    jnp.dot(
                        t2[by, :, s * packed : (s + 1) * packed],
                        ints[side][by * LATER + s],
                        preferred_element_type=jnp.float32,
                    ).astype(out_ref.dtype)
                    for by in range(n_cd)
                ]
            )
            first += width


def contract_later(n_cd, blocks, where, ints, parts):
    rows, cols = blocks[0].shape[-2:]
    slots = 4 * len(where[0][2])
    out = (slots * rows // n_cd, parts[0].shape[2] + ints[0].shape[2] * LATER)
    return pl.pallas_call(
        functools.partial(later_kernel, n_cd, len(blocks), where),
        out_shape=[jax.ShapeDtypeStruct(out, jnp.bfloat16)] * 2,
        in_specs=[VMEM] * (len(blocks) + 2 + len(parts)),
        out_specs=[VMEM] * 2,
        scratch_shapes=[pltpu.VMEM((slots, rows, cols), jnp.bfloat16)],
        compiler_params=params(),
        cost_estimate=CHEAP,
        name="contract_later",
    )(*blocks, *ints, *parts)


def finish_kernel(side, place, sums_ref, *rest):
    out_ref, both, made, sems = rest[-4:]
    blocks, rows, cols = made.shape
    left = lax.broadcasted_iota(jnp.int32, (rows, LANES), 1) < LANES // 2

    def copy_out(i):
        block = 2 * i + (lax.axis_index("core") ^ side)
        return pltpu.make_async_copy(made.at[i], out_ref.at[block], sems.at[i])

    for i in range(blocks):
        both[0] = sums_ref[i * rows : (i + 1) * rows]
        both[1] = half_turned(both[0])
        for q in range(cols // LANES):
            made[i, :, q * LANES : (q + 1) * LANES] = pick_pair(
                both, place[2 * q], place[2 * q + 1], left
            )
        copy_out(i).start()
    for i in range(blocks):
        copy_out(i).wait()


def finish(side, place, sums, rows, out=None):
    blocks, cols = sums.shape[0] // rows, sums.shape[1]
    before = [] if out is None else [out]
    return pl.pallas_call(
        functools.partial(finish_kernel, side),
        out_shape=jax.ShapeDtypeStruct((2 * blocks, rows, cols), jnp.bfloat16),
        in_specs=[SMEM, VMEM] + [ANY] * len(before),
        out_specs=ANY,
        scratch_shapes=[
            pltpu.VMEM((2, rows, cols), jnp.bfloat16),
            pltpu.VMEM((blocks, rows, cols), jnp.bfloat16),
            pltpu.SemaphoreType.DMA((blocks,)),
        ],
        input_output_aliases={2: 0} if before else {},
        compiler_params=params(),
        cost_estimate=CHEAP,
        name="finish",
    )(place, sums, *before)


SWAP = [(0, 1), (1, 0)]


def further(x, by):
    n_cd = lax.axis_size("cd")
    return lax.ppermute(x, "cd", [(i, (i + by) % n_cd) for i in range(n_cd)])


def to_plane(x, d):
    n_cd = lax.axis_size("cd")
    z_len = 2 * lax.axis_size("zh")
    rest = z_len // n_cd
    pairs = []
    for z in range(z_len):
        group, i = divmod(z, rest)
        for y in range(n_cd):
            pairs.append((z * n_cd + y, ((y * rest + i) ^ (2 * d)) * n_cd + group))
    return lax.ppermute(x, ("zh", "zl", "cd"), pairs)


def per_device(t2_amps, integrals, ab_sym, cd_sym):
    zh, n_cd = lax.axis_size("zh"), lax.axis_size("cd")
    def over(x, axis):
        return lax.ppermute(x, axis, SWAP)

    def along_zh(x):
        return [lax.ppermute(x, "zh", [(i, i ^ d) for i in range(zh)]) for d in range(1, zh)]

    first_later = tuple(range(NSYM - LATER, NSYM - LATER + FIRST_SENT))
    own, own_later, ints_later = sort_first(t2_amps, integrals, cd_sym, ab_sym, first_later)
    later = [[ints_later] + [further(ints_later, by) for by in range(1, n_cd)]]
    syms = (tuple(range(NSYM - LATER)), tuple(range(NSYM - LATER + FIRST_SENT, NSYM)))
    place, ints, ints_later = sort_ints(integrals, ab_sym, syms, own)
    x_o, block_l = over(own, "x"), over(own, "zl")
    blocks_h = along_zh(own)
    fence = join([y[None] for y in [block_l, *blocks_h]], [*later[0][1:], ints, x_o])
    x_lh = over(fence, "x")
    blocks_hl = [over(y, "zl") for y in blocks_h]
    ints = after(ints, fence)
    sib_ints = over(ints, "core")
    ints_later = after(ints_later, fence)
    later.append([ints_later] + [further(ints_later, by) for by in range(1, n_cd)])
    near = [to_plane(after(own_later, fence), d) for d in range(1, zh)]
    near = merge([to_plane(after(own_later, sib_ints), 0)] + near, [])
    blocks = [own, *blocks_h, block_l, *blocks_hl]
    where = [(k, True, tuple((zh * (k // 2) + d, None) for d in range(zh))) for k in (0, 2)]
    before = contract(n_cd, blocks, tuple(where), ints, sib_ints, [], [])
    x_hl = [over(after(y, before[0]), "x") for y in blocks_hl]
    blocks = [x_o, x_lh, *x_hl]
    where = (
        (1, True, ((0, None),) + tuple((1, d) for d in range(1, zh))),
        (3, True, ((1, 0),) + tuple((1 + d, None) for d in range(1, zh))),
    )
    made = contract(n_cd, blocks, where, ints, sib_ints, before, [near, *later[1][1:]])
    parts = [made[0]] + [further(made[by], by) for by in range(1, n_cd)]
    up, across = over(near, "zl"), over(near, "x")
    half = zh // 2
    blocks = [near, across, up, over(up[:half], "x"), over(across[half:], "zl")]
    where = [(k, False, tuple((k, i) for i in range(zh))) for k in range(3)]
    where.append((3, False, tuple((3 + i // half, i % half) for i in range(zh))))
    ints_later = join([x[by] for by in range(n_cd) for x in later], made[:1])
    ints_later = (ints_later, over(ints_later, "core"))
    sums, sib_sums = contract_later(n_cd, blocks, tuple(where), ints_later, parts)
    sib_sums = lax.ppermute(sib_sums, "core", SWAP)
    rows = t2_amps.shape[0]
    out = finish(0, place, sums, rows)
    out = finish(1, place, sib_sums, rows, out)
    return out.reshape(-1, out.shape[2])


def solution(mesh):
    n_blk, n_cd = mesh.devices.shape
    blk = ("zh", "zl", "x", "core")
    parted = Mesh(mesh.devices.reshape(n_blk // 8, 2, 2, 2, n_cd), blk + ("cd",))
    in_specs = (P(blk, "cd"), P(blk, None, "cd"), P(blk), P("cd"))
    return jax.shard_map(
        per_device, mesh=parted, in_specs=in_specs, out_specs=P("cd", blk), check_vma=False
    )
```

```python
import functools

import jax
import jax.numpy as jnp
from jax import lax
from jax.experimental import pallas as pl
from jax.experimental.pallas import tpu as pltpu
from jax.sharding import Mesh, PartitionSpec as P

NSYM = 8
LATER = 4
FIRST_SENT = 2
LANES = 128
VMEM_LIMIT = 20 * 2**20

ANY = pl.BlockSpec(memory_space=pl.ANY)
SMEM = pl.BlockSpec(memory_space=pltpu.SMEM)
VMEM = pl.BlockSpec(memory_space=pltpu.VMEM)

CHEAP = pl.CostEstimate(flops=1000, bytes_accessed=1000, transcendentals=0)


def params(limit=VMEM_LIMIT):
    return pltpu.CompilerParams(vmem_limit_bytes=limit)


def half_turned(x):
    half = LANES // 2
    return jnp.concatenate([x[:, half:], x[:, :half]], axis=1)


def rank_tiles(sym_ref, count_ref, order_ref, place_ref, tiles):
    for s in range(NSYM):
        count_ref[s] = s * (tiles // NSYM)

    def step(i, _):
        s = sym_ref[i]
        p = count_ref[s]
        count_ref[s] = p + 1
        order_ref[p] = i
        if place_ref is not None:
            place_ref[i] = p
        return 0

    lax.fori_loop(0, tiles, step, 0, unroll=8)


def pick_pair(both, a, b, left):
    columns = both.shape[2] // LANES
    a_col = lax.shift_right_logical(a, 1)
    b_col = lax.rem(lax.shift_right_logical(b + 1, 1) + columns - 1, columns)
    xa = both[a & 1, :, pl.ds(pl.multiple_of(a_col * LANES, LANES), LANES)]
    xb = both[(b & 1) ^ 1, :, pl.ds(pl.multiple_of(b_col * LANES, LANES), LANES)]
    return jnp.where(left, xa, xb)


def fetch_tiles(ints_ref, rows, order, syms, per_sym, sems):
    copies = []
    for sym in syms:
        for m in range(per_sym):
            p = len(copies)
            tile_ref = ints_ref.at[order[sym * per_sym + m]]
            copies.append(pltpu.make_async_copy(tile_ref, rows.at[p], sems.at[p]))
            copies[-1].start()
    return copies


def turn_tiles(rows, outs, per_sym):
    p = 0
    for out_ref in outs:
        for s in range(out_ref.shape[0]):
            tiles = rows[p : p + per_sym]
            out_ref[s] = tiles.reshape(per_sym * rows.shape[1], rows.shape[2]).T
            p += per_sym


def sort_first_kernel(syms, cd_ref, ab_ref, t2_ref, ints_ref, own_ref, later_ref, ints_out, *scratch):
    both, rows, count, order, order_ab, place, sem, sems = scratch
    load = pltpu.make_async_copy(t2_ref, both.at[0], sem)
    load.start()
    tiles = ab_ref.shape[0]
    rank_tiles(ab_ref, count, order_ab, place, tiles)
    copies = fetch_tiles(ints_ref, rows, order_ab, syms, tiles // NSYM, sems)
    rank_tiles(cd_ref, count, order, None, cd_ref.shape[0])
    load.wait()
    both[1] = half_turned(both[0])
    left = lax.broadcasted_iota(jnp.int32, (t2_ref.shape[0], LANES), 1) < LANES // 2
    q = 0
    for chunk in (own_ref, later_ref):
        for off in range(chunk.shape[1] // LANES):
            chunk[:, off * LANES : (off + 1) * LANES] = pick_pair(
                both, order[2 * q], order[2 * q + 1], left
            )
            q += 1
    for copy in copies:
        copy.wait()
    turn_tiles(rows, (ints_out,), tiles // NSYM)


def sort_first(t2, integrals, cd_sym, ab_sym, syms):
    rows, cols = t2.shape
    tiles, tile, packed = integrals.shape
    per_sym = tiles // NSYM
    return pl.pallas_call(
        functools.partial(sort_first_kernel, syms),
        out_shape=[
            jax.ShapeDtypeStruct((rows, cols // NSYM * m), t2.dtype) for m in (NSYM - LATER, LATER)
        ]
        + [jax.ShapeDtypeStruct((len(syms), packed, per_sym * tile), integrals.dtype)],
        in_specs=[SMEM, SMEM, ANY, ANY],
        out_specs=[VMEM] * 3,
        scratch_shapes=[
            pltpu.VMEM((2, rows, cols), t2.dtype),
            pltpu.VMEM((len(syms) * per_sym, tile, packed), integrals.dtype),
            pltpu.SMEM((NSYM,), jnp.int32),
            pltpu.SMEM((cd_sym.shape[0],), jnp.int32),
            pltpu.SMEM((tiles,), jnp.int32),
            pltpu.SMEM((tiles,), jnp.int32),
            pltpu.SemaphoreType.DMA,
            pltpu.SemaphoreType.DMA((len(syms) * per_sym,)),
        ],
        compiler_params=params(60 * 2**20),
        cost_estimate=CHEAP,
        name="sort_first",
    )(cd_sym, ab_sym, t2, integrals)


def sort_ints_kernel(syms, ab_ref, ints_ref, _, place, *rest):
    outs, (rows, count, order, sems) = rest[:-4], rest[-4:]
    tiles = ab_ref.shape[0]
    rank_tiles(ab_ref, count, order, place, tiles)
    every = [sym for part in syms for sym in part]
    for copy in fetch_tiles(ints_ref, rows, order, every, tiles // NSYM, sems):
        copy.wait()
    turn_tiles(rows, outs, tiles // NSYM)


def sort_ints(integrals, ab_sym, syms, earlier):
    tiles, tile, packed = integrals.shape
    per_sym = tiles // NSYM
    used = sum(len(part) for part in syms) * per_sym
    return pl.pallas_call(
        functools.partial(sort_ints_kernel, syms),
        out_shape=[jax.ShapeDtypeStruct((tiles,), jnp.int32)]
        + [
            jax.ShapeDtypeStruct((len(part), packed, per_sym * tile), integrals.dtype)
            for part in syms
        ],
        in_specs=[SMEM, ANY, ANY],
        out_specs=[SMEM] + [VMEM] * len(syms),
        scratch_shapes=[
            pltpu.VMEM((used, tile, packed), integrals.dtype),
            pltpu.SMEM((NSYM,), jnp.int32),
            pltpu.SMEM((tiles,), jnp.int32),
            pltpu.SemaphoreType.DMA((used,)),
        ],
        compiler_params=params(),
        cost_estimate=CHEAP,
        name="sort_ints",
    )(ab_sym, integrals, earlier)


def merge_kernel(n, *refs):
    blocks, out_ref = refs[:n], refs[-1]
    me = lax.axis_index("zh")
    for d, block in enumerate(blocks):
        out_ref[me ^ d] = block[...]


def merge(blocks, earlier):
    return pl.pallas_call(
        functools.partial(merge_kernel, len(blocks)),
        out_shape=jax.ShapeDtypeStruct((len(blocks),) + blocks[0].shape, blocks[0].dtype),
        in_specs=[VMEM] * len(blocks) + [ANY] * len(earlier),
        out_specs=VMEM,
        compiler_params=params(),
        cost_estimate=CHEAP,
        name="merge",
    )(*blocks, *earlier)


def nothing(*refs):
    pass


def after(x, *earlier):
    n = len(earlier)
    return pl.pallas_call(
        nothing,
        out_shape=jax.ShapeDtypeStruct(x.shape, x.dtype),
        in_specs=[ANY] * (n + 1),
        out_specs=ANY,
        input_output_aliases={n: 0},
        compiler_params=params(),
        cost_estimate=CHEAP,
        name="after",
    )(*earlier, x)


def lay_out(lhs, refs, where, place):
    h, z, x = lax.axis_index("zh"), lax.axis_index("zl"), lax.axis_index("x")
    for k, by_difference, quarter in where:
        for i, (array, entry) in enumerate(quarter):
            row = place(2 * (h ^ i if by_difference else i) + (z ^ (k // 2)), x ^ (k % 2))
            lhs[row] = refs[array][...] if entry is None else refs[array][entry]


def contract_kernel(n_cd, n_blocks, n_before, where, *refs):
    blocks, ints_refs = refs[:n_blocks], refs[n_blocks : n_blocks + 2]
    before = refs[n_blocks + 2 : n_blocks + 2 + n_before]
    outs, lhs = refs[-n_cd - 1 : -1], refs[-1]
    start = before[0].shape[1] if before else 0
    for out, ref in zip(outs, before):
        out[:, :start] = ref[...]
    z_len, rows, cols = lhs.shape
    packed, width = ints_refs[0].shape[1:]
    first = lax.axis_index("cd") * (z_len // n_cd)
    lay_out(lhs, blocks, where, lambda z, x: lax.rem(z + z_len - first, z_len))
    t2 = lhs[...].reshape(z_len * rows, cols)
    group_rows = t2.shape[0] // n_cd
    for side, ints in enumerate(ints_refs):
        for s in range(cols // packed):
            part = jnp.dot(
                t2[:, s * packed : (s + 1) * packed], ints[s], preferred_element_type=jnp.float32
            ).astype(outs[0].dtype)
            for by in range(n_cd):
                outs[by][side, start:, s * width : (s + 1) * width] = part[
                    by * group_rows : (by + 1) * group_rows
                ]


def contract(n_cd, blocks, where, ints, sib_ints, before, earlier):
    rows, cols = blocks[0].shape[-2:]
    z_len = 2 * len(where[0][2])
    packed, width = ints.shape[1:]
    start = before[0].shape[1] if before else 0
    out = (2, start + z_len * rows // n_cd, cols // packed * width)
    return pl.pallas_call(
        functools.partial(contract_kernel, n_cd, len(blocks), len(before), where),
        out_shape=[jax.ShapeDtypeStruct(out, jnp.bfloat16)] * n_cd,
        in_specs=[VMEM] * (len(blocks) + 2 + len(before)) + [ANY] * len(earlier),
        out_specs=[VMEM] * n_cd,
        scratch_shapes=[pltpu.VMEM((z_len, rows, cols), jnp.bfloat16)],
        compiler_params=params(),
        cost_estimate=CHEAP,
        name="contract",
    )(*blocks, ints, sib_ints, *before, *earlier)


def total(parts):
    value = parts[0].astype(jnp.float32)
    for part in parts[1:]:
        value += part.astype(jnp.float32)
    return value.astype(jnp.bfloat16)


def join_kernel(n, *refs):
    out_ref, first = refs[-1], 0
    for ref in refs[-n - 1 : -1]:
        out_ref[first : first + ref.shape[0]] = ref[...]
        first += ref.shape[0]


def join(arrays, earlier):
    n = len(arrays)
    out = (sum(x.shape[0] for x in arrays), *arrays[0].shape[1:])
    return pl.pallas_call(
        functools.partial(join_kernel, n),
        out_shape=jax.ShapeDtypeStruct(out, arrays[0].dtype),
        in_specs=[ANY] * len(earlier) + [VMEM] * n,
        out_specs=VMEM,
        compiler_params=params(),
        cost_estimate=CHEAP,
        name="join",
    )(*earlier, *arrays)


def later_kernel(n_cd, n_blocks, where, *refs):
    blocks, ints, parts = refs[:n_blocks], refs[n_blocks : n_blocks + 2], refs[n_blocks + 2 : -3]
    own_out, sib_out, lhs = refs[-3:]
    slots, rows, cols = lhs.shape
    packed, width = ints[0].shape[1:]
    per_group, me, x = slots // n_cd, lax.axis_index("cd"), lax.axis_index("x")

    def place(z, x):
        n = 2 * z + x
        group = lax.div(n, per_group)
        return lax.rem(me + n_cd - group, n_cd) * per_group + (n - group * per_group)

    lay_out(lhs, blocks, where, place)
    t2 = lhs[...].reshape(n_cd, per_group * rows, cols)
    for side, out_ref in enumerate((own_out, sib_out)):
        first = parts[0].shape[2]
        for half in range(2):
            for z in range(per_group // 2):
                these = pl.ds(pl.multiple_of((2 * z + (x ^ half)) * rows, rows), rows)
                at = (half * per_group // 2 + z) * rows
                out_ref[these, :first] = total([part[side, at : at + rows] for part in parts])
        for s in range(LATER):
            out_ref[:, first : first + width] = total(
                [
                    jnp.dot(
                        t2[by, :, s * packed : (s + 1) * packed],
                        ints[side][by * LATER + s],
                        preferred_element_type=jnp.float32,
                    ).astype(out_ref.dtype)
                    for by in range(n_cd)
                ]
            )
            first += width


def contract_later(n_cd, blocks, where, ints, parts):
    rows, cols = blocks[0].shape[-2:]
    slots = 4 * len(where[0][2])
    out = (slots * rows // n_cd, parts[0].shape[2] + ints[0].shape[2] * LATER)
    return pl.pallas_call(
        functools.partial(later_kernel, n_cd, len(blocks), where),
        out_shape=[jax.ShapeDtypeStruct(out, jnp.bfloat16)] * 2,
        in_specs=[VMEM] * (len(blocks) + 2 + len(parts)),
        out_specs=[VMEM] * 2,
        scratch_shapes=[pltpu.VMEM((slots, rows, cols), jnp.bfloat16)],
        compiler_params=params(),
        cost_estimate=CHEAP,
        name="contract_later",
    )(*blocks, *ints, *parts)


def finish_kernel(side, place, sums_ref, *rest):
    out_ref, both, made, sems = rest[-4:]
    blocks, rows, cols = made.shape
    step = both.shape[1] // rows
    left = lax.broadcasted_iota(jnp.int32, (step * rows, LANES), 1) < LANES // 2

    def copy_out(i):
        block = 2 * i + (lax.axis_index("core") ^ side)
        return pltpu.make_async_copy(made.at[i], out_ref.at[block], sems.at[i])

    for i in range(0, blocks, step):
        both[0] = sums_ref[i * rows : (i + step) * rows]
        both[1] = half_turned(both[0])
        for q in range(cols // LANES):
            pair = pick_pair(both, place[2 * q], place[2 * q + 1], left)
            made[i : i + step, :, q * LANES : (q + 1) * LANES] = pair.reshape(step, rows, LANES)
        for j in range(i, i + step):
            copy_out(j).start()
    for i in range(blocks):
        copy_out(i).wait()


def finish(side, place, sums, rows, out=None):
    blocks, cols = sums.shape[0] // rows, sums.shape[1]
    before = [] if out is None else [out]
    return pl.pallas_call(
        functools.partial(finish_kernel, side),
        out_shape=jax.ShapeDtypeStruct((2 * blocks, rows, cols), jnp.bfloat16),
        in_specs=[SMEM, VMEM] + [ANY] * len(before),
        out_specs=ANY,
        scratch_shapes=[
            pltpu.VMEM((2, (2 - blocks % 2) * rows, cols), jnp.bfloat16),
            pltpu.VMEM((blocks, rows, cols), jnp.bfloat16),
            pltpu.SemaphoreType.DMA((blocks,)),
        ],
        input_output_aliases={2: 0} if before else {},
        compiler_params=params(),
        cost_estimate=CHEAP,
        name="finish",
    )(place, sums, *before)


SWAP = [(0, 1), (1, 0)]


def further(x, by):
    n_cd = lax.axis_size("cd")
    return lax.ppermute(x, "cd", [(i, (i + by) % n_cd) for i in range(n_cd)])


def to_plane(x, d):
    n_cd = lax.axis_size("cd")
    z_len = 2 * lax.axis_size("zh")
    rest = z_len // n_cd
    pairs = []
    for z in range(z_len):
        group, i = divmod(z, rest)
        for y in range(n_cd):
            pairs.append((z * n_cd + y, ((y * rest + i) ^ (2 * d)) * n_cd + group))
    return lax.ppermute(x, ("zh", "zl", "cd"), pairs)


def per_device(t2_amps, integrals, ab_sym, cd_sym):
    zh, n_cd = lax.axis_size("zh"), lax.axis_size("cd")
    def over(x, axis):
        return lax.ppermute(x, axis, SWAP)

    def along_zh(x):
        return [lax.ppermute(x, "zh", [(i, i ^ d) for i in range(zh)]) for d in range(1, zh)]

    first_later = tuple(range(NSYM - LATER, NSYM - LATER + FIRST_SENT))
    own, own_later, ints_later = sort_first(t2_amps, integrals, cd_sym, ab_sym, first_later)
    later = [[ints_later] + [further(ints_later, by) for by in range(1, n_cd)]]
    syms = (tuple(range(NSYM - LATER)), tuple(range(NSYM - LATER + FIRST_SENT, NSYM)))
    place, ints, ints_later = sort_ints(integrals, ab_sym, syms, own)
    x_o, block_l = over(own, "x"), over(own, "zl")
    blocks_h = along_zh(own)
    fence = join([y[None] for y in [block_l, *blocks_h]], [*later[0][1:], ints, x_o])
    x_lh = over(fence, "x")
    blocks_hl = [over(y, "zl") for y in blocks_h]
    ints = after(ints, fence)
    sib_ints = over(ints, "core")
    ints_later = after(ints_later, fence)
    later.append([ints_later] + [further(ints_later, by) for by in range(1, n_cd)])
    near = [to_plane(after(own_later, fence), d) for d in range(1, zh)]
    near = merge([to_plane(after(own_later, sib_ints), 0)] + near, [])
    blocks = [own, *blocks_h, block_l, *blocks_hl]
    where = [(k, True, tuple((zh * (k // 2) + d, None) for d in range(zh))) for k in (0, 2)]
    before = contract(n_cd, blocks, tuple(where), ints, sib_ints, [], [])
    x_hl = [over(after(y, before[0]), "x") for y in blocks_hl]
    blocks = [x_o, x_lh, *x_hl]
    where = (
        (1, True, ((0, None),) + tuple((1, d) for d in range(1, zh))),
        (3, True, ((1, 0),) + tuple((1 + d, None) for d in range(1, zh))),
    )
    made = contract(n_cd, blocks, where, ints, sib_ints, before, [near, *later[1][1:]])
    parts = [made[0]] + [further(made[by], by) for by in range(1, n_cd)]
    up, across = over(near, "zl"), over(near, "x")
    half = zh // 2
    blocks = [near, across, up, over(up[:half], "x"), over(across[half:], "zl")]
    where = [(k, False, tuple((k, i) for i in range(zh))) for k in range(3)]
    where.append((3, False, tuple((3 + i // half, i % half) for i in range(zh))))
    ints_later = join([x[by] for by in range(n_cd) for x in later], made[:1])
    ints_later = (ints_later, over(ints_later, "core"))
    sums, sib_sums = contract_later(n_cd, blocks, tuple(where), ints_later, parts)
    sib_sums = lax.ppermute(sib_sums, "core", SWAP)
    rows = t2_amps.shape[0]
    out = finish(0, place, sums, rows)
    out = finish(1, place, sib_sums, rows, out)
    return out.reshape(-1, out.shape[2])


def solution(mesh):
    n_blk, n_cd = mesh.devices.shape
    blk = ("zh", "zl", "x", "core")
    parted = Mesh(mesh.devices.reshape(n_blk // 8, 2, 2, 2, n_cd), blk + ("cd",))
    in_specs = (P(blk, "cd"), P(blk, None, "cd"), P(blk), P("cd"))
    return jax.shard_map(
        per_device, mesh=parted, in_specs=in_specs, out_specs=P("cd", blk), check_vma=False
    )
```

```python
import functools

import jax
import jax.numpy as jnp
from jax import lax
from jax.experimental import pallas as pl
from jax.experimental.pallas import tpu as pltpu
from jax.sharding import Mesh, PartitionSpec as P

NSYM = 8
LATER = 4
FIRST_SENT = 2
LANES = 128
VMEM_LIMIT = 20 * 2**20

ANY = pl.BlockSpec(memory_space=pl.ANY)
SMEM = pl.BlockSpec(memory_space=pltpu.SMEM)
VMEM = pl.BlockSpec(memory_space=pltpu.VMEM)

CHEAP = pl.CostEstimate(flops=1000, bytes_accessed=1000, transcendentals=0)


def params(limit=VMEM_LIMIT):
    return pltpu.CompilerParams(vmem_limit_bytes=limit)


def half_turned(x):
    half = LANES // 2
    return jnp.concatenate([x[:, half:], x[:, :half]], axis=1)


def rank_tiles(sym_ref, count_ref, order_ref, place_ref, tiles):
    for s in range(NSYM):
        count_ref[s] = s * (tiles // NSYM)

    def step(i, _):
        s = sym_ref[i]
        p = count_ref[s]
        count_ref[s] = p + 1
        order_ref[p] = i
        if place_ref is not None:
            place_ref[i] = p
        return 0

    lax.fori_loop(0, tiles, step, 0, unroll=8)


def pick_pair(both, a, b, left):
    columns = both.shape[2] // LANES
    a_col = lax.shift_right_logical(a, 1)
    b_col = lax.rem(lax.shift_right_logical(b + 1, 1) + columns - 1, columns)
    xa = both[a & 1, :, pl.ds(pl.multiple_of(a_col * LANES, LANES), LANES)]
    xb = both[(b & 1) ^ 1, :, pl.ds(pl.multiple_of(b_col * LANES, LANES), LANES)]
    return jnp.where(left, xa, xb)


def fetch_tiles(ints_ref, rows, order, syms, per_sym, sems):
    copies = []
    for sym in syms:
        for m in range(per_sym):
            p = len(copies)
            tile_ref = ints_ref.at[order[sym * per_sym + m]]
            copies.append(pltpu.make_async_copy(tile_ref, rows.at[p], sems.at[p]))
            copies[-1].start()
    return copies


def turn_tiles(rows, outs, per_sym):
    p = 0
    for out_ref in outs:
        for s in range(out_ref.shape[0]):
            tiles = rows[p : p + per_sym]
            out_ref[s] = tiles.reshape(per_sym * rows.shape[1], rows.shape[2]).T
            p += per_sym


def sort_first_kernel(syms, cd_ref, ab_ref, t2_ref, ints_ref, own_ref, later_ref, ints_out, *scratch):
    both, rows, count, order, order_ab, place, sem, sems = scratch
    load = pltpu.make_async_copy(t2_ref, both.at[0], sem)
    load.start()
    tiles = ab_ref.shape[0]
    rank_tiles(ab_ref, count, order_ab, place, tiles)
    copies = fetch_tiles(ints_ref, rows, order_ab, syms, tiles // NSYM, sems)
    rank_tiles(cd_ref, count, order, None, cd_ref.shape[0])
    load.wait()
    both[1] = half_turned(both[0])
    left = lax.broadcasted_iota(jnp.int32, (t2_ref.shape[0], LANES), 1) < LANES // 2
    q = 0
    for chunk in (own_ref, later_ref):
        for off in range(chunk.shape[1] // LANES):
            chunk[:, off * LANES : (off + 1) * LANES] = pick_pair(
                both, order[2 * q], order[2 * q + 1], left
            )
            q += 1
    for copy in copies:
        copy.wait()
    turn_tiles(rows, (ints_out,), tiles // NSYM)


def sort_first(t2, integrals, cd_sym, ab_sym, syms):
    rows, cols = t2.shape
    tiles, tile, packed = integrals.shape
    per_sym = tiles // NSYM
    return pl.pallas_call(
        functools.partial(sort_first_kernel, syms),
        out_shape=[
            jax.ShapeDtypeStruct((rows, cols // NSYM * m), t2.dtype) for m in (NSYM - LATER, LATER)
        ]
        + [jax.ShapeDtypeStruct((len(syms), packed, per_sym * tile), integrals.dtype)],
        in_specs=[SMEM, SMEM, ANY, ANY],
        out_specs=[VMEM] * 3,
        scratch_shapes=[
            pltpu.VMEM((2, rows, cols), t2.dtype),
            pltpu.VMEM((len(syms) * per_sym, tile, packed), integrals.dtype),
            pltpu.SMEM((NSYM,), jnp.int32),
            pltpu.SMEM((cd_sym.shape[0],), jnp.int32),
            pltpu.SMEM((tiles,), jnp.int32),
            pltpu.SMEM((tiles,), jnp.int32),
            pltpu.SemaphoreType.DMA,
            pltpu.SemaphoreType.DMA((len(syms) * per_sym,)),
        ],
        compiler_params=params(60 * 2**20),
        cost_estimate=CHEAP,
        name="sort_first",
    )(cd_sym, ab_sym, t2, integrals)


def sort_ints_kernel(syms, ab_ref, ints_ref, _, place, *rest):
    outs, (rows, count, order, sems) = rest[:-4], rest[-4:]
    tiles = ab_ref.shape[0]
    rank_tiles(ab_ref, count, order, place, tiles)
    every = [sym for part in syms for sym in part]
    for copy in fetch_tiles(ints_ref, rows, order, every, tiles // NSYM, sems):
        copy.wait()
    turn_tiles(rows, outs, tiles // NSYM)


def sort_ints(integrals, ab_sym, syms, earlier):
    tiles, tile, packed = integrals.shape
    per_sym = tiles // NSYM
    used = sum(len(part) for part in syms) * per_sym
    return pl.pallas_call(
        functools.partial(sort_ints_kernel, syms),
        out_shape=[jax.ShapeDtypeStruct((tiles,), jnp.int32)]
        + [
            jax.ShapeDtypeStruct((len(part), packed, per_sym * tile), integrals.dtype)
            for part in syms
        ],
        in_specs=[SMEM, ANY, ANY],
        out_specs=[SMEM] + [VMEM] * len(syms),
        scratch_shapes=[
            pltpu.VMEM((used, tile, packed), integrals.dtype),
            pltpu.SMEM((NSYM,), jnp.int32),
            pltpu.SMEM((tiles,), jnp.int32),
            pltpu.SemaphoreType.DMA((used,)),
        ],
        compiler_params=params(),
        cost_estimate=CHEAP,
        name="sort_ints",
    )(ab_sym, integrals, earlier)


def merge_kernel(n, *refs):
    blocks, out_ref = refs[:n], refs[-1]
    me = lax.axis_index("zh")
    for d, block in enumerate(blocks):
        out_ref[me ^ d] = block[...]


def merge(blocks, earlier):
    return pl.pallas_call(
        functools.partial(merge_kernel, len(blocks)),
        out_shape=jax.ShapeDtypeStruct((len(blocks),) + blocks[0].shape, blocks[0].dtype),
        in_specs=[VMEM] * len(blocks) + [ANY] * len(earlier),
        out_specs=VMEM,
        compiler_params=params(),
        cost_estimate=CHEAP,
        name="merge",
    )(*blocks, *earlier)


def nothing(*refs):
    pass


def after(x, *earlier):
    n = len(earlier)
    return pl.pallas_call(
        nothing,
        out_shape=jax.ShapeDtypeStruct(x.shape, x.dtype),
        in_specs=[ANY] * (n + 1),
        out_specs=ANY,
        input_output_aliases={n: 0},
        compiler_params=params(),
        cost_estimate=CHEAP,
        name="after",
    )(*earlier, x)


def lay_out(lhs, refs, where, place):
    h, z, x = lax.axis_index("zh"), lax.axis_index("zl"), lax.axis_index("x")
    for k, by_difference, quarter in where:
        for i, (array, entry) in enumerate(quarter):
            row = place(2 * (h ^ i if by_difference else i) + (z ^ (k // 2)), x ^ (k % 2))
            lhs[row] = refs[array][...] if entry is None else refs[array][entry]


def contract_kernel(n_cd, n_blocks, n_before, where, *refs):
    blocks, ints_refs = refs[:n_blocks], refs[n_blocks : n_blocks + 2]
    before = refs[n_blocks + 2 : n_blocks + 2 + n_before]
    outs, lhs = refs[-n_cd - 1 : -1], refs[-1]
    start = before[0].shape[1] if before else 0
    for out, ref in zip(outs, before):
        out[:, :start] = ref[...]
    z_len, rows, cols = lhs.shape
    packed, width = ints_refs[0].shape[1:]
    first = lax.axis_index("cd") * (z_len // n_cd)
    lay_out(lhs, blocks, where, lambda z, x: lax.rem(z + z_len - first, z_len))
    t2 = lhs[...].reshape(z_len * rows, cols)
    group_rows = t2.shape[0] // n_cd
    for side, ints in enumerate(ints_refs):
        for s in range(cols // packed):
            part = jnp.dot(
                t2[:, s * packed : (s + 1) * packed], ints[s], preferred_element_type=jnp.float32
            ).astype(outs[0].dtype)
            for by in range(n_cd):
                outs[by][side, start:, s * width : (s + 1) * width] = part[
                    by * group_rows : (by + 1) * group_rows
                ]


def contract(n_cd, blocks, where, ints, sib_ints, before, earlier):
    rows, cols = blocks[0].shape[-2:]
    z_len = 2 * len(where[0][2])
    packed, width = ints.shape[1:]
    start = before[0].shape[1] if before else 0
    out = (2, start + z_len * rows // n_cd, cols // packed * width)
    return pl.pallas_call(
        functools.partial(contract_kernel, n_cd, len(blocks), len(before), where),
        out_shape=[jax.ShapeDtypeStruct(out, jnp.bfloat16)] * n_cd,
        in_specs=[VMEM] * (len(blocks) + 2 + len(before)) + [ANY] * len(earlier),
        out_specs=[VMEM] * n_cd,
        scratch_shapes=[pltpu.VMEM((z_len, rows, cols), jnp.bfloat16)],
        compiler_params=params(),
        cost_estimate=CHEAP,
        name="contract",
    )(*blocks, ints, sib_ints, *before, *earlier)


def total(parts):
    value = parts[0].astype(jnp.float32)
    for part in parts[1:]:
        value += part.astype(jnp.float32)
    return value.astype(jnp.bfloat16)


def join_kernel(n, *refs):
    out_ref, first = refs[-1], 0
    for ref in refs[-n - 1 : -1]:
        out_ref[first : first + ref.shape[0]] = ref[...]
        first += ref.shape[0]


def join(arrays, earlier):
    n = len(arrays)
    out = (sum(x.shape[0] for x in arrays), *arrays[0].shape[1:])
    return pl.pallas_call(
        functools.partial(join_kernel, n),
        out_shape=jax.ShapeDtypeStruct(out, arrays[0].dtype),
        in_specs=[ANY] * len(earlier) + [VMEM] * n,
        out_specs=VMEM,
        compiler_params=params(),
        cost_estimate=CHEAP,
        name="join",
    )(*earlier, *arrays)


def later_kernel(n_cd, n_blocks, where, *refs):
    blocks, ints = refs[:n_blocks], refs[n_blocks : n_blocks + 2]
    own_out, sib_out, lhs = refs[-3:]
    slots, rows, cols = lhs.shape
    packed, width = ints[0].shape[1:]
    per_group, me = slots // n_cd, lax.axis_index("cd")

    def place(z, x):
        n = 2 * z + x
        group = lax.div(n, per_group)
        return lax.rem(me + n_cd - group, n_cd) * per_group + (n - group * per_group)

    lay_out(lhs, blocks, where, place)
    t2 = lhs[...].reshape(n_cd, per_group * rows, cols)
    for side, out_ref in enumerate((own_out, sib_out)):
        for s in range(LATER):
            out_ref[:, s * width : (s + 1) * width] = total(
                [
                    jnp.dot(
                        t2[by, :, s * packed : (s + 1) * packed],
                        ints[side][by * LATER + s],
                        preferred_element_type=jnp.float32,
                    ).astype(out_ref.dtype)
                    for by in range(n_cd)
                ]
            )


def contract_later(n_cd, blocks, where, ints):
    rows, cols = blocks[0].shape[-2:]
    slots = 4 * len(where[0][2])
    out = (slots * rows // n_cd, ints[0].shape[2] * LATER)
    return pl.pallas_call(
        functools.partial(later_kernel, n_cd, len(blocks), where),
        out_shape=[jax.ShapeDtypeStruct(out, jnp.bfloat16)] * 2,
        in_specs=[VMEM] * (len(blocks) + 2),
        out_specs=[VMEM] * 2,
        scratch_shapes=[pltpu.VMEM((slots, rows, cols), jnp.bfloat16)],
        compiler_params=params(),
        cost_estimate=CHEAP,
        name="contract_later",
    )(*blocks, *ints)


def sum_kernel(rows, *refs):
    parts, later, outs = refs[:-4], refs[-4:-2], refs[-2:]
    x = lax.axis_index("x")
    half_rows = parts[0].shape[1] // 2
    first = parts[0].shape[2]
    for side, out_ref in enumerate(outs):
        out_ref[:, first:] = later[side][...]
        for half in range(2):
            for z in range(half_rows // rows):
                these = pl.ds(pl.multiple_of((2 * z + (x ^ half)) * rows, rows), rows)
                at = half * half_rows + z * rows
                out_ref[these, :first] = total([part[side, at : at + rows] for part in parts])


def sum_parts(parts, later, rows):
    out = (parts[0].shape[1], parts[0].shape[2] + later[0].shape[1])
    return pl.pallas_call(
        functools.partial(sum_kernel, rows),
        out_shape=[jax.ShapeDtypeStruct(out, jnp.bfloat16)] * 2,
        in_specs=[VMEM] * (len(parts) + 2),
        out_specs=[VMEM] * 2,
        compiler_params=params(),
        cost_estimate=CHEAP,
        name="sum_parts",
    )(*parts, *later)


def finish_kernel(side, place, sums_ref, *rest):
    out_ref, both, made, sems = rest[-4:]
    blocks, rows, cols = made.shape
    left = lax.broadcasted_iota(jnp.int32, (rows, LANES), 1) < LANES // 2

    def copy_out(i):
        block = 2 * i + (lax.axis_index("core") ^ side)
        return pltpu.make_async_copy(made.at[i], out_ref.at[block], sems.at[i])

    for i in range(blocks):
        both[0] = sums_ref[i * rows : (i + 1) * rows]
        both[1] = half_turned(both[0])
        for q in range(cols // LANES):
            made[i, :, q * LANES : (q + 1) * LANES] = pick_pair(
                both, place[2 * q], place[2 * q + 1], left
            )
        copy_out(i).start()
    for i in range(blocks):
        copy_out(i).wait()


def finish(side, place, sums, rows, out=None):
    blocks, cols = sums.shape[0] // rows, sums.shape[1]
    before = [] if out is None else [out]
    return pl.pallas_call(
        functools.partial(finish_kernel, side),
        out_shape=jax.ShapeDtypeStruct((2 * blocks, rows, cols), jnp.bfloat16),
        in_specs=[SMEM, VMEM] + [ANY] * len(before),
        out_specs=ANY,
        scratch_shapes=[
            pltpu.VMEM((2, rows, cols), jnp.bfloat16),
            pltpu.VMEM((blocks, rows, cols), jnp.bfloat16),
            pltpu.SemaphoreType.DMA((blocks,)),
        ],
        input_output_aliases={2: 0} if before else {},
        compiler_params=params(),
        cost_estimate=CHEAP,
        name="finish",
    )(place, sums, *before)


SWAP = [(0, 1), (1, 0)]


def further(x, by):
    n_cd = lax.axis_size("cd")
    return lax.ppermute(x, "cd", [(i, (i + by) % n_cd) for i in range(n_cd)])


def to_plane(x, d):
    n_cd = lax.axis_size("cd")
    z_len = 2 * lax.axis_size("zh")
    rest = z_len // n_cd
    pairs = []
    for z in range(z_len):
        group, i = divmod(z, rest)
        for y in range(n_cd):
            pairs.append((z * n_cd + y, ((y * rest + i) ^ (2 * d)) * n_cd + group))
    return lax.ppermute(x, ("zh", "zl", "cd"), pairs)


def per_device(t2_amps, integrals, ab_sym, cd_sym):
    zh, n_cd = lax.axis_size("zh"), lax.axis_size("cd")
    def over(x, axis):
        return lax.ppermute(x, axis, SWAP)

    def along_zh(x):
        return [lax.ppermute(x, "zh", [(i, i ^ d) for i in range(zh)]) for d in range(1, zh)]

    first_later = tuple(range(NSYM - LATER, NSYM - LATER + FIRST_SENT))
    own, own_later, ints_later = sort_first(t2_amps, integrals, cd_sym, ab_sym, first_later)
    later = [[ints_later] + [further(ints_later, by) for by in range(1, n_cd)]]
    syms = (tuple(range(NSYM - LATER)), tuple(range(NSYM - LATER + FIRST_SENT, NSYM)))
    place, ints, ints_later = sort_ints(integrals, ab_sym, syms, own)
    x_o, block_l = over(own, "x"), over(own, "zl")
    blocks_h = along_zh(own)
    fence = join([y[None] for y in [block_l, *blocks_h]], [*later[0][1:], ints, x_o])
    x_lh = over(fence, "x")
    blocks_hl = [over(y, "zl") for y in blocks_h]
    ints = after(ints, fence)
    sib_ints = over(ints, "core")
    ints_later = after(ints_later, fence)
    later.append([ints_later] + [further(ints_later, by) for by in range(1, n_cd)])
    near = [to_plane(after(own_later, fence), d) for d in range(1, zh)]
    near = merge([to_plane(after(own_later, sib_ints), 0)] + near, [])
    blocks = [own, *blocks_h, block_l, *blocks_hl]
    where = [(k, True, tuple((zh * (k // 2) + d, None) for d in range(zh))) for k in (0, 2)]
    before = contract(n_cd, blocks, tuple(where), ints, sib_ints, [], [])
    x_hl = [over(after(y, before[0]), "x") for y in blocks_hl]
    blocks = [x_o, x_lh, *x_hl]
    where = (
        (1, True, ((0, None),) + tuple((1, d) for d in range(1, zh))),
        (3, True, ((1, 0),) + tuple((1 + d, None) for d in range(1, zh))),
    )
    made = contract(n_cd, blocks, where, ints, sib_ints, before, [near, *later[1][1:]])
    parts = [made[0]] + [further(made[by], by) for by in range(1, n_cd)]
    up, across = over(near, "zl"), over(near, "x")
    half = zh // 2
    blocks = [near, across, up, over(up[:half], "x"), over(across[half:], "zl")]
    where = [(k, False, tuple((k, i) for i in range(zh))) for k in range(3)]
    where.append((3, False, tuple((3 + i // half, i % half) for i in range(zh))))
    ints_later = join([x[by] for by in range(n_cd) for x in later], made[:1])
    ints_later = (ints_later, over(ints_later, "core"))
    later_sums = contract_later(n_cd, blocks, tuple(where), ints_later)
    sums, sib_sums = sum_parts(parts, later_sums, t2_amps.shape[0])
    sib_sums = lax.ppermute(sib_sums, "core", SWAP)
    rows = t2_amps.shape[0]
    out = finish(0, place, sums, rows)
    out = finish(1, place, sib_sums, rows, out)
    return out.reshape(-1, out.shape[2])


def solution(mesh):
    n_blk, n_cd = mesh.devices.shape
    blk = ("zh", "zl", "x", "core")
    parted = Mesh(mesh.devices.reshape(n_blk // 8, 2, 2, 2, n_cd), blk + ("cd",))
    in_specs = (P(blk, "cd"), P(blk, None, "cd"), P(blk), P("cd"))
    return jax.shard_map(
        per_device, mesh=parted, in_specs=in_specs, out_specs=P("cd", blk), check_vma=False
    )
```

```python
import functools

import jax
import jax.numpy as jnp
from jax import lax
from jax.experimental import pallas as pl
from jax.experimental.pallas import tpu as pltpu
from jax.sharding import Mesh, PartitionSpec as P

NSYM = 8
LATER = 4
FIRST_SENT = 2
LANES = 128
VMEM_LIMIT = 20 * 2**20

ANY = pl.BlockSpec(memory_space=pl.ANY)
SMEM = pl.BlockSpec(memory_space=pltpu.SMEM)
VMEM = pl.BlockSpec(memory_space=pltpu.VMEM)

CHEAP = pl.CostEstimate(flops=1000, bytes_accessed=1000, transcendentals=0)


def params(limit=VMEM_LIMIT):
    return pltpu.CompilerParams(vmem_limit_bytes=limit)


def half_turned(x):
    half = LANES // 2
    return jnp.concatenate([x[:, half:], x[:, :half]], axis=1)


def rank_tiles(sym_ref, count_ref, order_ref, place_ref, tiles):
    for s in range(NSYM):
        count_ref[s] = s * (tiles // NSYM)

    def step(i, _):
        s = sym_ref[i]
        p = count_ref[s]
        count_ref[s] = p + 1
        order_ref[p] = i
        if place_ref is not None:
            place_ref[i] = p
        return 0

    lax.fori_loop(0, tiles, step, 0, unroll=8)


def pick_pair(both, a, b, left):
    columns = both.shape[2] // LANES
    a_col = lax.shift_right_logical(a, 1)
    b_col = lax.rem(lax.shift_right_logical(b + 1, 1) + columns - 1, columns)
    xa = both[a & 1, :, pl.ds(pl.multiple_of(a_col * LANES, LANES), LANES)]
    xb = both[(b & 1) ^ 1, :, pl.ds(pl.multiple_of(b_col * LANES, LANES), LANES)]
    return jnp.where(left, xa, xb)


def fetch_tiles(ints_ref, rows, order, syms, per_sym, sems):
    copies = []
    for sym in syms:
        for m in range(per_sym):
            p = len(copies)
            tile_ref = ints_ref.at[order[sym * per_sym + m]]
            copies.append(pltpu.make_async_copy(tile_ref, rows.at[p], sems.at[p]))
            copies[-1].start()
    return copies


def turn_tiles(rows, outs, per_sym):
    p = 0
    for out_ref in outs:
        for s in range(out_ref.shape[0]):
            tiles = rows[p : p + per_sym]
            out_ref[s] = tiles.reshape(per_sym * rows.shape[1], rows.shape[2]).T
            p += per_sym


def sort_first_kernel(syms, cd_ref, ab_ref, t2_ref, ints_ref, own_ref, later_ref, ints_out, *scratch):
    both, rows, count, order, order_ab, place, sem, sems = scratch
    load = pltpu.make_async_copy(t2_ref, both.at[0], sem)
    load.start()
    tiles = ab_ref.shape[0]
    rank_tiles(ab_ref, count, order_ab, place, tiles)
    copies = fetch_tiles(ints_ref, rows, order_ab, syms, tiles // NSYM, sems)
    rank_tiles(cd_ref, count, order, None, cd_ref.shape[0])
    load.wait()
    both[1] = half_turned(both[0])
    left = lax.broadcasted_iota(jnp.int32, (t2_ref.shape[0], LANES), 1) < LANES // 2
    q = 0
    for chunk in (own_ref, later_ref):
        for off in range(chunk.shape[1] // LANES):
            chunk[:, off * LANES : (off + 1) * LANES] = pick_pair(
                both, order[2 * q], order[2 * q + 1], left
            )
            q += 1
    for copy in copies:
        copy.wait()
    turn_tiles(rows, (ints_out,), tiles // NSYM)


def sort_first(t2, integrals, cd_sym, ab_sym, syms):
    rows, cols = t2.shape
    tiles, tile, packed = integrals.shape
    per_sym = tiles // NSYM
    return pl.pallas_call(
        functools.partial(sort_first_kernel, syms),
        out_shape=[
            jax.ShapeDtypeStruct((rows, cols // NSYM * m), t2.dtype) for m in (NSYM - LATER, LATER)
        ]
        + [jax.ShapeDtypeStruct((len(syms), packed, per_sym * tile), integrals.dtype)],
        in_specs=[SMEM, SMEM, ANY, ANY],
        out_specs=[VMEM] * 3,
        scratch_shapes=[
            pltpu.VMEM((2, rows, cols), t2.dtype),
            pltpu.VMEM((len(syms) * per_sym, tile, packed), integrals.dtype),
            pltpu.SMEM((NSYM,), jnp.int32),
            pltpu.SMEM((cd_sym.shape[0],), jnp.int32),
            pltpu.SMEM((tiles,), jnp.int32),
            pltpu.SMEM((tiles,), jnp.int32),
            pltpu.SemaphoreType.DMA,
            pltpu.SemaphoreType.DMA((len(syms) * per_sym,)),
        ],
        compiler_params=params(60 * 2**20),
        cost_estimate=CHEAP,
        name="sort_first",
    )(cd_sym, ab_sym, t2, integrals)


def sort_ints_kernel(syms, ab_ref, ints_ref, _, place, *rest):
    outs, (rows, count, order, sems) = rest[:-4], rest[-4:]
    tiles = ab_ref.shape[0]
    rank_tiles(ab_ref, count, order, place, tiles)
    every = [sym for part in syms for sym in part]
    for copy in fetch_tiles(ints_ref, rows, order, every, tiles // NSYM, sems):
        copy.wait()
    turn_tiles(rows, outs, tiles // NSYM)


def sort_ints(integrals, ab_sym, syms, earlier):
    tiles, tile, packed = integrals.shape
    per_sym = tiles // NSYM
    used = sum(len(part) for part in syms) * per_sym
    return pl.pallas_call(
        functools.partial(sort_ints_kernel, syms),
        out_shape=[jax.ShapeDtypeStruct((tiles,), jnp.int32)]
        + [
            jax.ShapeDtypeStruct((len(part), packed, per_sym * tile), integrals.dtype)
            for part in syms
        ],
        in_specs=[SMEM, ANY, ANY],
        out_specs=[SMEM] + [VMEM] * len(syms),
        scratch_shapes=[
            pltpu.VMEM((used, tile, packed), integrals.dtype),
            pltpu.SMEM((NSYM,), jnp.int32),
            pltpu.SMEM((tiles,), jnp.int32),
            pltpu.SemaphoreType.DMA((used,)),
        ],
        compiler_params=params(),
        cost_estimate=CHEAP,
        name="sort_ints",
    )(ab_sym, integrals, earlier)


def merge_kernel(n, *refs):
    blocks, out_ref = refs[:n], refs[-1]
    me = lax.axis_index("zh")
    for d, block in enumerate(blocks):
        out_ref[me ^ d] = block[...]


def merge(blocks, earlier):
    return pl.pallas_call(
        functools.partial(merge_kernel, len(blocks)),
        out_shape=jax.ShapeDtypeStruct((len(blocks),) + blocks[0].shape, blocks[0].dtype),
        in_specs=[VMEM] * len(blocks) + [ANY] * len(earlier),
        out_specs=VMEM,
        compiler_params=params(),
        cost_estimate=CHEAP,
        name="merge",
    )(*blocks, *earlier)


def nothing(*refs):
    pass


def after(x, *earlier):
    n = len(earlier)
    return pl.pallas_call(
        nothing,
        out_shape=jax.ShapeDtypeStruct(x.shape, x.dtype),
        in_specs=[ANY] * (n + 1),
        out_specs=ANY,
        input_output_aliases={n: 0},
        compiler_params=params(),
        cost_estimate=CHEAP,
        name="after",
    )(*earlier, x)


def lay_out(lhs, refs, where, place):
    h, z, x = lax.axis_index("zh"), lax.axis_index("zl"), lax.axis_index("x")
    for k, by_difference, quarter in where:
        for i, (array, entry) in enumerate(quarter):
            row = place(2 * (h ^ i if by_difference else i) + (z ^ (k // 2)), x ^ (k % 2))
            lhs[row] = refs[array][...] if entry is None else refs[array][entry]


def contract_kernel(n_cd, n_blocks, n_before, where, *refs):
    blocks, ints_refs = refs[:n_blocks], refs[n_blocks : n_blocks + 2]
    before = refs[n_blocks + 2 : n_blocks + 2 + n_before]
    outs, lhs = refs[-n_cd - 1 : -1], refs[-1]
    start = before[0].shape[1] if before else 0
    for out, ref in zip(outs, before):
        out[:, :start] = ref[...]
    z_len, rows, cols = lhs.shape
    packed, width = ints_refs[0].shape[1:]
    first = lax.axis_index("cd") * (z_len // n_cd)
    lay_out(lhs, blocks, where, lambda z, x: lax.rem(z + z_len - first, z_len))
    t2 = lhs[...].reshape(z_len * rows, cols)
    group_rows = t2.shape[0] // n_cd
    for side, ints in enumerate(ints_refs):
        for s in range(cols // packed):
            part = jnp.dot(
                t2[:, s * packed : (s + 1) * packed], ints[s], preferred_element_type=jnp.float32
            ).astype(outs[0].dtype)
            for by in range(n_cd):
                outs[by][side, start:, s * width : (s + 1) * width] = part[
                    by * group_rows : (by + 1) * group_rows
                ]


def contract(n_cd, blocks, where, ints, sib_ints, before, earlier):
    rows, cols = blocks[0].shape[-2:]
    z_len = 2 * len(where[0][2])
    packed, width = ints.shape[1:]
    start = before[0].shape[1] if before else 0
    out = (2, start + z_len * rows // n_cd, cols // packed * width)
    return pl.pallas_call(
        functools.partial(contract_kernel, n_cd, len(blocks), len(before), where),
        out_shape=[jax.ShapeDtypeStruct(out, jnp.bfloat16)] * n_cd,
        in_specs=[VMEM] * (len(blocks) + 2 + len(before)) + [ANY] * len(earlier),
        out_specs=[VMEM] * n_cd,
        scratch_shapes=[pltpu.VMEM((z_len, rows, cols), jnp.bfloat16)],
        compiler_params=params(),
        cost_estimate=CHEAP,
        name="contract",
    )(*blocks, ints, sib_ints, *before, *earlier)


def total(parts):
    value = parts[0].astype(jnp.float32)
    for part in parts[1:]:
        value += part.astype(jnp.float32)
    return value.astype(jnp.bfloat16)


def join_kernel(n, *refs):
    out_ref, first = refs[-1], 0
    for ref in refs[-n - 1 : -1]:
        out_ref[first : first + ref.shape[0]] = ref[...]
        first += ref.shape[0]


def join(arrays, earlier):
    n = len(arrays)
    out = (sum(x.shape[0] for x in arrays), *arrays[0].shape[1:])
    return pl.pallas_call(
        functools.partial(join_kernel, n),
        out_shape=jax.ShapeDtypeStruct(out, arrays[0].dtype),
        in_specs=[ANY] * len(earlier) + [VMEM] * n,
        out_specs=VMEM,
        compiler_params=params(),
        cost_estimate=CHEAP,
        name="join",
    )(*earlier, *arrays)


def later_kernel(n_cd, n_blocks, where, *refs):
    blocks, ints = refs[:n_blocks], refs[n_blocks : n_blocks + 2]
    own_out, sib_out, lhs = refs[-3:]
    slots, rows, cols = lhs.shape
    packed, width = ints[0].shape[1:]
    per_group, me = slots // n_cd, lax.axis_index("cd")

    def place(z, x):
        n = 2 * z + x
        group = lax.div(n, per_group)
        return lax.rem(me + n_cd - group, n_cd) * per_group + (n - group * per_group)

    lay_out(lhs, blocks, where, place)
    t2 = lhs[...].reshape(n_cd, per_group * rows, cols)
    for side, out_ref in enumerate((own_out, sib_out)):
        for s in range(LATER):
            out_ref[:, s * width : (s + 1) * width] = total(
                [
                    jnp.dot(
                        t2[by, :, s * packed : (s + 1) * packed],
                        ints[side][by * LATER + s],
                        preferred_element_type=jnp.float32,
                    ).astype(out_ref.dtype)
                    for by in range(n_cd)
                ]
            )


def contract_later(n_cd, blocks, where, ints):
    rows, cols = blocks[0].shape[-2:]
    slots = 4 * len(where[0][2])
    out = (slots * rows // n_cd, ints[0].shape[2] * LATER)
    return pl.pallas_call(
        functools.partial(later_kernel, n_cd, len(blocks), where),
        out_shape=[jax.ShapeDtypeStruct(out, jnp.bfloat16)] * 2,
        in_specs=[VMEM] * (len(blocks) + 2),
        out_specs=[VMEM] * 2,
        scratch_shapes=[pltpu.VMEM((slots, rows, cols), jnp.bfloat16)],
        compiler_params=params(),
        cost_estimate=CHEAP,
        name="contract_later",
    )(*blocks, *ints)


def sum_kernel(rows, *refs):
    parts, later, outs = refs[:-3], refs[-3], refs[-2:]
    x = lax.axis_index("x")
    half_rows = parts[0].shape[1] // 2
    first = parts[0].shape[2]
    for side, out_ref in enumerate(outs):
        if not side:
            out_ref[:, first:] = later[...]
        for half in range(2):
            for z in range(half_rows // rows):
                these = pl.ds(pl.multiple_of((2 * z + (x ^ half)) * rows, rows), rows)
                at = half * half_rows + z * rows
                out_ref[these, :first] = total([part[side, at : at + rows] for part in parts])


def sum_parts(parts, later, rows):
    rows_out, cols = parts[0].shape[1:]
    return pl.pallas_call(
        functools.partial(sum_kernel, rows),
        out_shape=[
            jax.ShapeDtypeStruct((rows_out, cols + later.shape[1]), jnp.bfloat16),
            jax.ShapeDtypeStruct((rows_out, cols), jnp.bfloat16),
        ],
        in_specs=[VMEM] * (len(parts) + 1),
        out_specs=[VMEM] * 2,
        compiler_params=params(),
        cost_estimate=CHEAP,
        name="sum_parts",
    )(*parts, later)


def finish_kernel(side, n_sums, place, *rest):
    sums = rest[:n_sums]
    out_ref, both, made, sems = rest[-4:]
    blocks, rows, cols = made.shape
    left = lax.broadcasted_iota(jnp.int32, (rows, LANES), 1) < LANES // 2

    def copy_out(i):
        block = 2 * i + (lax.axis_index("core") ^ side)
        return pltpu.make_async_copy(made.at[i], out_ref.at[block], sems.at[i])

    for i in range(blocks):
        first = 0
        for ref in sums:
            both[0, :, first : first + ref.shape[1]] = ref[i * rows : (i + 1) * rows]
            first += ref.shape[1]
        both[1] = half_turned(both[0])
        for q in range(cols // LANES):
            made[i, :, q * LANES : (q + 1) * LANES] = pick_pair(
                both, place[2 * q], place[2 * q + 1], left
            )
        copy_out(i).start()
    for i in range(blocks):
        copy_out(i).wait()


def finish(side, place, sums, rows, out=None):
    blocks, cols = sums[0].shape[0] // rows, sum(x.shape[1] for x in sums)
    before = [] if out is None else [out]
    return pl.pallas_call(
        functools.partial(finish_kernel, side, len(sums)),
        out_shape=jax.ShapeDtypeStruct((2 * blocks, rows, cols), jnp.bfloat16),
        in_specs=[SMEM] + [VMEM] * len(sums) + [ANY] * len(before),
        out_specs=ANY,
        scratch_shapes=[
            pltpu.VMEM((2, rows, cols), jnp.bfloat16),
            pltpu.VMEM((blocks, rows, cols), jnp.bfloat16),
            pltpu.SemaphoreType.DMA((blocks,)),
        ],
        input_output_aliases={1 + len(sums): 0} if before else {},
        compiler_params=params(),
        cost_estimate=CHEAP,
        name="finish",
    )(place, *sums, *before)


SWAP = [(0, 1), (1, 0)]


def further(x, by):
    n_cd = lax.axis_size("cd")
    return lax.ppermute(x, "cd", [(i, (i + by) % n_cd) for i in range(n_cd)])


def to_plane(x, d):
    n_cd = lax.axis_size("cd")
    z_len = 2 * lax.axis_size("zh")
    rest = z_len // n_cd
    pairs = []
    for z in range(z_len):
        group, i = divmod(z, rest)
        for y in range(n_cd):
            pairs.append((z * n_cd + y, ((y * rest + i) ^ (2 * d)) * n_cd + group))
    return lax.ppermute(x, ("zh", "zl", "cd"), pairs)


def per_device(t2_amps, integrals, ab_sym, cd_sym):
    zh, n_cd = lax.axis_size("zh"), lax.axis_size("cd")
    def over(x, axis):
        return lax.ppermute(x, axis, SWAP)

    def along_zh(x):
        return [lax.ppermute(x, "zh", [(i, i ^ d) for i in range(zh)]) for d in range(1, zh)]

    first_later = tuple(range(NSYM - LATER, NSYM - LATER + FIRST_SENT))
    own, own_later, ints_later = sort_first(t2_amps, integrals, cd_sym, ab_sym, first_later)
    later = [[ints_later] + [further(ints_later, by) for by in range(1, n_cd)]]
    syms = (tuple(range(NSYM - LATER)), tuple(range(NSYM - LATER + FIRST_SENT, NSYM)))
    place, ints, ints_later = sort_ints(integrals, ab_sym, syms, own)
    x_o, block_l = over(own, "x"), over(own, "zl")
    blocks_h = along_zh(own)
    fence = join([y[None] for y in [block_l, *blocks_h]], [*later[0][1:], ints, x_o])
    x_lh = over(fence, "x")
    blocks_hl = [over(y, "zl") for y in blocks_h]
    ints = after(ints, fence)
    sib_ints = over(ints, "core")
    ints_later = after(ints_later, fence)
    later.append([ints_later] + [further(ints_later, by) for by in range(1, n_cd)])
    near = [to_plane(after(own_later, fence), d) for d in range(1, zh)]
    near = merge([to_plane(after(own_later, sib_ints), 0)] + near, [])
    blocks = [own, *blocks_h, block_l, *blocks_hl]
    where = [(k, True, tuple((zh * (k // 2) + d, None) for d in range(zh))) for k in (0, 2)]
    before = contract(n_cd, blocks, tuple(where), ints, sib_ints, [], [])
    x_hl = [over(after(y, before[0]), "x") for y in blocks_hl]
    blocks = [x_o, x_lh, *x_hl]
    where = (
        (1, True, ((0, None),) + tuple((1, d) for d in range(1, zh))),
        (3, True, ((1, 0),) + tuple((1 + d, None) for d in range(1, zh))),
    )
    made = contract(n_cd, blocks, where, ints, sib_ints, before, [near, *later[1][1:]])
    parts = [made[0]] + [further(made[by], by) for by in range(1, n_cd)]
    up, across = over(near, "zl"), over(near, "x")
    half = zh // 2
    blocks = [near, across, up, over(up[:half], "x"), over(across[half:], "zl")]
    where = [(k, False, tuple((k, i) for i in range(zh))) for k in range(3)]
    where.append((3, False, tuple((3 + i // half, i % half) for i in range(zh))))
    ints_later = join([x[by] for by in range(n_cd) for x in later], made[:1])
    ints_later = (ints_later, over(ints_later, "core"))
    own_later, sib_later = contract_later(n_cd, blocks, tuple(where), ints_later)
    sib_later = over(sib_later, "core")
    sums, sib_sums = sum_parts(parts, own_later, t2_amps.shape[0])
    sib_sums = over(sib_sums, "core")
    rows = t2_amps.shape[0]
    out = finish(0, place, [sums], rows)
    out = finish(1, place, [sib_sums, sib_later], rows, out)
    return out.reshape(-1, out.shape[2])


def solution(mesh):
    n_blk, n_cd = mesh.devices.shape
    blk = ("zh", "zl", "x", "core")
    parted = Mesh(mesh.devices.reshape(n_blk // 8, 2, 2, 2, n_cd), blk + ("cd",))
    in_specs = (P(blk, "cd"), P(blk, None, "cd"), P(blk), P("cd"))
    return jax.shard_map(
        per_device, mesh=parted, in_specs=in_specs, out_specs=P("cd", blk), check_vma=False
    )
```

```python
import functools

import jax
import jax.numpy as jnp
from jax import lax
from jax.experimental import pallas as pl
from jax.experimental.pallas import tpu as pltpu
from jax.sharding import Mesh, PartitionSpec as P

NSYM = 8
LATER = 4
FIRST_SENT = 2
LANES = 128
VMEM_LIMIT = 20 * 2**20

ANY = pl.BlockSpec(memory_space=pl.ANY)
SMEM = pl.BlockSpec(memory_space=pltpu.SMEM)
VMEM = pl.BlockSpec(memory_space=pltpu.VMEM)

CHEAP = pl.CostEstimate(flops=1000, bytes_accessed=1000, transcendentals=0)


def params(limit=VMEM_LIMIT):
    return pltpu.CompilerParams(vmem_limit_bytes=limit)


def half_turned(x):
    half = LANES // 2
    return jnp.concatenate([x[:, half:], x[:, :half]], axis=1)


def rank_tiles(sym_ref, count_ref, order_ref, place_ref, tiles):
    for s in range(NSYM):
        count_ref[s] = s * (tiles // NSYM)

    def step(i, _):
        s = sym_ref[i]
        p = count_ref[s]
        count_ref[s] = p + 1
        order_ref[p] = i
        if place_ref is not None:
            place_ref[i] = p
        return 0

    lax.fori_loop(0, tiles, step, 0, unroll=8)


def pick_pair(both, a, b, left):
    columns = both.shape[2] // LANES
    a_col = lax.shift_right_logical(a, 1)
    b_col = lax.rem(lax.shift_right_logical(b + 1, 1) + columns - 1, columns)
    xa = both[a & 1, :, pl.ds(pl.multiple_of(a_col * LANES, LANES), LANES)]
    xb = both[(b & 1) ^ 1, :, pl.ds(pl.multiple_of(b_col * LANES, LANES), LANES)]
    return jnp.where(left, xa, xb)


def fetch_tiles(ints_ref, rows, order, syms, per_sym, sems):
    copies = []
    for sym in syms:
        for m in range(per_sym):
            p = len(copies)
            tile_ref = ints_ref.at[order[sym * per_sym + m]]
            copies.append(pltpu.make_async_copy(tile_ref, rows.at[p], sems.at[p]))
            copies[-1].start()
    return copies


def turn_tiles(rows, outs, per_sym):
    p = 0
    for out_ref in outs:
        for s in range(out_ref.shape[0]):
            tiles = rows[p : p + per_sym]
            out_ref[s] = tiles.reshape(per_sym * rows.shape[1], rows.shape[2]).T
            p += per_sym


def sort_first_kernel(syms, cd_ref, ab_ref, t2_ref, ints_ref, own_ref, later_ref, ints_out, *scratch):
    both, rows, count, order, order_ab, place, sem, sems = scratch
    load = pltpu.make_async_copy(t2_ref, both.at[0], sem)
    load.start()
    tiles = ab_ref.shape[0]
    rank_tiles(ab_ref, count, order_ab, place, tiles)
    copies = fetch_tiles(ints_ref, rows, order_ab, syms, tiles // NSYM, sems)
    rank_tiles(cd_ref, count, order, None, cd_ref.shape[0])
    load.wait()
    both[1] = half_turned(both[0])
    left = lax.broadcasted_iota(jnp.int32, (t2_ref.shape[0], LANES), 1) < LANES // 2
    q = 0
    for chunk in (own_ref, later_ref):
        for off in range(chunk.shape[1] // LANES):
            chunk[:, off * LANES : (off + 1) * LANES] = pick_pair(
                both, order[2 * q], order[2 * q + 1], left
            )
            q += 1
    for copy in copies:
        copy.wait()
    turn_tiles(rows, (ints_out,), tiles // NSYM)


def sort_first(t2, integrals, cd_sym, ab_sym, syms):
    rows, cols = t2.shape
    tiles, tile, packed = integrals.shape
    per_sym = tiles // NSYM
    return pl.pallas_call(
        functools.partial(sort_first_kernel, syms),
        out_shape=[
            jax.ShapeDtypeStruct((rows, cols // NSYM * m), t2.dtype) for m in (NSYM - LATER, LATER)
        ]
        + [jax.ShapeDtypeStruct((len(syms), packed, per_sym * tile), integrals.dtype)],
        in_specs=[SMEM, SMEM, ANY, ANY],
        out_specs=[VMEM] * 3,
        scratch_shapes=[
            pltpu.VMEM((2, rows, cols), t2.dtype),
            pltpu.VMEM((len(syms) * per_sym, tile, packed), integrals.dtype),
            pltpu.SMEM((NSYM,), jnp.int32),
            pltpu.SMEM((cd_sym.shape[0],), jnp.int32),
            pltpu.SMEM((tiles,), jnp.int32),
            pltpu.SMEM((tiles,), jnp.int32),
            pltpu.SemaphoreType.DMA,
            pltpu.SemaphoreType.DMA((len(syms) * per_sym,)),
        ],
        compiler_params=params(60 * 2**20),
        cost_estimate=CHEAP,
        name="sort_first",
    )(cd_sym, ab_sym, t2, integrals)


def sort_ints_kernel(syms, ab_ref, ints_ref, _, place, *rest):
    outs, (rows, count, order, sems) = rest[:-4], rest[-4:]
    tiles = ab_ref.shape[0]
    rank_tiles(ab_ref, count, order, place, tiles)
    every = [sym for part in syms for sym in part]
    for copy in fetch_tiles(ints_ref, rows, order, every, tiles // NSYM, sems):
        copy.wait()
    turn_tiles(rows, outs, tiles // NSYM)


def sort_ints(integrals, ab_sym, syms, earlier):
    tiles, tile, packed = integrals.shape
    per_sym = tiles // NSYM
    used = sum(len(part) for part in syms) * per_sym
    return pl.pallas_call(
        functools.partial(sort_ints_kernel, syms),
        out_shape=[jax.ShapeDtypeStruct((tiles,), jnp.int32)]
        + [
            jax.ShapeDtypeStruct((len(part), packed, per_sym * tile), integrals.dtype)
            for part in syms
        ],
        in_specs=[SMEM, ANY, ANY],
        out_specs=[SMEM] + [VMEM] * len(syms),
        scratch_shapes=[
            pltpu.VMEM((used, tile, packed), integrals.dtype),
            pltpu.SMEM((NSYM,), jnp.int32),
            pltpu.SMEM((tiles,), jnp.int32),
            pltpu.SemaphoreType.DMA((used,)),
        ],
        compiler_params=params(),
        cost_estimate=CHEAP,
        name="sort_ints",
    )(ab_sym, integrals, earlier)


def merge_kernel(n, *refs):
    blocks, out_ref = refs[:n], refs[-1]
    me = lax.axis_index("zh")
    for d, block in enumerate(blocks):
        out_ref[me ^ d] = block[...]


def merge(blocks, earlier):
    return pl.pallas_call(
        functools.partial(merge_kernel, len(blocks)),
        out_shape=jax.ShapeDtypeStruct((len(blocks),) + blocks[0].shape, blocks[0].dtype),
        in_specs=[VMEM] * len(blocks) + [ANY] * len(earlier),
        out_specs=VMEM,
        compiler_params=params(),
        cost_estimate=CHEAP,
        name="merge",
    )(*blocks, *earlier)


def nothing(*refs):
    pass


def after(x, *earlier):
    n = len(earlier)
    return pl.pallas_call(
        nothing,
        out_shape=jax.ShapeDtypeStruct(x.shape, x.dtype),
        in_specs=[ANY] * (n + 1),
        out_specs=ANY,
        input_output_aliases={n: 0},
        compiler_params=params(),
        cost_estimate=CHEAP,
        name="after",
    )(*earlier, x)


def lay_out(lhs, refs, where, place):
    h, z, x = lax.axis_index("zh"), lax.axis_index("zl"), lax.axis_index("x")
    for k, by_difference, quarter in where:
        for i, (array, entry) in enumerate(quarter):
            row = place(2 * (h ^ i if by_difference else i) + (z ^ (k // 2)), x ^ (k % 2))
            lhs[row] = refs[array][...] if entry is None else refs[array][entry]


def contract_kernel(n_cd, n_blocks, n_before, where, *refs):
    blocks, ints_refs = refs[:n_blocks], refs[n_blocks : n_blocks + 2]
    before = refs[n_blocks + 2 : n_blocks + 2 + n_before]
    outs, lhs = refs[-n_cd - 1 : -1], refs[-1]
    start = before[0].shape[1] if before else 0
    for out, ref in zip(outs, before):
        out[:, :start] = ref[...]
    z_len, rows, cols = lhs.shape
    packed, width = ints_refs[0].shape[1:]
    first = lax.axis_index("cd") * (z_len // n_cd)
    lay_out(lhs, blocks, where, lambda z, x: lax.rem(z + z_len - first, z_len))
    t2 = lhs[...].reshape(z_len * rows, cols)
    group_rows = t2.shape[0] // n_cd
    for side, ints in enumerate(ints_refs):
        for s in range(cols // packed):
            part = jnp.dot(
                t2[:, s * packed : (s + 1) * packed], ints[s], preferred_element_type=jnp.float32
            ).astype(outs[0].dtype)
            for by in range(n_cd):
                outs[by][side, start:, s * width : (s + 1) * width] = part[
                    by * group_rows : (by + 1) * group_rows
                ]


def contract(n_cd, blocks, where, ints, sib_ints, before, earlier):
    rows, cols = blocks[0].shape[-2:]
    z_len = 2 * len(where[0][2])
    packed, width = ints.shape[1:]
    start = before[0].shape[1] if before else 0
    out = (2, start + z_len * rows // n_cd, cols // packed * width)
    return pl.pallas_call(
        functools.partial(contract_kernel, n_cd, len(blocks), len(before), where),
        out_shape=[jax.ShapeDtypeStruct(out, jnp.bfloat16)] * n_cd,
        in_specs=[VMEM] * (len(blocks) + 2 + len(before)) + [ANY] * len(earlier),
        out_specs=[VMEM] * n_cd,
        scratch_shapes=[pltpu.VMEM((z_len, rows, cols), jnp.bfloat16)],
        compiler_params=params(),
        cost_estimate=CHEAP,
        name="contract",
    )(*blocks, ints, sib_ints, *before, *earlier)


def total(parts):
    value = parts[0].astype(jnp.float32)
    for part in parts[1:]:
        value += part.astype(jnp.float32)
    return value.astype(jnp.bfloat16)


def join_kernel(n, *refs):
    out_ref, first = refs[-1], 0
    for ref in refs[-n - 1 : -1]:
        out_ref[first : first + ref.shape[0]] = ref[...]
        first += ref.shape[0]


def join(arrays, earlier):
    n = len(arrays)
    out = (sum(x.shape[0] for x in arrays), *arrays[0].shape[1:])
    return pl.pallas_call(
        functools.partial(join_kernel, n),
        out_shape=jax.ShapeDtypeStruct(out, arrays[0].dtype),
        in_specs=[ANY] * len(earlier) + [VMEM] * n,
        out_specs=VMEM,
        compiler_params=params(),
        cost_estimate=CHEAP,
        name="join",
    )(*earlier, *arrays)


def later_kernel(n_cd, n_blocks, where, *refs):
    blocks, ints = refs[:n_blocks], refs[n_blocks : n_blocks + 2]
    own_out, sib_out, lhs = refs[-3:]
    slots, rows, cols = lhs.shape
    packed, width = ints[0].shape[1:]
    per_group, me = slots // n_cd, lax.axis_index("cd")

    def place(z, x):
        n = 2 * z + x
        group = lax.div(n, per_group)
        return lax.rem(me + n_cd - group, n_cd) * per_group + (n - group * per_group)

    lay_out(lhs, blocks, where, place)
    t2 = lhs[...].reshape(n_cd, per_group * rows, cols)
    for side, out_ref in enumerate((own_out, sib_out)):
        for s in range(LATER):
            out_ref[:, s * width : (s + 1) * width] = total(
                [
                    jnp.dot(
                        t2[by, :, s * packed : (s + 1) * packed],
                        ints[side][by * LATER + s],
                        preferred_element_type=jnp.float32,
                    ).astype(out_ref.dtype)
                    for by in range(n_cd)
                ]
            )


def contract_later(n_cd, blocks, where, ints):
    rows, cols = blocks[0].shape[-2:]
    slots = 4 * len(where[0][2])
    out = (slots * rows // n_cd, ints[0].shape[2] * LATER)
    return pl.pallas_call(
        functools.partial(later_kernel, n_cd, len(blocks), where),
        out_shape=[jax.ShapeDtypeStruct(out, jnp.bfloat16)] * 2,
        in_specs=[VMEM] * (len(blocks) + 2),
        out_specs=[VMEM] * 2,
        scratch_shapes=[pltpu.VMEM((slots, rows, cols), jnp.bfloat16)],
        compiler_params=params(),
        cost_estimate=CHEAP,
        name="contract_later",
    )(*blocks, *ints)


def sum_kernel(rows, *refs):
    parts, later, outs = refs[:-3], refs[-3], refs[-2:]
    x = lax.axis_index("x")
    half_rows = parts[0].shape[1] // 2
    first = parts[0].shape[2]
    for side, out_ref in enumerate(outs):
        if not side:
            out_ref[:, first:] = later[...]
        for half in range(2):
            for z in range(half_rows // rows):
                these = pl.ds(pl.multiple_of((2 * z + (x ^ half)) * rows, rows), rows)
                at = half * half_rows + z * rows
                out_ref[these, :first] = total([part[side, at : at + rows] for part in parts])


def sum_parts(parts, later, rows):
    rows_out, cols = parts[0].shape[1:]
    return pl.pallas_call(
        functools.partial(sum_kernel, rows),
        out_shape=[
            jax.ShapeDtypeStruct((rows_out, cols + later.shape[1]), jnp.bfloat16),
            jax.ShapeDtypeStruct((rows_out, cols), jnp.bfloat16),
        ],
        in_specs=[VMEM] * (len(parts) + 1),
        out_specs=[VMEM] * 2,
        compiler_params=params(),
        cost_estimate=CHEAP,
        name="sum_parts",
    )(*parts, later)


def finish_kernel(side, n_sums, place, *rest):
    sums = rest[:n_sums]
    out_ref, both, made, sems = rest[-4:]
    blocks, rows, cols = made.shape
    step = rows // 2
    left = lax.broadcasted_iota(jnp.int32, (step, LANES), 1) < LANES // 2

    def copy_out(i, at):
        block, these = 2 * i + (lax.axis_index("core") ^ side), pl.ds(at, step)
        source, target = made.at[i, these], out_ref.at[block, these]
        return pltpu.make_async_copy(source, target, sems.at[2 * i + at // step])

    pieces = [(i, at) for i in range(blocks) for at in (0, step)]
    for i, at in pieces:
        first = 0
        for ref in sums:
            these = slice(i * rows + at, i * rows + at + step)
            both[0, :, first : first + ref.shape[1]] = ref[these]
            first += ref.shape[1]
        both[1] = half_turned(both[0])
        for q in range(cols // LANES):
            made[i, at : at + step, q * LANES : (q + 1) * LANES] = pick_pair(
                both, place[2 * q], place[2 * q + 1], left
            )
        copy_out(i, at).start()
    for i, at in pieces:
        copy_out(i, at).wait()


def finish(side, place, sums, rows, out=None):
    blocks, cols = sums[0].shape[0] // rows, sum(x.shape[1] for x in sums)
    before = [] if out is None else [out]
    return pl.pallas_call(
        functools.partial(finish_kernel, side, len(sums)),
        out_shape=jax.ShapeDtypeStruct((2 * blocks, rows, cols), jnp.bfloat16),
        in_specs=[SMEM] + [VMEM] * len(sums) + [ANY] * len(before),
        out_specs=ANY,
        scratch_shapes=[
            pltpu.VMEM((2, rows // 2, cols), jnp.bfloat16),
            pltpu.VMEM((blocks, rows, cols), jnp.bfloat16),
            pltpu.SemaphoreType.DMA((2 * blocks,)),
        ],
        input_output_aliases={1 + len(sums): 0} if before else {},
        compiler_params=params(),
        cost_estimate=CHEAP,
        name="finish",
    )(place, *sums, *before)


SWAP = [(0, 1), (1, 0)]


def further(x, by):
    n_cd = lax.axis_size("cd")
    return lax.ppermute(x, "cd", [(i, (i + by) % n_cd) for i in range(n_cd)])


def to_plane(x, d):
    n_cd = lax.axis_size("cd")
    z_len = 2 * lax.axis_size("zh")
    rest = z_len // n_cd
    pairs = []
    for z in range(z_len):
        group, i = divmod(z, rest)
        for y in range(n_cd):
            pairs.append((z * n_cd + y, ((y * rest + i) ^ (2 * d)) * n_cd + group))
    return lax.ppermute(x, ("zh", "zl", "cd"), pairs)


def per_device(t2_amps, integrals, ab_sym, cd_sym):
    zh, n_cd = lax.axis_size("zh"), lax.axis_size("cd")
    def over(x, axis):
        return lax.ppermute(x, axis, SWAP)

    def along_zh(x):
        return [lax.ppermute(x, "zh", [(i, i ^ d) for i in range(zh)]) for d in range(1, zh)]

    first_later = tuple(range(NSYM - LATER, NSYM - LATER + FIRST_SENT))
    own, own_later, ints_later = sort_first(t2_amps, integrals, cd_sym, ab_sym, first_later)
    later = [[ints_later] + [further(ints_later, by) for by in range(1, n_cd)]]
    syms = (tuple(range(NSYM - LATER)), tuple(range(NSYM - LATER + FIRST_SENT, NSYM)))
    place, ints, ints_later = sort_ints(integrals, ab_sym, syms, own)
    x_o, block_l = over(own, "x"), over(own, "zl")
    blocks_h = along_zh(own)
    fence = join([y[None] for y in [block_l, *blocks_h]], [*later[0][1:], ints, x_o])
    x_lh = over(fence, "x")
    blocks_hl = [over(y, "zl") for y in blocks_h]
    ints = after(ints, fence)
    sib_ints = over(ints, "core")
    ints_later = after(ints_later, fence)
    later.append([ints_later] + [further(ints_later, by) for by in range(1, n_cd)])
    near = [to_plane(after(own_later, fence), d) for d in range(1, zh)]
    near = merge([to_plane(after(own_later, sib_ints), 0)] + near, [])
    blocks = [own, *blocks_h, block_l, *blocks_hl]
    where = [(k, True, tuple((zh * (k // 2) + d, None) for d in range(zh))) for k in (0, 2)]
    before = contract(n_cd, blocks, tuple(where), ints, sib_ints, [], [])
    x_hl = [over(after(y, before[0]), "x") for y in blocks_hl]
    blocks = [x_o, x_lh, *x_hl]
    where = (
        (1, True, ((0, None),) + tuple((1, d) for d in range(1, zh))),
        (3, True, ((1, 0),) + tuple((1 + d, None) for d in range(1, zh))),
    )
    made = contract(n_cd, blocks, where, ints, sib_ints, before, [near, *later[1][1:]])
    parts = [made[0]] + [further(made[by], by) for by in range(1, n_cd)]
    up, across = over(near, "zl"), over(near, "x")
    half = zh // 2
    blocks = [near, across, up, over(up[:half], "x"), over(across[half:], "zl")]
    where = [(k, False, tuple((k, i) for i in range(zh))) for k in range(3)]
    where.append((3, False, tuple((3 + i // half, i % half) for i in range(zh))))
    ints_later = join([x[by] for by in range(n_cd) for x in later], made[:1])
    ints_later = (ints_later, over(ints_later, "core"))
    own_later, sib_later = contract_later(n_cd, blocks, tuple(where), ints_later)
    sib_later = over(sib_later, "core")
    sums, sib_sums = sum_parts(parts, own_later, t2_amps.shape[0])
    sib_sums = over(sib_sums, "core")
    rows = t2_amps.shape[0]
    out = finish(0, place, [sums], rows)
    out = finish(1, place, [sib_sums, sib_later], rows, out)
    return out.reshape(-1, out.shape[2])


def solution(mesh):
    n_blk, n_cd = mesh.devices.shape
    blk = ("zh", "zl", "x", "core")
    parted = Mesh(mesh.devices.reshape(n_blk // 8, 2, 2, 2, n_cd), blk + ("cd",))
    in_specs = (P(blk, "cd"), P(blk, None, "cd"), P(blk), P("cd"))
    return jax.shard_map(
        per_device, mesh=parted, in_specs=in_specs, out_specs=P("cd", blk), check_vma=False
    )
```
